32 devices in a mesh: dp: 8 (over y, x, core), seq: 4 (over z).
Axes of the slice: x: 2, y: 2, z: 4, core: 2. Of those that a mesh axis runs over, the one named last changes fastest.
Arguments:
- text: bfloat16 [64, 128, 768], P('dp', 'seq'), may hold values from -6 to 6
- image: bfloat16 [64, 128, 1024], P('dp', 'seq'), may hold values from -6 to 6
- text_len: int32 [64], P('dp'), may hold values from 72 to 128, as said below
- region_count: int32 [64], P('dp'), may hold values from 10 to 100, as said below
- text_cot: bfloat16 [64, 128, 768], P('dp', 'seq'), may hold values from -8 to 8
- image_cot: bfloat16 [64, 128, 1024], P('dp', 'seq'), may hold values from -8 to 8
- selfproject: bfloat16 [768, 3, 768], P('dp'), may hold values from -0.21875 to 0.21875
- selfbiases: bfloat16 [2, 768], P(None, 'dp'), may hold values from -1.25 to 1.25
- selfoutput: bfloat16 [768, 768], P('dp'), may hold values from -0.875 to 0.875
- textcoproject: bfloat16 [768, 3, 1024], P('dp'), may hold values from -0.21875 to 0.21875
- textcobiases: bfloat16 [2, 1024], P(None, 'dp'), may hold values from -1.25 to 1.25
- imagecoproject: bfloat16 [1024, 3, 1024], P('dp'), may hold values from -0.1875 to 0.1875
- imagecobiases: bfloat16 [2, 1024], P(None, 'dp'), may hold values from -1.25 to 1.25
- textcooutput: bfloat16 [1024, 768], P('dp'), may hold values from -0.5 to 0.5
- imagecooutput: bfloat16 [1024, 1024], P('dp'), may hold values from -0.75 to 0.75
- textffinner: bfloat16 [768, 3072], P('dp'), may hold values from -0.21875 to 0.21875
- textffinbias: bfloat16 [3072], P('dp'), may hold values from -1.25 to 1.25
- textffouter: bfloat16 [3072, 768], P('dp'), may hold values from -0.109375 to 0.109375
- imageffinner: bfloat16 [1024, 1024], P('dp'), may hold values from -0.1875 to 0.1875
- imageffinbias: bfloat16 [1024], P('dp'), may hold values from -1.25 to 1.25
- imageffouter: bfloat16 [1024, 1024], P('dp'), may hold values from -0.1875 to 0.1875
- textgains: bfloat16 [3, 768], P(None, 'dp'), may hold values from 0.5 to 1.5
- textshifts: bfloat16 [3, 768], P(None, 'dp'), may hold values from -1.25 to 1.25
- textbiases: bfloat16 [3, 768], P(None, 'dp'), may hold values from -1.25 to 1.25
- imagegains: bfloat16 [2, 1024], P(None, 'dp'), may hold values from 0.5 to 1.5
- imageshifts: bfloat16 [2, 1024], P(None, 'dp'), may hold values from -1.25 to 1.25
- imagebiases: bfloat16 [2, 1024], P(None, 'dp'), may hold values from -1.25 to 1.25
Outputs:
- text_out: bfloat16 [64, 128, 768], P('dp', 'seq')
- image_out: bfloat16 [64, 128, 1024], P('dp', 'seq')
- text_grad: bfloat16 [64, 128, 768], P('dp', 'seq')
- image_grad: bfloat16 [64, 128, 1024], P('dp', 'seq')
- grad_selfproject: float32 [768, 3, 768], P('dp')
- grad_selfbiases: float32 [2, 768], P(None, 'dp')
- grad_selfoutput: float32 [768, 768], P('dp')
- grad_textcoproject: float32 [768, 3, 1024], P('dp')
- grad_textcobiases: float32 [2, 1024], P(None, 'dp')
- grad_imagecoproject: float32 [1024, 3, 1024], P('dp')
- grad_imagecobiases: float32 [2, 1024], P(None, 'dp')
- grad_textcooutput: float32 [1024, 768], P('dp')
- grad_imagecooutput: float32 [1024, 1024], P('dp')
- grad_textffinner: float32 [768, 3072], P('dp')
- grad_textffinbias: float32 [3072], P('dp')
- grad_textffouter: float32 [3072, 768], P('dp')
- grad_imageffinner: float32 [1024, 1024], P('dp')
- grad_imageffinbias: float32 [1024], P('dp')
- grad_imageffouter: float32 [1024, 1024], P('dp')
- grad_textgains: float32 [3, 768], P(None, 'dp')
- grad_textshifts: float32 [3, 768], P(None, 'dp')
- grad_textbiases: float32 [3, 768], P(None, 'dp')
- grad_imagegains: float32 [2, 1024], P(None, 'dp')
- grad_imageshifts: float32 [2, 1024], P(None, 'dp')
- grad_imagebiases: float32 [2, 1024], P(None, 'dp')
The draws below stay inside these ranges and needn't reach their ends.
Inputs may be any that keep to these rules, and one draw needn't show every extreme that they name: Each pair's caption fills its first text_len slots of 128; in every aligned block of 8 pairs (those of one index of dp) one caption fills all 128 slots. Each pair's regions fill its first region_count slots of 128; in every aligned block of 8 pairs one image has 100 regions.
All inputs are finite; a program needn't handle non-finite values.
Results may differ from the reference program's by a relative error of at most 0.023.
Values may be sent and summed in bfloat16 or wider, within the bound.
A program may use at most 256 MiB of HBM per device.

```python
import jax
import jax.numpy as jnp
from jax import lax

DT = 768
HT = 12
FT = 3072
DV = 1024
FV = 1024
DC = 1024
HC = 8
CAP = 128
RSLOT = 128
PAIRS_DEV = 8
PAIRS = 64


def mark_blocks(key, values, highest):
    chosen = jax.random.randint(key, (PAIRS // PAIRS_DEV,), 0, PAIRS_DEV)
    places = jnp.arange(PAIRS)
    owners = jnp.take(chosen, places // PAIRS_DEV)
    return jnp.where(places % PAIRS_DEV == owners, highest, values).astype(jnp.int32)


def draw_text_len(key, part):
    key = jax.random.fold_in(key, 11)
    spread_key, pick_key = jax.random.split(key)
    lengths = jax.random.randint(spread_key, (PAIRS,), CAP * 9 // 16, CAP + 1)
    return mark_blocks(pick_key, lengths, CAP)


def draw_region_count(key, part):
    key = jax.random.fold_in(key, 23)
    first_key, second_key, pick_key = jax.random.split(key, 3)
    lowest = RSLOT * 5 // 64
    highest = RSLOT * 25 // 32
    spread = highest - lowest
    factor_one = jax.random.randint(first_key, (PAIRS,), 0, spread + 1)
    factor_two = jax.random.randint(second_key, (PAIRS,), 0, spread + 1)
    return mark_blocks(pick_key, lowest + factor_one * factor_two // spread, highest)


def with_spikes(entries, rng, source, target, parts, factor):
    def block_of(position):
        return (jnp.arange(entries.shape[position]) // (entries.shape[position] // parts)).reshape((-1,) + (1,) * (entries.ndim - 1 - position))

    one_side = jax.random.permutation(rng, parts)[block_of(target)]
    second = (block_of(target) + parts // 2) % parts
    return jnp.where((block_of(source) == one_side) | (block_of(source) == second), factor * entries, entries)


def block_levels(own_key, extent, cuts, low, top_value):
    def one(position, shards_of):
        steps = jax.random.uniform(jax.random.fold_in(jax.random.fold_in(own_key, 6), position), (shards_of,), jnp.float32, low / len(cuts), top_value / len(cuts))
        return jnp.repeat(jnp.exp(steps), extent[position] // shards_of).reshape((-1,) + (1,) * (len(extent) - position - 1))

    loudness = one(*cuts[0])
    for cut in cuts[1:]:
        loudness = loudness * one(*cut)
    return loudness


def normal_values(rng, shape, width, most, cuts=(), dtype=jnp.bfloat16):
    gain = block_levels(rng, shape, cuts, -0.22, 0.18) if cuts else 1.0
    array = jax.random.normal(rng, shape, jnp.float32) * width * gain
    return jnp.minimum(jnp.maximum(array, -most), most).astype(dtype)


def gaussian_with(own_key, shape, scale, bound, cuts, heavy, held_as=jnp.bfloat16):
    array = scale * jax.random.normal(own_key, shape, jnp.float32)
    if cuts:
        array = array * block_levels(own_key, shape, cuts, -0.22, 0.18)
    return jnp.clip(with_spikes(array, jax.random.fold_in(own_key, 3), *heavy), -bound, bound).astype(held_as)


def setup_inputs(seed: int = 0) -> dict:
    seeds = jax.random.split(jax.random.key(seed), 28)
    text = normal_values(seeds[0], (PAIRS, CAP, DT), 1.0, 6.0, ((0, 8), (1, 4)))
    image = normal_values(seeds[1], (PAIRS, RSLOT, DV), 1.0, 6.0, ((0, 8), (1, 4)))
    text_len = draw_text_len(jax.random.fold_in(seeds[27], 71), 0)
    region_count = draw_region_count(jax.random.fold_in(seeds[27], 71), 0)
    text_cot = gaussian_with(seeds[4], (PAIRS, CAP, DT), 1.0, 8.0, ((0, 8), (1, 4)), (0, 2, 8, 2.0))
    image_cot = gaussian_with(seeds[5], (PAIRS, RSLOT, DV), 1.0, 8.0, ((0, 8), (1, 4)), (0, 2, 8, 2.0))
    selfproject = normal_values(seeds[6], (DT, 3, DT), DT ** -0.5, 0.21875, ((0, 8),))
    selfbiases = normal_values(seeds[7], (2, DT), 0.2, 1.25, ((1, 8),))
    selfoutput = normal_values(seeds[8], (DT, DT), (DT // 16) ** -0.5, 0.875, ((0, 8),))
    textcoproject = normal_values(seeds[9], (DT, 3, DC), DT ** -0.5, 0.21875, ((0, 8),))
    textcobiases = normal_values(seeds[10], (2, DC), 0.2, 1.25, ((1, 8),))
    imagecoproject = normal_values(seeds[11], (DV, 3, DC), DV ** -0.5, 0.1875, ((0, 8),))
    imagecobiases = normal_values(seeds[12], (2, DC), 0.2, 1.25, ((1, 8),))
    textcooutput = normal_values(seeds[13], (DC, DT), (DC // 8) ** -0.5, 0.5, ((0, 8),))
    imagecooutput = normal_values(seeds[14], (DC, DV), (DC // 16) ** -0.5, 0.75, ((0, 8),))
    textffinner = normal_values(seeds[15], (DT, FT), DT ** -0.5, 0.21875, ((0, 8),))
    textffinbias = normal_values(seeds[16], (FT,), 0.2, 1.25, ((0, 8),))
    textffouter = normal_values(seeds[17], (FT, DT), FT ** -0.5, 0.109375, ((0, 8),))
    imageffinner = normal_values(seeds[18], (DV, FV), DV ** -0.5, 0.1875, ((0, 8),))
    imageffinbias = normal_values(seeds[19], (FV,), 0.2, 1.25, ((0, 8),))
    imageffouter = normal_values(seeds[20], (FV, DV), FV ** -0.5, 0.1875, ((0, 8),))
    textgains = jnp.clip(1.0 + 0.1 * jax.random.normal(seeds[21], (3, DT), jnp.float32), 0.5, 1.5).astype(jnp.bfloat16)
    textshifts = normal_values(seeds[22], (3, DT), 0.2, 1.25, ((1, 8),))
    textbiases = normal_values(seeds[23], (3, DT), 0.2, 1.25, ((1, 8),))
    imagegains = jnp.clip(1.0 + 0.1 * jax.random.normal(seeds[24], (2, DV), jnp.float32), 0.5, 1.5).astype(jnp.bfloat16)
    imageshifts = normal_values(seeds[25], (2, DV), 0.2, 1.25, ((1, 8),))
    imagebiases = normal_values(seeds[26], (2, DV), 0.2, 1.25, ((1, 8),))
    return dict(text=text, image=image, text_len=text_len, region_count=region_count, text_cot=text_cot, image_cot=image_cot, selfproject=selfproject, selfbiases=selfbiases, selfoutput=selfoutput, textcoproject=textcoproject, textcobiases=textcobiases, imagecoproject=imagecoproject, imagecobiases=imagecobiases, textcooutput=textcooutput, imagecooutput=imagecooutput, textffinner=textffinner, textffinbias=textffinbias, textffouter=textffouter, imageffinner=imageffinner, imageffinbias=imageffinbias, imageffouter=imageffouter, textgains=textgains, textshifts=textshifts, textbiases=textbiases, imagegains=imagegains, imageshifts=imageshifts, imagebiases=imagebiases)


EPSILON = 1e-05
NEG_FILL = -1e+30
PRECISE = lax.Precision.HIGHEST

@jax.custom_vjp
def low(v):
    return lax.optimization_barrier(v.astype(jnp.bfloat16)).astype(jnp.float32)

@jax.custom_vjp
def low_back(v):
    return v

def low_keep(v):
    return (low(v), None)

def low_pass(kept, grad):
    return (grad,)

def back_keep(v):
    return (v, None)

def back_low(kept, grad):
    return (low(grad),)
low.defvjp(low_keep, low_pass)
low_back.defvjp(back_keep, back_low)

def both_round(values):
    return low(low_back(values))

def layer_norm(hidden, factor, offset):
    centre = hidden - lax.optimization_barrier(jnp.mean(hidden, axis=-1, keepdims=True))
    spread = lax.optimization_barrier(jnp.mean(centre * centre, axis=-1, keepdims=True))
    return centre * lax.rsqrt(spread + EPSILON) * factor + offset

def linear(inputs, weight):
    return jnp.einsum('pte,ef->ptf', inputs, weight, precision=PRECISE)

def project(inputs, weight, biases):
    stacked = jnp.stack([biases[0], jnp.zeros_like(biases[0]), biases[1]])
    return both_round(jnp.einsum('pte,ekf->ptkf', inputs, weight, precision=PRECISE) + stacked)

def split_heads(values, head_count):
    return values.reshape(values.shape[0], values.shape[1], head_count, values.shape[2] // head_count)

def attention(queries, keyvals, keymask, head_count):
    query_heads = split_heads(queries, head_count)
    key_heads = split_heads(keyvals[:, :, 0], head_count)
    value_heads = split_heads(keyvals[:, :, 1], head_count)
    shrink = query_heads.shape[-1] ** (-0.5)
    scores = low_back(jnp.einsum('pthd,pshd->phts', query_heads, key_heads, precision=PRECISE) * shrink)
    scores = jnp.where(keymask[:, None, None, :], scores, NEG_FILL)
    highest = lax.optimization_barrier(jnp.max(scores, axis=-1, keepdims=True))
    powers = jnp.exp(scores - highest)
    prob_table = low(powers / lax.optimization_barrier(jnp.sum(powers, axis=-1, keepdims=True)))
    mixture = jnp.einsum('phts,pshd->pthd', prob_table, value_heads, precision=PRECISE)
    return both_round(mixture.reshape(queries.shape))

def feed_forward(inputs, weight_in, bias_in, weight_out, bias_out, factor, offset):
    inner_sum = low_back(linear(inputs, weight_in) + bias_in)
    active = low(jax.nn.gelu(inner_sum, approximate=False))
    branch = low_back(linear(active, weight_out) + bias_out)
    return layer_norm(inputs + branch, factor, offset)

def forward(text, image, weights, text_mask, region_mask):
    selfproject, selfbiases, selfoutput, textcoproject, textcobiases, imagecoproject, imagecobiases, textcooutput, imagecooutput, textffinner, textffinbias, textffouter, imageffinner, imageffinbias, imageffouter, textgains, textshifts, textbiases, imagegains, imageshifts, imagebiases = weights
    self_triple = project(text, selfproject, selfbiases)
    self_mixed = attention(self_triple[:, :, 0], self_triple[:, :, 1:], text_mask, HT)
    self_branch = low_back(linear(self_mixed, selfoutput) + textbiases[0])
    text_one = low(layer_norm(text + self_branch, textgains[0], textshifts[0]))
    text_triple = project(text_one, textcoproject, textcobiases)
    image_triple = project(image, imagecoproject, imagecobiases)
    text_mixed = attention(text_triple[:, :, 0], image_triple[:, :, 1:], region_mask, HC)
    image_mixed = attention(image_triple[:, :, 0], text_triple[:, :, 1:], text_mask, HC)
    text_branch = low_back(linear(text_mixed, textcooutput) + textbiases[1])
    text_two = low(layer_norm(text_one + text_branch, textgains[1], textshifts[1]))
    image_branch = low_back(linear(image_mixed, imagecooutput) + imagebiases[0])
    image_two = low(layer_norm(image + image_branch, imagegains[0], imageshifts[0]))
    text_three = feed_forward(text_two, textffinner, textffinbias, textffouter, textbiases[2], textgains[2], textshifts[2])
    image_three = feed_forward(image_two, imageffinner, imageffinbias, imageffouter, imagebiases[1], imagegains[1], imageshifts[1])
    return (text_three, image_three)

def reference(text, image, text_len, region_count, text_cot, image_cot, selfproject, selfbiases, selfoutput, textcoproject, textcobiases, imagecoproject, imagecobiases, textcooutput, imagecooutput, textffinner, textffinbias, textffouter, imageffinner, imageffinbias, imageffouter, textgains, textshifts, textbiases, imagegains, imageshifts, imagebiases):
    weights = tuple((element.astype(jnp.float32) for element in (selfproject, selfbiases, selfoutput, textcoproject, textcobiases, imagecoproject, imagecobiases, textcooutput, imagecooutput, textffinner, textffinbias, textffouter, imageffinner, imageffinbias, imageffouter, textgains, textshifts, textbiases, imagegains, imageshifts, imagebiases)))
    group_count = PAIRS // PAIRS_DEV

    def regroup(values):
        return values.reshape((group_count, PAIRS_DEV) + values.shape[1:])
    stacked = (regroup(text.astype(jnp.float32)), regroup(image.astype(jnp.float32)), regroup(text_len), regroup(region_count), regroup(text_cot.astype(jnp.float32)), regroup(image_cot.astype(jnp.float32)))

    def group_step(totals, group_data):
        text_part, image_part, lengths, counts, text_back, image_back = group_data
        text_mask = jnp.arange(CAP)[None, :] < lengths[:, None]
        region_mask = jnp.arange(RSLOT)[None, :] < counts[:, None]

        def run_layer(text_arg, image_arg, weight_arg):
            return forward(text_arg, image_arg, weight_arg, text_mask, region_mask)
        outputs, pullback = jax.vjp(run_layer, text_part, image_part, weights)
        text_back_grad, image_back_grad, weight_grads = pullback((text_back, image_back))
        totals = jax.tree.map(jnp.add, totals, weight_grads)
        return (totals, (outputs[0].astype(jnp.bfloat16), outputs[1].astype(jnp.bfloat16), text_back_grad.astype(jnp.bfloat16), image_back_grad.astype(jnp.bfloat16)))
    zero_grads = jax.tree.map(jnp.zeros_like, weights)
    totals, row_lists = lax.scan(group_step, zero_grads, stacked)

    def flatten(values):
        return values.reshape((PAIRS,) + values.shape[2:])
    return (flatten(row_lists[0]), flatten(row_lists[1]), flatten(row_lists[2]), flatten(row_lists[3]), totals[0], totals[1], totals[2], totals[3], totals[4], totals[5], totals[6], totals[7], totals[8], totals[9], totals[10], totals[11], totals[12], totals[13], totals[14], totals[15], totals[16], totals[17], totals[18], totals[19], totals[20])
```

```python
import functools

import jax
import jax.numpy as jnp
from jax import lax
from jax.experimental import pallas as pl
from jax.experimental.pallas import tpu as pltpu
from jax.sharding import PartitionSpec as P

HT = 12
HC = 8
MB = 2


EPSILON = 1e-05
NEG_FILL = -1e30


def layer_norm(hidden, factor, offset):
    centre = hidden - jnp.mean(hidden, axis=-1, keepdims=True)
    spread = jnp.mean(centre * centre, axis=-1, keepdims=True)
    return centre * lax.rsqrt(spread + EPSILON) * factor + offset


def norm_back(hidden, factor, offset, upstream):
    outcome, pullback = jax.vjp(layer_norm, hidden, factor, offset)
    return pullback(upstream)


def gelu_exact(hidden):
    return jax.nn.gelu(hidden, approximate=False)


def gelu_back(hidden, upstream):
    outcome, pullback = jax.vjp(gelu_exact, hidden)
    return pullback(upstream)[0]


def linear(inputs, weight):
    return jnp.einsum("pte,ef->ptf", inputs, weight, preferred_element_type=jnp.float32)


def linear_weight(inputs, gradient):
    return jnp.einsum("pte,ptf->ef", inputs, gradient, preferred_element_type=jnp.float32)


def linear_input(gradient, weight):
    return jnp.einsum("ptf,ef->pte", gradient, weight, preferred_element_type=jnp.float32)


def row_total(gradient):
    return jnp.sum(gradient, axis=(0, 1), dtype=jnp.float32)


def project(inputs, weight, biases):
    bias_rows = biases.astype(jnp.float32)
    stacked = jnp.stack([bias_rows[0], jnp.zeros_like(bias_rows[0]), bias_rows[1]])
    triple = jnp.einsum("pte,ekf->ptkf", inputs, weight, preferred_element_type=jnp.float32)
    return (triple + stacked).astype(jnp.bfloat16)


def project_back(inputs, gradient, weight):
    weight_grad = jnp.einsum("pte,ptkf->ekf", inputs, gradient, preferred_element_type=jnp.float32)
    totals = row_total(gradient)
    input_grad = jnp.einsum("ptkf,ekf->pte", gradient, weight, preferred_element_type=jnp.float32)
    return (weight_grad, jnp.stack([totals[0], totals[2]]), input_grad)


def split_heads(values, head_count):
    return values.reshape(
        values.shape[0], values.shape[1], head_count, values.shape[2] // head_count
    )


def score_table(queries, keyvals, keymask, head_count):
    query_heads = split_heads(queries, head_count)
    key_heads = split_heads(keyvals[:, :, 0], head_count)
    shrink = query_heads.shape[-1] ** (-0.5)
    scores = (
        jnp.einsum("pthd,pshd->phts", query_heads, key_heads, preferred_element_type=jnp.float32)
        * shrink
    )
    scores = jnp.where(keymask[:, None, None, :], scores, NEG_FILL)
    return (scores, query_heads, key_heads, shrink)


def attend(queries, keyvals, keymask, head_count):
    scores, query_heads, key_heads, shrink = score_table(queries, keyvals, keymask, head_count)
    highest = jnp.max(scores, axis=-1, keepdims=True)
    powers = jnp.exp(scores - highest)
    totals = jnp.sum(powers, axis=-1, keepdims=True)
    prob_table = (powers / totals).astype(jnp.bfloat16)
    value_heads = split_heads(keyvals[:, :, 1], head_count)
    mixture = jnp.einsum(
        "phts,pshd->pthd", prob_table, value_heads, preferred_element_type=jnp.float32
    )
    return (mixture.reshape(queries.shape).astype(jnp.bfloat16), highest + jnp.log(totals))


def attend_back(upstream, queries, keyvals, keymask, logsum, head_count):
    scores, query_heads, key_heads, shrink = score_table(queries, keyvals, keymask, head_count)
    prob_table = jnp.exp(scores - logsum)
    value_heads = split_heads(keyvals[:, :, 1], head_count)
    upper_heads = split_heads(upstream, head_count)
    value_grad = jnp.einsum(
        "phts,pthd->pshd",
        prob_table.astype(jnp.bfloat16),
        upper_heads,
        preferred_element_type=jnp.float32,
    )
    prob_grad = jnp.einsum(
        "pthd,pshd->phts", upper_heads, value_heads, preferred_element_type=jnp.float32
    )
    score_grad = prob_table * (prob_grad - jnp.sum(prob_grad * prob_table, axis=-1, keepdims=True))
    score_grad = score_grad.astype(jnp.bfloat16)
    query_grad = (
        jnp.einsum("phts,pshd->pthd", score_grad, key_heads, preferred_element_type=jnp.float32)
        * shrink
    )
    key_grad = (
        jnp.einsum("phts,pthd->pshd", score_grad, query_heads, preferred_element_type=jnp.float32)
        * shrink
    )
    keyval_grad = jnp.stack([key_grad, value_grad], axis=2).reshape(keyvals.shape)
    return (query_grad.reshape(queries.shape), keyval_grad)


def feed_forward(inputs, weight_in, bias_in, weight_out, bias_out):
    inner_sum = linear(inputs, weight_in) + bias_in.astype(jnp.float32)
    active = gelu_exact(inner_sum).astype(jnp.bfloat16)
    totals = inputs.astype(jnp.float32) + linear(active, weight_out) + bias_out
    return (inner_sum, active, totals)


def feed_back(upstream, inputs, inner_sum, active, totals, factor, offset, weight_in, weight_out):
    sum_grad, factor_grad, offset_grad = norm_back(totals, factor, offset, upstream)
    branch_grad = sum_grad.astype(jnp.bfloat16)
    outer_grad = linear_weight(active, branch_grad)
    outbias_grad = row_total(branch_grad)
    active_grad = linear_input(branch_grad, weight_out)
    inner_grad = gelu_back(inner_sum, active_grad).astype(jnp.bfloat16)
    weightin_grad = linear_weight(inputs, inner_grad)
    inbias_grad = row_total(inner_grad)
    input_grad = linear_input(inner_grad, weight_in) + sum_grad
    return (
        input_grad,
        weightin_grad,
        inbias_grad,
        outer_grad,
        outbias_grad,
        factor_grad,
        offset_grad,
    )


def micro_step(
    fetched, text, image, text_len, region_count, text_cot, image_cot, caption_slots, region_slots
):
    (
        selfproject,
        selfbiases,
        selfoutput,
        textcoproject,
        textcobiases,
        imagecoproject,
        imagecobiases,
        textcooutput,
        imagecooutput,
        textffinner,
        textffinbias,
        textffouter,
        imageffinner,
        imageffinbias,
        imageffouter,
        textgains,
        textshifts,
        textbiases,
        imagegains,
        imageshifts,
        imagebiases,
    ) = fetched
    text_factor = textgains.astype(jnp.float32)
    text_offset = textshifts.astype(jnp.float32)
    text_bias = textbiases.astype(jnp.float32)
    image_factor = imagegains.astype(jnp.float32)
    image_offset = imageshifts.astype(jnp.float32)
    image_bias = imagebiases.astype(jnp.float32)
    text_mask = jnp.arange(caption_slots)[None, :] < text_len[:, None]
    region_mask = jnp.arange(region_slots)[None, :] < region_count[:, None]
    self_triple = project(text, selfproject, selfbiases)
    self_keys = lax.all_gather(self_triple[:, :, 1:], "seq", axis=1, tiled=True)
    self_mixed, self_logsum = attend(self_triple[:, :, 0], self_keys, text_mask, HT)
    self_sum = text.astype(jnp.float32) + linear(self_mixed, selfoutput) + text_bias[0]
    text_one = layer_norm(self_sum, text_factor[0], text_offset[0]).astype(jnp.bfloat16)
    text_triple = project(text_one, textcoproject, textcobiases)
    image_triple = project(image, imagecoproject, imagecobiases)
    text_keys, image_keys = (
        lax.all_gather(text_triple[:, :, 1:], "seq", axis=1, tiled=True),
        lax.all_gather(image_triple[:, :, 1:], "seq", axis=1, tiled=True),
    )
    text_mixed, text_logsum = attend(text_triple[:, :, 0], image_keys, region_mask, HC)
    image_mixed, image_logsum = attend(image_triple[:, :, 0], text_keys, text_mask, HC)
    text_sum = text_one.astype(jnp.float32) + linear(text_mixed, textcooutput) + text_bias[1]
    text_two = layer_norm(text_sum, text_factor[1], text_offset[1]).astype(jnp.bfloat16)
    image_sum = image.astype(jnp.float32) + linear(image_mixed, imagecooutput) + image_bias[0]
    image_two = layer_norm(image_sum, image_factor[0], image_offset[0]).astype(jnp.bfloat16)
    text_inner, text_active, text_total = feed_forward(
        text_two, textffinner, textffinbias, textffouter, text_bias[2]
    )
    text_three = layer_norm(text_total, text_factor[2], text_offset[2]).astype(jnp.bfloat16)
    image_inner, image_active, image_total = feed_forward(
        image_two, imageffinner, imageffinbias, imageffouter, image_bias[1]
    )
    image_three = layer_norm(image_total, image_factor[1], image_offset[1]).astype(jnp.bfloat16)
    (
        text_twograd,
        textin_grad,
        textinb_grad,
        textout_grad,
        textoutb_grad,
        factor_tthree,
        offset_tthree,
    ) = feed_back(
        text_cot.astype(jnp.float32),
        text_two,
        text_inner,
        text_active,
        text_total,
        text_factor[2],
        text_offset[2],
        textffinner,
        textffouter,
    )
    (
        image_twograd,
        imagein_grad,
        imageinb_grad,
        imageout_grad,
        imageoutb_grad,
        factor_itwo,
        offset_itwo,
    ) = feed_back(
        image_cot.astype(jnp.float32),
        image_two,
        image_inner,
        image_active,
        image_total,
        image_factor[1],
        image_offset[1],
        imageffinner,
        imageffouter,
    )
    textsum_grad, factor_ttwo, offset_ttwo = norm_back(
        text_sum, text_factor[1], text_offset[1], text_twograd
    )
    textbranch_grad = textsum_grad.astype(jnp.bfloat16)
    textco_outgrad = linear_weight(text_mixed, textbranch_grad)
    textco_biasgrad = row_total(textbranch_grad)
    textmix_grad = linear_input(textbranch_grad, textcooutput).astype(jnp.bfloat16)
    imagesum_grad, factor_ione, offset_ione = norm_back(
        image_sum, image_factor[0], image_offset[0], image_twograd
    )
    imagebranch_grad = imagesum_grad.astype(jnp.bfloat16)
    imageco_outgrad = linear_weight(image_mixed, imagebranch_grad)
    imageco_biasgrad = row_total(imagebranch_grad)
    imagemix_grad = linear_input(imagebranch_grad, imagecooutput).astype(jnp.bfloat16)
    textquery_grad, imagekv_part = attend_back(
        textmix_grad, text_triple[:, :, 0], image_keys, region_mask, text_logsum, HC
    )
    imagequery_grad, textkv_part = attend_back(
        imagemix_grad, image_triple[:, :, 0], text_keys, text_mask, image_logsum, HC
    )
    textkv_grad, imagekv_grad = (
        lax.psum_scatter(
            textkv_part.astype(jnp.bfloat16), "seq", scatter_dimension=1, tiled=True
        ).astype(jnp.float32),
        lax.psum_scatter(
            imagekv_part.astype(jnp.bfloat16), "seq", scatter_dimension=1, tiled=True
        ).astype(jnp.float32),
    )
    texttriple_grad = jnp.concatenate(
        [textquery_grad[:, :, None].astype(jnp.bfloat16), textkv_grad.astype(jnp.bfloat16)], axis=2
    )
    imagetriple_grad = jnp.concatenate(
        [imagequery_grad[:, :, None].astype(jnp.bfloat16), imagekv_grad.astype(jnp.bfloat16)],
        axis=2,
    )
    textco_projgrad, textco_qvgrad, textone_grad = project_back(
        text_one, texttriple_grad, textcoproject
    )
    textone_grad = textone_grad + textsum_grad
    imageco_projgrad, imageco_qvgrad, image_ingrad = project_back(
        image, imagetriple_grad, imagecoproject
    )
    image_ingrad = image_ingrad + imagesum_grad
    selfsum_grad, factor_tone, offset_tone = norm_back(
        self_sum, text_factor[0], text_offset[0], textone_grad
    )
    selfbranch_grad = selfsum_grad.astype(jnp.bfloat16)
    selfout_grad = linear_weight(self_mixed, selfbranch_grad)
    selfbias_grad = row_total(selfbranch_grad)
    selfmix_grad = linear_input(selfbranch_grad, selfoutput).astype(jnp.bfloat16)
    selfquery_grad, selfkv_part = attend_back(
        selfmix_grad, self_triple[:, :, 0], self_keys, text_mask, self_logsum, HT
    )
    selfkv_grad = lax.psum_scatter(
        selfkv_part.astype(jnp.bfloat16), "seq", scatter_dimension=1, tiled=True
    )
    selftriple_grad = jnp.concatenate(
        [selfquery_grad[:, :, None].astype(jnp.bfloat16), selfkv_grad], axis=2
    )
    selfproj_grad, selfqv_grad, text_ingrad = project_back(text, selftriple_grad, selfproject)
    text_ingrad = text_ingrad + selfsum_grad
    gradients = (
        selfproj_grad,
        selfqv_grad,
        selfout_grad,
        textco_projgrad,
        textco_qvgrad,
        imageco_projgrad,
        imageco_qvgrad,
        textco_outgrad,
        imageco_outgrad,
        textin_grad,
        textinb_grad,
        textout_grad,
        imagein_grad,
        imageinb_grad,
        imageout_grad,
        jnp.stack([factor_tone, factor_ttwo, factor_tthree]),
        jnp.stack([offset_tone, offset_ttwo, offset_tthree]),
        jnp.stack([selfbias_grad, textco_biasgrad, textoutb_grad]),
        jnp.stack([factor_ione, factor_itwo]),
        jnp.stack([offset_ione, offset_itwo]),
        jnp.stack([imageco_biasgrad, imageoutb_grad]),
    )
    outputs = (
        text_three,
        image_three,
        text_ingrad.astype(jnp.bfloat16),
        image_ingrad.astype(jnp.bfloat16),
    )
    return (outputs, gradients)


def local_plain(
    text,
    image,
    text_len,
    region_count,
    text_cot,
    image_cot,
    selfproject,
    selfbiases,
    selfoutput,
    textcoproject,
    textcobiases,
    imagecoproject,
    imagecobiases,
    textcooutput,
    imagecooutput,
    textffinner,
    textffinbias,
    textffouter,
    imageffinner,
    imageffinbias,
    imageffouter,
    textgains,
    textshifts,
    textbiases,
    imagegains,
    imageshifts,
    imagebiases,
):
    seq_count = lax.axis_size("seq")
    micro_pairs = text.shape[0] // MB
    shards = (
        selfproject,
        selfbiases,
        selfoutput,
        textcoproject,
        textcobiases,
        imagecoproject,
        imagecobiases,
        textcooutput,
        imagecooutput,
        textffinner,
        textffinbias,
        textffouter,
        imageffinner,
        imageffinbias,
        imageffouter,
        textgains,
        textshifts,
        textbiases,
        imagegains,
        imageshifts,
        imagebiases,
    )
    accumulated = None
    text_rows = []
    image_rows = []
    textgrad_rows = []
    imagegrad_rows = []
    for micro_index in range(MB):
        fetched = (
            lax.all_gather(shards[0], "dp", axis=0, tiled=True),
            lax.all_gather(shards[1], "dp", axis=1, tiled=True),
            lax.all_gather(shards[2], "dp", axis=0, tiled=True),
            lax.all_gather(shards[3], "dp", axis=0, tiled=True),
            lax.all_gather(shards[4], "dp", axis=1, tiled=True),
            lax.all_gather(shards[5], "dp", axis=0, tiled=True),
            lax.all_gather(shards[6], "dp", axis=1, tiled=True),
            lax.all_gather(shards[7], "dp", axis=0, tiled=True),
            lax.all_gather(shards[8], "dp", axis=0, tiled=True),
            lax.all_gather(shards[9], "dp", axis=0, tiled=True),
            lax.all_gather(shards[10], "dp", axis=0, tiled=True),
            lax.all_gather(shards[11], "dp", axis=0, tiled=True),
            lax.all_gather(shards[12], "dp", axis=0, tiled=True),
            lax.all_gather(shards[13], "dp", axis=0, tiled=True),
            lax.all_gather(shards[14], "dp", axis=0, tiled=True),
            lax.all_gather(shards[15], "dp", axis=1, tiled=True),
            lax.all_gather(shards[16], "dp", axis=1, tiled=True),
            lax.all_gather(shards[17], "dp", axis=1, tiled=True),
            lax.all_gather(shards[18], "dp", axis=1, tiled=True),
            lax.all_gather(shards[19], "dp", axis=1, tiled=True),
            lax.all_gather(shards[20], "dp", axis=1, tiled=True),
        )
        begin_row = micro_index * micro_pairs
        end_row = begin_row + micro_pairs
        outputs, gradients = micro_step(
            fetched,
            text[begin_row:end_row],
            image[begin_row:end_row],
            text_len[begin_row:end_row],
            region_count[begin_row:end_row],
            text_cot[begin_row:end_row],
            image_cot[begin_row:end_row],
            text.shape[1] * seq_count,
            image.shape[1] * seq_count,
        )
        text_rows.append(outputs[0])
        image_rows.append(outputs[1])
        textgrad_rows.append(outputs[2])
        imagegrad_rows.append(outputs[3])
        pieces = (
            lax.psum_scatter(gradients[0], "dp", scatter_dimension=0, tiled=True),
            lax.psum_scatter(gradients[1], "dp", scatter_dimension=1, tiled=True),
            lax.psum_scatter(gradients[2], "dp", scatter_dimension=0, tiled=True),
            lax.psum_scatter(gradients[3], "dp", scatter_dimension=0, tiled=True),
            lax.psum_scatter(gradients[4], "dp", scatter_dimension=1, tiled=True),
            lax.psum_scatter(gradients[5], "dp", scatter_dimension=0, tiled=True),
            lax.psum_scatter(gradients[6], "dp", scatter_dimension=1, tiled=True),
            lax.psum_scatter(gradients[7], "dp", scatter_dimension=0, tiled=True),
            lax.psum_scatter(gradients[8], "dp", scatter_dimension=0, tiled=True),
            lax.psum_scatter(gradients[9], "dp", scatter_dimension=0, tiled=True),
            lax.psum_scatter(gradients[10], "dp", scatter_dimension=0, tiled=True),
            lax.psum_scatter(gradients[11], "dp", scatter_dimension=0, tiled=True),
            lax.psum_scatter(gradients[12], "dp", scatter_dimension=0, tiled=True),
            lax.psum_scatter(gradients[13], "dp", scatter_dimension=0, tiled=True),
            lax.psum_scatter(gradients[14], "dp", scatter_dimension=0, tiled=True),
            lax.psum_scatter(gradients[15], "dp", scatter_dimension=1, tiled=True),
            lax.psum_scatter(gradients[16], "dp", scatter_dimension=1, tiled=True),
            lax.psum_scatter(gradients[17], "dp", scatter_dimension=1, tiled=True),
            lax.psum_scatter(gradients[18], "dp", scatter_dimension=1, tiled=True),
            lax.psum_scatter(gradients[19], "dp", scatter_dimension=1, tiled=True),
            lax.psum_scatter(gradients[20], "dp", scatter_dimension=1, tiled=True),
        )
        accumulated = pieces if accumulated is None else jax.tree.map(jnp.add, accumulated, pieces)
    summed = (
        lax.psum(accumulated[0].astype(jnp.bfloat16), "seq").astype(jnp.float32),
        lax.psum(accumulated[1].astype(jnp.bfloat16), "seq").astype(jnp.float32),
        lax.psum(accumulated[2].astype(jnp.bfloat16), "seq").astype(jnp.float32),
        lax.psum(accumulated[3].astype(jnp.bfloat16), "seq").astype(jnp.float32),
        lax.psum(accumulated[4].astype(jnp.bfloat16), "seq").astype(jnp.float32),
        lax.psum(accumulated[5].astype(jnp.bfloat16), "seq").astype(jnp.float32),
        lax.psum(accumulated[6].astype(jnp.bfloat16), "seq").astype(jnp.float32),
        lax.psum(accumulated[7].astype(jnp.bfloat16), "seq").astype(jnp.float32),
        lax.psum(accumulated[8].astype(jnp.bfloat16), "seq").astype(jnp.float32),
        lax.psum(accumulated[9].astype(jnp.bfloat16), "seq").astype(jnp.float32),
        lax.psum(accumulated[10].astype(jnp.bfloat16), "seq").astype(jnp.float32),
        lax.psum(accumulated[11].astype(jnp.bfloat16), "seq").astype(jnp.float32),
        lax.psum(accumulated[12].astype(jnp.bfloat16), "seq").astype(jnp.float32),
        lax.psum(accumulated[13].astype(jnp.bfloat16), "seq").astype(jnp.float32),
        lax.psum(accumulated[14].astype(jnp.bfloat16), "seq").astype(jnp.float32),
        lax.psum(accumulated[15].astype(jnp.bfloat16), "seq").astype(jnp.float32),
        lax.psum(accumulated[16].astype(jnp.bfloat16), "seq").astype(jnp.float32),
        lax.psum(accumulated[17].astype(jnp.bfloat16), "seq").astype(jnp.float32),
        lax.psum(accumulated[18].astype(jnp.bfloat16), "seq").astype(jnp.float32),
        lax.psum(accumulated[19].astype(jnp.bfloat16), "seq").astype(jnp.float32),
        lax.psum(accumulated[20].astype(jnp.bfloat16), "seq").astype(jnp.float32),
    )
    text_out = jnp.concatenate(text_rows, axis=0)
    image_out = jnp.concatenate(image_rows, axis=0)
    text_grad = jnp.concatenate(textgrad_rows, axis=0)
    image_grad = jnp.concatenate(imagegrad_rows, axis=0)
    return (text_out, image_out, text_grad, image_grad) + tuple(summed)


MESH = pl.DeviceIdType.MESH
ANY = pl.BlockSpec(memory_space=pl.ANY)
VMEM = pl.BlockSpec(memory_space=pltpu.VMEM)


def place():
    dp = lax.axis_index("dp")
    z = lax.axis_index("seq")
    row = dp // 4
    col = (dp // 2) % 2
    core = dp % 2
    return (dp, z, row, col, core)


def partners(row, col, core, first_row):
    near_row = row + first_row * (1 - 2 * row)
    near_col = col + (1 - first_row) * (1 - 2 * col)
    far_row = row + (1 - first_row) * (1 - 2 * row)
    far_col = col + first_row * (1 - 2 * col)
    near = near_row * 4 + near_col * 2 + core
    far = far_row * 4 + far_col * 2 + core
    return (near, far)


def greet(devices):
    barrier = pltpu.get_barrier_semaphore()
    for device in devices:
        pl.semaphore_signal(barrier, inc=1, device_id=device, device_id_type=MESH)
    pl.semaphore_wait(barrier, len(devices))


def remote(source, target, send_sem, recv_sem, device):
    return pltpu.make_async_remote_copy(
        src_ref=source,
        dst_ref=target,
        send_sem=send_sem,
        recv_sem=recv_sem,
        device_id=device,
        device_id_type=MESH,
    )


def gather_kernel(weight_count, *refs):
    total = weight_count + 4
    blocks = refs[:weight_count]
    states = refs[weight_count:total]
    wholes = refs[total : total + weight_count]
    pairs = refs[total + weight_count : 2 * total]
    send_sem, recv_sem, swap_send, swap_recv, own_sem = refs[2 * total :]
    dp, z, row, col, core = place()
    near, far = partners(row, col, core, 1 - core)
    sibling = dp + 1 - 2 * core
    diagonal = (1 - row) * 4 + (1 - col) * 2 + core
    others = [lax.rem(z + step, 4) for step in (1, 2, 3)]
    greet([(near, z), (far, z), (sibling, z)] + [(dp, other) for other in others])

    def rows_of(whole, index):
        depth = whole.shape[1] // 8
        return whole.at[:, pl.ds(pl.multiple_of(index * depth, 16), depth), :]

    started = []

    def send(array, lane, source, index, device):
        copy = remote(
            source,
            rows_of(wholes[array], index),
            send_sem.at[array, lane],
            recv_sem.at[array, lane],
            (device, z),
        )
        copy.start()
        started.append(copy)
        return copy

    locals_ = []
    first = []
    for array in range(weight_count):
        block = blocks[array]
        first.append(
            (
                send(array, 0, block, dp, near),
                send(array, 1, block, dp, far),
                send(array, 2, block, dp, sibling),
            )
        )
        keep = pltpu.make_async_copy(block, rows_of(wholes[array], dp), own_sem.at[array])
        keep.start()
        locals_.append(keep)
    swaps = []
    for array in range(4):
        source, target = states[array], pairs[array]
        count = source.shape[0] // 4
        slots = source.shape[1]
        here = target.at[:, pl.ds(pl.multiple_of(z * slots, 16), slots), :]
        for step, other in enumerate(others):
            copy = remote(
                source.at[pl.ds(other * count, count)],
                here,
                swap_send.at[array, step],
                swap_recv.at[array, step],
                (dp, other),
            )
            copy.start()
            swaps.append(copy)
        keep = pltpu.make_async_copy(
            source.at[pl.ds(z * count, count)], here, own_sem.at[weight_count + array]
        )
        keep.start()
        locals_.append(keep)
    second = []
    for array in range(weight_count):
        first[array][0].wait_recv()
        arrived = rows_of(wholes[array], near)
        second.append(
            (
                send(array, 3, arrived, near, far),
                send(array, 4, arrived, near, sibling),
            )
        )
    for array in range(weight_count):
        first[array][1].wait_recv()
        second.append((send(array, 5, rows_of(wholes[array], far), far, sibling),))
    for array in range(weight_count):
        second[array][0].wait_recv()
        second.append((send(array, 6, rows_of(wholes[array], diagonal), diagonal, sibling),))
    for array in range(weight_count):
        first[array][2].wait_recv()
        second[array][1].wait_recv()
        second[weight_count + array][0].wait_recv()
        second[2 * weight_count + array][0].wait_recv()
    for copy in started:
        copy.wait_send()
    for copy in swaps:
        copy.wait()
    for copy in locals_:
        copy.wait()


def gather(blocks, states):
    weight_count = len(blocks)
    out_shape = [
        jax.ShapeDtypeStruct((b.shape[0], b.shape[1] * 8, b.shape[2]), b.dtype) for b in blocks
    ] + [
        jax.ShapeDtypeStruct((s.shape[0] // 4, s.shape[1] * 4, s.shape[2]), s.dtype) for s in states
    ]
    dma = pltpu.SemaphoreType.DMA
    results = pl.pallas_call(
        functools.partial(gather_kernel, weight_count),
        out_shape=out_shape,
        in_specs=[ANY] * (weight_count + 4),
        out_specs=[ANY] * (weight_count + 4),
        scratch_shapes=[
            dma((weight_count, 7)),
            dma((weight_count, 7)),
            dma((4, 3)),
            dma((4, 3)),
            dma((weight_count + 4,)),
        ],
        compiler_params=pltpu.CompilerParams(collective_id=0, has_side_effects=True),
        name="gather",
    )(*blocks, *states)
    return (results[:weight_count], results[weight_count:])


CHUNKS = (9, 9, 3)
TILES = (4, 3, 1)
ROWS = (96, 128, 384)
STARTS = ((9, 12, 24), (12, 15, 19, 23), ())
STEPS = 21
LAG_NEAR, LAG_FAR, LAG_SUM, LAG_MID, LAG_END = 1, 3, 5, 7, 9


def reduce_kernel(*refs):
    inputs = refs[0:3]
    grads = refs[3:6]
    small = refs[6]
    states = refs[7:11]
    result, small_result = refs[11:13]
    pairs = refs[13:17]
    (
        out_box, chip, near_sum, plane, line, cross,
        s_out, s_chip, s_near, s_plane, s_line, s_cross,
        core_send, core_recv, near_send, near_recv, far_send, far_recv,
        end_send, end_recv, mid_send, mid_recv, back_send, back_recv,
        write_sem, swap_send, swap_recv, own_sem,
    ) = refs[17:]
    dp, z, row, col, core = place()
    near, far = partners(row, col, core, core)
    sibling = dp + 1 - 2 * core
    others = [lax.rem(z + step, 4) for step in (1, 2, 3)]
    near_bit = col + core * (row - col)
    far_bit = row + core * (col - row)

    def block_of(near_index, far_index):
        return near_index * (1 + core) + far_index * (2 - core)

    is_end = (z == 0) | (z == 3)
    is_mid = (z == 1) | (z == 2)
    middle = 1 + z // 2
    other_mid = 3 - z
    end = 3 * (z // 2)
    greet([(near, z), (far, z), (sibling, z)] + [(dp, other) for other in others])

    copies = []
    for array in range(4):
        source, target = states[array], pairs[array]
        count = source.shape[0]
        slots = source.shape[1] // 4
        there = target.at[pl.ds(z * count, count)]
        for step, other in enumerate(others):
            copy = remote(
                source.at[:, pl.ds(pl.multiple_of(other * slots, 16), slots), :],
                there,
                swap_send.at[array, step],
                swap_recv.at[array, step],
                (dp, other),
            )
            copy.start()
            copies.append(copy)
        keep = pltpu.make_async_copy(
            source.at[:, pl.ds(pl.multiple_of(z * slots, 16), slots), :], there, own_sem.at[array]
        )
        keep.start()
        copies.append(keep)

    def products(index, half, use):
        base = 0
        for kind in range(3):
            count, tiles, rows = CHUNKS[kind], TILES[kind], ROWS[kind]
            chosen = (index >= base) & (index < base + count)

            def work(kind=kind, base=base, tiles=tiles, rows=rows):
                for tile in range(tiles):
                    which = (index - base) * tiles + tile
                    weight = 0
                    for bound in STARTS[kind]:
                        weight = weight + jnp.where(which >= bound, 1, 0)
                    left = inputs[kind][weight, half]
                    right = grads[kind][:, pl.ds(pl.multiple_of(which * 256, 256), 256)]
                    part = jnp.dot(left, right, preferred_element_type=jnp.float32)
                    for block in range(4):
                        for side in range(2):
                            use(
                                block,
                                (tile * 2 + side) * rows,
                                rows,
                                part[block * rows : (block + 1) * rows, side * 128 : side * 128 + 128],
                            )

            pl.when(chosen)(work)
            base += count

    def core_copy(index):
        return remote(
            out_box.at[lax.rem(index, 2)], chip.at[index], core_send.at[index], core_recv.at[index], (sibling, z)
        )

    def near_copy(index, far_index):
        return remote(
            chip.at[index, block_of(1 - near_bit, far_index)],
            near_sum.at[index, far_index],
            near_send.at[index, far_index],
            near_recv.at[index, far_index],
            (near, z),
        )

    def far_copy(index):
        return remote(
            near_sum.at[index, 1 - far_bit], plane.at[index], far_send.at[index], far_recv.at[index], (far, z)
        )

    def end_copy(index):
        return remote(plane.at[index], line.at[index], end_send.at[index], end_recv.at[index], (dp, middle))

    def mid_copy(index):
        return remote(line.at[index], cross.at[index], mid_send.at[index], mid_recv.at[index], (dp, other_mid))

    def back_copy(index):
        return remote(cross.at[index], line.at[index], back_send.at[index], back_recv.at[index], (dp, end))

    def mid_write(index):
        return pltpu.make_async_copy(cross.at[index], result.at[index], write_sem.at[index])

    def end_write(index):
        return pltpu.make_async_copy(line.at[index], result.at[index], write_sem.at[index])

    def wide(values):
        return values.astype(jnp.float32)

    def stage_core(index):
        @pl.when(index >= 2)
        def _():
            core_copy(index - 2).wait_send()

        slot = lax.rem(index, 2)

        def put(block, first, rows, values):
            out_box[slot, block, first : first + rows, :] = values.astype(jnp.bfloat16)

        products(index, 1 - core, put)
        core_copy(index).start()

    def stage_near(index):
        core_copy(index).wait_recv()

        def add(block, first, rows, values):
            window = (index, block, slice(first, first + rows), slice(None))
            chip[window] = (wide(chip[window]) + values).astype(jnp.bfloat16)

        products(index, core, add)
        near_copy(index, 1 - far_bit).start()
        near_copy(index, far_bit).start()

    def stage_far(index):
        for far_index in (1 - far_bit, far_bit):
            near_copy(index, far_index).wait_recv()
            mine = chip[index, block_of(near_bit, far_index)]
            near_sum[index, far_index] = (wide(near_sum[index, far_index]) + wide(mine)).astype(jnp.bfloat16)
            if far_index is not far_bit:
                far_copy(index).start()

    def stage_sum(index):
        far_copy(index).wait_recv()
        plane[index] = (wide(plane[index]) + wide(near_sum[index, far_bit])).astype(jnp.bfloat16)

        @pl.when(is_end)
        def _():
            end_copy(index).start()

    def stage_mid(index):
        @pl.when(is_mid)
        def _():
            end_copy(index).wait_recv()
            line[index] = (wide(line[index]) + wide(plane[index])).astype(jnp.bfloat16)
            mid_copy(index).start()

    def stage_end(index):
        @pl.when(is_mid)
        def _():
            mid_copy(index).wait_recv()
            cross[index] = (wide(cross[index]) + wide(line[index])).astype(jnp.bfloat16)
            back_copy(index).start()
            mid_write(index).start()

    def stage_write(index):
        @pl.when(is_end)
        def _():
            back_copy(index).wait_recv()
            end_write(index).start()

    stages = (
        (stage_core, 0),
        (stage_near, LAG_NEAR),
        (stage_far, LAG_FAR),
        (stage_sum, LAG_SUM),
        (stage_mid, LAG_MID),
        (stage_end, LAG_END),
        (stage_write, LAG_END + 2),
    )

    last = STEPS
    sm_core = remote(small.at[1 - core], s_chip, core_send.at[last], core_recv.at[last], (sibling, z))
    sm_near = [
        remote(
            s_chip.at[block_of(1 - near_bit, j)], s_near.at[j], near_send.at[last, j], near_recv.at[last, j], (near, z)
        )
        for j in (0, 1)
    ]
    sm_far = remote(s_near.at[1 - far_bit], s_plane, far_send.at[last], far_recv.at[last], (far, z))
    sm_end = remote(s_plane, s_line, end_send.at[last], end_recv.at[last], (dp, middle))
    sm_mid = remote(s_line, s_cross, mid_send.at[last], mid_recv.at[last], (dp, other_mid))
    sm_back = remote(s_cross, s_line, back_send.at[last], back_recv.at[last], (dp, end))
    sm_core.start()

    def small_steps(turn):
        @pl.when(turn == 1)
        def _():
            sm_core.wait_recv()
            s_chip[...] += small[core]
            for copy in sm_near:
                copy.start()

        @pl.when(turn == 3)
        def _():
            for j in (0, 1):
                sm_near[j].wait_recv()
                s_near[j] += s_chip[block_of(near_bit, j)]
            sm_far.start()

        @pl.when(turn == 5)
        def _():
            sm_far.wait_recv()
            s_plane[...] += s_near[far_bit]

        @pl.when((turn == 5) & is_end)
        def _():
            sm_end.start()

        @pl.when((turn == 7) & is_mid)
        def _():
            sm_end.wait_recv()
            s_line[...] += s_plane[...]
            sm_mid.start()

        @pl.when((turn == 9) & is_mid)
        def _():
            sm_mid.wait_recv()
            s_cross[...] += s_line[...]
            sm_back.start()
            small_result[...] = s_cross[...]

        @pl.when((turn == 11) & is_end)
        def _():
            sm_back.wait_recv()
            small_result[...] = s_line[...]

    def turn_body(turn, carry):
        for stage, lag in stages:
            index = turn - lag

            @pl.when((index >= 0) & (index < STEPS))
            def _(stage=stage, index=index):
                stage(index)

        small_steps(turn)
        return carry

    lax.fori_loop(0, STEPS + LAG_END + 2, turn_body, 0)

    core_copy(STEPS - 2).wait_send()
    core_copy(STEPS - 1).wait_send()
    sm_core.wait_send()
    for copy in sm_near:
        copy.wait_send()
    sm_far.wait_send()

    def settle(index, carry):
        near_copy(index, 0).wait_send()
        near_copy(index, 1).wait_send()
        far_copy(index).wait_send()

        @pl.when(is_end)
        def _():
            end_copy(index).wait_send()
            end_write(index).wait()

        @pl.when(is_mid)
        def _():
            mid_copy(index).wait_send()
            back_copy(index).wait_send()
            mid_write(index).wait()

        return carry

    lax.fori_loop(0, STEPS, settle, 0)

    @pl.when(is_end)
    def _():
        sm_end.wait_send()

    @pl.when(is_mid)
    def _():
        sm_mid.wait_send()
        sm_back.wait_send()

    for copy in copies:
        copy.wait()


def reduce_all(inputs, grads, small, states):
    dma = pltpu.SemaphoreType.DMA
    narrow = jnp.bfloat16
    block = (768, 128)
    tiny = small.shape[2:]
    steps = STEPS + 1
    one = [dma((steps,))] * 2
    results = pl.pallas_call(
        reduce_kernel,
        out_shape=[
            jax.ShapeDtypeStruct((STEPS,) + block, narrow),
            jax.ShapeDtypeStruct(tiny, jnp.float32),
        ]
        + [jax.ShapeDtypeStruct((s.shape[0] * 4, s.shape[1] // 4, s.shape[2]), s.dtype) for s in states],
        in_specs=[VMEM] * 7 + [ANY] * 4,
        out_specs=[ANY, VMEM] + [ANY] * 4,
        scratch_shapes=[
            pltpu.VMEM((2, 4) + block, narrow),
            pltpu.VMEM((STEPS, 4) + block, narrow),
            pltpu.VMEM((STEPS, 2) + block, narrow),
            pltpu.VMEM((STEPS,) + block, narrow),
            pltpu.VMEM((STEPS,) + block, narrow),
            pltpu.VMEM((STEPS,) + block, narrow),
            pltpu.VMEM((4,) + tiny, jnp.float32),
            pltpu.VMEM((4,) + tiny, jnp.float32),
            pltpu.VMEM((2,) + tiny, jnp.float32),
            pltpu.VMEM(tiny, jnp.float32),
            pltpu.VMEM(tiny, jnp.float32),
            pltpu.VMEM(tiny, jnp.float32),
        ]
        + one
        + [dma((steps, 2))] * 2
        + one * 4
        + [dma((steps,)), dma((4, 3)), dma((4, 3)), dma((4,))],
        compiler_params=pltpu.CompilerParams(
            collective_id=1, has_side_effects=True, vmem_limit_bytes=61 * 2**20
        ),
        name="reduce_all",
    )(*inputs, *grads, small, *states)
    return (results[0], results[1], results[2:])


SMALL = ((2, 96), (2, 128), (2, 128), (1, 384), (1, 128), (3, 96), (3, 96), (3, 96), (2, 128), (2, 128), (2, 128))
SMALL_ROWS = 32


def pack_small(arrays):
    rows = []
    for (count, width), array in zip(SMALL, arrays):
        flat = array.reshape(count, width)
        if width > 128:
            flat = flat.reshape(width // 128, 128)
        rows.append(jnp.pad(flat, ((0, 0), (0, 128 - flat.shape[1]))))
    packed = jnp.concatenate(rows, axis=0)
    return jnp.pad(packed, ((0, SMALL_ROWS - packed.shape[0]), (0, 0)))


def unpack_small(packed, lead):
    arrays = []
    first = 0
    for count, width in SMALL:
        lines = count * max(width // 128, 1)
        part = packed[:, first : first + lines, : min(width, 128)]
        first += lines
        if width > 128:
            arrays.append(part.reshape(lead * width))
        else:
            whole = part.transpose(1, 0, 2).reshape(count, lead * width)
            arrays.append(whole)
    return arrays


def spread_small(arrays):
    rows = []
    for (count, width), array in zip(SMALL, arrays):
        if width > 128:
            part = array.reshape(8, width // 128, 128)
        else:
            part = array.reshape(count, 8, width).transpose(1, 0, 2)
        rows.append(jnp.pad(part, ((0, 0), (0, 0), (0, 128 - part.shape[2]))))
    packed = jnp.concatenate(rows, axis=1)
    return jnp.pad(packed, ((0, 0), (0, SMALL_ROWS - packed.shape[1]), (0, 0)))


def mm(left, right):
    return jnp.dot(left, right, preferred_element_type=jnp.float32)


def mm_t(left, right):
    return lax.dot_general(left, right, (((1,), (1,)), ((), ())), preferred_element_type=jnp.float32)


def triple_of(inputs, weight, biases):
    narrow = jnp.bfloat16
    query = (mm(inputs, weight[0]) + biases[0].astype(jnp.float32)).astype(narrow)
    key = mm(inputs, weight[1]).astype(narrow)
    value = (mm(inputs, weight[2]) + biases[1].astype(jnp.float32)).astype(narrow)
    return (query, key, value)


def heads_of(values, heads):
    return values.reshape(-1, 128, heads, values.shape[-1] // heads)


def att(query, key, value, mask, heads):
    q, k, v = (heads_of(a, heads) for a in (query, key, value))
    shrink = q.shape[-1] ** (-0.5)
    scores = jnp.einsum("pthd,pshd->phts", q, k, preferred_element_type=jnp.float32) * shrink
    scores = jnp.where(mask[:, None, None, :], scores, NEG_FILL)
    powers = jnp.exp(scores - jnp.max(scores, axis=-1, keepdims=True))
    table = powers / jnp.sum(powers, axis=-1, keepdims=True)
    mixed = jnp.einsum("phts,pshd->pthd", table.astype(jnp.bfloat16), v, preferred_element_type=jnp.float32)
    return (mixed.reshape(query.shape).astype(jnp.bfloat16), table)


def att_back(upstream, query, key, value, table, heads):
    q, k, v, o = (heads_of(a, heads) for a in (query, key, value, upstream))
    narrow = jnp.bfloat16
    shrink = q.shape[-1] ** (-0.5)
    value_grad = jnp.einsum("phts,pthd->pshd", table.astype(narrow), o, preferred_element_type=jnp.float32)
    table_grad = jnp.einsum("pthd,pshd->phts", o, v, preferred_element_type=jnp.float32)
    score_grad = table * (table_grad - jnp.sum(table_grad * table, axis=-1, keepdims=True))
    score_grad = score_grad.astype(narrow)
    query_grad = jnp.einsum("phts,pshd->pthd", score_grad, k, preferred_element_type=jnp.float32) * shrink
    key_grad = jnp.einsum("phts,pthd->pshd", score_grad, q, preferred_element_type=jnp.float32) * shrink
    return tuple(g.reshape(query.shape).astype(narrow) for g in (query_grad, key_grad, value_grad))


def by_owner(inputs):
    tokens, rows = inputs.shape
    flipped = inputs.T.reshape(4, 2, rows // 8, tokens)
    return flipped.transpose(1, 0, 2, 3).reshape(2, rows // 2, tokens)


def col_sum(values):
    return jnp.sum(values, axis=0, dtype=jnp.float32)


def ff_back(upstream, inputs, inner, active, totals, factor, offset, weight_in, weight_out):
    total_grad, factor_grad, offset_grad = norm_back(totals, factor, offset, upstream)
    branch = total_grad.astype(jnp.bfloat16)
    inner_grad = gelu_back(inner, mm_t(branch, weight_out)).astype(jnp.bfloat16)
    return (branch, inner_grad, mm_t(inner_grad, weight_in) + total_grad, factor_grad, offset_grad)


def project_input(grads, weight):
    return mm_t(grads[0], weight[0]) + mm_t(grads[1], weight[1]) + mm_t(grads[2], weight[2])


def local_fast(
    text, image, text_len, region_count, text_cot, image_cot,
    selfproject, selfbiases, selfoutput, textcoproject, textcobiases, imagecoproject, imagecobiases,
    textcooutput, imagecooutput, textffinner, textffinbias, textffouter,
    imageffinner, imageffinbias, imageffouter,
    textgains, textshifts, textbiases, imagegains, imageshifts, imagebiases,
):
    narrow, wide = jnp.bfloat16, jnp.float32
    z = lax.axis_index("seq")
    packed = pack_small(
        (
            selfbiases, textcobiases, imagecobiases, textffinbias, imageffinbias,
            textgains, textshifts, textbiases, imagegains, imageshifts, imagebiases,
        )
    )
    blocks = [
        selfproject.transpose(1, 0, 2), selfoutput[None], textcoproject.transpose(1, 0, 2),
        imagecoproject.transpose(1, 0, 2), textcooutput[None], imagecooutput[None],
        textffinner[None], textffouter[None], imageffinner[None], imageffouter[None], packed[None],
    ]
    wholes, pairs = gather(blocks, [text, image, text_cot, image_cot])
    w_self, w_selfout, w_textco, w_imageco = wholes[0], wholes[1][0], wholes[2], wholes[3]
    w_textout, w_imageout = wholes[4][0], wholes[5][0]
    w_tin, w_tout, w_iin, w_iout = (w[0] for w in wholes[6:10])
    (
        selfbiases, textcobiases, imagecobiases, textffinbias, imageffinbias,
        textgains, textshifts, textbiases, imagegains, imageshifts, imagebiases,
    ) = [a.astype(wide) for a in unpack_small(wholes[10].reshape(8, SMALL_ROWS, 128), 8)]
    imageffinbias = imageffinbias.reshape(-1)
    text, image, text_cot, image_cot = (p.reshape(-1, p.shape[-1]) for p in pairs)
    lengths = lax.dynamic_slice(text_len, (z * 2,), (2,))
    counts = lax.dynamic_slice(region_count, (z * 2,), (2,))
    text_mask = jnp.arange(128)[None, :] < lengths[:, None]
    region_mask = jnp.arange(128)[None, :] < counts[:, None]

    self_q, self_k, self_v = triple_of(text, w_self, selfbiases)
    self_mixed, self_table = att(self_q, self_k, self_v, text_mask, HT)
    self_sum = text.astype(wide) + mm(self_mixed, w_selfout) + textbiases[0]
    text_one = layer_norm(self_sum, textgains[0], textshifts[0]).astype(narrow)
    text_q, text_k, text_v = triple_of(text_one, w_textco, textcobiases)
    image_q, image_k, image_v = triple_of(image, w_imageco, imagecobiases)
    text_mixed, text_table = att(text_q, image_k, image_v, region_mask, HC)
    image_mixed, image_table = att(image_q, text_k, text_v, text_mask, HC)
    text_sum = text_one.astype(wide) + mm(text_mixed, w_textout) + textbiases[1]
    text_two = layer_norm(text_sum, textgains[1], textshifts[1]).astype(narrow)
    image_sum = image.astype(wide) + mm(image_mixed, w_imageout) + imagebiases[0]
    image_two = layer_norm(image_sum, imagegains[0], imageshifts[0]).astype(narrow)
    text_inner = mm(text_two, w_tin) + textffinbias
    text_active = gelu_exact(text_inner).astype(narrow)
    text_total = text_two.astype(wide) + mm(text_active, w_tout) + textbiases[2]
    text_out = layer_norm(text_total, textgains[2], textshifts[2]).astype(narrow)
    image_inner = mm(image_two, w_iin) + imageffinbias
    image_active = gelu_exact(image_inner).astype(narrow)
    image_total = image_two.astype(wide) + mm(image_active, w_iout) + imagebiases[1]
    image_out = layer_norm(image_total, imagegains[1], imageshifts[1]).astype(narrow)

    b_tff, d_tin, g_two, f_t2, o_t2 = ff_back(
        text_cot.astype(wide), text_two, text_inner, text_active, text_total,
        textgains[2], textshifts[2], w_tin, w_tout,
    )
    b_iff, d_iin, g_itwo, f_i1, o_i1 = ff_back(
        image_cot.astype(wide), image_two, image_inner, image_active, image_total,
        imagegains[1], imageshifts[1], w_iin, w_iout,
    )
    text_sumgrad, f_t1, o_t1 = norm_back(text_sum, textgains[1], textshifts[1], g_two)
    b_tco = text_sumgrad.astype(narrow)
    textmix_grad = mm_t(b_tco, w_textout).astype(narrow)
    image_sumgrad, f_i0, o_i0 = norm_back(image_sum, imagegains[0], imageshifts[0], g_itwo)
    b_ico = image_sumgrad.astype(narrow)
    imagemix_grad = mm_t(b_ico, w_imageout).astype(narrow)
    d_tq, d_ik, d_iv = att_back(textmix_grad, text_q, image_k, image_v, text_table, HC)
    d_iq, d_tk, d_tv = att_back(imagemix_grad, image_q, text_k, text_v, image_table, HC)
    one_grad = project_input((d_tq, d_tk, d_tv), w_textco) + text_sumgrad
    image_grad = project_input((d_iq, d_ik, d_iv), w_imageco) + image_sumgrad
    self_sumgrad, f_t0, o_t0 = norm_back(self_sum, textgains[0], textshifts[0], one_grad)
    b_self = self_sumgrad.astype(narrow)
    selfmix_grad = mm_t(b_self, w_selfout).astype(narrow)
    d_sq, d_sk, d_sv = att_back(selfmix_grad, self_q, self_k, self_v, self_table, HT)
    text_grad = project_input((d_sq, d_sk, d_sv), w_self) + self_sumgrad

    small = spread_small(
        (
            jnp.stack([col_sum(d_sq), col_sum(d_sv)]),
            jnp.stack([col_sum(d_tq), col_sum(d_tv)]),
            jnp.stack([col_sum(d_iq), col_sum(d_iv)]),
            col_sum(d_tin)[None],
            col_sum(d_iin)[None],
            jnp.stack([f_t0, f_t1, f_t2]),
            jnp.stack([o_t0, o_t1, o_t2]),
            jnp.stack([col_sum(b_self), col_sum(b_tco), col_sum(b_tff)]),
            jnp.stack([f_i0, f_i1]),
            jnp.stack([o_i0, o_i1]),
            jnp.stack([col_sum(b_ico), col_sum(b_iff)]),
        )
    )
    small = small.reshape(4, 2, SMALL_ROWS, 128).transpose(1, 0, 2, 3)
    inputs = [
        jnp.stack([by_owner(a) for a in (text, self_mixed, text_one, text_two)]),
        jnp.stack([by_owner(a) for a in (image, text_mixed, image_mixed, image_two, image_active)]),
        by_owner(text_active)[None],
    ]
    grads = [
        jnp.concatenate((d_sq, d_sk, d_sv, b_self, d_tq, d_tk, d_tv, d_tin), axis=1),
        jnp.concatenate((d_iq, d_ik, d_iv, b_tco, b_ico, d_iin, b_iff), axis=1),
        b_tff,
    ]
    states = [a.astype(narrow).reshape(2, 128, -1) for a in (text_out, image_out, text_grad, image_grad)]
    summed, small_sum, outputs = reduce_all(inputs, grads, small, states)

    def columns(kind):
        start = sum(CHUNKS[:kind])
        part = summed[start : start + CHUNKS[kind]].reshape(-1, ROWS[kind], 128)
        return part.transpose(1, 0, 2).reshape(ROWS[kind], -1).astype(wide)

    flat = [columns(kind) for kind in range(3)]

    def threefold(part):
        return part.reshape(part.shape[0], 3, -1)

    one, two = flat[0], flat[1]
    s = unpack_small(small_sum[None], 1)
    return tuple(outputs) + (
        threefold(one[:, :2304]), s[0], one[:, 2304:3072], threefold(one[:, 3072:6144]), s[1],
        threefold(two[:, :3072]), s[2], two[:, 3072:3840], two[:, 3840:4864],
        one[:, 6144:], s[3], flat[2], two[:, 4864:5888], s[4].reshape(-1), two[:, 5888:],
        s[5], s[6], s[7], s[8], s[9], s[10],
    )


def solution(mesh):
    in_specs = (
        P("dp", "seq", None),
        P("dp", "seq", None),
        P("dp"),
        P("dp"),
        P("dp", "seq", None),
        P("dp", "seq", None),
        P("dp", None, None),
        P(None, "dp"),
        P("dp", None),
        P("dp", None, None),
        P(None, "dp"),
        P("dp", None, None),
        P(None, "dp"),
        P("dp", None),
        P("dp", None),
        P("dp", None),
        P("dp"),
        P("dp", None),
        P("dp", None),
        P("dp"),
        P("dp", None),
        P(None, "dp"),
        P(None, "dp"),
        P(None, "dp"),
        P(None, "dp"),
        P(None, "dp"),
        P(None, "dp"),
    )
    out_specs = (
        P("dp", "seq", None),
        P("dp", "seq", None),
        P("dp", "seq", None),
        P("dp", "seq", None),
        P("dp", None, None),
        P(None, "dp"),
        P("dp", None),
        P("dp", None, None),
        P(None, "dp"),
        P("dp", None, None),
        P(None, "dp"),
        P("dp", None),
        P("dp", None),
        P("dp", None),
        P("dp"),
        P("dp", None),
        P("dp", None),
        P("dp"),
        P("dp", None),
        P(None, "dp"),
        P(None, "dp"),
        P(None, "dp"),
        P(None, "dp"),
        P(None, "dp"),
        P(None, "dp"),
    )
    sizes = mesh.shape
    local = local_fast if (sizes["dp"], sizes["seq"]) == (8, 4) else local_plain
    return jax.shard_map(local, mesh=mesh, in_specs=in_specs, out_specs=out_specs, check_vma=False)
```

```python
import functools
import types

import jax
import jax.numpy as jnp
from jax import lax
from jax.experimental import pallas as pl
from jax.experimental.pallas import tpu as pltpu
from jax.sharding import PartitionSpec as P

HT = 12
HC = 8
MB = 2


EPSILON = 1e-05
NEG_FILL = -1e30


def layer_norm(hidden, factor, offset):
    centre = hidden - jnp.mean(hidden, axis=-1, keepdims=True)
    spread = jnp.mean(centre * centre, axis=-1, keepdims=True)
    return centre * lax.rsqrt(spread + EPSILON) * factor + offset


def norm_back(hidden, factor, offset, upstream):
    outcome, pullback = jax.vjp(layer_norm, hidden, factor, offset)
    return pullback(upstream)


def gelu_exact(hidden):
    return jax.nn.gelu(hidden, approximate=False)


def gelu_back(hidden, upstream):
    outcome, pullback = jax.vjp(gelu_exact, hidden)
    return pullback(upstream)[0]


def linear(inputs, weight):
    return jnp.einsum("pte,ef->ptf", inputs, weight, preferred_element_type=jnp.float32)


def linear_weight(inputs, gradient):
    return jnp.einsum("pte,ptf->ef", inputs, gradient, preferred_element_type=jnp.float32)


def linear_input(gradient, weight):
    return jnp.einsum("ptf,ef->pte", gradient, weight, preferred_element_type=jnp.float32)


def row_total(gradient):
    return jnp.sum(gradient, axis=(0, 1), dtype=jnp.float32)


def project(inputs, weight, biases):
    bias_rows = biases.astype(jnp.float32)
    stacked = jnp.stack([bias_rows[0], jnp.zeros_like(bias_rows[0]), bias_rows[1]])
    triple = jnp.einsum("pte,ekf->ptkf", inputs, weight, preferred_element_type=jnp.float32)
    return (triple + stacked).astype(jnp.bfloat16)


def project_back(inputs, gradient, weight):
    weight_grad = jnp.einsum("pte,ptkf->ekf", inputs, gradient, preferred_element_type=jnp.float32)
    totals = row_total(gradient)
    input_grad = jnp.einsum("ptkf,ekf->pte", gradient, weight, preferred_element_type=jnp.float32)
    return (weight_grad, jnp.stack([totals[0], totals[2]]), input_grad)


def split_heads(values, head_count):
    return values.reshape(
        values.shape[0], values.shape[1], head_count, values.shape[2] // head_count
    )


def score_table(queries, keyvals, keymask, head_count):
    query_heads = split_heads(queries, head_count)
    key_heads = split_heads(keyvals[:, :, 0], head_count)
    shrink = query_heads.shape[-1] ** (-0.5)
    scores = (
        jnp.einsum("pthd,pshd->phts", query_heads, key_heads, preferred_element_type=jnp.float32)
        * shrink
    )
    scores = jnp.where(keymask[:, None, None, :], scores, NEG_FILL)
    return (scores, query_heads, key_heads, shrink)


def attend(queries, keyvals, keymask, head_count):
    scores, query_heads, key_heads, shrink = score_table(queries, keyvals, keymask, head_count)
    highest = jnp.max(scores, axis=-1, keepdims=True)
    powers = jnp.exp(scores - highest)
    totals = jnp.sum(powers, axis=-1, keepdims=True)
    prob_table = (powers / totals).astype(jnp.bfloat16)
    value_heads = split_heads(keyvals[:, :, 1], head_count)
    mixture = jnp.einsum(
        "phts,pshd->pthd", prob_table, value_heads, preferred_element_type=jnp.float32
    )
    return (mixture.reshape(queries.shape).astype(jnp.bfloat16), highest + jnp.log(totals))


def attend_back(upstream, queries, keyvals, keymask, logsum, head_count):
    scores, query_heads, key_heads, shrink = score_table(queries, keyvals, keymask, head_count)
    prob_table = jnp.exp(scores - logsum)
    value_heads = split_heads(keyvals[:, :, 1], head_count)
    upper_heads = split_heads(upstream, head_count)
    value_grad = jnp.einsum(
        "phts,pthd->pshd",
        prob_table.astype(jnp.bfloat16),
        upper_heads,
        preferred_element_type=jnp.float32,
    )
    prob_grad = jnp.einsum(
        "pthd,pshd->phts", upper_heads, value_heads, preferred_element_type=jnp.float32
    )
    score_grad = prob_table * (prob_grad - jnp.sum(prob_grad * prob_table, axis=-1, keepdims=True))
    score_grad = score_grad.astype(jnp.bfloat16)
    query_grad = (
        jnp.einsum("phts,pshd->pthd", score_grad, key_heads, preferred_element_type=jnp.float32)
        * shrink
    )
    key_grad = (
        jnp.einsum("phts,pthd->pshd", score_grad, query_heads, preferred_element_type=jnp.float32)
        * shrink
    )
    keyval_grad = jnp.stack([key_grad, value_grad], axis=2).reshape(keyvals.shape)
    return (query_grad.reshape(queries.shape), keyval_grad)


def feed_forward(inputs, weight_in, bias_in, weight_out, bias_out):
    inner_sum = linear(inputs, weight_in) + bias_in.astype(jnp.float32)
    active = gelu_exact(inner_sum).astype(jnp.bfloat16)
    totals = inputs.astype(jnp.float32) + linear(active, weight_out) + bias_out
    return (inner_sum, active, totals)


def feed_back(upstream, inputs, inner_sum, active, totals, factor, offset, weight_in, weight_out):
    sum_grad, factor_grad, offset_grad = norm_back(totals, factor, offset, upstream)
    branch_grad = sum_grad.astype(jnp.bfloat16)
    outer_grad = linear_weight(active, branch_grad)
    outbias_grad = row_total(branch_grad)
    active_grad = linear_input(branch_grad, weight_out)
    inner_grad = gelu_back(inner_sum, active_grad).astype(jnp.bfloat16)
    weightin_grad = linear_weight(inputs, inner_grad)
    inbias_grad = row_total(inner_grad)
    input_grad = linear_input(inner_grad, weight_in) + sum_grad
    return (
        input_grad,
        weightin_grad,
        inbias_grad,
        outer_grad,
        outbias_grad,
        factor_grad,
        offset_grad,
    )


def micro_step(
    fetched, text, image, text_len, region_count, text_cot, image_cot, caption_slots, region_slots
):
    (
        selfproject,
        selfbiases,
        selfoutput,
        textcoproject,
        textcobiases,
        imagecoproject,
        imagecobiases,
        textcooutput,
        imagecooutput,
        textffinner,
        textffinbias,
        textffouter,
        imageffinner,
        imageffinbias,
        imageffouter,
        textgains,
        textshifts,
        textbiases,
        imagegains,
        imageshifts,
        imagebiases,
    ) = fetched
    text_factor = textgains.astype(jnp.float32)
    text_offset = textshifts.astype(jnp.float32)
    text_bias = textbiases.astype(jnp.float32)
    image_factor = imagegains.astype(jnp.float32)
    image_offset = imageshifts.astype(jnp.float32)
    image_bias = imagebiases.astype(jnp.float32)
    text_mask = jnp.arange(caption_slots)[None, :] < text_len[:, None]
    region_mask = jnp.arange(region_slots)[None, :] < region_count[:, None]
    self_triple = project(text, selfproject, selfbiases)
    self_keys = lax.all_gather(self_triple[:, :, 1:], "seq", axis=1, tiled=True)
    self_mixed, self_logsum = attend(self_triple[:, :, 0], self_keys, text_mask, HT)
    self_sum = text.astype(jnp.float32) + linear(self_mixed, selfoutput) + text_bias[0]
    text_one = layer_norm(self_sum, text_factor[0], text_offset[0]).astype(jnp.bfloat16)
    text_triple = project(text_one, textcoproject, textcobiases)
    image_triple = project(image, imagecoproject, imagecobiases)
    text_keys, image_keys = (
        lax.all_gather(text_triple[:, :, 1:], "seq", axis=1, tiled=True),
        lax.all_gather(image_triple[:, :, 1:], "seq", axis=1, tiled=True),
    )
    text_mixed, text_logsum = attend(text_triple[:, :, 0], image_keys, region_mask, HC)
    image_mixed, image_logsum = attend(image_triple[:, :, 0], text_keys, text_mask, HC)
    text_sum = text_one.astype(jnp.float32) + linear(text_mixed, textcooutput) + text_bias[1]
    text_two = layer_norm(text_sum, text_factor[1], text_offset[1]).astype(jnp.bfloat16)
    image_sum = image.astype(jnp.float32) + linear(image_mixed, imagecooutput) + image_bias[0]
    image_two = layer_norm(image_sum, image_factor[0], image_offset[0]).astype(jnp.bfloat16)
    text_inner, text_active, text_total = feed_forward(
        text_two, textffinner, textffinbias, textffouter, text_bias[2]
    )
    text_three = layer_norm(text_total, text_factor[2], text_offset[2]).astype(jnp.bfloat16)
    image_inner, image_active, image_total = feed_forward(
        image_two, imageffinner, imageffinbias, imageffouter, image_bias[1]
    )
    image_three = layer_norm(image_total, image_factor[1], image_offset[1]).astype(jnp.bfloat16)
    (
        text_twograd,
        textin_grad,
        textinb_grad,
        textout_grad,
        textoutb_grad,
        factor_tthree,
        offset_tthree,
    ) = feed_back(
        text_cot.astype(jnp.float32),
        text_two,
        text_inner,
        text_active,
        text_total,
        text_factor[2],
        text_offset[2],
        textffinner,
        textffouter,
    )
    (
        image_twograd,
        imagein_grad,
        imageinb_grad,
        imageout_grad,
        imageoutb_grad,
        factor_itwo,
        offset_itwo,
    ) = feed_back(
        image_cot.astype(jnp.float32),
        image_two,
        image_inner,
        image_active,
        image_total,
        image_factor[1],
        image_offset[1],
        imageffinner,
        imageffouter,
    )
    textsum_grad, factor_ttwo, offset_ttwo = norm_back(
        text_sum, text_factor[1], text_offset[1], text_twograd
    )
    textbranch_grad = textsum_grad.astype(jnp.bfloat16)
    textco_outgrad = linear_weight(text_mixed, textbranch_grad)
    textco_biasgrad = row_total(textbranch_grad)
    textmix_grad = linear_input(textbranch_grad, textcooutput).astype(jnp.bfloat16)
    imagesum_grad, factor_ione, offset_ione = norm_back(
        image_sum, image_factor[0], image_offset[0], image_twograd
    )
    imagebranch_grad = imagesum_grad.astype(jnp.bfloat16)
    imageco_outgrad = linear_weight(image_mixed, imagebranch_grad)
    imageco_biasgrad = row_total(imagebranch_grad)
    imagemix_grad = linear_input(imagebranch_grad, imagecooutput).astype(jnp.bfloat16)
    textquery_grad, imagekv_part = attend_back(
        textmix_grad, text_triple[:, :, 0], image_keys, region_mask, text_logsum, HC
    )
    imagequery_grad, textkv_part = attend_back(
        imagemix_grad, image_triple[:, :, 0], text_keys, text_mask, image_logsum, HC
    )
    textkv_grad, imagekv_grad = (
        lax.psum_scatter(
            textkv_part.astype(jnp.bfloat16), "seq", scatter_dimension=1, tiled=True
        ).astype(jnp.float32),
        lax.psum_scatter(
            imagekv_part.astype(jnp.bfloat16), "seq", scatter_dimension=1, tiled=True
        ).astype(jnp.float32),
    )
    texttriple_grad = jnp.concatenate(
        [textquery_grad[:, :, None].astype(jnp.bfloat16), textkv_grad.astype(jnp.bfloat16)], axis=2
    )
    imagetriple_grad = jnp.concatenate(
        [imagequery_grad[:, :, None].astype(jnp.bfloat16), imagekv_grad.astype(jnp.bfloat16)],
        axis=2,
    )
    textco_projgrad, textco_qvgrad, textone_grad = project_back(
        text_one, texttriple_grad, textcoproject
    )
    textone_grad = textone_grad + textsum_grad
    imageco_projgrad, imageco_qvgrad, image_ingrad = project_back(
        image, imagetriple_grad, imagecoproject
    )
    image_ingrad = image_ingrad + imagesum_grad
    selfsum_grad, factor_tone, offset_tone = norm_back(
        self_sum, text_factor[0], text_offset[0], textone_grad
    )
    selfbranch_grad = selfsum_grad.astype(jnp.bfloat16)
    selfout_grad = linear_weight(self_mixed, selfbranch_grad)
    selfbias_grad = row_total(selfbranch_grad)
    selfmix_grad = linear_input(selfbranch_grad, selfoutput).astype(jnp.bfloat16)
    selfquery_grad, selfkv_part = attend_back(
        selfmix_grad, self_triple[:, :, 0], self_keys, text_mask, self_logsum, HT
    )
    selfkv_grad = lax.psum_scatter(
        selfkv_part.astype(jnp.bfloat16), "seq", scatter_dimension=1, tiled=True
    )
    selftriple_grad = jnp.concatenate(
        [selfquery_grad[:, :, None].astype(jnp.bfloat16), selfkv_grad], axis=2
    )
    selfproj_grad, selfqv_grad, text_ingrad = project_back(text, selftriple_grad, selfproject)
    text_ingrad = text_ingrad + selfsum_grad
    gradients = (
        selfproj_grad,
        selfqv_grad,
        selfout_grad,
        textco_projgrad,
        textco_qvgrad,
        imageco_projgrad,
        imageco_qvgrad,
        textco_outgrad,
        imageco_outgrad,
        textin_grad,
        textinb_grad,
        textout_grad,
        imagein_grad,
        imageinb_grad,
        imageout_grad,
        jnp.stack([factor_tone, factor_ttwo, factor_tthree]),
        jnp.stack([offset_tone, offset_ttwo, offset_tthree]),
        jnp.stack([selfbias_grad, textco_biasgrad, textoutb_grad]),
        jnp.stack([factor_ione, factor_itwo]),
        jnp.stack([offset_ione, offset_itwo]),
        jnp.stack([imageco_biasgrad, imageoutb_grad]),
    )
    outputs = (
        text_three,
        image_three,
        text_ingrad.astype(jnp.bfloat16),
        image_ingrad.astype(jnp.bfloat16),
    )
    return (outputs, gradients)


def local_plain(
    text,
    image,
    text_len,
    region_count,
    text_cot,
    image_cot,
    selfproject,
    selfbiases,
    selfoutput,
    textcoproject,
    textcobiases,
    imagecoproject,
    imagecobiases,
    textcooutput,
    imagecooutput,
    textffinner,
    textffinbias,
    textffouter,
    imageffinner,
    imageffinbias,
    imageffouter,
    textgains,
    textshifts,
    textbiases,
    imagegains,
    imageshifts,
    imagebiases,
):
    seq_count = lax.axis_size("seq")
    micro_pairs = text.shape[0] // MB
    shards = (
        selfproject,
        selfbiases,
        selfoutput,
        textcoproject,
        textcobiases,
        imagecoproject,
        imagecobiases,
        textcooutput,
        imagecooutput,
        textffinner,
        textffinbias,
        textffouter,
        imageffinner,
        imageffinbias,
        imageffouter,
        textgains,
        textshifts,
        textbiases,
        imagegains,
        imageshifts,
        imagebiases,
    )
    accumulated = None
    text_rows = []
    image_rows = []
    textgrad_rows = []
    imagegrad_rows = []
    for micro_index in range(MB):
        fetched = (
            lax.all_gather(shards[0], "dp", axis=0, tiled=True),
            lax.all_gather(shards[1], "dp", axis=1, tiled=True),
            lax.all_gather(shards[2], "dp", axis=0, tiled=True),
            lax.all_gather(shards[3], "dp", axis=0, tiled=True),
            lax.all_gather(shards[4], "dp", axis=1, tiled=True),
            lax.all_gather(shards[5], "dp", axis=0, tiled=True),
            lax.all_gather(shards[6], "dp", axis=1, tiled=True),
            lax.all_gather(shards[7], "dp", axis=0, tiled=True),
            lax.all_gather(shards[8], "dp", axis=0, tiled=True),
            lax.all_gather(shards[9], "dp", axis=0, tiled=True),
            lax.all_gather(shards[10], "dp", axis=0, tiled=True),
            lax.all_gather(shards[11], "dp", axis=0, tiled=True),
            lax.all_gather(shards[12], "dp", axis=0, tiled=True),
            lax.all_gather(shards[13], "dp", axis=0, tiled=True),
            lax.all_gather(shards[14], "dp", axis=0, tiled=True),
            lax.all_gather(shards[15], "dp", axis=1, tiled=True),
            lax.all_gather(shards[16], "dp", axis=1, tiled=True),
            lax.all_gather(shards[17], "dp", axis=1, tiled=True),
            lax.all_gather(shards[18], "dp", axis=1, tiled=True),
            lax.all_gather(shards[19], "dp", axis=1, tiled=True),
            lax.all_gather(shards[20], "dp", axis=1, tiled=True),
        )
        begin_row = micro_index * micro_pairs
        end_row = begin_row + micro_pairs
        outputs, gradients = micro_step(
            fetched,
            text[begin_row:end_row],
            image[begin_row:end_row],
            text_len[begin_row:end_row],
            region_count[begin_row:end_row],
            text_cot[begin_row:end_row],
            image_cot[begin_row:end_row],
            text.shape[1] * seq_count,
            image.shape[1] * seq_count,
        )
        text_rows.append(outputs[0])
        image_rows.append(outputs[1])
        textgrad_rows.append(outputs[2])
        imagegrad_rows.append(outputs[3])
        pieces = (
            lax.psum_scatter(gradients[0], "dp", scatter_dimension=0, tiled=True),
            lax.psum_scatter(gradients[1], "dp", scatter_dimension=1, tiled=True),
            lax.psum_scatter(gradients[2], "dp", scatter_dimension=0, tiled=True),
            lax.psum_scatter(gradients[3], "dp", scatter_dimension=0, tiled=True),
            lax.psum_scatter(gradients[4], "dp", scatter_dimension=1, tiled=True),
            lax.psum_scatter(gradients[5], "dp", scatter_dimension=0, tiled=True),
            lax.psum_scatter(gradients[6], "dp", scatter_dimension=1, tiled=True),
            lax.psum_scatter(gradients[7], "dp", scatter_dimension=0, tiled=True),
            lax.psum_scatter(gradients[8], "dp", scatter_dimension=0, tiled=True),
            lax.psum_scatter(gradients[9], "dp", scatter_dimension=0, tiled=True),
            lax.psum_scatter(gradients[10], "dp", scatter_dimension=0, tiled=True),
            lax.psum_scatter(gradients[11], "dp", scatter_dimension=0, tiled=True),
            lax.psum_scatter(gradients[12], "dp", scatter_dimension=0, tiled=True),
            lax.psum_scatter(gradients[13], "dp", scatter_dimension=0, tiled=True),
            lax.psum_scatter(gradients[14], "dp", scatter_dimension=0, tiled=True),
            lax.psum_scatter(gradients[15], "dp", scatter_dimension=1, tiled=True),
            lax.psum_scatter(gradients[16], "dp", scatter_dimension=1, tiled=True),
            lax.psum_scatter(gradients[17], "dp", scatter_dimension=1, tiled=True),
            lax.psum_scatter(gradients[18], "dp", scatter_dimension=1, tiled=True),
            lax.psum_scatter(gradients[19], "dp", scatter_dimension=1, tiled=True),
            lax.psum_scatter(gradients[20], "dp", scatter_dimension=1, tiled=True),
        )
        accumulated = pieces if accumulated is None else jax.tree.map(jnp.add, accumulated, pieces)
    summed = (
        lax.psum(accumulated[0].astype(jnp.bfloat16), "seq").astype(jnp.float32),
        lax.psum(accumulated[1].astype(jnp.bfloat16), "seq").astype(jnp.float32),
        lax.psum(accumulated[2].astype(jnp.bfloat16), "seq").astype(jnp.float32),
        lax.psum(accumulated[3].astype(jnp.bfloat16), "seq").astype(jnp.float32),
        lax.psum(accumulated[4].astype(jnp.bfloat16), "seq").astype(jnp.float32),
        lax.psum(accumulated[5].astype(jnp.bfloat16), "seq").astype(jnp.float32),
        lax.psum(accumulated[6].astype(jnp.bfloat16), "seq").astype(jnp.float32),
        lax.psum(accumulated[7].astype(jnp.bfloat16), "seq").astype(jnp.float32),
        lax.psum(accumulated[8].astype(jnp.bfloat16), "seq").astype(jnp.float32),
        lax.psum(accumulated[9].astype(jnp.bfloat16), "seq").astype(jnp.float32),
        lax.psum(accumulated[10].astype(jnp.bfloat16), "seq").astype(jnp.float32),
        lax.psum(accumulated[11].astype(jnp.bfloat16), "seq").astype(jnp.float32),
        lax.psum(accumulated[12].astype(jnp.bfloat16), "seq").astype(jnp.float32),
        lax.psum(accumulated[13].astype(jnp.bfloat16), "seq").astype(jnp.float32),
        lax.psum(accumulated[14].astype(jnp.bfloat16), "seq").astype(jnp.float32),
        lax.psum(accumulated[15].astype(jnp.bfloat16), "seq").astype(jnp.float32),
        lax.psum(accumulated[16].astype(jnp.bfloat16), "seq").astype(jnp.float32),
        lax.psum(accumulated[17].astype(jnp.bfloat16), "seq").astype(jnp.float32),
        lax.psum(accumulated[18].astype(jnp.bfloat16), "seq").astype(jnp.float32),
        lax.psum(accumulated[19].astype(jnp.bfloat16), "seq").astype(jnp.float32),
        lax.psum(accumulated[20].astype(jnp.bfloat16), "seq").astype(jnp.float32),
    )
    text_out = jnp.concatenate(text_rows, axis=0)
    image_out = jnp.concatenate(image_rows, axis=0)
    text_grad = jnp.concatenate(textgrad_rows, axis=0)
    image_grad = jnp.concatenate(imagegrad_rows, axis=0)
    return (text_out, image_out, text_grad, image_grad) + tuple(summed)


MESH = pl.DeviceIdType.MESH
ANY = pl.BlockSpec(memory_space=pl.ANY)
VMEM = pl.BlockSpec(memory_space=pltpu.VMEM)


def place():
    dp = lax.axis_index("dp")
    z = lax.axis_index("seq")
    row = dp // 4
    col = (dp // 2) % 2
    core = dp % 2
    return (dp, z, row, col, core)


def partners(row, col, core, first_row):
    near_row = row + first_row * (1 - 2 * row)
    near_col = col + (1 - first_row) * (1 - 2 * col)
    far_row = row + (1 - first_row) * (1 - 2 * row)
    far_col = col + first_row * (1 - 2 * col)
    near = near_row * 4 + near_col * 2 + core
    far = far_row * 4 + far_col * 2 + core
    return (near, far)


def greet(devices):
    barrier = pltpu.get_barrier_semaphore()
    for device in devices:
        pl.semaphore_signal(barrier, inc=1, device_id=device, device_id_type=MESH)
    pl.semaphore_wait(barrier, len(devices))


def remote(source, target, send_sem, recv_sem, device):
    return pltpu.make_async_remote_copy(
        src_ref=source,
        dst_ref=target,
        send_sem=send_sem,
        recv_sem=recv_sem,
        device_id=device,
        device_id_type=MESH,
    )


SMALL_PLACES = (
    (0, 2, 96),
    (16, 2, 128),
    (18, 2, 128),
    (27, 3, 128),
    (20, 1, 128),
    (2, 3, 96),
    (5, 3, 96),
    (8, 3, 96),
    (21, 2, 128),
    (23, 2, 128),
    (25, 2, 128),
)
SMALL_COUNT = len(SMALL_PLACES)
SMALL_ROWS = 32
ROOT_HALF = 0.7071067811865476
ROOT_TURN = 0.3989422804014327
WEIGHT_SHAPES = (
    (3, 768, 768), (1, 768, 768), (3, 1024, 1024), (3, 768, 1024), (1, 1024, 768),
    (1, 1024, 1024), (1, 768, 3072), (1, 3072, 768), (1, 1024, 1024), (1, 1024, 1024),
)
W_SELF, W_SELFOUT, W_IMAGECO, W_TEXTCO, W_TEXTOUT, W_IMAGEOUT, W_TIN, W_TOUT, W_IIN, W_IOUT, W_SMALL = range(11)
SAVED = dict(
    qkv_s=((3, 256, 768), jnp.bfloat16),
    qkv_t=((3, 256, 1024), jnp.bfloat16),
    qkv_i=((3, 256, 1024), jnp.bfloat16),
    tab_s=((12, 256, 128), jnp.bfloat16),
    tab_t=((16, 128, 128), jnp.bfloat16),
    tab_i=((16, 128, 128), jnp.bfloat16),
    sum_s=((256, 768), jnp.float32),
    sum_t=((256, 768), jnp.float32),
    sum_i=((256, 1024), jnp.float32),
    tot_t=((256, 768), jnp.float32),
    tot_i=((256, 1024), jnp.float32),
    slope_t=((256, 3072), jnp.bfloat16),
    slope_i=((256, 1024), jnp.bfloat16),
    xt768=((4, 2, 384, 256), jnp.bfloat16),
    xt1024=((5, 2, 512, 256), jnp.bfloat16),
    xt3072=((1, 2, 1536, 256), jnp.bfloat16),
    out_t=((256, 768), jnp.bfloat16),
    out_i=((256, 1024), jnp.bfloat16),
    vec96=((16, 768), jnp.float32),
    vec128=((16, 1024), jnp.float32),
)
WORK = dict(
    text=((2, 128, 768), jnp.bfloat16),
    image=((2, 128, 1024), jnp.bfloat16),
    mix_s=((256, 768), jnp.bfloat16),
    one=((256, 768), jnp.bfloat16),
    mix_t=((256, 1024), jnp.bfloat16),
    mix_i=((256, 1024), jnp.bfloat16),
    two_t=((256, 768), jnp.bfloat16),
    two_i=((256, 1024), jnp.bfloat16),
    bias_in=((8, 3072), jnp.float32),
    pack=((SMALL_ROWS, 128), jnp.float32),
)


def mm(left, right):
    return jnp.dot(left, right, preferred_element_type=jnp.float32)


def mm_t(left, right):
    return lax.dot_general(left, right, (((1,), (1,)), ((), ())), preferred_element_type=jnp.float32)


def mm_0(left, right):
    return lax.dot_general(left, right, (((0,), (0,)), ((), ())), preferred_element_type=jnp.float32)


def lanes(index, width):
    return pl.ds(pl.multiple_of(index * width, width), width)


def head_masks():
    spot = lax.broadcasted_iota(jnp.int32, (1, 128), 1)
    low = jnp.where(spot < 64, 1.0, 0.0)
    return (low, 1.0 - low)


def key_mask(length):
    return lax.broadcasted_iota(jnp.int32, (1, 128), 1) < length


def table_of(scores, keep, shrink):
    scores = jnp.where(keep, scores * shrink, NEG_FILL)
    powers = jnp.exp(scores - jnp.max(scores, axis=-1, keepdims=True))
    return (powers / jnp.sum(powers, axis=-1, keepdims=True)).astype(jnp.bfloat16)


def forward_kernel(*refs):
    refs = list(refs)

    def take(count):
        taken = refs[:count]
        del refs[:count]
        return taken

    narrow, wide = jnp.bfloat16, jnp.float32
    weight_count = len(WEIGHT_SHAPES)
    array_count = weight_count + 1
    blocks = take(weight_count)
    small_in = take(SMALL_COUNT)
    states = take(4)
    text_len, region_count = take(2)
    whole_out = take(weight_count)
    saved_out = take(len(SAVED))
    cots = take(2)
    wholes = take(array_count)
    saved_refs = take(len(SAVED))
    saved = types.SimpleNamespace(**dict(zip(SAVED, saved_refs)))
    work = types.SimpleNamespace(**dict(zip(WORK, take(len(WORK)))))
    send_sem, recv_sem, swap_send, swap_recv, own_sem, out_sem, save_sem = refs
    dp, z, row, col, core = place()
    near, far = partners(row, col, core, 1 - core)
    sibling = dp + 1 - 2 * core
    diagonal = (1 - row) * 4 + (1 - col) * 2 + core
    others = [lax.rem(z + step, 4) for step in (1, 2, 3)]

    pack = work.pack
    pack[...] = jnp.zeros((SMALL_ROWS, 128), wide)
    for (first, rows, width), ref in zip(SMALL_PLACES, small_in):
        pack[first : first + rows, :width] = ref[...].astype(wide)
    sources = blocks + [pack]

    greet([(near, z), (far, z), (sibling, z)] + [(dp, other) for other in others])

    def rows_of(whole, index):
        depth = whole.shape[1] // 8
        return whole.at[:, pl.ds(pl.multiple_of(index * depth, 16), depth), :]

    def own(array):
        source = sources[array]
        return source if array < weight_count else source.reshape(1, SMALL_ROWS, 128)

    def copy_of(array, lane, source, index, device):
        return remote(
            source, rows_of(wholes[array], index), send_sem.at[array, lane], recv_sem.at[array, lane], (device, z)
        )

    sent = {}

    def send(array, lane, source, index, device):
        copy = copy_of(array, lane, source, index, device)
        copy.start()
        sent[array, lane] = copy

    kept = {}

    def start(array):
        send(array, 0, own(array), dp, near)
        send(array, 1, own(array), dp, far)
        send(array, 2, own(array), dp, sibling)
        kept[array] = pltpu.make_async_copy(own(array), rows_of(wholes[array], dp), own_sem.at[array])
        kept[array].start()

    def relay(array):
        sent[array, 0].wait_recv()
        arrived = rows_of(wholes[array], near)
        send(array, 3, arrived, near, far)
        send(array, 4, arrived, near, sibling)
        sent[array, 1].wait_recv()
        send(array, 5, rows_of(wholes[array], far), far, sibling)

    def pass_on(array):
        sent[array, 3].wait_recv()
        send(array, 6, rows_of(wholes[array], diagonal), diagonal, sibling)

    outs = []

    def ready(array):
        for lane in (2, 4, 5, 6):
            sent[array, lane].wait_recv()
        kept[array].wait()
        if array < weight_count:
            copy = pltpu.make_async_copy(wholes[array], whole_out[array], out_sem.at[array])
            copy.start()
            outs.append(copy)

    def save(ref):
        spot = [ref is other for other in saved_refs].index(True)
        copy = pltpu.make_async_copy(ref, saved_out[spot], save_sem.at[spot])
        copy.start()
        outs.append(copy)

    swaps = []

    def swap(array, target):
        source = states[array]
        count = source.shape[0] // 4
        slots = source.shape[1]
        here = target.at[:, pl.ds(pl.multiple_of(z * slots, 16), slots), :]
        made = []
        for step, other in enumerate(others):
            copy = remote(
                source.at[pl.ds(other * count, count)],
                here,
                swap_send.at[array, step],
                swap_recv.at[array, step],
                (dp, other),
            )
            copy.start()
            made.append(copy)
        keep = pltpu.make_async_copy(source.at[pl.ds(z * count, count)], here, own_sem.at[array_count + array])
        keep.start()
        made.append(keep)
        return made

    order = (W_SMALL, W_SELF, W_SELFOUT, W_IMAGECO, W_TEXTCO, W_TEXTOUT, W_IMAGEOUT, W_TIN, W_TOUT, W_IIN, W_IOUT)
    progress = [0, 0, 0, 0]

    def advance(started, relayed, passed, completed):
        while progress[0] < min(started, len(order)):
            start(order[progress[0]])
            progress[0] += 1
        while progress[1] < min(relayed, len(order)):
            relay(order[progress[1]])
            progress[1] += 1
        while progress[2] < min(passed, len(order)):
            pass_on(order[progress[2]])
            progress[2] += 1
        while progress[3] < min(completed, len(order)):
            ready(order[progress[3]])
            progress[3] += 1

    def upto(array):
        at = order.index(array) + 1
        advance(at + 3, 0, 0, 0)
        advance(at + 3, at + 1, at, at)

    text_in = swap(0, work.text)
    advance(2, 0, 0, 0)
    image_in = swap(1, work.image)
    advance(4, 0, 0, 0)
    swaps += swap(2, cots[0]) + swap(3, cots[1])

    vec96, vec128, bias_in = saved.vec96, saved.vec128, work.bias_in

    def flip(values, width, target, which, first_block):
        turned = values.T
        for block in range(values.shape[1] // width):
            owner = first_block + block
            target[which, owner % 2, owner // 2 * width : (owner // 2 + 1) * width, :] = turned[
                block * width : (block + 1) * width
            ]

    def norm_rows(source, gain, shift, targets):
        def body(step, carry):
            window = pl.ds(pl.multiple_of(step * 32, 32), 32)
            hidden = source[window, :]
            centre = hidden - jnp.mean(hidden, axis=-1, keepdims=True)
            spread = jnp.mean(centre * centre, axis=-1, keepdims=True)
            result = centre * lax.rsqrt(spread + EPSILON) * gain + shift
            targets[window, :] = result.astype(narrow)
            return carry

        lax.fori_loop(0, 8, body, 0)

    def project_all(inputs, array, target, biases):
        width = target.shape[2]
        for k in range(3):

            def body(tile, carry, k=k):
                where = lanes(tile, 256)
                part = mm(inputs, wholes[array][k, :, where])
                if k == 0:
                    part = part + biases[0][:, where]
                if k == 2:
                    part = part + biases[1][:, where]
                target[k, :, where] = part.astype(narrow)
                return carry

            lax.fori_loop(0, width // 256, body, 0)

    def branch(inputs, array, base, bias, target):
        width = target.shape[1]

        def body(tile, carry):
            where = lanes(tile, 256)
            part = mm(inputs, wholes[array][0, :, where])
            target[:, where] = part + base[..., where].reshape(256, 256).astype(wide) + bias[:, where]
            return carry

        lax.fori_loop(0, width // 256, body, 0)

    class Row:
        def __init__(self, ref, index):
            self.ref, self.index = ref, index

        def __getitem__(self, key):
            return self.ref[self.index : self.index + 1, key[1]]

    upto(W_SMALL)
    packed = wholes[W_SMALL]
    for owner in range(8):
        base = owner * SMALL_ROWS
        vec96[:, owner * 96 : owner * 96 + 96] = packed[0, base : base + 16, :96]
        vec128[:, owner * 128 : owner * 128 + 128] = packed[0, base + 16 : base + 32, :]
        for part in range(3):
            at = owner * 384 + part * 128
            bias_in[0:1, at : at + 128] = packed[0, base + 27 + part : base + 28 + part, :]
    save(saved.vec96)
    save(saved.vec128)
    text_lengths = [text_len[z * 2 + pair] for pair in range(2)]
    region_counts = [region_count[z * 2 + pair] for pair in range(2)]
    low, high = head_masks()
    low_narrow, high_narrow = low.astype(narrow), high.astype(narrow)

    for copy in text_in:
        copy.wait()
    upto(W_SELF)
    text = work.text[...].reshape(256, 768)
    qkv_s = saved.qkv_s
    project_all(text, W_SELF, qkv_s, (Row(vec96, 0), Row(vec96, 1)))
    save(saved.qkv_s)

    def self_heads(tile, carry):
        where = lanes(tile, 128)
        for pair in range(2):
            rows = slice(pair * 128, pair * 128 + 128)
            q2, k2, v2 = (qkv_s[k, rows, where] for k in range(3))
            both = jnp.concatenate([q2 * low_narrow, q2 * high_narrow], axis=0)
            table = table_of(mm_t(both, k2), key_mask(text_lengths[pair]), 0.125)
            saved.tab_s[pair * 6 + tile] = table
            mixed = mm(table, v2)
            work.mix_s[rows, where] = (mixed[:128] * low + mixed[128:] * high).astype(narrow)
        return carry

    lax.fori_loop(0, 6, self_heads, 0)
    save(saved.tab_s)
    flip(text, 96, saved.xt768, 0, 0)
    flip(work.mix_s[...], 96, saved.xt768, 1, 0)
    upto(W_SELFOUT)
    branch(work.mix_s[...], W_SELFOUT, work.text, Row(vec96, 8), saved.sum_s)
    norm_rows(saved.sum_s, vec96[2:3], vec96[5:6], work.one)
    save(saved.sum_s)
    flip(work.one[...], 96, saved.xt768, 2, 0)

    for copy in image_in:
        copy.wait()
    upto(W_IMAGECO)
    image = work.image[...].reshape(256, 1024)
    qkv_i, qkv_t = saved.qkv_i, saved.qkv_t
    project_all(image, W_IMAGECO, qkv_i, (Row(vec128, 2), Row(vec128, 3)))
    save(saved.qkv_i)
    flip(image, 128, saved.xt1024, 0, 0)
    upto(W_TEXTCO)
    project_all(work.one[...], W_TEXTCO, qkv_t, (Row(vec128, 0), Row(vec128, 1)))
    save(saved.qkv_t)

    def co_heads(head, carry):
        where = lanes(head, 128)
        shrink = 128**-0.5
        for pair in range(2):
            rows = slice(pair * 128, pair * 128 + 128)
            tq, tk, tv = (qkv_t[k, rows, where] for k in range(3))
            iq, ik, iv = (qkv_i[k, rows, where] for k in range(3))
            table = table_of(mm_t(tq, ik), key_mask(region_counts[pair]), shrink)
            saved.tab_t[pair * 8 + head] = table
            work.mix_t[rows, where] = mm(table, iv).astype(narrow)
            table = table_of(mm_t(iq, tk), key_mask(text_lengths[pair]), shrink)
            saved.tab_i[pair * 8 + head] = table
            work.mix_i[rows, where] = mm(table, tv).astype(narrow)
        return carry

    lax.fori_loop(0, 8, co_heads, 0)
    save(saved.tab_t)
    save(saved.tab_i)
    flip(work.mix_t[...], 128, saved.xt1024, 1, 0)
    flip(work.mix_i[...], 128, saved.xt1024, 2, 0)
    upto(W_TEXTOUT)
    branch(work.mix_t[...], W_TEXTOUT, work.one, Row(vec96, 9), saved.sum_t)
    norm_rows(saved.sum_t, vec96[3:4], vec96[6:7], work.two_t)
    save(saved.sum_t)
    flip(work.two_t[...], 96, saved.xt768, 3, 0)
    save(saved.xt768)
    upto(W_IMAGEOUT)
    branch(work.mix_i[...], W_IMAGEOUT, work.image, Row(vec128, 9), saved.sum_i)
    norm_rows(saved.sum_i, vec128[5:6], vec128[7:8], work.two_i)
    save(saved.sum_i)
    flip(work.two_i[...], 128, saved.xt1024, 3, 0)

    def activate(inner):
        share = 0.5 + 0.5 * lax.erf(inner * ROOT_HALF)
        slope = share + inner * (ROOT_TURN * jnp.exp(-0.5 * inner * inner))
        return ((inner * share).astype(narrow), slope.astype(narrow))

    upto(W_TIN)
    upto(W_TOUT)
    two_t = work.two_t
    tot_t = saved.tot_t
    tot_t[...] = two_t[...].astype(wide) + vec96[10:11]

    def text_inner(owner, carry):
        where = lanes(owner, 384)
        inner = mm(two_t[...], wholes[W_TIN][0, :, where]) + bias_in[0:1, where]
        active, slope = activate(inner)
        saved.slope_t[:, where] = slope
        saved.xt3072[0, lax.rem(owner, 2), pl.ds(pl.multiple_of(lax.div(owner, 2) * 384, 384), 384), :] = active.T
        tot_t[...] += mm(active, wholes[W_TOUT][0, where, :])
        return carry

    lax.fori_loop(0, 8, text_inner, 0)
    save(saved.slope_t)
    save(saved.xt3072)
    save(saved.tot_t)
    norm_rows(tot_t, vec96[4:5], vec96[7:8], saved.out_t)
    save(saved.out_t)

    upto(W_IIN)
    two_i = work.two_i
    tot_i = saved.tot_i
    for part in range(4):
        where = slice(part * 256, part * 256 + 256)
        inner = mm(two_i[...], wholes[W_IIN][0, :, where]) + vec128[4:5, where]
        active, slope = activate(inner)
        saved.slope_i[:, where] = slope
        flip(active, 128, saved.xt1024, 4, part * 2)
        work.mix_i[:, where] = active
    save(saved.slope_i)
    save(saved.xt1024)
    upto(W_IOUT)
    branch(work.mix_i[...], W_IOUT, two_i, Row(vec128, 10), tot_i)
    save(saved.tot_i)
    norm_rows(tot_i, vec128[6:7], vec128[8:9], saved.out_i)
    save(saved.out_i)

    for copy in sent.values():
        copy.wait_send()
    for copy in swaps:
        copy.wait()
    for copy in outs:
        copy.wait()


def forward_all(blocks, small, states, text_len, region_count):
    dma = pltpu.SemaphoreType.DMA
    narrow = jnp.bfloat16
    count = len(WEIGHT_SHAPES)
    shape = jax.ShapeDtypeStruct
    out_shape = [shape(w, narrow) for w in WEIGHT_SHAPES]
    out_shape += [shape(dims, kind) for dims, kind in SAVED.values()]
    out_shape += [shape((s.shape[0] // 4, s.shape[1] * 4, s.shape[2]), s.dtype) for s in states[2:]]
    scratch = [pltpu.VMEM(w, narrow) for w in WEIGHT_SHAPES]
    scratch += [pltpu.VMEM((1, 8 * SMALL_ROWS, 128), jnp.float32)]
    scratch += [pltpu.VMEM(dims, kind) for dims, kind in (*SAVED.values(), *WORK.values())]
    scratch += [
        dma((count + 1, 7)),
        dma((count + 1, 7)),
        dma((4, 3)),
        dma((4, 3)),
        dma((count + 5,)),
        dma((count,)),
        dma((len(SAVED),)),
    ]
    results = pl.pallas_call(
        forward_kernel,
        out_shape=out_shape,
        in_specs=[ANY] * count
        + [VMEM] * SMALL_COUNT
        + [ANY] * 4
        + [pl.BlockSpec(memory_space=pltpu.SMEM)] * 2,
        out_specs=[ANY] * len(out_shape),
        scratch_shapes=scratch,
        compiler_params=pltpu.CompilerParams(
            collective_id=0, has_side_effects=True, vmem_limit_bytes=62 * 2**20
        ),
        name="forward_all",
    )(*blocks, *small, *states, text_len, region_count)
    wholes = results[:count]
    saved = types.SimpleNamespace(**dict(zip(SAVED, results[count : count + len(SAVED)])))
    return (wholes, saved, results[count + len(SAVED) :])


CHUNKS = (9, 9, 3)
TILES = (4, 3, 1)
ROWS = (96, 128, 384)
STARTS = ((9, 12, 24), (12, 15, 19, 23), ())
ORDER = ((2, 0, 3), (0, 6, 3), (1, 4, 5), (0, 3, 3), (1, 0, 4), (0, 0, 3))
STEPS = 21
LAG_NEAR, LAG_FAR, LAG_SUM, LAG_MID, LAG_END, LAG_WRITE = 1, 3, 5, 7, 9, 11
SMALL_TURN = 18
CHIP_SLOTS, NEAR_SLOTS, PLANE_SLOTS = 7, 9, 9
AT_BSELF, AT_TEXTCO, AT_TIN = 2304, 3072, 6144
AT_BTEXT, AT_BIMAGE, AT_IIN, AT_BIFF = 3072, 3840, 4864, 5888


def backward_kernel(*refs):
    refs = list(refs)

    def take(count):
        taken = refs[:count]
        del refs[:count]
        return taken

    narrow, wide = jnp.bfloat16, jnp.float32
    weights = take(len(WEIGHT_SHAPES))
    saved = types.SimpleNamespace(**dict(zip(SAVED, take(len(SAVED)))))
    cot_t, cot_i = take(2)
    result, small_result = take(2)
    pairs = take(4)
    out_box, chip, near_sum, plane, line, cross = take(6)
    s_own, s_chip, s_near, s_plane, s_line, s_cross = take(6)
    w_p, w_q, w_i, w_o = take(4)
    dz768, dz1024, dz3072 = take(3)
    xt = take(3)
    tab_s, tab_t, tab_i, sum_s, sum_t, sum_i, tot_t, tot_i, vec96, vec128 = take(10)
    mix_t, mix_i, back_t, back_i, sums96, sums128, sums_in = take(7)
    (
        core_send, core_recv, near_send, near_recv, far_send, far_recv,
        end_send, end_recv, mid_send, mid_recv, back_send, back_recv,
        write_sem, swap_send, swap_recv, own_sem, load_sem,
    ) = refs
    dp, z, row, col, core = place()
    near, far = partners(row, col, core, core)
    sibling = dp + 1 - 2 * core
    others = [lax.rem(z + step, 4) for step in (1, 2, 3)]
    near_bit = col + core * (row - col)
    far_bit = row + core * (col - row)

    def block_of(near_index, far_index):
        return near_index * (1 + core) + far_index * (2 - core)

    is_end = (z == 0) | (z == 3)
    is_mid = (z == 1) | (z == 2)
    middle = 1 + z // 2
    other_mid = 3 - z
    end = 3 * (z // 2)

    def span(ref, first, width):
        return ref.at[:, first : first + width]

    loads = []

    def load(*moves):
        made = []
        for source, target in moves:
            copy = pltpu.make_async_copy(source, target, load_sem.at[len(loads)])
            loads.append(copy)
            made.append(copy)
        return made

    def begin(group):
        for copy in group:
            copy.start()

    def finish(group):
        for copy in group:
            copy.wait()

    get_text3 = load(
        (saved.tot_t, tot_t),
        (cot_t.reshape(256, 768), span(dz768, AT_BSELF, 768)),
        (saved.vec96, vec96),
        *((weights[W_TOUT].at[0, pl.ds(i * 768, 768), :], w_q.at[i]) for i in range(4)),
    )
    get_text_in = load(
        (saved.xt3072, xt[2]),
        (saved.xt768, xt[0]),
        (saved.slope_t, span(dz768, AT_TIN, 3072)),
        *((weights[W_TIN].at[0, :, pl.ds(i * 1024, 1024)], w_p.at[i]) for i in range(3)),
    )
    get_image = load(
        (saved.tot_i, tot_i),
        (cot_i.reshape(256, 1024), span(dz1024, AT_BIMAGE, 1024)),
        (saved.vec128, vec128),
        (weights[W_IOUT].at[0], w_i.at[0]),
        (saved.slope_i, span(dz1024, AT_IIN, 1024)),
        (weights[W_IIN].at[0], w_i.at[1]),
    )
    get_co = load(
        (saved.sum_t, sum_t),
        (weights[W_TEXTOUT].at[0], w_o),
        (saved.sum_i, sum_i),
        (weights[W_IMAGEOUT].at[0], w_i.at[2]),
    )
    get_heads = load(
        (saved.xt1024, xt[1]),
        *((saved.qkv_t.at[k], span(dz768, AT_TEXTCO + k * 1024, 1024)) for k in range(3)),
        *((saved.qkv_i.at[k], span(dz1024, k * 1024, 1024)) for k in range(3)),
        (saved.tab_t, tab_t),
        (saved.tab_i, tab_i),
    )
    get_self = load(
        (saved.sum_s, sum_s),
        *((saved.qkv_s.at[k], span(dz768, k * 768, 768)) for k in range(3)),
        (saved.tab_s, tab_s),
    )
    get_textco = load((weights[W_TEXTCO], w_p))
    get_selfs = load((weights[W_SELF], w_q.at[pl.ds(0, 3)]), (weights[W_SELFOUT].at[0], w_q.at[3]))
    get_imageco = load((weights[W_IMAGECO], w_i))
    for group in (get_text3, get_text_in, get_image, get_co, get_heads, get_self):
        begin(group)
    sums96[...] = jnp.zeros((16, 768), wide)
    sums128[...] = jnp.zeros((16, 1024), wide)
    s_own[...] = jnp.zeros((2, 4, SMALL_ROWS, 128), wide)

    greet([(near, z), (far, z), (sibling, z)] + [(dp, other) for other in others])

    def swap(array, source):
        target = pairs[array]
        count, slots = source.shape[0], source.shape[1] // 4
        there = target.at[pl.ds(z * count, count)]

        def part(other):
            return source.at[:, pl.ds(pl.multiple_of(other * slots, 16), slots), :]

        made = [
            remote(part(other), there, swap_send.at[array, step], swap_recv.at[array, step], (dp, other))
            for step, other in enumerate(others)
        ]
        made.append(pltpu.make_async_copy(part(z), there, own_sem.at[array]))
        return made

    swaps = [
        swap(0, saved.out_t.reshape(2, 128, 768)),
        swap(1, saved.out_i.reshape(2, 128, 1024)),
        swap(2, back_t),
        swap(3, back_i),
    ]
    begin(swaps[0] + swaps[1])

    grads = (dz768, dz1024, dz3072)

    def products(index, half, use):
        place_ = 0
        for kind in range(3):
            chunk, chosen = 0, False
            first = 0
            for kind_, start, count in ORDER:
                if kind_ == kind:
                    inside = (index >= first) & (index < first + count)
                    chunk = jnp.where(inside, index - first + start, chunk)
                    chosen = chosen | inside
                first += count

            def work(kind=kind, chunk=chunk):
                tiles, rows = TILES[kind], ROWS[kind]
                for tile in range(tiles):
                    which = chunk * tiles + tile
                    weight = 0
                    for bound in STARTS[kind]:
                        weight = weight + jnp.where(which >= bound, 1, 0)
                    part = mm(xt[kind][weight, half], grads[kind][:, lanes(which, 256)])
                    for block in range(4):
                        for side in range(2):
                            use(
                                block,
                                (tile * 2 + side) * rows,
                                rows,
                                part[block * rows : (block + 1) * rows, side * 128 : side * 128 + 128],
                            )

            pl.when(chosen)(work)

    def core_copy(index):
        return remote(
            out_box.at[lax.rem(index, 2)],
            chip.at[lax.rem(index, CHIP_SLOTS)],
            core_send.at[index],
            core_recv.at[index],
            (sibling, z),
        )

    def near_copy(index, far_index):
        return remote(
            chip.at[lax.rem(index, CHIP_SLOTS), block_of(1 - near_bit, far_index)],
            near_sum.at[lax.rem(index, NEAR_SLOTS), far_index],
            near_send.at[index, far_index],
            near_recv.at[index, far_index],
            (near, z),
        )

    def far_copy(index):
        return remote(
            near_sum.at[lax.rem(index, NEAR_SLOTS), 1 - far_bit],
            plane.at[lax.rem(index, PLANE_SLOTS)],
            far_send.at[index],
            far_recv.at[index],
            (far, z),
        )

    def end_copy(index):
        return remote(
            plane.at[lax.rem(index, PLANE_SLOTS)], line.at[index], end_send.at[index], end_recv.at[index], (dp, middle)
        )

    def mid_copy(index):
        return remote(line.at[index], cross.at[index], mid_send.at[index], mid_recv.at[index], (dp, other_mid))

    def back_copy(index):
        return remote(cross.at[index], line.at[index], back_send.at[index], back_recv.at[index], (dp, end))

    def mid_write(index):
        return pltpu.make_async_copy(cross.at[index], result.at[index], write_sem.at[index])

    def end_write(index):
        return pltpu.make_async_copy(line.at[index], result.at[index], write_sem.at[index])

    def add(left, right):
        return (left.astype(wide) + right.astype(wide)).astype(narrow)

    def stage_core(index):
        @pl.when(index >= 2)
        def _():
            core_copy(index - 2).wait_send()

        slot = lax.rem(index, 2)

        def put(block, first, rows, values):
            out_box[slot, block, first : first + rows, :] = values.astype(narrow)

        products(index, 1 - core, put)
        core_copy(index).start()

    def stage_near(index):
        core_copy(index).wait_recv()
        slot = lax.rem(index, CHIP_SLOTS)

        def put(block, first, rows, values):
            window = (slot, block, slice(first, first + rows), slice(None))
            chip[window] = (chip[window].astype(wide) + values).astype(narrow)

        products(index, core, put)
        near_copy(index, 1 - far_bit).start()
        near_copy(index, far_bit).start()

    def stage_far(index):
        chip_slot, slot = lax.rem(index, CHIP_SLOTS), lax.rem(index, NEAR_SLOTS)
        for far_index in (1 - far_bit, far_bit):
            near_copy(index, far_index).wait_recv()
            near_sum[slot, far_index] = add(near_sum[slot, far_index], chip[chip_slot, block_of(near_bit, far_index)])
            if far_index is not far_bit:
                far_copy(index).start()
        near_copy(index, 0).wait_send()
        near_copy(index, 1).wait_send()

    def stage_sum(index):
        slot = lax.rem(index, PLANE_SLOTS)
        far_copy(index).wait_recv()
        plane[slot] = add(plane[slot], near_sum[lax.rem(index, NEAR_SLOTS), far_bit])

        @pl.when(is_end)
        def _():
            end_copy(index).start()

        far_copy(index).wait_send()

    def stage_mid(index):
        @pl.when(is_mid)
        def _():
            end_copy(index).wait_recv()
            line[index] = add(line[index], plane[lax.rem(index, PLANE_SLOTS)])
            mid_copy(index).start()

        @pl.when(is_end)
        def _():
            end_copy(index).wait_send()

    def stage_end(index):
        @pl.when(is_mid)
        def _():
            mid_copy(index).wait_recv()
            cross[index] = add(cross[index], line[index])
            back_copy(index).start()
            mid_write(index).start()

    def stage_write(index):
        @pl.when(is_end)
        def _():
            back_copy(index).wait_recv()
            end_write(index).start()

    stages = (
        (stage_core, 0),
        (stage_near, LAG_NEAR),
        (stage_far, LAG_FAR),
        (stage_sum, LAG_SUM),
        (stage_mid, LAG_MID),
        (stage_end, LAG_END),
        (stage_write, LAG_WRITE),
    )

    last = STEPS
    sm_core = remote(s_own.at[1 - core], s_chip, core_send.at[last], core_recv.at[last], (sibling, z))
    sm_near = [
        remote(
            s_chip.at[block_of(1 - near_bit, j)], s_near.at[j], near_send.at[last, j], near_recv.at[last, j], (near, z)
        )
        for j in (0, 1)
    ]
    sm_far = remote(s_near.at[1 - far_bit], s_plane, far_send.at[last], far_recv.at[last], (far, z))
    sm_end = remote(s_plane, s_line, end_send.at[last], end_recv.at[last], (dp, middle))
    sm_mid = remote(s_line, s_cross, mid_send.at[last], mid_recv.at[last], (dp, other_mid))
    sm_back = remote(s_cross, s_line, back_send.at[last], back_recv.at[last], (dp, end))

    def small_start():
        for owner in range(8):
            spot = s_own.at[owner % 2, owner // 2]
            spot[0:16, :96] = sums96[:, owner * 96 : owner * 96 + 96]
            spot[16:27, :] = sums128[0:11, owner * 128 : owner * 128 + 128]
            for part in range(3):
                at = owner * 384 + part * 128
                spot[27 + part : 28 + part, :] = sums_in[0:1, at : at + 128]
        sm_core.start()

    def small_near():
        sm_core.wait_recv()
        s_chip[...] += s_own[core]
        begin(sm_near)

    def small_far():
        for j in (0, 1):
            sm_near[j].wait_recv()
            s_near[j] += s_chip[block_of(near_bit, j)]
        sm_far.start()

    def small_sum():
        sm_far.wait_recv()
        s_plane[...] += s_near[far_bit]
        pl.when(is_end)(sm_end.start)

    def small_mid():
        @pl.when(is_mid)
        def _():
            sm_end.wait_recv()
            s_line[...] += s_plane[...]
            sm_mid.start()

    def small_end():
        @pl.when(is_mid)
        def _():
            sm_mid.wait_recv()
            s_cross[...] += s_line[...]
            sm_back.start()
            small_result[...] = s_cross[...]

    def small_write():
        @pl.when(is_end)
        def _():
            sm_back.wait_recv()
            small_result[...] = s_line[...]

    def norm_step(source, upstream, gain, target, first, sums, rows):
        width = source.shape[1]

        def body(step, carry):
            window = pl.ds(pl.multiple_of(step * 32, 32), 32)
            hidden = source[window, :]
            dy = upstream[window, first[0] : first[0] + width].astype(wide)
            centre = hidden - jnp.mean(hidden, axis=-1, keepdims=True)
            spread = jnp.mean(centre * centre, axis=-1, keepdims=True)
            scale = lax.rsqrt(spread + EPSILON)
            unit = centre * scale
            inner = dy * gain
            back = scale * (
                inner
                - jnp.mean(inner, axis=-1, keepdims=True)
                - unit * jnp.mean(inner * unit, axis=-1, keepdims=True)
            )
            rounded = back.astype(narrow)
            source[window, :] = back
            target[window, first[1] : first[1] + width] = rounded
            parts = (dy * unit, dy, rounded.astype(wide))
            return tuple(c + p.reshape(4, 8, width).sum(axis=0) for c, p in zip(carry, parts))

        zero = jnp.zeros((8, width), wide)
        totals = lax.fori_loop(0, 8, body, (zero, zero, zero))
        for at, total in zip(rows, totals):
            sums[at : at + 1, :] = jnp.sum(total, axis=0, keepdims=True)

    def col_sum(values):
        return jnp.sum(values.astype(wide), axis=0, keepdims=True)

    def text_three():
        finish(get_text3)
        norm_step(tot_t, dz768, vec96[4:5], dz3072, (AT_BSELF, 0), sums96, (4, 7, 10))

    def text_inner(turn):
        for part in range(4):
            which = turn * 4 + part
            where = pl.ds(pl.multiple_of(AT_TIN + which * 256, 256), 256)
            out_rows = w_q[lax.div(which, 3), pl.ds(pl.multiple_of(lax.rem(which, 3) * 256, 256), 256), :]
            inner = (dz768[:, where].astype(wide) * mm_t(dz3072[...], out_rows)).astype(narrow)
            dz768[:, where] = inner
            sums_in[0:1, lanes(which, 256)] = col_sum(inner)
            tot_t[...] += mm_t(inner, w_p[turn, :, part * 256 : part * 256 + 256])

    def image_three():
        begin(get_textco)
        begin(get_selfs)
        finish(get_image)
        norm_step(tot_i, dz1024, vec128[6:7], dz1024, (AT_BIMAGE, AT_BIFF), sums128, (6, 8, 10))
        branch = dz1024[:, AT_BIFF : AT_BIFF + 1024]
        for part in range(4):
            at = part * 256
            where = slice(AT_IIN + at, AT_IIN + at + 256)
            inner = (dz1024[:, where].astype(wide) * mm_t(branch, w_i[0, at : at + 256, :])).astype(narrow)
            dz1024[:, where] = inner
            sums128[4:5, at : at + 256] = col_sum(inner)
            tot_i[...] += mm_t(inner, w_i[1, :, at : at + 256])

    def text_second():
        finish(get_co)
        norm_step(sum_t, tot_t, vec96[3:4], dz1024, (0, AT_BTEXT), sums96, (3, 6, 9))
        mix_t[...] = mm_t(dz1024[:, AT_BTEXT : AT_BTEXT + 768], w_o[...]).astype(narrow)

    def image_second():
        norm_step(sum_i, tot_i, vec128[5:6], dz1024, (0, AT_BIMAGE), sums128, (5, 7, 9))
        mix_i[...] = mm_t(dz1024[:, AT_BIMAGE : AT_BIMAGE + 1024], w_i[2]).astype(narrow)
        begin(get_imageco)
        finish(get_heads)

    def table_back(table, upper_value):
        probs = table.astype(wide)
        return (probs * (upper_value - jnp.sum(upper_value * probs, axis=-1, keepdims=True))).astype(narrow)

    def co_head(head):
        shrink = 128**-0.5
        for pair in range(2):
            rows = slice(pair * 128, pair * 128 + 128)
            t_at = [pl.ds(pl.multiple_of(AT_TEXTCO + k * 1024 + head * 128, 128), 128) for k in range(3)]
            i_at = [pl.ds(pl.multiple_of(k * 1024 + head * 128, 128), 128) for k in range(3)]
            tq, tk, tv = (dz768[rows, at] for at in t_at)
            iq, ik, iv = (dz1024[rows, at] for at in i_at)
            for q, k, v, table, mixed, spots in (
                (tq, ik, iv, tab_t, mix_t, ((dz768, t_at[0]), (dz1024, i_at[1]), (dz1024, i_at[2]))),
                (iq, tk, tv, tab_i, mix_i, ((dz1024, i_at[0]), (dz768, t_at[1]), (dz768, t_at[2]))),
            ):
                probs = table[pair * 8 + head]
                upper = mixed[rows, lanes(head, 128)]
                score = table_back(probs, mm_t(upper, v))
                grads_ = (mm(score, k) * shrink, mm_0(score, q) * shrink, mm_0(probs, upper))
                for (ref, at), value in zip(spots, grads_):
                    ref[rows, at] = value.astype(narrow)

    def co_heads(turn):
        co_head(turn * 2 - 12)
        co_head(turn * 2 - 11)

    def text_one_back():
        finish(get_textco)
        for k in range(3):
            where = slice(AT_TEXTCO + k * 1024, AT_TEXTCO + (k + 1) * 1024)
            sum_t[...] += mm_t(dz768[:, where], w_p[k])
        sums128[0:1, :] = col_sum(dz768[:, AT_TEXTCO : AT_TEXTCO + 1024])
        sums128[1:2, :] = col_sum(dz768[:, AT_TEXTCO + 2048 : AT_TEXTCO + 3072])

    def self_second():
        finish(get_self)
        finish(get_selfs)
        norm_step(sum_s, sum_t, vec96[2:3], dz768, (0, AT_BSELF), sums96, (2, 5, 8))
        mix_t[:, 0:768] = mm_t(dz768[:, AT_BSELF : AT_BSELF + 768], w_q[3]).astype(narrow)

    def image_back():
        finish(get_imageco)
        for k in range(3):
            sum_i[...] += mm_t(dz1024[:, k * 1024 : (k + 1) * 1024], w_i[k])
        sums128[2:3, :] = col_sum(dz1024[:, 0:1024])
        sums128[3:4, :] = col_sum(dz1024[:, 2048:3072])
        back_i[...] = sum_i[...].astype(narrow).reshape(2, 128, 1024)
        begin(swaps[3])

    low, high = head_masks()
    low_narrow, high_narrow = low.astype(narrow), high.astype(narrow)

    def self_heads(turn):
        tile = turn - 12
        for pair in range(2):
            rows = slice(pair * 128, pair * 128 + 128)
            at = [pl.ds(pl.multiple_of(k * 768 + tile * 128, 128), 128) for k in range(3)]
            q2, k2, v2 = (dz768[rows, where] for where in at)
            upper = mix_t[rows, lanes(tile, 128)]
            uppers = jnp.concatenate([upper * low_narrow, upper * high_narrow], axis=0)
            queries = jnp.concatenate([q2 * low_narrow, q2 * high_narrow], axis=0)
            probs = tab_s[pair * 6 + tile]
            score = table_back(probs, mm_t(uppers, v2))
            query = mm(score, k2)
            dz768[rows, at[0]] = ((query[:128] * low + query[128:] * high) * 0.125).astype(narrow)
            dz768[rows, at[1]] = (mm_0(score, queries) * 0.125).astype(narrow)
            dz768[rows, at[2]] = mm_0(probs, uppers).astype(narrow)

    def text_back():
        for k in range(3):
            sum_s[...] += mm_t(dz768[:, k * 768 : (k + 1) * 768], w_q[k])
        sums96[0:1, :] = col_sum(dz768[:, 0:768])
        sums96[1:2, :] = col_sum(dz768[:, 1536:2304])
        back_t[...] = sum_s[...].astype(narrow).reshape(2, 128, 768)
        begin(swaps[2])
        small_start()

    text_three()
    finish(get_text_in)

    def turn_body(turn, carry):
        for stage, lag in stages:
            index = turn - lag

            @pl.when((index >= 0) & (index < STEPS))
            def _(stage=stage, index=index):
                stage(index)

        pl.when(turn < 3)(lambda: text_inner(turn))
        pl.when(turn == 3)(image_three)
        pl.when(turn == 4)(text_second)
        pl.when(turn == 5)(image_second)
        pl.when((turn >= 6) & (turn < 10))(lambda: co_heads(turn))

        @pl.when(turn == 10)
        def _():
            text_one_back()
            image_back()

        pl.when(turn == 11)(self_second)
        pl.when((turn >= 12) & (turn < 18))(lambda: self_heads(turn))
        pl.when(turn == SMALL_TURN)(text_back)
        for lag, step in (
            (LAG_NEAR, small_near),
            (LAG_FAR, small_far),
            (LAG_SUM, small_sum),
            (LAG_MID, small_mid),
            (LAG_END, small_end),
            (LAG_WRITE, small_write),
        ):
            pl.when(turn == SMALL_TURN + lag)(step)
        return carry

    lax.fori_loop(0, STEPS + LAG_WRITE, turn_body, 0)

    core_copy(STEPS - 2).wait_send()
    core_copy(STEPS - 1).wait_send()
    sm_core.wait_send()
    for copy in sm_near:
        copy.wait_send()
    sm_far.wait_send()

    def settle(index, carry):
        @pl.when(is_end)
        def _():
            end_write(index).wait()

        @pl.when(is_mid)
        def _():
            mid_copy(index).wait_send()
            back_copy(index).wait_send()
            mid_write(index).wait()

        return carry

    lax.fori_loop(0, STEPS, settle, 0)

    @pl.when(is_end)
    def _():
        sm_end.wait_send()

    @pl.when(is_mid)
    def _():
        sm_mid.wait_send()
        sm_back.wait_send()

    for group in swaps:
        finish(group)


def backward_all(weights, saved, cots):
    dma = pltpu.SemaphoreType.DMA
    shape = jax.ShapeDtypeStruct
    vmem = pltpu.VMEM
    narrow, wide = jnp.bfloat16, jnp.float32
    block = (768, 128)
    tiny = (SMALL_ROWS, 128)
    kept = [getattr(saved, name) for name in SAVED]
    one = [dma((STEPS + 1,))] * 2
    results = pl.pallas_call(
        backward_kernel,
        out_shape=[
            shape((STEPS,) + block, narrow),
            shape(tiny, wide),
            shape((8, 32, 768), narrow),
            shape((8, 32, 1024), narrow),
            shape((8, 32, 768), narrow),
            shape((8, 32, 1024), narrow),
        ],
        in_specs=[ANY] * (len(weights) + len(kept) + 2),
        out_specs=[ANY, VMEM] + [ANY] * 4,
        scratch_shapes=[
            vmem((2, 4) + block, narrow),
            vmem((CHIP_SLOTS, 4) + block, narrow),
            vmem((NEAR_SLOTS, 2) + block, narrow),
            vmem((PLANE_SLOTS,) + block, narrow),
            vmem((STEPS,) + block, narrow),
            vmem((STEPS,) + block, narrow),
            vmem((2, 4) + tiny, wide),
            vmem((4,) + tiny, wide),
            vmem((2,) + tiny, wide),
            vmem(tiny, wide),
            vmem(tiny, wide),
            vmem(tiny, wide),
            vmem((3, 768, 1024), narrow),
            vmem((4, 768, 768), narrow),
            vmem((3, 1024, 1024), narrow),
            vmem((1024, 768), narrow),
            vmem((256, 9216), narrow),
            vmem((256, 6912), narrow),
            vmem((256, 768), narrow),
            vmem((4, 2, 384, 256), narrow),
            vmem((5, 2, 512, 256), narrow),
            vmem((1, 2, 1536, 256), narrow),
            vmem((12, 256, 128), narrow),
            vmem((16, 128, 128), narrow),
            vmem((16, 128, 128), narrow),
            vmem((256, 768), wide),
            vmem((256, 768), wide),
            vmem((256, 1024), wide),
            vmem((256, 768), wide),
            vmem((256, 1024), wide),
            vmem((16, 768), wide),
            vmem((16, 1024), wide),
            vmem((256, 1024), narrow),
            vmem((256, 1024), narrow),
            vmem((2, 128, 768), narrow),
            vmem((2, 128, 1024), narrow),
            vmem((16, 768), wide),
            vmem((16, 1024), wide),
            vmem((8, 3072), wide),
        ]
        + one
        + [dma((STEPS + 1, 2))] * 2
        + one * 4
        + [dma((STEPS,)), dma((4, 3)), dma((4, 3)), dma((4,)), dma((48,))],
        compiler_params=pltpu.CompilerParams(
            collective_id=1, has_side_effects=True, vmem_limit_bytes=62 * 2**20
        ),
        name="backward_all",
    )(*weights, *kept, *cots)
    return (results[0], results[1], results[2:])


UNPACK = (
    ((0, 18, 6), (1, 6, 6), (3, 24, 8), (6, 24, 24)),
    ((2, 24, 8), (4, 6, 6), (5, 8, 8), (8, 8, 8), (9, 8, 8)),
    ((7, 6, 6),),
)


def unpack_kernel(*refs):
    summed, small = refs[:2]
    states = refs[2:6]
    weights = refs[6:16]
    smalls = refs[16 : 16 + SMALL_COUNT]
    targets = refs[16 + SMALL_COUNT : 20 + SMALL_COUNT]
    sem = refs[-1]
    copies = [pltpu.make_async_copy(states[i], targets[i], sem.at[i]) for i in range(4)]
    for copy in copies:
        copy.start()
    places = [{}, {}, {}]
    turn = 0
    for kind, start, count in ORDER:
        for chunk in range(start, start + count):
            places[kind][chunk] = turn
            turn += 1
    for kind in range(3):
        rows = ROWS[kind]
        tile = 0
        for weight, tiles, width in UNPACK[kind]:
            for own_tile in range(tiles):
                at, side = divmod(tile, TILES[kind] * 2)
                values = summed[places[kind][at], side * rows : (side + 1) * rows, :]
                part, column = divmod(own_tile, width)
                weights[weight][part, :, column * 128 : column * 128 + 128] = values.astype(jnp.float32)
                tile += 1
    for (first, rows, width), ref in zip(SMALL_PLACES, smalls):
        ref[...] = small[first : first + rows, :width]
    for copy in copies:
        copy.wait()


def unpack(summed, small, states):
    shape = jax.ShapeDtypeStruct
    out_shape = [shape((w[0], w[1] // 8, w[2]), jnp.float32) for w in WEIGHT_SHAPES]
    out_shape += [shape((rows, width), jnp.float32) for first, rows, width in SMALL_PLACES]
    out_shape += [shape(s.shape, s.dtype) for s in states]
    results = pl.pallas_call(
        unpack_kernel,
        out_shape=out_shape,
        in_specs=[VMEM] * 2 + [ANY] * 4,
        out_specs=[VMEM] * (10 + SMALL_COUNT) + [ANY] * 4,
        scratch_shapes=[pltpu.SemaphoreType.DMA((4,))],
        compiler_params=pltpu.CompilerParams(vmem_limit_bytes=40 * 2**20),
        name="unpack",
    )(summed, small, *states)
    return (results[:10], results[10 : 10 + SMALL_COUNT], results[10 + SMALL_COUNT :])


def local_fast(
    text, image, text_len, region_count, text_cot, image_cot,
    selfproject, selfbiases, selfoutput, textcoproject, textcobiases, imagecoproject, imagecobiases,
    textcooutput, imagecooutput, textffinner, textffinbias, textffouter,
    imageffinner, imageffinbias, imageffouter,
    textgains, textshifts, textbiases, imagegains, imageshifts, imagebiases,
):
    blocks = [
        selfproject.transpose(1, 0, 2), selfoutput[None], imagecoproject.transpose(1, 0, 2),
        textcoproject.transpose(1, 0, 2), textcooutput[None], imagecooutput[None],
        textffinner[None], textffouter[None], imageffinner[None], imageffouter[None],
    ]
    small = [
        selfbiases, textcobiases, imagecobiases, textffinbias.reshape(3, 128), imageffinbias.reshape(1, 128),
        textgains, textshifts, textbiases, imagegains, imageshifts, imagebiases,
    ]
    weights, saved, cots = forward_all(blocks, small, [text, image, text_cot, image_cot], text_len, region_count)
    summed, small_sum, outputs = backward_all(weights, saved, cots)
    g, s, outputs = unpack(summed, small_sum, outputs)
    return tuple(outputs) + (
        g[W_SELF].transpose(1, 0, 2), s[0], g[W_SELFOUT][0], g[W_TEXTCO].transpose(1, 0, 2), s[1],
        g[W_IMAGECO].transpose(1, 0, 2), s[2], g[W_TEXTOUT][0], g[W_IMAGEOUT][0],
        g[W_TIN][0], s[3].reshape(-1), g[W_TOUT][0], g[W_IIN][0], s[4].reshape(-1), g[W_IOUT][0],
        s[5], s[6], s[7], s[8], s[9], s[10],
    )


def solution(mesh):
    in_specs = (
        P("dp", "seq", None),
        P("dp", "seq", None),
        P("dp"),
        P("dp"),
        P("dp", "seq", None),
        P("dp", "seq", None),
        P("dp", None, None),
        P(None, "dp"),
        P("dp", None),
        P("dp", None, None),
        P(None, "dp"),
        P("dp", None, None),
        P(None, "dp"),
        P("dp", None),
        P("dp", None),
        P("dp", None),
        P("dp"),
        P("dp", None),
        P("dp", None),
        P("dp"),
        P("dp", None),
        P(None, "dp"),
        P(None, "dp"),
        P(None, "dp"),
        P(None, "dp"),
        P(None, "dp"),
        P(None, "dp"),
    )
    out_specs = (
        P("dp", "seq", None),
        P("dp", "seq", None),
        P("dp", "seq", None),
        P("dp", "seq", None),
        P("dp", None, None),
        P(None, "dp"),
        P("dp", None),
        P("dp", None, None),
        P(None, "dp"),
        P("dp", None, None),
        P(None, "dp"),
        P("dp", None),
        P("dp", None),
        P("dp", None),
        P("dp"),
        P("dp", None),
        P("dp", None),
        P("dp"),
        P("dp", None),
        P(None, "dp"),
        P(None, "dp"),
        P(None, "dp"),
        P(None, "dp"),
        P(None, "dp"),
        P(None, "dp"),
    )
    sizes = mesh.shape
    local = local_fast if (sizes["dp"], sizes["seq"]) == (8, 4) else local_plain
    return jax.shard_map(local, mesh=mesh, in_specs=in_specs, out_specs=out_specs, check_vma=False)
```

```python
import functools
import types

import jax
import jax.numpy as jnp
from jax import lax
from jax.experimental import pallas as pl
from jax.experimental.pallas import tpu as pltpu
from jax.sharding import PartitionSpec as P

HT = 12
HC = 8
MB = 2


EPSILON = 1e-05
NEG_FILL = -1e30


def layer_norm(hidden, factor, offset):
    centre = hidden - jnp.mean(hidden, axis=-1, keepdims=True)
    spread = jnp.mean(centre * centre, axis=-1, keepdims=True)
    return centre * lax.rsqrt(spread + EPSILON) * factor + offset


def norm_back(hidden, factor, offset, upstream):
    outcome, pullback = jax.vjp(layer_norm, hidden, factor, offset)
    return pullback(upstream)


def gelu_exact(hidden):
    return jax.nn.gelu(hidden, approximate=False)


def gelu_back(hidden, upstream):
    outcome, pullback = jax.vjp(gelu_exact, hidden)
    return pullback(upstream)[0]


def linear(inputs, weight):
    return jnp.einsum("pte,ef->ptf", inputs, weight, preferred_element_type=jnp.float32)


def linear_weight(inputs, gradient):
    return jnp.einsum("pte,ptf->ef", inputs, gradient, preferred_element_type=jnp.float32)


def linear_input(gradient, weight):
    return jnp.einsum("ptf,ef->pte", gradient, weight, preferred_element_type=jnp.float32)


def row_total(gradient):
    return jnp.sum(gradient, axis=(0, 1), dtype=jnp.float32)


def project(inputs, weight, biases):
    bias_rows = biases.astype(jnp.float32)
    stacked = jnp.stack([bias_rows[0], jnp.zeros_like(bias_rows[0]), bias_rows[1]])
    triple = jnp.einsum("pte,ekf->ptkf", inputs, weight, preferred_element_type=jnp.float32)
    return (triple + stacked).astype(jnp.bfloat16)


def project_back(inputs, gradient, weight):
    weight_grad = jnp.einsum("pte,ptkf->ekf", inputs, gradient, preferred_element_type=jnp.float32)
    totals = row_total(gradient)
    input_grad = jnp.einsum("ptkf,ekf->pte", gradient, weight, preferred_element_type=jnp.float32)
    return (weight_grad, jnp.stack([totals[0], totals[2]]), input_grad)


def split_heads(values, head_count):
    return values.reshape(
        values.shape[0], values.shape[1], head_count, values.shape[2] // head_count
    )


def score_table(queries, keyvals, keymask, head_count):
    query_heads = split_heads(queries, head_count)
    key_heads = split_heads(keyvals[:, :, 0], head_count)
    shrink = query_heads.shape[-1] ** (-0.5)
    scores = (
        jnp.einsum("pthd,pshd->phts", query_heads, key_heads, preferred_element_type=jnp.float32)
        * shrink
    )
    scores = jnp.where(keymask[:, None, None, :], scores, NEG_FILL)
    return (scores, query_heads, key_heads, shrink)


def attend(queries, keyvals, keymask, head_count):
    scores, query_heads, key_heads, shrink = score_table(queries, keyvals, keymask, head_count)
    highest = jnp.max(scores, axis=-1, keepdims=True)
    powers = jnp.exp(scores - highest)
    totals = jnp.sum(powers, axis=-1, keepdims=True)
    prob_table = (powers / totals).astype(jnp.bfloat16)
    value_heads = split_heads(keyvals[:, :, 1], head_count)
    mixture = jnp.einsum(
        "phts,pshd->pthd", prob_table, value_heads, preferred_element_type=jnp.float32
    )
    return (mixture.reshape(queries.shape).astype(jnp.bfloat16), highest + jnp.log(totals))


def attend_back(upstream, queries, keyvals, keymask, logsum, head_count):
    scores, query_heads, key_heads, shrink = score_table(queries, keyvals, keymask, head_count)
    prob_table = jnp.exp(scores - logsum)
    value_heads = split_heads(keyvals[:, :, 1], head_count)
    upper_heads = split_heads(upstream, head_count)
    value_grad = jnp.einsum(
        "phts,pthd->pshd",
        prob_table.astype(jnp.bfloat16),
        upper_heads,
        preferred_element_type=jnp.float32,
    )
    prob_grad = jnp.einsum(
        "pthd,pshd->phts", upper_heads, value_heads, preferred_element_type=jnp.float32
    )
    score_grad = prob_table * (prob_grad - jnp.sum(prob_grad * prob_table, axis=-1, keepdims=True))
    score_grad = score_grad.astype(jnp.bfloat16)
    query_grad = (
        jnp.einsum("phts,pshd->pthd", score_grad, key_heads, preferred_element_type=jnp.float32)
        * shrink
    )
    key_grad = (
        jnp.einsum("phts,pthd->pshd", score_grad, query_heads, preferred_element_type=jnp.float32)
        * shrink
    )
    keyval_grad = jnp.stack([key_grad, value_grad], axis=2).reshape(keyvals.shape)
    return (query_grad.reshape(queries.shape), keyval_grad)


def feed_forward(inputs, weight_in, bias_in, weight_out, bias_out):
    inner_sum = linear(inputs, weight_in) + bias_in.astype(jnp.float32)
    active = gelu_exact(inner_sum).astype(jnp.bfloat16)
    totals = inputs.astype(jnp.float32) + linear(active, weight_out) + bias_out
    return (inner_sum, active, totals)


def feed_back(upstream, inputs, inner_sum, active, totals, factor, offset, weight_in, weight_out):
    sum_grad, factor_grad, offset_grad = norm_back(totals, factor, offset, upstream)
    branch_grad = sum_grad.astype(jnp.bfloat16)
    outer_grad = linear_weight(active, branch_grad)
    outbias_grad = row_total(branch_grad)
    active_grad = linear_input(branch_grad, weight_out)
    inner_grad = gelu_back(inner_sum, active_grad).astype(jnp.bfloat16)
    weightin_grad = linear_weight(inputs, inner_grad)
    inbias_grad = row_total(inner_grad)
    input_grad = linear_input(inner_grad, weight_in) + sum_grad
    return (
        input_grad,
        weightin_grad,
        inbias_grad,
        outer_grad,
        outbias_grad,
        factor_grad,
        offset_grad,
    )


def micro_step(
    fetched, text, image, text_len, region_count, text_cot, image_cot, caption_slots, region_slots
):
    (
        selfproject,
        selfbiases,
        selfoutput,
        textcoproject,
        textcobiases,
        imagecoproject,
        imagecobiases,
        textcooutput,
        imagecooutput,
        textffinner,
        textffinbias,
        textffouter,
        imageffinner,
        imageffinbias,
        imageffouter,
        textgains,
        textshifts,
        textbiases,
        imagegains,
        imageshifts,
        imagebiases,
    ) = fetched
    text_factor = textgains.astype(jnp.float32)
    text_offset = textshifts.astype(jnp.float32)
    text_bias = textbiases.astype(jnp.float32)
    image_factor = imagegains.astype(jnp.float32)
    image_offset = imageshifts.astype(jnp.float32)
    image_bias = imagebiases.astype(jnp.float32)
    text_mask = jnp.arange(caption_slots)[None, :] < text_len[:, None]
    region_mask = jnp.arange(region_slots)[None, :] < region_count[:, None]
    self_triple = project(text, selfproject, selfbiases)
    self_keys = lax.all_gather(self_triple[:, :, 1:], "seq", axis=1, tiled=True)
    self_mixed, self_logsum = attend(self_triple[:, :, 0], self_keys, text_mask, HT)
    self_sum = text.astype(jnp.float32) + linear(self_mixed, selfoutput) + text_bias[0]
    text_one = layer_norm(self_sum, text_factor[0], text_offset[0]).astype(jnp.bfloat16)
    text_triple = project(text_one, textcoproject, textcobiases)
    image_triple = project(image, imagecoproject, imagecobiases)
    text_keys, image_keys = (
        lax.all_gather(text_triple[:, :, 1:], "seq", axis=1, tiled=True),
        lax.all_gather(image_triple[:, :, 1:], "seq", axis=1, tiled=True),
    )
    text_mixed, text_logsum = attend(text_triple[:, :, 0], image_keys, region_mask, HC)
    image_mixed, image_logsum = attend(image_triple[:, :, 0], text_keys, text_mask, HC)
    text_sum = text_one.astype(jnp.float32) + linear(text_mixed, textcooutput) + text_bias[1]
    text_two = layer_norm(text_sum, text_factor[1], text_offset[1]).astype(jnp.bfloat16)
    image_sum = image.astype(jnp.float32) + linear(image_mixed, imagecooutput) + image_bias[0]
    image_two = layer_norm(image_sum, image_factor[0], image_offset[0]).astype(jnp.bfloat16)
    text_inner, text_active, text_total = feed_forward(
        text_two, textffinner, textffinbias, textffouter, text_bias[2]
    )
    text_three = layer_norm(text_total, text_factor[2], text_offset[2]).astype(jnp.bfloat16)
    image_inner, image_active, image_total = feed_forward(
        image_two, imageffinner, imageffinbias, imageffouter, image_bias[1]
    )
    image_three = layer_norm(image_total, image_factor[1], image_offset[1]).astype(jnp.bfloat16)
    (
        text_twograd,
        textin_grad,
        textinb_grad,
        textout_grad,
        textoutb_grad,
        factor_tthree,
        offset_tthree,
    ) = feed_back(
        text_cot.astype(jnp.float32),
        text_two,
        text_inner,
        text_active,
        text_total,
        text_factor[2],
        text_offset[2],
        textffinner,
        textffouter,
    )
    (
        image_twograd,
        imagein_grad,
        imageinb_grad,
        imageout_grad,
        imageoutb_grad,
        factor_itwo,
        offset_itwo,
    ) = feed_back(
        image_cot.astype(jnp.float32),
        image_two,
        image_inner,
        image_active,
        image_total,
        image_factor[1],
        image_offset[1],
        imageffinner,
        imageffouter,
    )
    textsum_grad, factor_ttwo, offset_ttwo = norm_back(
        text_sum, text_factor[1], text_offset[1], text_twograd
    )
    textbranch_grad = textsum_grad.astype(jnp.bfloat16)
    textco_outgrad = linear_weight(text_mixed, textbranch_grad)
    textco_biasgrad = row_total(textbranch_grad)
    textmix_grad = linear_input(textbranch_grad, textcooutput).astype(jnp.bfloat16)
    imagesum_grad, factor_ione, offset_ione = norm_back(
        image_sum, image_factor[0], image_offset[0], image_twograd
    )
    imagebranch_grad = imagesum_grad.astype(jnp.bfloat16)
    imageco_outgrad = linear_weight(image_mixed, imagebranch_grad)
    imageco_biasgrad = row_total(imagebranch_grad)
    imagemix_grad = linear_input(imagebranch_grad, imagecooutput).astype(jnp.bfloat16)
    textquery_grad, imagekv_part = attend_back(
        textmix_grad, text_triple[:, :, 0], image_keys, region_mask, text_logsum, HC
    )
    imagequery_grad, textkv_part = attend_back(
        imagemix_grad, image_triple[:, :, 0], text_keys, text_mask, image_logsum, HC
    )
    textkv_grad, imagekv_grad = (
        lax.psum_scatter(
            textkv_part.astype(jnp.bfloat16), "seq", scatter_dimension=1, tiled=True
        ).astype(jnp.float32),
        lax.psum_scatter(
            imagekv_part.astype(jnp.bfloat16), "seq", scatter_dimension=1, tiled=True
        ).astype(jnp.float32),
    )
    texttriple_grad = jnp.concatenate(
        [textquery_grad[:, :, None].astype(jnp.bfloat16), textkv_grad.astype(jnp.bfloat16)], axis=2
    )
    imagetriple_grad = jnp.concatenate(
        [imagequery_grad[:, :, None].astype(jnp.bfloat16), imagekv_grad.astype(jnp.bfloat16)],
        axis=2,
    )
    textco_projgrad, textco_qvgrad, textone_grad = project_back(
        text_one, texttriple_grad, textcoproject
    )
    textone_grad = textone_grad + textsum_grad
    imageco_projgrad, imageco_qvgrad, image_ingrad = project_back(
        image, imagetriple_grad, imagecoproject
    )
    image_ingrad = image_ingrad + imagesum_grad
    selfsum_grad, factor_tone, offset_tone = norm_back(
        self_sum, text_factor[0], text_offset[0], textone_grad
    )
    selfbranch_grad = selfsum_grad.astype(jnp.bfloat16)
    selfout_grad = linear_weight(self_mixed, selfbranch_grad)
    selfbias_grad = row_total(selfbranch_grad)
    selfmix_grad = linear_input(selfbranch_grad, selfoutput).astype(jnp.bfloat16)
    selfquery_grad, selfkv_part = attend_back(
        selfmix_grad, self_triple[:, :, 0], self_keys, text_mask, self_logsum, HT
    )
    selfkv_grad = lax.psum_scatter(
        selfkv_part.astype(jnp.bfloat16), "seq", scatter_dimension=1, tiled=True
    )
    selftriple_grad = jnp.concatenate(
        [selfquery_grad[:, :, None].astype(jnp.bfloat16), selfkv_grad], axis=2
    )
    selfproj_grad, selfqv_grad, text_ingrad = project_back(text, selftriple_grad, selfproject)
    text_ingrad = text_ingrad + selfsum_grad
    gradients = (
        selfproj_grad,
        selfqv_grad,
        selfout_grad,
        textco_projgrad,
        textco_qvgrad,
        imageco_projgrad,
        imageco_qvgrad,
        textco_outgrad,
        imageco_outgrad,
        textin_grad,
        textinb_grad,
        textout_grad,
        imagein_grad,
        imageinb_grad,
        imageout_grad,
        jnp.stack([factor_tone, factor_ttwo, factor_tthree]),
        jnp.stack([offset_tone, offset_ttwo, offset_tthree]),
        jnp.stack([selfbias_grad, textco_biasgrad, textoutb_grad]),
        jnp.stack([factor_ione, factor_itwo]),
        jnp.stack([offset_ione, offset_itwo]),
        jnp.stack([imageco_biasgrad, imageoutb_grad]),
    )
    outputs = (
        text_three,
        image_three,
        text_ingrad.astype(jnp.bfloat16),
        image_ingrad.astype(jnp.bfloat16),
    )
    return (outputs, gradients)


def local_plain(
    text,
    image,
    text_len,
    region_count,
    text_cot,
    image_cot,
    selfproject,
    selfbiases,
    selfoutput,
    textcoproject,
    textcobiases,
    imagecoproject,
    imagecobiases,
    textcooutput,
    imagecooutput,
    textffinner,
    textffinbias,
    textffouter,
    imageffinner,
    imageffinbias,
    imageffouter,
    textgains,
    textshifts,
    textbiases,
    imagegains,
    imageshifts,
    imagebiases,
):
    seq_count = lax.axis_size("seq")
    micro_pairs = text.shape[0] // MB
    shards = (
        selfproject,
        selfbiases,
        selfoutput,
        textcoproject,
        textcobiases,
        imagecoproject,
        imagecobiases,
        textcooutput,
        imagecooutput,
        textffinner,
        textffinbias,
        textffouter,
        imageffinner,
        imageffinbias,
        imageffouter,
        textgains,
        textshifts,
        textbiases,
        imagegains,
        imageshifts,
        imagebiases,
    )
    accumulated = None
    text_rows = []
    image_rows = []
    textgrad_rows = []
    imagegrad_rows = []
    for micro_index in range(MB):
        fetched = (
            lax.all_gather(shards[0], "dp", axis=0, tiled=True),
            lax.all_gather(shards[1], "dp", axis=1, tiled=True),
            lax.all_gather(shards[2], "dp", axis=0, tiled=True),
            lax.all_gather(shards[3], "dp", axis=0, tiled=True),
            lax.all_gather(shards[4], "dp", axis=1, tiled=True),
            lax.all_gather(shards[5], "dp", axis=0, tiled=True),
            lax.all_gather(shards[6], "dp", axis=1, tiled=True),
            lax.all_gather(shards[7], "dp", axis=0, tiled=True),
            lax.all_gather(shards[8], "dp", axis=0, tiled=True),
            lax.all_gather(shards[9], "dp", axis=0, tiled=True),
            lax.all_gather(shards[10], "dp", axis=0, tiled=True),
            lax.all_gather(shards[11], "dp", axis=0, tiled=True),
            lax.all_gather(shards[12], "dp", axis=0, tiled=True),
            lax.all_gather(shards[13], "dp", axis=0, tiled=True),
            lax.all_gather(shards[14], "dp", axis=0, tiled=True),
            lax.all_gather(shards[15], "dp", axis=1, tiled=True),
            lax.all_gather(shards[16], "dp", axis=1, tiled=True),
            lax.all_gather(shards[17], "dp", axis=1, tiled=True),
            lax.all_gather(shards[18], "dp", axis=1, tiled=True),
            lax.all_gather(shards[19], "dp", axis=1, tiled=True),
            lax.all_gather(shards[20], "dp", axis=1, tiled=True),
        )
        begin_row = micro_index * micro_pairs
        end_row = begin_row + micro_pairs
        outputs, gradients = micro_step(
            fetched,
            text[begin_row:end_row],
            image[begin_row:end_row],
            text_len[begin_row:end_row],
            region_count[begin_row:end_row],
            text_cot[begin_row:end_row],
            image_cot[begin_row:end_row],
            text.shape[1] * seq_count,
            image.shape[1] * seq_count,
        )
        text_rows.append(outputs[0])
        image_rows.append(outputs[1])
        textgrad_rows.append(outputs[2])
        imagegrad_rows.append(outputs[3])
        pieces = (
            lax.psum_scatter(gradients[0], "dp", scatter_dimension=0, tiled=True),
            lax.psum_scatter(gradients[1], "dp", scatter_dimension=1, tiled=True),
            lax.psum_scatter(gradients[2], "dp", scatter_dimension=0, tiled=True),
            lax.psum_scatter(gradients[3], "dp", scatter_dimension=0, tiled=True),
            lax.psum_scatter(gradients[4], "dp", scatter_dimension=1, tiled=True),
            lax.psum_scatter(gradients[5], "dp", scatter_dimension=0, tiled=True),
            lax.psum_scatter(gradients[6], "dp", scatter_dimension=1, tiled=True),
            lax.psum_scatter(gradients[7], "dp", scatter_dimension=0, tiled=True),
            lax.psum_scatter(gradients[8], "dp", scatter_dimension=0, tiled=True),
            lax.psum_scatter(gradients[9], "dp", scatter_dimension=0, tiled=True),
            lax.psum_scatter(gradients[10], "dp", scatter_dimension=0, tiled=True),
            lax.psum_scatter(gradients[11], "dp", scatter_dimension=0, tiled=True),
            lax.psum_scatter(gradients[12], "dp", scatter_dimension=0, tiled=True),
            lax.psum_scatter(gradients[13], "dp", scatter_dimension=0, tiled=True),
            lax.psum_scatter(gradients[14], "dp", scatter_dimension=0, tiled=True),
            lax.psum_scatter(gradients[15], "dp", scatter_dimension=1, tiled=True),
            lax.psum_scatter(gradients[16], "dp", scatter_dimension=1, tiled=True),
            lax.psum_scatter(gradients[17], "dp", scatter_dimension=1, tiled=True),
            lax.psum_scatter(gradients[18], "dp", scatter_dimension=1, tiled=True),
            lax.psum_scatter(gradients[19], "dp", scatter_dimension=1, tiled=True),
            lax.psum_scatter(gradients[20], "dp", scatter_dimension=1, tiled=True),
        )
        accumulated = pieces if accumulated is None else jax.tree.map(jnp.add, accumulated, pieces)
    summed = (
        lax.psum(accumulated[0].astype(jnp.bfloat16), "seq").astype(jnp.float32),
        lax.psum(accumulated[1].astype(jnp.bfloat16), "seq").astype(jnp.float32),
        lax.psum(accumulated[2].astype(jnp.bfloat16), "seq").astype(jnp.float32),
        lax.psum(accumulated[3].astype(jnp.bfloat16), "seq").astype(jnp.float32),
        lax.psum(accumulated[4].astype(jnp.bfloat16), "seq").astype(jnp.float32),
        lax.psum(accumulated[5].astype(jnp.bfloat16), "seq").astype(jnp.float32),
        lax.psum(accumulated[6].astype(jnp.bfloat16), "seq").astype(jnp.float32),
        lax.psum(accumulated[7].astype(jnp.bfloat16), "seq").astype(jnp.float32),
        lax.psum(accumulated[8].astype(jnp.bfloat16), "seq").astype(jnp.float32),
        lax.psum(accumulated[9].astype(jnp.bfloat16), "seq").astype(jnp.float32),
        lax.psum(accumulated[10].astype(jnp.bfloat16), "seq").astype(jnp.float32),
        lax.psum(accumulated[11].astype(jnp.bfloat16), "seq").astype(jnp.float32),
        lax.psum(accumulated[12].astype(jnp.bfloat16), "seq").astype(jnp.float32),
        lax.psum(accumulated[13].astype(jnp.bfloat16), "seq").astype(jnp.float32),
        lax.psum(accumulated[14].astype(jnp.bfloat16), "seq").astype(jnp.float32),
        lax.psum(accumulated[15].astype(jnp.bfloat16), "seq").astype(jnp.float32),
        lax.psum(accumulated[16].astype(jnp.bfloat16), "seq").astype(jnp.float32),
        lax.psum(accumulated[17].astype(jnp.bfloat16), "seq").astype(jnp.float32),
        lax.psum(accumulated[18].astype(jnp.bfloat16), "seq").astype(jnp.float32),
        lax.psum(accumulated[19].astype(jnp.bfloat16), "seq").astype(jnp.float32),
        lax.psum(accumulated[20].astype(jnp.bfloat16), "seq").astype(jnp.float32),
    )
    text_out = jnp.concatenate(text_rows, axis=0)
    image_out = jnp.concatenate(image_rows, axis=0)
    text_grad = jnp.concatenate(textgrad_rows, axis=0)
    image_grad = jnp.concatenate(imagegrad_rows, axis=0)
    return (text_out, image_out, text_grad, image_grad) + tuple(summed)


MESH = pl.DeviceIdType.MESH
ANY = pl.BlockSpec(memory_space=pl.ANY)
VMEM = pl.BlockSpec(memory_space=pltpu.VMEM)


def place():
    dp = lax.axis_index("dp")
    z = lax.axis_index("seq")
    row = dp // 4
    col = (dp // 2) % 2
    core = dp % 2
    return (dp, z, row, col, core)


def partners(row, col, core, first_row):
    near_row = row + first_row * (1 - 2 * row)
    near_col = col + (1 - first_row) * (1 - 2 * col)
    far_row = row + (1 - first_row) * (1 - 2 * row)
    far_col = col + first_row * (1 - 2 * col)
    near = near_row * 4 + near_col * 2 + core
    far = far_row * 4 + far_col * 2 + core
    return (near, far)


def greet(devices):
    barrier = pltpu.get_barrier_semaphore()
    for device in devices:
        pl.semaphore_signal(barrier, inc=1, device_id=device, device_id_type=MESH)
    pl.semaphore_wait(barrier, len(devices))


def remote(source, target, send_sem, recv_sem, device):
    return pltpu.make_async_remote_copy(
        src_ref=source,
        dst_ref=target,
        send_sem=send_sem,
        recv_sem=recv_sem,
        device_id=device,
        device_id_type=MESH,
    )


SMALL_PLACES = (
    (0, 2, 96),
    (16, 2, 128),
    (18, 2, 128),
    (27, 3, 128),
    (20, 1, 128),
    (2, 3, 96),
    (5, 3, 96),
    (8, 3, 96),
    (21, 2, 128),
    (23, 2, 128),
    (25, 2, 128),
)
SMALL_COUNT = len(SMALL_PLACES)
SMALL_ROWS = 32
ROOT_HALF = 0.7071067811865476
ROOT_TURN = 0.3989422804014327
WEIGHT_SHAPES = (
    (3, 768, 768), (1, 768, 768), (3, 1024, 1024), (3, 768, 1024), (1, 1024, 768),
    (1, 1024, 1024), (1, 768, 3072), (1, 3072, 768), (1, 1024, 1024), (1, 1024, 1024),
)
W_SELF, W_SELFOUT, W_IMAGECO, W_TEXTCO, W_TEXTOUT, W_IMAGEOUT, W_TIN, W_TOUT, W_IIN, W_IOUT, W_SMALL = range(11)
PIECES = (
    (W_SMALL, 0, 0, 32, 0, 128, 2),
    *((W_SELF, k, 0, 96, 0, 768, k) for k in range(3)),
    (W_SELFOUT, 0, 0, 96, 0, 768, 2),
    *((W_IMAGECO, k, 0, 128, 0, 1024, k) for k in range(3)),
    *((W_TEXTCO, k, 0, 96, 0, 1024, k) for k in range(3)),
    (W_TEXTOUT, 0, 0, 128, 0, 768, 2),
    (W_IMAGEOUT, 0, 0, 128, 0, 1024, 2),
    *((W_TIN, 0, 0, 96, k * 1024, 1024, k) for k in range(3)),
    *((W_TOUT, 0, k * 128, 128, 0, 768, k) for k in range(3)),
    (W_IIN, 0, 0, 128, 0, 1024, 2),
    (W_IOUT, 0, 0, 128, 0, 1024, 2),
)
LAG_ACROSS = 5
AHEAD = 3
SAVED = dict(
    qkv_s=((3, 256, 768), jnp.bfloat16),
    qkv_t=((3, 256, 1024), jnp.bfloat16),
    qkv_i=((3, 256, 1024), jnp.bfloat16),
    tab_s=((12, 256, 128), jnp.bfloat16),
    tab_t=((16, 128, 128), jnp.bfloat16),
    tab_i=((16, 128, 128), jnp.bfloat16),
    sum_s=((256, 768), jnp.float32),
    sum_t=((256, 768), jnp.float32),
    sum_i=((256, 1024), jnp.float32),
    tot_t=((256, 768), jnp.float32),
    tot_i=((256, 1024), jnp.float32),
    slope_t=((256, 3072), jnp.bfloat16),
    slope_i=((256, 1024), jnp.bfloat16),
    xt768=((4, 2, 384, 256), jnp.bfloat16),
    xt1024=((5, 2, 512, 256), jnp.bfloat16),
    xt3072=((1, 2, 1536, 256), jnp.bfloat16),
    out_t=((256, 768), jnp.bfloat16),
    out_i=((256, 1024), jnp.bfloat16),
    vec96=((16, 768), jnp.float32),
    vec128=((16, 1024), jnp.float32),
)
WORK = dict(
    text=((2, 128, 768), jnp.bfloat16),
    image=((2, 128, 1024), jnp.bfloat16),
    mix_s=((256, 768), jnp.bfloat16),
    one=((256, 768), jnp.bfloat16),
    mix_t=((256, 1024), jnp.bfloat16),
    mix_i=((256, 1024), jnp.bfloat16),
    two_t=((256, 768), jnp.bfloat16),
    two_i=((256, 1024), jnp.bfloat16),
    active=((256, 3072), jnp.bfloat16),
    bias_in=((8, 3072), jnp.float32),
    pack=((SMALL_ROWS, 128), jnp.float32),
)


def mm(left, right):
    return jnp.dot(left, right, preferred_element_type=jnp.float32)


def mm_t(left, right):
    return lax.dot_general(left, right, (((1,), (1,)), ((), ())), preferred_element_type=jnp.float32)


def mm_0(left, right):
    return lax.dot_general(left, right, (((0,), (0,)), ((), ())), preferred_element_type=jnp.float32)


def lanes(index, width):
    return pl.ds(pl.multiple_of(index * width, width), width)


def head_masks():
    spot = lax.broadcasted_iota(jnp.int32, (1, 128), 1)
    low = jnp.where(spot < 64, 1.0, 0.0)
    return (low, 1.0 - low)


def key_mask(length):
    return lax.broadcasted_iota(jnp.int32, (1, 128), 1) < length


def table_of(scores, keep, shrink):
    scores = jnp.where(keep, scores * shrink, NEG_FILL)
    powers = jnp.exp(scores - jnp.max(scores, axis=-1, keepdims=True))
    return (powers / jnp.sum(powers, axis=-1, keepdims=True)).astype(jnp.bfloat16)


def forward_kernel(*refs):
    refs = list(refs)

    def take(count):
        taken = refs[:count]
        del refs[:count]
        return taken

    narrow, wide = jnp.bfloat16, jnp.float32
    weight_count = len(WEIGHT_SHAPES)
    array_count = weight_count + 1
    blocks = take(weight_count)
    small_in = take(SMALL_COUNT)
    states = take(4)
    text_len, region_count = take(2)
    whole_out = take(weight_count)
    saved_out = take(len(SAVED))
    cots = take(2)
    wholes = take(array_count)
    saved_refs = take(len(SAVED))
    saved = types.SimpleNamespace(**dict(zip(SAVED, saved_refs)))
    work = types.SimpleNamespace(**dict(zip(WORK, take(len(WORK)))))
    send_sem, recv_sem, swap_send, swap_recv, own_sem, out_sem, save_sem = refs
    dp, z, row, col, core = place()
    near, far = partners(row, col, core, 1 - core)
    sibling = dp + 1 - 2 * core
    diagonal = (1 - row) * 4 + (1 - col) * 2 + core
    others = [lax.rem(z + step, 4) for step in (1, 2, 3)]

    pack = work.pack
    pack[...] = jnp.zeros((SMALL_ROWS, 128), wide)
    for (first, rows, width), ref in zip(SMALL_PLACES, small_in):
        pack[first : first + rows, :width] = ref[...].astype(wide)

    greet([(near, z), (far, z), (sibling, z)] + [(dp, other) for other in others])

    def window(piece, index):
        array, k, row0, rows, col0, cols, planes = PIECES[piece]
        depth = wholes[array].shape[1] // 8
        first = pl.multiple_of(index * depth + row0, 16)
        return wholes[array].at[k, pl.ds(first, rows), pl.ds(col0, cols)]

    def own(piece):
        array, k, row0, rows, col0, cols, planes = PIECES[piece]
        if array == W_SMALL:
            return pack
        return blocks[array].at[k, pl.ds(row0, rows), pl.ds(col0, cols)]

    partner = z + 1 - 2 * lax.rem(z, 2)
    always, fetching = [], {0: [], 1: []}

    def copy_of(piece, send_lane, recv_lane, source, index, device):
        copy = remote(
            source, window(piece, index), send_sem.at[piece, send_lane], recv_sem.at[piece, recv_lane], device
        )
        return copy

    def siblings(piece, lane, source, index):
        copy = copy_of(piece, lane, lane, source, index, (sibling, z))
        always.append(copy)
        return copy

    def by_plane(piece, fetch, other=None):
        planes = PIECES[piece][6]
        if planes == 2:
            if fetch:
                fetch()
            return
        if fetch:
            pl.when(lax.rem(z, 2) == planes)(fetch)
        if other:
            pl.when(lax.rem(z, 2) != planes)(other)

    def begin(copies):
        for copy in copies:
            copy.start()

    def noted(piece, *moves):
        copies = [copy_of(piece, *move) for move in moves]
        planes = PIECES[piece][6]
        (always if planes == 2 else fetching[planes]).extend(copies)
        return copies

    def across(piece, lane, index):
        if PIECES[piece][6] == 2:
            return []
        return noted(piece, (lane + 7, lane, window(piece, index), index, (dp, partner)))

    def arrived(piece, lane, index):
        copy_of(piece, lane, lane, window(piece, index), index, (sibling, z)).wait_recv()

    def start(piece):
        block = own(piece)
        copies = noted(piece, (0, 0, block, dp, (near, z)), (1, 1, block, dp, (far, z)))
        by_plane(piece, lambda: begin(copies))
        siblings(piece, 2, block, dp).start()

    onward = {}

    def relay(piece):
        block, block_far = window(piece, near), window(piece, far)
        first = noted(piece, (3, 3, block, near, (far, z))) + across(piece, 0, near)
        second = across(piece, 1, far)
        onward[piece] = (
            siblings(piece, 4, block, near),
            siblings(piece, 5, block_far, far),
            siblings(piece, 6, window(piece, diagonal), diagonal),
        )

        def go():
            arrived(piece, 0, near)
            begin(first)
            onward[piece][0].start()
            arrived(piece, 1, far)
            begin(second)
            onward[piece][1].start()

        by_plane(piece, go)

    def pass_on(piece):
        third = across(piece, 3, diagonal)

        def go():
            arrived(piece, 3, diagonal)
            begin(third)
            onward[piece][2].start()

        by_plane(piece, go)

    def receive(piece):
        def go():
            arrived(piece, 0, near)
            onward[piece][0].start()
            arrived(piece, 1, far)
            onward[piece][1].start()

        by_plane(piece, None, go)

    def receive_last(piece):
        def go():
            arrived(piece, 3, diagonal)
            onward[piece][2].start()

        by_plane(piece, None, go)

    outs, kept, met = [], {}, []

    def ready(piece):
        array = PIECES[piece][0]
        for lane in (2, 4, 5, 6):
            arrived(piece, lane, near)
        if array not in met:
            kept[array].wait()
        met.append(array)
        if array < weight_count and met.count(array) == sum(p[0] == array for p in PIECES):
            copy = pltpu.make_async_copy(wholes[array], whole_out[array], out_sem.at[array])
            copy.start()
            outs.append(copy)

    progress = [0, 0]

    def lag_of(piece):
        return 2 if PIECES[piece][6] == 2 else LAG_ACROSS

    def tick():
        turn = progress[1]
        if turn >= len(PIECES) + LAG_ACROSS:
            return
        while progress[0] < min(turn + AHEAD, len(PIECES)):
            start(progress[0])
            progress[0] += 1
        for step, lag in ((relay, 0), (pass_on, 1), (receive, LAG_ACROSS - 2), (receive_last, LAG_ACROSS - 1)):
            if 0 <= turn - lag < len(PIECES):
                step(turn - lag)
        for piece in (turn - LAG_ACROSS, turn - 2):
            if 0 <= piece < len(PIECES) and lag_of(piece) == turn - piece:
                ready(piece)
        progress[1] += 1

    def need(array, k=None):
        last = max(i + lag_of(i) for i, piece in enumerate(PIECES) if piece[0] == array and k in (None, piece[1]))
        while progress[1] <= last:
            tick()

    def save(ref):
        spot = [ref is other for other in saved_refs].index(True)
        copy = pltpu.make_async_copy(ref, saved_out[spot], save_sem.at[spot])
        copy.start()
        outs.append(copy)

    swaps = []

    def swap(array, target):
        source = states[array]
        count = source.shape[0] // 4
        slots = source.shape[1]
        here = target.at[:, pl.ds(pl.multiple_of(z * slots, 16), slots), :]
        made = []
        for step, other in enumerate(others):
            copy = remote(
                source.at[pl.ds(other * count, count)],
                here,
                swap_send.at[array, step],
                swap_recv.at[array, step],
                (dp, other),
            )
            copy.start()
            made.append(copy)
        keep = pltpu.make_async_copy(source.at[pl.ds(z * count, count)], here, own_sem.at[array_count + array])
        keep.start()
        made.append(keep)
        return made

    for array in range(array_count):
        depth = wholes[array].shape[1] // 8
        mine = pl.ds(pl.multiple_of(dp * depth, 16), depth)
        if array == W_SMALL:
            keep = pltpu.make_async_copy(pack, wholes[array].at[0, mine], own_sem.at[array])
        else:
            keep = pltpu.make_async_copy(blocks[array], wholes[array].at[:, mine], own_sem.at[array])
        kept[array] = keep
    text_in = swap(0, work.text)
    for piece in range(2):
        start(piece)
    image_in = swap(1, work.image)
    progress[0] = 2
    for keep in kept.values():
        keep.start()

    vec96, vec128, bias_in = saved.vec96, saved.vec128, work.bias_in

    def flip(values, width, target, which, first_block):
        turned = values.T
        for block in range(values.shape[1] // width):
            owner = first_block + block
            target[which, owner % 2, owner // 2 * width : (owner // 2 + 1) * width, :] = turned[
                block * width : (block + 1) * width
            ]

    def norm_rows(source, gain, shift, targets):
        def body(step, carry):
            window = pl.ds(pl.multiple_of(step * 32, 32), 32)
            hidden = source[window, :]
            centre = hidden - jnp.mean(hidden, axis=-1, keepdims=True)
            spread = jnp.mean(centre * centre, axis=-1, keepdims=True)
            result = centre * lax.rsqrt(spread + EPSILON) * gain + shift
            targets[window, :] = result.astype(narrow)
            return carry

        lax.fori_loop(0, 8, body, 0)

    def project_all(inputs, array, target, biases):
        width = target.shape[2]
        for k in range(3):
            need(array, k)

            def body(tile, carry, k=k):
                where = lanes(tile, 256)
                part = mm(inputs, wholes[array][k, :, where])
                if k == 0:
                    part = part + biases[0][:, where]
                if k == 2:
                    part = part + biases[1][:, where]
                target[k, :, where] = part.astype(narrow)
                return carry

            lax.fori_loop(0, width // 256, body, 0)

    def branch(inputs, array, base, bias, target):
        width = target.shape[1]

        def body(tile, carry):
            where = lanes(tile, 256)
            part = mm(inputs, wholes[array][0, :, where])
            target[:, where] = part + base[..., where].reshape(256, 256).astype(wide) + bias[:, where]
            return carry

        lax.fori_loop(0, width // 256, body, 0)

    class Row:
        def __init__(self, ref, index):
            self.ref, self.index = ref, index

        def __getitem__(self, key):
            return self.ref[self.index : self.index + 1, key[1]]

    need(W_SMALL)
    packed = wholes[W_SMALL]
    for owner in range(8):
        base = owner * SMALL_ROWS
        vec96[:, owner * 96 : owner * 96 + 96] = packed[0, base : base + 16, :96]
        vec128[:, owner * 128 : owner * 128 + 128] = packed[0, base + 16 : base + 32, :]
        for part in range(3):
            at = owner * 384 + part * 128
            bias_in[0:1, at : at + 128] = packed[0, base + 27 + part : base + 28 + part, :]
    save(saved.vec96)
    save(saved.vec128)
    text_lengths = [text_len[z * 2 + pair] for pair in range(2)]
    region_counts = [region_count[z * 2 + pair] for pair in range(2)]
    low, high = head_masks()
    low_narrow, high_narrow = low.astype(narrow), high.astype(narrow)

    for copy in text_in:
        copy.wait()
    text = work.text[...].reshape(256, 768)
    qkv_s = saved.qkv_s
    project_all(text, W_SELF, qkv_s, (Row(vec96, 0), Row(vec96, 1)))
    save(saved.qkv_s)

    def self_heads(tile, carry):
        where = lanes(tile, 128)
        for pair in range(2):
            rows = slice(pair * 128, pair * 128 + 128)
            q2, k2, v2 = (qkv_s[k, rows, where] for k in range(3))
            both = jnp.concatenate([q2 * low_narrow, q2 * high_narrow], axis=0)
            table = table_of(mm_t(both, k2), key_mask(text_lengths[pair]), 0.125)
            saved.tab_s[pair * 6 + tile] = table
            mixed = mm(table, v2)
            work.mix_s[rows, where] = (mixed[:128] * low + mixed[128:] * high).astype(narrow)
        return carry

    tick()
    lax.fori_loop(0, 3, self_heads, 0)
    tick()
    lax.fori_loop(3, 6, self_heads, 0)
    tick()
    save(saved.tab_s)
    flip(text, 96, saved.xt768, 0, 0)
    flip(work.mix_s[...], 96, saved.xt768, 1, 0)
    need(W_SELFOUT)
    branch(work.mix_s[...], W_SELFOUT, work.text, Row(vec96, 8), saved.sum_s)
    norm_rows(saved.sum_s, vec96[2:3], vec96[5:6], work.one)
    save(saved.sum_s)
    flip(work.one[...], 96, saved.xt768, 2, 0)

    for copy in image_in:
        copy.wait()
    image = work.image[...].reshape(256, 1024)
    qkv_i, qkv_t = saved.qkv_i, saved.qkv_t
    project_all(image, W_IMAGECO, qkv_i, (Row(vec128, 2), Row(vec128, 3)))
    save(saved.qkv_i)
    flip(image, 128, saved.xt1024, 0, 0)
    project_all(work.one[...], W_TEXTCO, qkv_t, (Row(vec128, 0), Row(vec128, 1)))
    save(saved.qkv_t)

    def co_heads(head, carry):
        where = lanes(head, 128)
        shrink = 128**-0.5
        for pair in range(2):
            rows = slice(pair * 128, pair * 128 + 128)
            tq, tk, tv = (qkv_t[k, rows, where] for k in range(3))
            iq, ik, iv = (qkv_i[k, rows, where] for k in range(3))
            table = table_of(mm_t(tq, ik), key_mask(region_counts[pair]), shrink)
            saved.tab_t[pair * 8 + head] = table
            work.mix_t[rows, where] = mm(table, iv).astype(narrow)
            table = table_of(mm_t(iq, tk), key_mask(text_lengths[pair]), shrink)
            saved.tab_i[pair * 8 + head] = table
            work.mix_i[rows, where] = mm(table, tv).astype(narrow)
        return carry

    swaps += swap(2, cots[0]) + swap(3, cots[1])
    for head in (0, 2, 4, 6):
        tick()
        lax.fori_loop(head, head + 2, co_heads, 0)
    save(saved.tab_t)
    save(saved.tab_i)
    flip(work.mix_t[...], 128, saved.xt1024, 1, 0)
    flip(work.mix_i[...], 128, saved.xt1024, 2, 0)
    need(W_TEXTOUT)
    branch(work.mix_t[...], W_TEXTOUT, work.one, Row(vec96, 9), saved.sum_t)
    norm_rows(saved.sum_t, vec96[3:4], vec96[6:7], work.two_t)
    save(saved.sum_t)
    flip(work.two_t[...], 96, saved.xt768, 3, 0)
    save(saved.xt768)
    need(W_IMAGEOUT)
    branch(work.mix_i[...], W_IMAGEOUT, work.image, Row(vec128, 9), saved.sum_i)
    norm_rows(saved.sum_i, vec128[5:6], vec128[7:8], work.two_i)
    save(saved.sum_i)
    flip(work.two_i[...], 128, saved.xt1024, 3, 0)

    def activate(inner):
        share = 0.5 + 0.5 * lax.erf(inner * ROOT_HALF)
        slope = share + inner * (ROOT_TURN * jnp.exp(-0.5 * inner * inner))
        return ((inner * share).astype(narrow), slope.astype(narrow))

    two_t = work.two_t
    tot_t = saved.tot_t

    def text_inner(owner, carry):
        where = lanes(owner, 384)
        inner = mm(two_t[...], wholes[W_TIN][0, :, where]) + bias_in[0:1, where]
        active, slope = activate(inner)
        saved.slope_t[:, where] = slope
        work.active[:, where] = active
        place_ = pl.ds(pl.multiple_of(lax.div(owner, 2) * 384, 384), 384)
        saved.xt3072[0, lax.rem(owner, 2), place_, :] = active.T
        return carry

    need(W_TIN)
    for owner in (0, 2, 4, 6):
        lax.fori_loop(owner, owner + 2, text_inner, 0)
        tick()
    save(saved.slope_t)
    save(saved.xt3072)
    need(W_TOUT)
    branch(work.active[...], W_TOUT, two_t, Row(vec96, 10), tot_t)
    save(saved.tot_t)
    norm_rows(tot_t, vec96[4:5], vec96[7:8], saved.out_t)
    save(saved.out_t)

    need(W_IIN)
    two_i = work.two_i
    tot_i = saved.tot_i
    for part in range(4):
        where = slice(part * 256, part * 256 + 256)
        inner = mm(two_i[...], wholes[W_IIN][0, :, where]) + vec128[4:5, where]
        active, slope = activate(inner)
        saved.slope_i[:, where] = slope
        flip(active, 128, saved.xt1024, 4, part * 2)
        work.mix_i[:, where] = active
    save(saved.slope_i)
    save(saved.xt1024)
    need(W_IOUT)
    branch(work.mix_i[...], W_IOUT, two_i, Row(vec128, 10), tot_i)
    save(saved.tot_i)
    norm_rows(tot_i, vec128[6:7], vec128[8:9], saved.out_i)
    save(saved.out_i)

    for copy in always:
        copy.wait_send()
    for planes in (0, 1):

        @pl.when(lax.rem(z, 2) == planes)
        def _(planes=planes):
            for copy in fetching[planes]:
                copy.wait_send()

    for copy in swaps:
        copy.wait()
    for copy in outs:
        copy.wait()


def forward_all(blocks, small, states, text_len, region_count):
    dma = pltpu.SemaphoreType.DMA
    narrow = jnp.bfloat16
    count = len(WEIGHT_SHAPES)
    shape = jax.ShapeDtypeStruct
    out_shape = [shape(w, narrow) for w in WEIGHT_SHAPES]
    out_shape += [shape(dims, kind) for dims, kind in SAVED.values()]
    out_shape += [shape((s.shape[0] // 4, s.shape[1] * 4, s.shape[2]), s.dtype) for s in states[2:]]
    scratch = [pltpu.VMEM(w, narrow) for w in WEIGHT_SHAPES]
    scratch += [pltpu.VMEM((1, 8 * SMALL_ROWS, 128), jnp.float32)]
    scratch += [pltpu.VMEM(dims, kind) for dims, kind in (*SAVED.values(), *WORK.values())]
    scratch += [
        dma((len(PIECES), 11)),
        dma((len(PIECES), 7)),
        dma((4, 3)),
        dma((4, 3)),
        dma((count + 5,)),
        dma((count,)),
        dma((len(SAVED),)),
    ]
    results = pl.pallas_call(
        forward_kernel,
        out_shape=out_shape,
        in_specs=[ANY] * count
        + [VMEM] * SMALL_COUNT
        + [ANY] * 4
        + [pl.BlockSpec(memory_space=pltpu.SMEM)] * 2,
        out_specs=[ANY] * len(out_shape),
        scratch_shapes=scratch,
        compiler_params=pltpu.CompilerParams(
            collective_id=0, has_side_effects=True, vmem_limit_bytes=62 * 2**20
        ),
        name="forward_all",
    )(*blocks, *small, *states, text_len, region_count)
    wholes = results[:count]
    saved = types.SimpleNamespace(**dict(zip(SAVED, results[count : count + len(SAVED)])))
    return (wholes, saved, results[count + len(SAVED) :])


CHUNKS = (9, 9, 3)
TILES = (4, 3, 1)
ROWS = (96, 128, 384)
STARTS = ((9, 12, 24), (12, 15, 19, 23), ())
ORDER = ((2, 0, 3), (0, 6, 3), (1, 4, 5), (0, 3, 3), (1, 0, 4), (0, 0, 3))
STEPS = 21
LAG_NEAR, LAG_FAR, LAG_SUM, LAG_MID, LAG_END, LAG_WRITE = 1, 3, 5, 7, 9, 11
SMALL_TURN = 18
CHIP_SLOTS, NEAR_SLOTS, PLANE_SLOTS = 7, 9, 9
AT_BSELF, AT_TEXTCO, AT_TIN = 2304, 3072, 6144
AT_BTEXT, AT_BIMAGE, AT_IIN, AT_BIFF = 3072, 3840, 4864, 5888


def backward_kernel(*refs):
    refs = list(refs)

    def take(count):
        taken = refs[:count]
        del refs[:count]
        return taken

    narrow, wide = jnp.bfloat16, jnp.float32
    weights = take(len(WEIGHT_SHAPES))
    saved = types.SimpleNamespace(**dict(zip(SAVED, take(len(SAVED)))))
    cot_t, cot_i = take(2)
    result, small_result = take(2)
    pairs = take(4)
    out_box, chip, near_sum, plane, line, cross = take(6)
    s_own, s_chip, s_near, s_plane, s_line, s_cross = take(6)
    w_p, w_q, w_i, w_o = take(4)
    dz768, dz1024, dz3072 = take(3)
    xt = take(3)
    tab_s, tab_t, tab_i, sum_s, sum_t, sum_i, tot_t, tot_i, vec96, vec128 = take(10)
    mix_t, mix_i, back_t, back_i, sums96, sums128, sums_in = take(7)
    (
        core_send, core_recv, near_send, near_recv, far_send, far_recv,
        end_send, end_recv, mid_send, mid_recv, back_send, back_recv,
        write_sem, swap_send, swap_recv, own_sem, load_sem,
    ) = refs
    dp, z, row, col, core = place()
    near, far = partners(row, col, core, core)
    sibling = dp + 1 - 2 * core
    others = [lax.rem(z + step, 4) for step in (1, 2, 3)]
    near_bit = col + core * (row - col)
    far_bit = row + core * (col - row)

    def block_of(near_index, far_index):
        return near_index * (1 + core) + far_index * (2 - core)

    is_end = (z == 0) | (z == 3)
    is_mid = (z == 1) | (z == 2)
    middle = 1 + z // 2
    other_mid = 3 - z
    end = 3 * (z // 2)

    def span(ref, first, width):
        return ref.at[:, first : first + width]

    loads = []

    def load(*moves):
        made = []
        for source, target in moves:
            copy = pltpu.make_async_copy(source, target, load_sem.at[len(loads)])
            loads.append(copy)
            made.append(copy)
        return made

    def begin(group):
        for copy in group:
            copy.start()

    def finish(group):
        for copy in group:
            copy.wait()

    get_text3 = load(
        (saved.tot_t, tot_t),
        (cot_t.reshape(256, 768), span(dz768, AT_BSELF, 768)),
        (saved.vec96, vec96),
        *((weights[W_TOUT].at[0, pl.ds(i * 768, 768), :], w_q.at[i]) for i in range(4)),
    )
    get_text_in = load(
        (saved.xt3072, xt[2]),
        (saved.xt768, xt[0]),
        (saved.slope_t, span(dz768, AT_TIN, 3072)),
        *((weights[W_TIN].at[0, :, pl.ds(i * 1024, 1024)], w_p.at[i]) for i in range(3)),
    )
    get_image = load(
        (saved.tot_i, tot_i),
        (cot_i.reshape(256, 1024), span(dz1024, AT_BIMAGE, 1024)),
        (saved.vec128, vec128),
        (weights[W_IOUT].at[0], w_i.at[0]),
        (saved.slope_i, span(dz1024, AT_IIN, 1024)),
        (weights[W_IIN].at[0], w_i.at[1]),
    )
    get_co = load(
        (saved.sum_t, sum_t),
        (weights[W_TEXTOUT].at[0], w_o),
        (saved.sum_i, sum_i),
        (weights[W_IMAGEOUT].at[0], w_i.at[2]),
    )
    get_heads = load(
        (saved.xt1024, xt[1]),
        *((saved.qkv_t.at[k], span(dz768, AT_TEXTCO + k * 1024, 1024)) for k in range(3)),
        *((saved.qkv_i.at[k], span(dz1024, k * 1024, 1024)) for k in range(3)),
        (saved.tab_t, tab_t),
        (saved.tab_i, tab_i),
    )
    get_self = load(
        (saved.sum_s, sum_s),
        *((saved.qkv_s.at[k], span(dz768, k * 768, 768)) for k in range(3)),
        (saved.tab_s, tab_s),
    )
    get_textco = load((weights[W_TEXTCO], w_p))
    get_selfs = load((weights[W_SELF], w_q.at[pl.ds(0, 3)]), (weights[W_SELFOUT].at[0], w_q.at[3]))
    get_imageco = load((weights[W_IMAGECO], w_i))
    for group in (get_text3, get_text_in, get_image, get_co, get_heads, get_self):
        begin(group)
    sums96[...] = jnp.zeros((16, 768), wide)
    sums128[...] = jnp.zeros((16, 1024), wide)
    s_own[...] = jnp.zeros((2, 4, SMALL_ROWS, 128), wide)

    greet([(near, z), (far, z), (sibling, z)] + [(dp, other) for other in others])

    def swap(array, source):
        target = pairs[array]
        count, slots = source.shape[0], source.shape[1] // 4
        there = target.at[pl.ds(z * count, count)]

        def part(other):
            return source.at[:, pl.ds(pl.multiple_of(other * slots, 16), slots), :]

        made = [
            remote(part(other), there, swap_send.at[array, step], swap_recv.at[array, step], (dp, other))
            for step, other in enumerate(others)
        ]
        made.append(pltpu.make_async_copy(part(z), there, own_sem.at[array]))
        return made

    swaps = [
        swap(0, saved.out_t.reshape(2, 128, 768)),
        swap(1, saved.out_i.reshape(2, 128, 1024)),
        swap(2, back_t),
        swap(3, back_i),
    ]
    begin(swaps[0] + swaps[1])

    grads = (dz768, dz1024, dz3072)

    def products(index, half, use):
        place_ = 0
        for kind in range(3):
            chunk, chosen = 0, False
            first = 0
            for kind_, start, count in ORDER:
                if kind_ == kind:
                    inside = (index >= first) & (index < first + count)
                    chunk = jnp.where(inside, index - first + start, chunk)
                    chosen = chosen | inside
                first += count

            def work(kind=kind, chunk=chunk):
                tiles, rows = TILES[kind], ROWS[kind]
                for tile in range(tiles):
                    which = chunk * tiles + tile
                    weight = 0
                    for bound in STARTS[kind]:
                        weight = weight + jnp.where(which >= bound, 1, 0)
                    part = mm(xt[kind][weight, half], grads[kind][:, lanes(which, 256)])
                    for block in range(4):
                        for side in range(2):
                            use(
                                block,
                                (tile * 2 + side) * rows,
                                rows,
                                part[block * rows : (block + 1) * rows, side * 128 : side * 128 + 128],
                            )

            pl.when(chosen)(work)

    def core_copy(index):
        return remote(
            out_box.at[lax.rem(index, 2)],
            chip.at[lax.rem(index, CHIP_SLOTS)],
            core_send.at[index],
            core_recv.at[index],
            (sibling, z),
        )

    def near_copy(index, far_index):
        return remote(
            chip.at[lax.rem(index, CHIP_SLOTS), block_of(1 - near_bit, far_index)],
            near_sum.at[lax.rem(index, NEAR_SLOTS), far_index],
            near_send.at[index, far_index],
            near_recv.at[index, far_index],
            (near, z),
        )

    def far_copy(index):
        return remote(
            near_sum.at[lax.rem(index, NEAR_SLOTS), 1 - far_bit],
            plane.at[lax.rem(index, PLANE_SLOTS)],
            far_send.at[index],
            far_recv.at[index],
            (far, z),
        )

    def end_copy(index):
        return remote(
            plane.at[lax.rem(index, PLANE_SLOTS)], line.at[index], end_send.at[index], end_recv.at[index], (dp, middle)
        )

    def mid_copy(index):
        return remote(line.at[index], cross.at[index], mid_send.at[index], mid_recv.at[index], (dp, other_mid))

    def back_copy(index):
        return remote(cross.at[index], line.at[index], back_send.at[index], back_recv.at[index], (dp, end))

    def mid_write(index):
        return pltpu.make_async_copy(cross.at[index], result.at[index], write_sem.at[index])

    def end_write(index):
        return pltpu.make_async_copy(line.at[index], result.at[index], write_sem.at[index])

    def add(left, right):
        return (left.astype(wide) + right.astype(wide)).astype(narrow)

    def stage_core(index):
        @pl.when(index >= 2)
        def _():
            core_copy(index - 2).wait_send()

        slot = lax.rem(index, 2)

        def put(block, first, rows, values):
            out_box[slot, block, first : first + rows, :] = values.astype(narrow)

        products(index, 1 - core, put)
        core_copy(index).start()

    def stage_near(index):
        core_copy(index).wait_recv()
        slot = lax.rem(index, CHIP_SLOTS)

        def put(block, first, rows, values):
            window = (slot, block, slice(first, first + rows), slice(None))
            chip[window] = (chip[window].astype(wide) + values).astype(narrow)

        products(index, core, put)
        near_copy(index, 1 - far_bit).start()
        near_copy(index, far_bit).start()

    def stage_far(index):
        chip_slot, slot = lax.rem(index, CHIP_SLOTS), lax.rem(index, NEAR_SLOTS)
        for far_index in (1 - far_bit, far_bit):
            near_copy(index, far_index).wait_recv()
            near_sum[slot, far_index] = add(near_sum[slot, far_index], chip[chip_slot, block_of(near_bit, far_index)])
            if far_index is not far_bit:
                far_copy(index).start()
        near_copy(index, 0).wait_send()
        near_copy(index, 1).wait_send()

    def stage_sum(index):
        slot = lax.rem(index, PLANE_SLOTS)
        far_copy(index).wait_recv()
        plane[slot] = add(plane[slot], near_sum[lax.rem(index, NEAR_SLOTS), far_bit])

        @pl.when(is_end)
        def _():
            end_copy(index).start()

        far_copy(index).wait_send()

    def stage_mid(index):
        @pl.when(is_mid)
        def _():
            end_copy(index).wait_recv()
            line[index] = add(line[index], plane[lax.rem(index, PLANE_SLOTS)])
            mid_copy(index).start()

        @pl.when(is_end)
        def _():
            end_copy(index).wait_send()

    def stage_end(index):
        @pl.when(is_mid)
        def _():
            mid_copy(index).wait_recv()
            cross[index] = add(cross[index], line[index])
            back_copy(index).start()
            mid_write(index).start()

    def stage_write(index):
        @pl.when(is_end)
        def _():
            back_copy(index).wait_recv()
            end_write(index).start()

    stages = (
        (stage_core, 0),
        (stage_near, LAG_NEAR),
        (stage_far, LAG_FAR),
        (stage_sum, LAG_SUM),
        (stage_mid, LAG_MID),
        (stage_end, LAG_END),
        (stage_write, LAG_WRITE),
    )

    last = STEPS
    sm_core = remote(s_own.at[1 - core], s_chip, core_send.at[last], core_recv.at[last], (sibling, z))
    sm_near = [
        remote(
            s_chip.at[block_of(1 - near_bit, j)], s_near.at[j], near_send.at[last, j], near_recv.at[last, j], (near, z)
        )
        for j in (0, 1)
    ]
    sm_far = remote(s_near.at[1 - far_bit], s_plane, far_send.at[last], far_recv.at[last], (far, z))
    sm_end = remote(s_plane, s_line, end_send.at[last], end_recv.at[last], (dp, middle))
    sm_mid = remote(s_line, s_cross, mid_send.at[last], mid_recv.at[last], (dp, other_mid))
    sm_back = remote(s_cross, s_line, back_send.at[last], back_recv.at[last], (dp, end))

    def small_start():
        for owner in range(8):
            spot = s_own.at[owner % 2, owner // 2]
            spot[0:16, :96] = sums96[:, owner * 96 : owner * 96 + 96]
            spot[16:27, :] = sums128[0:11, owner * 128 : owner * 128 + 128]
            for part in range(3):
                at = owner * 384 + part * 128
                spot[27 + part : 28 + part, :] = sums_in[0:1, at : at + 128]
        sm_core.start()

    def small_near():
        sm_core.wait_recv()
        s_chip[...] += s_own[core]
        begin(sm_near)

    def small_far():
        for j in (0, 1):
            sm_near[j].wait_recv()
            s_near[j] += s_chip[block_of(near_bit, j)]
        sm_far.start()

    def small_sum():
        sm_far.wait_recv()
        s_plane[...] += s_near[far_bit]
        pl.when(is_end)(sm_end.start)

    def small_mid():
        @pl.when(is_mid)
        def _():
            sm_end.wait_recv()
            s_line[...] += s_plane[...]
            sm_mid.start()

    def small_end():
        @pl.when(is_mid)
        def _():
            sm_mid.wait_recv()
            s_cross[...] += s_line[...]
            sm_back.start()
            small_result[...] = s_cross[...]

    def small_write():
        @pl.when(is_end)
        def _():
            sm_back.wait_recv()
            small_result[...] = s_line[...]

    def norm_step(source, upstream, gain, target, first, sums, rows):
        width = source.shape[1]

        def body(step, carry):
            window = pl.ds(pl.multiple_of(step * 32, 32), 32)
            hidden = source[window, :]
            dy = upstream[window, first[0] : first[0] + width].astype(wide)
            centre = hidden - jnp.mean(hidden, axis=-1, keepdims=True)
            spread = jnp.mean(centre * centre, axis=-1, keepdims=True)
            scale = lax.rsqrt(spread + EPSILON)
            unit = centre * scale
            inner = dy * gain
            back = scale * (
                inner
                - jnp.mean(inner, axis=-1, keepdims=True)
                - unit * jnp.mean(inner * unit, axis=-1, keepdims=True)
            )
            rounded = back.astype(narrow)
            source[window, :] = back
            target[window, first[1] : first[1] + width] = rounded
            parts = (dy * unit, dy, rounded.astype(wide))
            return tuple(c + p.reshape(4, 8, width).sum(axis=0) for c, p in zip(carry, parts))

        zero = jnp.zeros((8, width), wide)
        totals = lax.fori_loop(0, 8, body, (zero, zero, zero))
        for at, total in zip(rows, totals):
            sums[at : at + 1, :] = jnp.sum(total, axis=0, keepdims=True)

    def col_sum(values):
        return jnp.sum(values.astype(wide), axis=0, keepdims=True)

    def text_three():
        finish(get_text3)
        norm_step(tot_t, dz768, vec96[4:5], dz3072, (AT_BSELF, 0), sums96, (4, 7, 10))

    def text_inner(turn):
        for part in range(4):
            which = turn * 4 + part
            where = pl.ds(pl.multiple_of(AT_TIN + which * 256, 256), 256)
            out_rows = w_q[lax.div(which, 3), pl.ds(pl.multiple_of(lax.rem(which, 3) * 256, 256), 256), :]
            inner = (dz768[:, where].astype(wide) * mm_t(dz3072[...], out_rows)).astype(narrow)
            dz768[:, where] = inner
            sums_in[0:1, lanes(which, 256)] = col_sum(inner)
            tot_t[...] += mm_t(inner, w_p[turn, :, part * 256 : part * 256 + 256])

    def image_three():
        begin(get_textco)
        begin(get_selfs)
        finish(get_image)
        norm_step(tot_i, dz1024, vec128[6:7], dz1024, (AT_BIMAGE, AT_BIFF), sums128, (6, 8, 10))
        branch = dz1024[:, AT_BIFF : AT_BIFF + 1024]
        for part in range(4):
            at = part * 256
            where = slice(AT_IIN + at, AT_IIN + at + 256)
            inner = (dz1024[:, where].astype(wide) * mm_t(branch, w_i[0, at : at + 256, :])).astype(narrow)
            dz1024[:, where] = inner
            sums128[4:5, at : at + 256] = col_sum(inner)
            tot_i[...] += mm_t(inner, w_i[1, :, at : at + 256])

    def text_second():
        finish(get_co)
        norm_step(sum_t, tot_t, vec96[3:4], dz1024, (0, AT_BTEXT), sums96, (3, 6, 9))
        mix_t[...] = mm_t(dz1024[:, AT_BTEXT : AT_BTEXT + 768], w_o[...]).astype(narrow)

    def image_second():
        norm_step(sum_i, tot_i, vec128[5:6], dz1024, (0, AT_BIMAGE), sums128, (5, 7, 9))
        mix_i[...] = mm_t(dz1024[:, AT_BIMAGE : AT_BIMAGE + 1024], w_i[2]).astype(narrow)
        begin(get_imageco)
        finish(get_heads)

    def table_back(table, upper_value):
        probs = table.astype(wide)
        return (probs * (upper_value - jnp.sum(upper_value * probs, axis=-1, keepdims=True))).astype(narrow)

    def co_head(head):
        shrink = 128**-0.5
        for pair in range(2):
            rows = slice(pair * 128, pair * 128 + 128)
            t_at = [pl.ds(pl.multiple_of(AT_TEXTCO + k * 1024 + head * 128, 128), 128) for k in range(3)]
            i_at = [pl.ds(pl.multiple_of(k * 1024 + head * 128, 128), 128) for k in range(3)]
            tq, tk, tv = (dz768[rows, at] for at in t_at)
            iq, ik, iv = (dz1024[rows, at] for at in i_at)
            for q, k, v, table, mixed, spots in (
                (tq, ik, iv, tab_t, mix_t, ((dz768, t_at[0]), (dz1024, i_at[1]), (dz1024, i_at[2]))),
                (iq, tk, tv, tab_i, mix_i, ((dz1024, i_at[0]), (dz768, t_at[1]), (dz768, t_at[2]))),
            ):
                probs = table[pair * 8 + head]
                upper = mixed[rows, lanes(head, 128)]
                score = table_back(probs, mm_t(upper, v))
                grads_ = (mm(score, k) * shrink, mm_0(score, q) * shrink, mm_0(probs, upper))
                for (ref, at), value in zip(spots, grads_):
                    ref[rows, at] = value.astype(narrow)

    def co_heads(turn):
        co_head(turn * 2 - 12)
        co_head(turn * 2 - 11)

    def text_one_back():
        finish(get_textco)
        for k in range(3):
            where = slice(AT_TEXTCO + k * 1024, AT_TEXTCO + (k + 1) * 1024)
            sum_t[...] += mm_t(dz768[:, where], w_p[k])
        sums128[0:1, :] = col_sum(dz768[:, AT_TEXTCO : AT_TEXTCO + 1024])
        sums128[1:2, :] = col_sum(dz768[:, AT_TEXTCO + 2048 : AT_TEXTCO + 3072])

    def self_second():
        finish(get_self)
        finish(get_selfs)
        norm_step(sum_s, sum_t, vec96[2:3], dz768, (0, AT_BSELF), sums96, (2, 5, 8))
        mix_t[:, 0:768] = mm_t(dz768[:, AT_BSELF : AT_BSELF + 768], w_q[3]).astype(narrow)

    def image_back():
        finish(get_imageco)
        for k in range(3):
            sum_i[...] += mm_t(dz1024[:, k * 1024 : (k + 1) * 1024], w_i[k])
        sums128[2:3, :] = col_sum(dz1024[:, 0:1024])
        sums128[3:4, :] = col_sum(dz1024[:, 2048:3072])
        back_i[...] = sum_i[...].astype(narrow).reshape(2, 128, 1024)
        begin(swaps[3])

    low, high = head_masks()
    low_narrow, high_narrow = low.astype(narrow), high.astype(narrow)

    def self_heads(turn):
        tile = turn - 12
        for pair in range(2):
            rows = slice(pair * 128, pair * 128 + 128)
            at = [pl.ds(pl.multiple_of(k * 768 + tile * 128, 128), 128) for k in range(3)]
            q2, k2, v2 = (dz768[rows, where] for where in at)
            upper = mix_t[rows, lanes(tile, 128)]
            uppers = jnp.concatenate([upper * low_narrow, upper * high_narrow], axis=0)
            queries = jnp.concatenate([q2 * low_narrow, q2 * high_narrow], axis=0)
            probs = tab_s[pair * 6 + tile]
            score = table_back(probs, mm_t(uppers, v2))
            query = mm(score, k2)
            dz768[rows, at[0]] = ((query[:128] * low + query[128:] * high) * 0.125).astype(narrow)
            dz768[rows, at[1]] = (mm_0(score, queries) * 0.125).astype(narrow)
            dz768[rows, at[2]] = mm_0(probs, uppers).astype(narrow)

    def text_back():
        for k in range(3):
            sum_s[...] += mm_t(dz768[:, k * 768 : (k + 1) * 768], w_q[k])
        sums96[0:1, :] = col_sum(dz768[:, 0:768])
        sums96[1:2, :] = col_sum(dz768[:, 1536:2304])
        back_t[...] = sum_s[...].astype(narrow).reshape(2, 128, 768)
        begin(swaps[2])
        small_start()

    text_three()
    finish(get_text_in)

    def turn_body(turn, carry):
        for stage, lag in stages:
            index = turn - lag

            @pl.when((index >= 0) & (index < STEPS))
            def _(stage=stage, index=index):
                stage(index)

        pl.when(turn < 3)(lambda: text_inner(turn))
        pl.when(turn == 3)(image_three)
        pl.when(turn == 4)(text_second)
        pl.when(turn == 5)(image_second)
        pl.when((turn >= 6) & (turn < 10))(lambda: co_heads(turn))

        @pl.when(turn == 10)
        def _():
            text_one_back()
            image_back()

        pl.when(turn == 11)(self_second)
        pl.when((turn >= 12) & (turn < 18))(lambda: self_heads(turn))
        pl.when(turn == SMALL_TURN)(text_back)
        for lag, step in (
            (LAG_NEAR, small_near),
            (LAG_FAR, small_far),
            (LAG_SUM, small_sum),
            (LAG_MID, small_mid),
            (LAG_END, small_end),
            (LAG_WRITE, small_write),
        ):
            pl.when(turn == SMALL_TURN + lag)(step)
        return carry

    lax.fori_loop(0, STEPS + LAG_WRITE, turn_body, 0)

    core_copy(STEPS - 2).wait_send()
    core_copy(STEPS - 1).wait_send()
    sm_core.wait_send()
    for copy in sm_near:
        copy.wait_send()
    sm_far.wait_send()

    def settle(index, carry):
        @pl.when(is_end)
        def _():
            end_write(index).wait()

        @pl.when(is_mid)
        def _():
            mid_copy(index).wait_send()
            back_copy(index).wait_send()
            mid_write(index).wait()

        return carry

    lax.fori_loop(0, STEPS, settle, 0)

    @pl.when(is_end)
    def _():
        sm_end.wait_send()

    @pl.when(is_mid)
    def _():
        sm_mid.wait_send()
        sm_back.wait_send()

    for group in swaps:
        finish(group)


def backward_all(weights, saved, cots):
    dma = pltpu.SemaphoreType.DMA
    shape = jax.ShapeDtypeStruct
    vmem = pltpu.VMEM
    narrow, wide = jnp.bfloat16, jnp.float32
    block = (768, 128)
    tiny = (SMALL_ROWS, 128)
    kept = [getattr(saved, name) for name in SAVED]
    one = [dma((STEPS + 1,))] * 2
    results = pl.pallas_call(
        backward_kernel,
        out_shape=[
            shape((STEPS,) + block, narrow),
            shape(tiny, wide),
            shape((8, 32, 768), narrow),
            shape((8, 32, 1024), narrow),
            shape((8, 32, 768), narrow),
            shape((8, 32, 1024), narrow),
        ],
        in_specs=[ANY] * (len(weights) + len(kept) + 2),
        out_specs=[ANY, VMEM] + [ANY] * 4,
        scratch_shapes=[
            vmem((2, 4) + block, narrow),
            vmem((CHIP_SLOTS, 4) + block, narrow),
            vmem((NEAR_SLOTS, 2) + block, narrow),
            vmem((PLANE_SLOTS,) + block, narrow),
            vmem((STEPS,) + block, narrow),
            vmem((STEPS,) + block, narrow),
            vmem((2, 4) + tiny, wide),
            vmem((4,) + tiny, wide),
            vmem((2,) + tiny, wide),
            vmem(tiny, wide),
            vmem(tiny, wide),
            vmem(tiny, wide),
            vmem((3, 768, 1024), narrow),
            vmem((4, 768, 768), narrow),
            vmem((3, 1024, 1024), narrow),
            vmem((1024, 768), narrow),
            vmem((256, 9216), narrow),
            vmem((256, 6912), narrow),
            vmem((256, 768), narrow),
            vmem((4, 2, 384, 256), narrow),
            vmem((5, 2, 512, 256), narrow),
            vmem((1, 2, 1536, 256), narrow),
            vmem((12, 256, 128), narrow),
            vmem((16, 128, 128), narrow),
            vmem((16, 128, 128), narrow),
            vmem((256, 768), wide),
            vmem((256, 768), wide),
            vmem((256, 1024), wide),
            vmem((256, 768), wide),
            vmem((256, 1024), wide),
            vmem((16, 768), wide),
            vmem((16, 1024), wide),
            vmem((256, 1024), narrow),
            vmem((256, 1024), narrow),
            vmem((2, 128, 768), narrow),
            vmem((2, 128, 1024), narrow),
            vmem((16, 768), wide),
            vmem((16, 1024), wide),
            vmem((8, 3072), wide),
        ]
        + one
        + [dma((STEPS + 1, 2))] * 2
        + one * 4
        + [dma((STEPS,)), dma((4, 3)), dma((4, 3)), dma((4,)), dma((48,))],
        compiler_params=pltpu.CompilerParams(
            collective_id=1, has_side_effects=True, vmem_limit_bytes=62 * 2**20
        ),
        name="backward_all",
    )(*weights, *kept, *cots)
    return (results[0], results[1], results[2:])


UNPACK = (
    ((0, 18, 6), (1, 6, 6), (3, 24, 8), (6, 24, 24)),
    ((2, 24, 8), (4, 6, 6), (5, 8, 8), (8, 8, 8), (9, 8, 8)),
    ((7, 6, 6),),
)


def unpack_kernel(*refs):
    summed, small = refs[:2]
    states = refs[2:6]
    weights = refs[6:16]
    smalls = refs[16 : 16 + SMALL_COUNT]
    targets = refs[16 + SMALL_COUNT :]
    for state, target in zip(states, targets):
        target[...] = state[...]
    places = [{}, {}, {}]
    turn = 0
    for kind, start, count in ORDER:
        for chunk in range(start, start + count):
            places[kind][chunk] = turn
            turn += 1
    for kind in range(3):
        rows = ROWS[kind]
        tile = 0
        for weight, tiles, width in UNPACK[kind]:
            for own_tile in range(tiles):
                at, side = divmod(tile, TILES[kind] * 2)
                values = summed[places[kind][at], side * rows : (side + 1) * rows, :]
                part, column = divmod(own_tile, width)
                weights[weight][part, :, column * 128 : column * 128 + 128] = values.astype(jnp.float32)
                tile += 1
    for (first, rows, width), ref in zip(SMALL_PLACES, smalls):
        ref[...] = small[first : first + rows, :width]


def unpack(summed, small, states):
    shape = jax.ShapeDtypeStruct
    out_shape = [shape((w[0], w[1] // 8, w[2]), jnp.float32) for w in WEIGHT_SHAPES]
    out_shape += [shape((rows, width), jnp.float32) for first, rows, width in SMALL_PLACES]
    out_shape += [shape(s.shape, s.dtype) for s in states]
    results = pl.pallas_call(
        unpack_kernel,
        out_shape=out_shape,
        in_specs=[VMEM] * 6,
        out_specs=[VMEM] * (14 + SMALL_COUNT),
        compiler_params=pltpu.CompilerParams(vmem_limit_bytes=61 * 2**20),
        name="unpack",
    )(summed, small, *states)
    return (results[:10], results[10 : 10 + SMALL_COUNT], results[10 + SMALL_COUNT :])


def local_fast(
    text, image, text_len, region_count, text_cot, image_cot,
    selfproject, selfbiases, selfoutput, textcoproject, textcobiases, imagecoproject, imagecobiases,
    textcooutput, imagecooutput, textffinner, textffinbias, textffouter,
    imageffinner, imageffinbias, imageffouter,
    textgains, textshifts, textbiases, imagegains, imageshifts, imagebiases,
):
    blocks = [
        selfproject.transpose(1, 0, 2), selfoutput[None], imagecoproject.transpose(1, 0, 2),
        textcoproject.transpose(1, 0, 2), textcooutput[None], imagecooutput[None],
        textffinner[None], textffouter[None], imageffinner[None], imageffouter[None],
    ]
    small = [
        selfbiases, textcobiases, imagecobiases, textffinbias.reshape(3, 128), imageffinbias.reshape(1, 128),
        textgains, textshifts, textbiases, imagegains, imageshifts, imagebiases,
    ]
    weights, saved, cots = forward_all(blocks, small, [text, image, text_cot, image_cot], text_len, region_count)
    summed, small_sum, outputs = backward_all(weights, saved, cots)
    g, s, outputs = unpack(summed, small_sum, outputs)
    return tuple(outputs) + (
        g[W_SELF].transpose(1, 0, 2), s[0], g[W_SELFOUT][0], g[W_TEXTCO].transpose(1, 0, 2), s[1],
        g[W_IMAGECO].transpose(1, 0, 2), s[2], g[W_TEXTOUT][0], g[W_IMAGEOUT][0],
        g[W_TIN][0], s[3].reshape(-1), g[W_TOUT][0], g[W_IIN][0], s[4].reshape(-1), g[W_IOUT][0],
        s[5], s[6], s[7], s[8], s[9], s[10],
    )


def solution(mesh):
    in_specs = (
        P("dp", "seq", None),
        P("dp", "seq", None),
        P("dp"),
        P("dp"),
        P("dp", "seq", None),
        P("dp", "seq", None),
        P("dp", None, None),
        P(None, "dp"),
        P("dp", None),
        P("dp", None, None),
        P(None, "dp"),
        P("dp", None, None),
        P(None, "dp"),
        P("dp", None),
        P("dp", None),
        P("dp", None),
        P("dp"),
        P("dp", None),
        P("dp", None),
        P("dp"),
        P("dp", None),
        P(None, "dp"),
        P(None, "dp"),
        P(None, "dp"),
        P(None, "dp"),
        P(None, "dp"),
        P(None, "dp"),
    )
    out_specs = (
        P("dp", "seq", None),
        P("dp", "seq", None),
        P("dp", "seq", None),
        P("dp", "seq", None),
        P("dp", None, None),
        P(None, "dp"),
        P("dp", None),
        P("dp", None, None),
        P(None, "dp"),
        P("dp", None, None),
        P(None, "dp"),
        P("dp", None),
        P("dp", None),
        P("dp", None),
        P("dp"),
        P("dp", None),
        P("dp", None),
        P("dp"),
        P("dp", None),
        P(None, "dp"),
        P(None, "dp"),
        P(None, "dp"),
        P(None, "dp"),
        P(None, "dp"),
        P(None, "dp"),
    )
    sizes = mesh.shape
    local = local_fast if (sizes["dp"], sizes["seq"]) == (8, 4) else local_plain
    return jax.shard_map(local, mesh=mesh, in_specs=in_specs, out_specs=out_specs, check_vma=False)
```

```python
import functools
import types

import jax
import jax.numpy as jnp
from jax import lax
from jax.experimental import pallas as pl
from jax.experimental.pallas import tpu as pltpu
from jax.sharding import PartitionSpec as P

HT = 12
HC = 8
MB = 2


EPSILON = 1e-05
NEG_FILL = -1e30


def layer_norm(hidden, factor, offset):
    centre = hidden - jnp.mean(hidden, axis=-1, keepdims=True)
    spread = jnp.mean(centre * centre, axis=-1, keepdims=True)
    return centre * lax.rsqrt(spread + EPSILON) * factor + offset


def norm_back(hidden, factor, offset, upstream):
    outcome, pullback = jax.vjp(layer_norm, hidden, factor, offset)
    return pullback(upstream)


def gelu_exact(hidden):
    return jax.nn.gelu(hidden, approximate=False)


def gelu_back(hidden, upstream):
    outcome, pullback = jax.vjp(gelu_exact, hidden)
    return pullback(upstream)[0]


def linear(inputs, weight):
    return jnp.einsum("pte,ef->ptf", inputs, weight, preferred_element_type=jnp.float32)


def linear_weight(inputs, gradient):
    return jnp.einsum("pte,ptf->ef", inputs, gradient, preferred_element_type=jnp.float32)


def linear_input(gradient, weight):
    return jnp.einsum("ptf,ef->pte", gradient, weight, preferred_element_type=jnp.float32)


def row_total(gradient):
    return jnp.sum(gradient, axis=(0, 1), dtype=jnp.float32)


def project(inputs, weight, biases):
    bias_rows = biases.astype(jnp.float32)
    stacked = jnp.stack([bias_rows[0], jnp.zeros_like(bias_rows[0]), bias_rows[1]])
    triple = jnp.einsum("pte,ekf->ptkf", inputs, weight, preferred_element_type=jnp.float32)
    return (triple + stacked).astype(jnp.bfloat16)


def project_back(inputs, gradient, weight):
    weight_grad = jnp.einsum("pte,ptkf->ekf", inputs, gradient, preferred_element_type=jnp.float32)
    totals = row_total(gradient)
    input_grad = jnp.einsum("ptkf,ekf->pte", gradient, weight, preferred_element_type=jnp.float32)
    return (weight_grad, jnp.stack([totals[0], totals[2]]), input_grad)


def split_heads(values, head_count):
    return values.reshape(
        values.shape[0], values.shape[1], head_count, values.shape[2] // head_count
    )


def score_table(queries, keyvals, keymask, head_count):
    query_heads = split_heads(queries, head_count)
    key_heads = split_heads(keyvals[:, :, 0], head_count)
    shrink = query_heads.shape[-1] ** (-0.5)
    scores = (
        jnp.einsum("pthd,pshd->phts", query_heads, key_heads, preferred_element_type=jnp.float32)
        * shrink
    )
    scores = jnp.where(keymask[:, None, None, :], scores, NEG_FILL)
    return (scores, query_heads, key_heads, shrink)


def attend(queries, keyvals, keymask, head_count):
    scores, query_heads, key_heads, shrink = score_table(queries, keyvals, keymask, head_count)
    highest = jnp.max(scores, axis=-1, keepdims=True)
    powers = jnp.exp(scores - highest)
    totals = jnp.sum(powers, axis=-1, keepdims=True)
    prob_table = (powers / totals).astype(jnp.bfloat16)
    value_heads = split_heads(keyvals[:, :, 1], head_count)
    mixture = jnp.einsum(
        "phts,pshd->pthd", prob_table, value_heads, preferred_element_type=jnp.float32
    )
    return (mixture.reshape(queries.shape).astype(jnp.bfloat16), highest + jnp.log(totals))


def attend_back(upstream, queries, keyvals, keymask, logsum, head_count):
    scores, query_heads, key_heads, shrink = score_table(queries, keyvals, keymask, head_count)
    prob_table = jnp.exp(scores - logsum)
    value_heads = split_heads(keyvals[:, :, 1], head_count)
    upper_heads = split_heads(upstream, head_count)
    value_grad = jnp.einsum(
        "phts,pthd->pshd",
        prob_table.astype(jnp.bfloat16),
        upper_heads,
        preferred_element_type=jnp.float32,
    )
    prob_grad = jnp.einsum(
        "pthd,pshd->phts", upper_heads, value_heads, preferred_element_type=jnp.float32
    )
    score_grad = prob_table * (prob_grad - jnp.sum(prob_grad * prob_table, axis=-1, keepdims=True))
    score_grad = score_grad.astype(jnp.bfloat16)
    query_grad = (
        jnp.einsum("phts,pshd->pthd", score_grad, key_heads, preferred_element_type=jnp.float32)
        * shrink
    )
    key_grad = (
        jnp.einsum("phts,pthd->pshd", score_grad, query_heads, preferred_element_type=jnp.float32)
        * shrink
    )
    keyval_grad = jnp.stack([key_grad, value_grad], axis=2).reshape(keyvals.shape)
    return (query_grad.reshape(queries.shape), keyval_grad)


def feed_forward(inputs, weight_in, bias_in, weight_out, bias_out):
    inner_sum = linear(inputs, weight_in) + bias_in.astype(jnp.float32)
    active = gelu_exact(inner_sum).astype(jnp.bfloat16)
    totals = inputs.astype(jnp.float32) + linear(active, weight_out) + bias_out
    return (inner_sum, active, totals)


def feed_back(upstream, inputs, inner_sum, active, totals, factor, offset, weight_in, weight_out):
    sum_grad, factor_grad, offset_grad = norm_back(totals, factor, offset, upstream)
    branch_grad = sum_grad.astype(jnp.bfloat16)
    outer_grad = linear_weight(active, branch_grad)
    outbias_grad = row_total(branch_grad)
    active_grad = linear_input(branch_grad, weight_out)
    inner_grad = gelu_back(inner_sum, active_grad).astype(jnp.bfloat16)
    weightin_grad = linear_weight(inputs, inner_grad)
    inbias_grad = row_total(inner_grad)
    input_grad = linear_input(inner_grad, weight_in) + sum_grad
    return (
        input_grad,
        weightin_grad,
        inbias_grad,
        outer_grad,
        outbias_grad,
        factor_grad,
        offset_grad,
    )


def micro_step(
    fetched, text, image, text_len, region_count, text_cot, image_cot, caption_slots, region_slots
):
    (
        selfproject,
        selfbiases,
        selfoutput,
        textcoproject,
        textcobiases,
        imagecoproject,
        imagecobiases,
        textcooutput,
        imagecooutput,
        textffinner,
        textffinbias,
        textffouter,
        imageffinner,
        imageffinbias,
        imageffouter,
        textgains,
        textshifts,
        textbiases,
        imagegains,
        imageshifts,
        imagebiases,
    ) = fetched
    text_factor = textgains.astype(jnp.float32)
    text_offset = textshifts.astype(jnp.float32)
    text_bias = textbiases.astype(jnp.float32)
    image_factor = imagegains.astype(jnp.float32)
    image_offset = imageshifts.astype(jnp.float32)
    image_bias = imagebiases.astype(jnp.float32)
    text_mask = jnp.arange(caption_slots)[None, :] < text_len[:, None]
    region_mask = jnp.arange(region_slots)[None, :] < region_count[:, None]
    self_triple = project(text, selfproject, selfbiases)
    self_keys = lax.all_gather(self_triple[:, :, 1:], "seq", axis=1, tiled=True)
    self_mixed, self_logsum = attend(self_triple[:, :, 0], self_keys, text_mask, HT)
    self_sum = text.astype(jnp.float32) + linear(self_mixed, selfoutput) + text_bias[0]
    text_one = layer_norm(self_sum, text_factor[0], text_offset[0]).astype(jnp.bfloat16)
    text_triple = project(text_one, textcoproject, textcobiases)
    image_triple = project(image, imagecoproject, imagecobiases)
    text_keys, image_keys = (
        lax.all_gather(text_triple[:, :, 1:], "seq", axis=1, tiled=True),
        lax.all_gather(image_triple[:, :, 1:], "seq", axis=1, tiled=True),
    )
    text_mixed, text_logsum = attend(text_triple[:, :, 0], image_keys, region_mask, HC)
    image_mixed, image_logsum = attend(image_triple[:, :, 0], text_keys, text_mask, HC)
    text_sum = text_one.astype(jnp.float32) + linear(text_mixed, textcooutput) + text_bias[1]
    text_two = layer_norm(text_sum, text_factor[1], text_offset[1]).astype(jnp.bfloat16)
    image_sum = image.astype(jnp.float32) + linear(image_mixed, imagecooutput) + image_bias[0]
    image_two = layer_norm(image_sum, image_factor[0], image_offset[0]).astype(jnp.bfloat16)
    text_inner, text_active, text_total = feed_forward(
        text_two, textffinner, textffinbias, textffouter, text_bias[2]
    )
    text_three = layer_norm(text_total, text_factor[2], text_offset[2]).astype(jnp.bfloat16)
    image_inner, image_active, image_total = feed_forward(
        image_two, imageffinner, imageffinbias, imageffouter, image_bias[1]
    )
    image_three = layer_norm(image_total, image_factor[1], image_offset[1]).astype(jnp.bfloat16)
    (
        text_twograd,
        textin_grad,
        textinb_grad,
        textout_grad,
        textoutb_grad,
        factor_tthree,
        offset_tthree,
    ) = feed_back(
        text_cot.astype(jnp.float32),
        text_two,
        text_inner,
        text_active,
        text_total,
        text_factor[2],
        text_offset[2],
        textffinner,
        textffouter,
    )
    (
        image_twograd,
        imagein_grad,
        imageinb_grad,
        imageout_grad,
        imageoutb_grad,
        factor_itwo,
        offset_itwo,
    ) = feed_back(
        image_cot.astype(jnp.float32),
        image_two,
        image_inner,
        image_active,
        image_total,
        image_factor[1],
        image_offset[1],
        imageffinner,
        imageffouter,
    )
    textsum_grad, factor_ttwo, offset_ttwo = norm_back(
        text_sum, text_factor[1], text_offset[1], text_twograd
    )
    textbranch_grad = textsum_grad.astype(jnp.bfloat16)
    textco_outgrad = linear_weight(text_mixed, textbranch_grad)
    textco_biasgrad = row_total(textbranch_grad)
    textmix_grad = linear_input(textbranch_grad, textcooutput).astype(jnp.bfloat16)
    imagesum_grad, factor_ione, offset_ione = norm_back(
        image_sum, image_factor[0], image_offset[0], image_twograd
    )
    imagebranch_grad = imagesum_grad.astype(jnp.bfloat16)
    imageco_outgrad = linear_weight(image_mixed, imagebranch_grad)
    imageco_biasgrad = row_total(imagebranch_grad)
    imagemix_grad = linear_input(imagebranch_grad, imagecooutput).astype(jnp.bfloat16)
    textquery_grad, imagekv_part = attend_back(
        textmix_grad, text_triple[:, :, 0], image_keys, region_mask, text_logsum, HC
    )
    imagequery_grad, textkv_part = attend_back(
        imagemix_grad, image_triple[:, :, 0], text_keys, text_mask, image_logsum, HC
    )
    textkv_grad, imagekv_grad = (
        lax.psum_scatter(
            textkv_part.astype(jnp.bfloat16), "seq", scatter_dimension=1, tiled=True
        ).astype(jnp.float32),
        lax.psum_scatter(
            imagekv_part.astype(jnp.bfloat16), "seq", scatter_dimension=1, tiled=True
        ).astype(jnp.float32),
    )
    texttriple_grad = jnp.concatenate(
        [textquery_grad[:, :, None].astype(jnp.bfloat16), textkv_grad.astype(jnp.bfloat16)], axis=2
    )
    imagetriple_grad = jnp.concatenate(
        [imagequery_grad[:, :, None].astype(jnp.bfloat16), imagekv_grad.astype(jnp.bfloat16)],
        axis=2,
    )
    textco_projgrad, textco_qvgrad, textone_grad = project_back(
        text_one, texttriple_grad, textcoproject
    )
    textone_grad = textone_grad + textsum_grad
    imageco_projgrad, imageco_qvgrad, image_ingrad = project_back(
        image, imagetriple_grad, imagecoproject
    )
    image_ingrad = image_ingrad + imagesum_grad
    selfsum_grad, factor_tone, offset_tone = norm_back(
        self_sum, text_factor[0], text_offset[0], textone_grad
    )
    selfbranch_grad = selfsum_grad.astype(jnp.bfloat16)
    selfout_grad = linear_weight(self_mixed, selfbranch_grad)
    selfbias_grad = row_total(selfbranch_grad)
    selfmix_grad = linear_input(selfbranch_grad, selfoutput).astype(jnp.bfloat16)
    selfquery_grad, selfkv_part = attend_back(
        selfmix_grad, self_triple[:, :, 0], self_keys, text_mask, self_logsum, HT
    )
    selfkv_grad = lax.psum_scatter(
        selfkv_part.astype(jnp.bfloat16), "seq", scatter_dimension=1, tiled=True
    )
    selftriple_grad = jnp.concatenate(
        [selfquery_grad[:, :, None].astype(jnp.bfloat16), selfkv_grad], axis=2
    )
    selfproj_grad, selfqv_grad, text_ingrad = project_back(text, selftriple_grad, selfproject)
    text_ingrad = text_ingrad + selfsum_grad
    gradients = (
        selfproj_grad,
        selfqv_grad,
        selfout_grad,
        textco_projgrad,
        textco_qvgrad,
        imageco_projgrad,
        imageco_qvgrad,
        textco_outgrad,
        imageco_outgrad,
        textin_grad,
        textinb_grad,
        textout_grad,
        imagein_grad,
        imageinb_grad,
        imageout_grad,
        jnp.stack([factor_tone, factor_ttwo, factor_tthree]),
        jnp.stack([offset_tone, offset_ttwo, offset_tthree]),
        jnp.stack([selfbias_grad, textco_biasgrad, textoutb_grad]),
        jnp.stack([factor_ione, factor_itwo]),
        jnp.stack([offset_ione, offset_itwo]),
        jnp.stack([imageco_biasgrad, imageoutb_grad]),
    )
    outputs = (
        text_three,
        image_three,
        text_ingrad.astype(jnp.bfloat16),
        image_ingrad.astype(jnp.bfloat16),
    )
    return (outputs, gradients)


def local_plain(
    text,
    image,
    text_len,
    region_count,
    text_cot,
    image_cot,
    selfproject,
    selfbiases,
    selfoutput,
    textcoproject,
    textcobiases,
    imagecoproject,
    imagecobiases,
    textcooutput,
    imagecooutput,
    textffinner,
    textffinbias,
    textffouter,
    imageffinner,
    imageffinbias,
    imageffouter,
    textgains,
    textshifts,
    textbiases,
    imagegains,
    imageshifts,
    imagebiases,
):
    seq_count = lax.axis_size("seq")
    micro_pairs = text.shape[0] // MB
    shards = (
        selfproject,
        selfbiases,
        selfoutput,
        textcoproject,
        textcobiases,
        imagecoproject,
        imagecobiases,
        textcooutput,
        imagecooutput,
        textffinner,
        textffinbias,
        textffouter,
        imageffinner,
        imageffinbias,
        imageffouter,
        textgains,
        textshifts,
        textbiases,
        imagegains,
        imageshifts,
        imagebiases,
    )
    accumulated = None
    text_rows = []
    image_rows = []
    textgrad_rows = []
    imagegrad_rows = []
    for micro_index in range(MB):
        fetched = (
            lax.all_gather(shards[0], "dp", axis=0, tiled=True),
            lax.all_gather(shards[1], "dp", axis=1, tiled=True),
            lax.all_gather(shards[2], "dp", axis=0, tiled=True),
            lax.all_gather(shards[3], "dp", axis=0, tiled=True),
            lax.all_gather(shards[4], "dp", axis=1, tiled=True),
            lax.all_gather(shards[5], "dp", axis=0, tiled=True),
            lax.all_gather(shards[6], "dp", axis=1, tiled=True),
            lax.all_gather(shards[7], "dp", axis=0, tiled=True),
            lax.all_gather(shards[8], "dp", axis=0, tiled=True),
            lax.all_gather(shards[9], "dp", axis=0, tiled=True),
            lax.all_gather(shards[10], "dp", axis=0, tiled=True),
            lax.all_gather(shards[11], "dp", axis=0, tiled=True),
            lax.all_gather(shards[12], "dp", axis=0, tiled=True),
            lax.all_gather(shards[13], "dp", axis=0, tiled=True),
            lax.all_gather(shards[14], "dp", axis=0, tiled=True),
            lax.all_gather(shards[15], "dp", axis=1, tiled=True),
            lax.all_gather(shards[16], "dp", axis=1, tiled=True),
            lax.all_gather(shards[17], "dp", axis=1, tiled=True),
            lax.all_gather(shards[18], "dp", axis=1, tiled=True),
            lax.all_gather(shards[19], "dp", axis=1, tiled=True),
            lax.all_gather(shards[20], "dp", axis=1, tiled=True),
        )
        begin_row = micro_index * micro_pairs
        end_row = begin_row + micro_pairs
        outputs, gradients = micro_step(
            fetched,
            text[begin_row:end_row],
            image[begin_row:end_row],
            text_len[begin_row:end_row],
            region_count[begin_row:end_row],
            text_cot[begin_row:end_row],
            image_cot[begin_row:end_row],
            text.shape[1] * seq_count,
            image.shape[1] * seq_count,
        )
        text_rows.append(outputs[0])
        image_rows.append(outputs[1])
        textgrad_rows.append(outputs[2])
        imagegrad_rows.append(outputs[3])
        pieces = (
            lax.psum_scatter(gradients[0], "dp", scatter_dimension=0, tiled=True),
            lax.psum_scatter(gradients[1], "dp", scatter_dimension=1, tiled=True),
            lax.psum_scatter(gradients[2], "dp", scatter_dimension=0, tiled=True),
            lax.psum_scatter(gradients[3], "dp", scatter_dimension=0, tiled=True),
            lax.psum_scatter(gradients[4], "dp", scatter_dimension=1, tiled=True),
            lax.psum_scatter(gradients[5], "dp", scatter_dimension=0, tiled=True),
            lax.psum_scatter(gradients[6], "dp", scatter_dimension=1, tiled=True),
            lax.psum_scatter(gradients[7], "dp", scatter_dimension=0, tiled=True),
            lax.psum_scatter(gradients[8], "dp", scatter_dimension=0, tiled=True),
            lax.psum_scatter(gradients[9], "dp", scatter_dimension=0, tiled=True),
            lax.psum_scatter(gradients[10], "dp", scatter_dimension=0, tiled=True),
            lax.psum_scatter(gradients[11], "dp", scatter_dimension=0, tiled=True),
            lax.psum_scatter(gradients[12], "dp", scatter_dimension=0, tiled=True),
            lax.psum_scatter(gradients[13], "dp", scatter_dimension=0, tiled=True),
            lax.psum_scatter(gradients[14], "dp", scatter_dimension=0, tiled=True),
            lax.psum_scatter(gradients[15], "dp", scatter_dimension=1, tiled=True),
            lax.psum_scatter(gradients[16], "dp", scatter_dimension=1, tiled=True),
            lax.psum_scatter(gradients[17], "dp", scatter_dimension=1, tiled=True),
            lax.psum_scatter(gradients[18], "dp", scatter_dimension=1, tiled=True),
            lax.psum_scatter(gradients[19], "dp", scatter_dimension=1, tiled=True),
            lax.psum_scatter(gradients[20], "dp", scatter_dimension=1, tiled=True),
        )
        accumulated = pieces if accumulated is None else jax.tree.map(jnp.add, accumulated, pieces)
    summed = (
        lax.psum(accumulated[0].astype(jnp.bfloat16), "seq").astype(jnp.float32),
        lax.psum(accumulated[1].astype(jnp.bfloat16), "seq").astype(jnp.float32),
        lax.psum(accumulated[2].astype(jnp.bfloat16), "seq").astype(jnp.float32),
        lax.psum(accumulated[3].astype(jnp.bfloat16), "seq").astype(jnp.float32),
        lax.psum(accumulated[4].astype(jnp.bfloat16), "seq").astype(jnp.float32),
        lax.psum(accumulated[5].astype(jnp.bfloat16), "seq").astype(jnp.float32),
        lax.psum(accumulated[6].astype(jnp.bfloat16), "seq").astype(jnp.float32),
        lax.psum(accumulated[7].astype(jnp.bfloat16), "seq").astype(jnp.float32),
        lax.psum(accumulated[8].astype(jnp.bfloat16), "seq").astype(jnp.float32),
        lax.psum(accumulated[9].astype(jnp.bfloat16), "seq").astype(jnp.float32),
        lax.psum(accumulated[10].astype(jnp.bfloat16), "seq").astype(jnp.float32),
        lax.psum(accumulated[11].astype(jnp.bfloat16), "seq").astype(jnp.float32),
        lax.psum(accumulated[12].astype(jnp.bfloat16), "seq").astype(jnp.float32),
        lax.psum(accumulated[13].astype(jnp.bfloat16), "seq").astype(jnp.float32),
        lax.psum(accumulated[14].astype(jnp.bfloat16), "seq").astype(jnp.float32),
        lax.psum(accumulated[15].astype(jnp.bfloat16), "seq").astype(jnp.float32),
        lax.psum(accumulated[16].astype(jnp.bfloat16), "seq").astype(jnp.float32),
        lax.psum(accumulated[17].astype(jnp.bfloat16), "seq").astype(jnp.float32),
        lax.psum(accumulated[18].astype(jnp.bfloat16), "seq").astype(jnp.float32),
        lax.psum(accumulated[19].astype(jnp.bfloat16), "seq").astype(jnp.float32),
        lax.psum(accumulated[20].astype(jnp.bfloat16), "seq").astype(jnp.float32),
    )
    text_out = jnp.concatenate(text_rows, axis=0)
    image_out = jnp.concatenate(image_rows, axis=0)
    text_grad = jnp.concatenate(textgrad_rows, axis=0)
    image_grad = jnp.concatenate(imagegrad_rows, axis=0)
    return (text_out, image_out, text_grad, image_grad) + tuple(summed)


MESH = pl.DeviceIdType.MESH
ANY = pl.BlockSpec(memory_space=pl.ANY)
VMEM = pl.BlockSpec(memory_space=pltpu.VMEM)


def place():
    dp = lax.axis_index("dp")
    z = lax.axis_index("seq")
    row = dp // 4
    col = (dp // 2) % 2
    core = dp % 2
    return (dp, z, row, col, core)


def partners(row, col, core, first_row):
    near_row = row + first_row * (1 - 2 * row)
    near_col = col + (1 - first_row) * (1 - 2 * col)
    far_row = row + (1 - first_row) * (1 - 2 * row)
    far_col = col + first_row * (1 - 2 * col)
    near = near_row * 4 + near_col * 2 + core
    far = far_row * 4 + far_col * 2 + core
    return (near, far)


def greet(devices):
    barrier = pltpu.get_barrier_semaphore()
    for device in devices:
        pl.semaphore_signal(barrier, inc=1, device_id=device, device_id_type=MESH)
    pl.semaphore_wait(barrier, len(devices))


def remote(source, target, send_sem, recv_sem, device):
    return pltpu.make_async_remote_copy(
        src_ref=source,
        dst_ref=target,
        send_sem=send_sem,
        recv_sem=recv_sem,
        device_id=device,
        device_id_type=MESH,
    )


SMALL_PLACES = (
    (0, 2, 96),
    (16, 2, 128),
    (18, 2, 128),
    (27, 3, 128),
    (20, 1, 128),
    (2, 3, 96),
    (5, 3, 96),
    (8, 3, 96),
    (21, 2, 128),
    (23, 2, 128),
    (25, 2, 128),
)
SMALL_COUNT = len(SMALL_PLACES)
SMALL_ROWS = 32
ROOT_HALF = 0.7071067811865476
ROOT_TURN = 0.3989422804014327
WEIGHT_SHAPES = (
    (3, 768, 768), (1, 768, 768), (3, 1024, 1024), (3, 768, 1024), (1, 1024, 768),
    (1, 1024, 1024), (1, 768, 3072), (1, 3072, 768), (1, 1024, 1024), (1, 1024, 1024),
)
W_SELF, W_SELFOUT, W_IMAGECO, W_TEXTCO, W_TEXTOUT, W_IMAGEOUT, W_TIN, W_TOUT, W_IIN, W_IOUT, W_SMALL = range(11)
PIECES = (
    (W_SMALL, 0, 0, 32, 0, 128, 2),
    *((W_SELF, k, 0, 96, 0, 768, 2) for k in range(3)),
    (W_SELFOUT, 0, 0, 96, 0, 768, 0),
    *((W_IMAGECO, k, 0, 128, 0, 1024, (0, 1, 2)[k]) for k in range(3)),
    *((W_TEXTCO, k, 0, 96, 0, 1024, (0, 1, 2)[k]) for k in range(3)),
    (W_TEXTOUT, 0, 0, 128, 0, 768, 0),
    (W_IMAGEOUT, 0, 0, 128, 0, 1024, 1),
    (W_TIN, 0, 0, 96, 0, 1152, 0),
    (W_TIN, 0, 0, 96, 1152, 1152, 1),
    (W_TIN, 0, 0, 96, 2304, 768, 2),
    *((W_TOUT, 0, k * 128, 128, 0, 768, 2) for k in range(3)),
    (W_IIN, 0, 0, 128, 0, 1024, 2),
    (W_IOUT, 0, 0, 128, 0, 1024, 2),
)
LAG_ACROSS = 4
AHEAD = 3
SAVED = dict(
    qkv_s=((3, 256, 768), jnp.bfloat16),
    qkv_t=((3, 256, 1024), jnp.bfloat16),
    qkv_i=((3, 256, 1024), jnp.bfloat16),
    tab_s=((12, 256, 128), jnp.bfloat16),
    tab_t=((16, 128, 128), jnp.bfloat16),
    tab_i=((16, 128, 128), jnp.bfloat16),
    sum_s=((256, 768), jnp.float32),
    sum_t=((256, 768), jnp.float32),
    sum_i=((256, 1024), jnp.float32),
    tot_t=((256, 768), jnp.float32),
    tot_i=((256, 1024), jnp.float32),
    slope_t=((256, 3072), jnp.bfloat16),
    slope_i=((256, 1024), jnp.bfloat16),
    xt768=((4, 2, 384, 256), jnp.bfloat16),
    xt1024=((5, 2, 512, 256), jnp.bfloat16),
    xt3072=((1, 2, 1536, 256), jnp.bfloat16),
    out_t=((256, 768), jnp.bfloat16),
    out_i=((256, 1024), jnp.bfloat16),
    vec96=((16, 768), jnp.float32),
    vec128=((16, 1024), jnp.float32),
)
WORK = dict(
    text=((2, 128, 768), jnp.bfloat16),
    image=((2, 128, 1024), jnp.bfloat16),
    mix_s=((256, 768), jnp.bfloat16),
    one=((256, 768), jnp.bfloat16),
    mix_t=((256, 1024), jnp.bfloat16),
    mix_i=((256, 1024), jnp.bfloat16),
    two_t=((256, 768), jnp.bfloat16),
    two_i=((256, 1024), jnp.bfloat16),
    active=((256, 3072), jnp.bfloat16),
    bias_in=((8, 3072), jnp.float32),
    pack=((SMALL_ROWS, 128), jnp.float32),
)


def mm(left, right):
    return jnp.dot(left, right, preferred_element_type=jnp.float32)


def mm_t(left, right):
    return lax.dot_general(left, right, (((1,), (1,)), ((), ())), preferred_element_type=jnp.float32)


def mm_0(left, right):
    return lax.dot_general(left, right, (((0,), (0,)), ((), ())), preferred_element_type=jnp.float32)


def lanes(index, width):
    return pl.ds(pl.multiple_of(index * width, width), width)


def head_masks():
    spot = lax.broadcasted_iota(jnp.int32, (1, 128), 1)
    low = jnp.where(spot < 64, 1.0, 0.0)
    return (low, 1.0 - low)


def key_mask(length):
    return lax.broadcasted_iota(jnp.int32, (1, 128), 1) < length


def table_of(scores, keep, shrink):
    scores = jnp.where(keep, scores * shrink, NEG_FILL)
    powers = jnp.exp(scores - jnp.max(scores, axis=-1, keepdims=True))
    return (powers / jnp.sum(powers, axis=-1, keepdims=True)).astype(jnp.bfloat16)


def forward_kernel(*refs):
    refs = list(refs)

    def take(count):
        taken = refs[:count]
        del refs[:count]
        return taken

    narrow, wide = jnp.bfloat16, jnp.float32
    weight_count = len(WEIGHT_SHAPES)
    array_count = weight_count + 1
    blocks = take(weight_count)
    small_in = take(SMALL_COUNT)
    states = take(4)
    text_len, region_count = take(2)
    whole_out = take(weight_count)
    saved_out = take(len(SAVED))
    cots = take(2)
    wholes = take(array_count)
    saved_refs = take(len(SAVED))
    saved = types.SimpleNamespace(**dict(zip(SAVED, saved_refs)))
    work = types.SimpleNamespace(**dict(zip(WORK, take(len(WORK)))))
    send_sem, recv_sem, swap_send, swap_recv, own_sem, out_sem, save_sem = refs
    dp, z, row, col, core = place()
    near, far = partners(row, col, core, 1 - core)
    sibling = dp + 1 - 2 * core
    diagonal = (1 - row) * 4 + (1 - col) * 2 + core
    others = [lax.rem(z + step, 4) for step in (1, 2, 3)]

    pack = work.pack
    pack[...] = jnp.zeros((SMALL_ROWS, 128), wide)
    for (first, rows, width), ref in zip(SMALL_PLACES, small_in):
        pack[first : first + rows, :width] = ref[...].astype(wide)

    greet([(near, z), (far, z), (sibling, z)] + [(dp, other) for other in others])

    def window(piece, index):
        array, k, row0, rows, col0, cols, planes = PIECES[piece]
        depth = wholes[array].shape[1] // 8
        first = pl.multiple_of(index * depth + row0, 16)
        return wholes[array].at[k, pl.ds(first, rows), pl.ds(col0, cols)]

    def own(piece):
        array, k, row0, rows, col0, cols, planes = PIECES[piece]
        if array == W_SMALL:
            return pack
        return blocks[array].at[k, pl.ds(row0, rows), pl.ds(col0, cols)]

    partner = z + 1 - 2 * lax.rem(z, 2)
    always, fetching = [], {0: [], 1: []}

    def copy_of(piece, send_lane, recv_lane, source, index, device):
        copy = remote(
            source, window(piece, index), send_sem.at[piece, send_lane], recv_sem.at[piece, recv_lane], device
        )
        return copy

    def siblings(piece, lane, source, index):
        copy = copy_of(piece, lane, lane, source, index, (sibling, z))
        always.append(copy)
        return copy

    def by_plane(piece, fetch, other=None):
        planes = PIECES[piece][6]
        if planes == 2:
            if fetch:
                fetch()
            return
        if fetch:
            pl.when(lax.rem(z, 2) == planes)(fetch)
        if other:
            pl.when(lax.rem(z, 2) != planes)(other)

    def begin(copies):
        for copy in copies:
            copy.start()

    def noted(piece, *moves):
        copies = [copy_of(piece, *move) for move in moves]
        planes = PIECES[piece][6]
        (always if planes == 2 else fetching[planes]).extend(copies)
        return copies

    def across(piece, lane, index):
        if PIECES[piece][6] == 2:
            return []
        return noted(piece, (lane + 7, lane, window(piece, index), index, (dp, partner)))

    def arrived(piece, lane, index):
        copy_of(piece, lane, lane, window(piece, index), index, (sibling, z)).wait_recv()

    def start(piece):
        block = own(piece)
        copies = noted(piece, (0, 0, block, dp, (near, z)), (1, 1, block, dp, (far, z)))
        by_plane(piece, lambda: begin(copies))
        siblings(piece, 2, block, dp).start()

    onward = {}

    def relay(piece):
        block, block_far = window(piece, near), window(piece, far)
        first = noted(piece, (3, 3, block, near, (far, z))) + across(piece, 0, near)
        second = across(piece, 1, far)
        onward[piece] = (
            siblings(piece, 4, block, near),
            siblings(piece, 5, block_far, far),
            siblings(piece, 6, window(piece, diagonal), diagonal),
        )

        def go():
            arrived(piece, 0, near)
            begin(first)
            onward[piece][0].start()
            arrived(piece, 1, far)
            begin(second)
            onward[piece][1].start()

        by_plane(piece, go)

    def pass_on(piece):
        third = across(piece, 3, diagonal)

        def go():
            arrived(piece, 3, diagonal)
            begin(third)
            onward[piece][2].start()

        by_plane(piece, go)

    def receive(piece):
        def go():
            arrived(piece, 0, near)
            onward[piece][0].start()
            arrived(piece, 1, far)
            onward[piece][1].start()

        by_plane(piece, None, go)

    def receive_last(piece):
        def go():
            arrived(piece, 3, diagonal)
            onward[piece][2].start()

        by_plane(piece, None, go)

    outs, kept, met = [], {}, []

    def ready(piece):
        array = PIECES[piece][0]
        for lane in (2, 4, 5, 6):
            arrived(piece, lane, near)
        if array not in met:
            kept[array].wait()
        met.append(array)
        if array < weight_count and met.count(array) == sum(p[0] == array for p in PIECES):
            copy = pltpu.make_async_copy(wholes[array], whole_out[array], out_sem.at[array])
            copy.start()
            outs.append(copy)

    progress = [0, 0]

    def lag_of(piece):
        return 2 if PIECES[piece][6] == 2 else LAG_ACROSS

    def tick():
        turn = progress[1]
        if turn >= len(PIECES) + LAG_ACROSS:
            return
        while progress[0] < min(turn + AHEAD, len(PIECES)):
            start(progress[0])
            progress[0] += 1
        for step, lag in ((relay, 0), (pass_on, 1), (receive, LAG_ACROSS - 2), (receive_last, LAG_ACROSS - 1)):
            if 0 <= turn - lag < len(PIECES):
                step(turn - lag)
        for piece in (turn - LAG_ACROSS, turn - 2):
            if 0 <= piece < len(PIECES) and lag_of(piece) == turn - piece:
                ready(piece)
        progress[1] += 1

    def need(array, count=3):
        places = [i for i, piece in enumerate(PIECES) if piece[0] == array][:count]
        last = max(i + lag_of(i) for i in places)
        while progress[1] <= last:
            tick()

    def save(ref):
        spot = [ref is other for other in saved_refs].index(True)
        copy = pltpu.make_async_copy(ref, saved_out[spot], save_sem.at[spot])
        copy.start()
        outs.append(copy)

    swaps = []

    def swap(array, target):
        source = states[array]
        count = source.shape[0] // 4
        slots = source.shape[1]
        here = target.at[:, pl.ds(pl.multiple_of(z * slots, 16), slots), :]
        made = []
        for step, other in enumerate(others):
            copy = remote(
                source.at[pl.ds(other * count, count)],
                here,
                swap_send.at[array, step],
                swap_recv.at[array, step],
                (dp, other),
            )
            copy.start()
            made.append(copy)
        keep = pltpu.make_async_copy(source.at[pl.ds(z * count, count)], here, own_sem.at[array_count + array])
        keep.start()
        made.append(keep)
        return made

    for array in range(array_count):
        depth = wholes[array].shape[1] // 8
        mine = pl.ds(pl.multiple_of(dp * depth, 16), depth)
        if array == W_SMALL:
            keep = pltpu.make_async_copy(pack, wholes[array].at[0, mine], own_sem.at[array])
        else:
            keep = pltpu.make_async_copy(blocks[array], wholes[array].at[:, mine], own_sem.at[array])
        kept[array] = keep
    text_in = swap(0, work.text)
    for piece in range(2):
        start(piece)
    image_in = swap(1, work.image)
    progress[0] = 2
    for keep in kept.values():
        keep.start()

    vec96, vec128, bias_in = saved.vec96, saved.vec128, work.bias_in

    def flip(values, width, target, which, first_block):
        turned = values.T
        for block in range(values.shape[1] // width):
            owner = first_block + block
            target[which, owner % 2, owner // 2 * width : (owner // 2 + 1) * width, :] = turned[
                block * width : (block + 1) * width
            ]

    def norm_rows(source, gain, shift, targets):
        def body(step, carry):
            window = pl.ds(pl.multiple_of(step * 32, 32), 32)
            hidden = source[window, :]
            centre = hidden - jnp.mean(hidden, axis=-1, keepdims=True)
            spread = jnp.mean(centre * centre, axis=-1, keepdims=True)
            result = centre * lax.rsqrt(spread + EPSILON) * gain + shift
            targets[window, :] = result.astype(narrow)
            return carry

        lax.fori_loop(0, 8, body, 0)

    def project_all(inputs, array, target, biases):
        width = target.shape[2]
        for k in range(3):
            need(array, k + 1)

            def body(tile, carry, k=k):
                where = lanes(tile, 256)
                part = mm(inputs, wholes[array][k, :, where])
                if k == 0:
                    part = part + biases[0][:, where]
                if k == 2:
                    part = part + biases[1][:, where]
                target[k, :, where] = part.astype(narrow)
                return carry

            lax.fori_loop(0, width // 256, body, 0)

    def branch(inputs, array, base, bias, target):
        width = target.shape[1]

        def body(tile, carry):
            where = lanes(tile, 256)
            part = mm(inputs, wholes[array][0, :, where])
            target[:, where] = part + base[..., where].reshape(256, 256).astype(wide) + bias[:, where]
            return carry

        lax.fori_loop(0, width // 256, body, 0)

    class Row:
        def __init__(self, ref, index):
            self.ref, self.index = ref, index

        def __getitem__(self, key):
            return self.ref[self.index : self.index + 1, key[1]]

    need(W_SMALL)
    packed = wholes[W_SMALL]
    for owner in range(8):
        base = owner * SMALL_ROWS
        vec96[:, owner * 96 : owner * 96 + 96] = packed[0, base : base + 16, :96]
        vec128[:, owner * 128 : owner * 128 + 128] = packed[0, base + 16 : base + 32, :]
        for part in range(3):
            at = owner * 384 + part * 128
            bias_in[0:1, at : at + 128] = packed[0, base + 27 + part : base + 28 + part, :]
    save(saved.vec96)
    save(saved.vec128)
    text_lengths = [text_len[z * 2 + pair] for pair in range(2)]
    region_counts = [region_count[z * 2 + pair] for pair in range(2)]
    low, high = head_masks()
    low_narrow, high_narrow = low.astype(narrow), high.astype(narrow)

    for copy in text_in:
        copy.wait()
    text = work.text[...].reshape(256, 768)
    qkv_s = saved.qkv_s
    project_all(text, W_SELF, qkv_s, (Row(vec96, 0), Row(vec96, 1)))
    save(saved.qkv_s)

    def self_heads(tile, carry):
        where = lanes(tile, 128)
        for pair in range(2):
            rows = slice(pair * 128, pair * 128 + 128)
            q2, k2, v2 = (qkv_s[k, rows, where] for k in range(3))
            both = jnp.concatenate([q2 * low_narrow, q2 * high_narrow], axis=0)
            table = table_of(mm_t(both, k2), key_mask(text_lengths[pair]), 0.125)
            saved.tab_s[pair * 6 + tile] = table
            mixed = mm(table, v2)
            work.mix_s[rows, where] = (mixed[:128] * low + mixed[128:] * high).astype(narrow)
        return carry

    tick()
    lax.fori_loop(0, 3, self_heads, 0)
    tick()
    lax.fori_loop(3, 6, self_heads, 0)
    tick()
    save(saved.tab_s)
    flip(text, 96, saved.xt768, 0, 0)
    flip(work.mix_s[...], 96, saved.xt768, 1, 0)
    need(W_SELFOUT)
    branch(work.mix_s[...], W_SELFOUT, work.text, Row(vec96, 8), saved.sum_s)
    norm_rows(saved.sum_s, vec96[2:3], vec96[5:6], work.one)
    save(saved.sum_s)
    flip(work.one[...], 96, saved.xt768, 2, 0)

    for copy in image_in:
        copy.wait()
    image = work.image[...].reshape(256, 1024)
    qkv_i, qkv_t = saved.qkv_i, saved.qkv_t
    project_all(image, W_IMAGECO, qkv_i, (Row(vec128, 2), Row(vec128, 3)))
    save(saved.qkv_i)
    flip(image, 128, saved.xt1024, 0, 0)
    project_all(work.one[...], W_TEXTCO, qkv_t, (Row(vec128, 0), Row(vec128, 1)))
    save(saved.qkv_t)

    def co_heads(head, carry):
        where = lanes(head, 128)
        shrink = 128**-0.5
        for pair in range(2):
            rows = slice(pair * 128, pair * 128 + 128)
            tq, tk, tv = (qkv_t[k, rows, where] for k in range(3))
            iq, ik, iv = (qkv_i[k, rows, where] for k in range(3))
            table = table_of(mm_t(tq, ik), key_mask(region_counts[pair]), shrink)
            saved.tab_t[pair * 8 + head] = table
            work.mix_t[rows, where] = mm(table, iv).astype(narrow)
            table = table_of(mm_t(iq, tk), key_mask(text_lengths[pair]), shrink)
            saved.tab_i[pair * 8 + head] = table
            work.mix_i[rows, where] = mm(table, tv).astype(narrow)
        return carry

    for head in (0, 2, 4, 6):
        tick()
        lax.fori_loop(head, head + 2, co_heads, 0)
    save(saved.tab_t)
    save(saved.tab_i)
    flip(work.mix_t[...], 128, saved.xt1024, 1, 0)
    flip(work.mix_i[...], 128, saved.xt1024, 2, 0)
    need(W_TEXTOUT)
    branch(work.mix_t[...], W_TEXTOUT, work.one, Row(vec96, 9), saved.sum_t)
    norm_rows(saved.sum_t, vec96[3:4], vec96[6:7], work.two_t)
    save(saved.sum_t)
    flip(work.two_t[...], 96, saved.xt768, 3, 0)
    save(saved.xt768)
    need(W_IMAGEOUT)
    branch(work.mix_i[...], W_IMAGEOUT, work.image, Row(vec128, 9), saved.sum_i)
    norm_rows(saved.sum_i, vec128[5:6], vec128[7:8], work.two_i)
    save(saved.sum_i)
    flip(work.two_i[...], 128, saved.xt1024, 3, 0)

    def activate(inner):
        share = 0.5 + 0.5 * lax.erf(inner * ROOT_HALF)
        slope = share + inner * (ROOT_TURN * jnp.exp(-0.5 * inner * inner))
        return ((inner * share).astype(narrow), slope.astype(narrow))

    two_t = work.two_t
    tot_t = saved.tot_t

    def text_inner(owner, carry):
        where = lanes(owner, 384)
        inner = mm(two_t[...], wholes[W_TIN][0, :, where]) + bias_in[0:1, where]
        active, slope = activate(inner)
        saved.slope_t[:, where] = slope
        work.active[:, where] = active
        place_ = pl.ds(pl.multiple_of(lax.div(owner, 2) * 384, 384), 384)
        saved.xt3072[0, lax.rem(owner, 2), place_, :] = active.T
        return carry

    for part in range(3):
        need(W_TIN, part + 1)
        if part == 1:
            swaps += swap(2, cots[0]) + swap(3, cots[1])
        lax.fori_loop(part * 3, min(part * 3 + 3, 8), text_inner, 0)
        tick()
    save(saved.slope_t)
    save(saved.xt3072)
    need(W_TOUT)
    branch(work.active[...], W_TOUT, two_t, Row(vec96, 10), tot_t)
    save(saved.tot_t)
    norm_rows(tot_t, vec96[4:5], vec96[7:8], saved.out_t)
    save(saved.out_t)

    need(W_IIN)
    two_i = work.two_i
    tot_i = saved.tot_i
    for part in range(4):
        where = slice(part * 256, part * 256 + 256)
        inner = mm(two_i[...], wholes[W_IIN][0, :, where]) + vec128[4:5, where]
        active, slope = activate(inner)
        saved.slope_i[:, where] = slope
        flip(active, 128, saved.xt1024, 4, part * 2)
        work.mix_i[:, where] = active
    save(saved.slope_i)
    save(saved.xt1024)
    need(W_IOUT)
    branch(work.mix_i[...], W_IOUT, two_i, Row(vec128, 10), tot_i)
    save(saved.tot_i)
    norm_rows(tot_i, vec128[6:7], vec128[8:9], saved.out_i)
    save(saved.out_i)

    for copy in always:
        copy.wait_send()
    for planes in (0, 1):

        @pl.when(lax.rem(z, 2) == planes)
        def _(planes=planes):
            for copy in fetching[planes]:
                copy.wait_send()

    for copy in swaps:
        copy.wait()
    for copy in outs:
        copy.wait()


def forward_all(blocks, small, states, text_len, region_count):
    dma = pltpu.SemaphoreType.DMA
    narrow = jnp.bfloat16
    count = len(WEIGHT_SHAPES)
    shape = jax.ShapeDtypeStruct
    out_shape = [shape(w, narrow) for w in WEIGHT_SHAPES]
    out_shape += [shape(dims, kind) for dims, kind in SAVED.values()]
    out_shape += [shape((s.shape[0] // 4, s.shape[1] * 4, s.shape[2]), s.dtype) for s in states[2:]]
    scratch = [pltpu.VMEM(w, narrow) for w in WEIGHT_SHAPES]
    scratch += [pltpu.VMEM((1, 8 * SMALL_ROWS, 128), jnp.float32)]
    scratch += [pltpu.VMEM(dims, kind) for dims, kind in (*SAVED.values(), *WORK.values())]
    scratch += [
        dma((len(PIECES), 11)),
        dma((len(PIECES), 7)),
        dma((4, 3)),
        dma((4, 3)),
        dma((count + 5,)),
        dma((count,)),
        dma((len(SAVED),)),
    ]
    results = pl.pallas_call(
        forward_kernel,
        out_shape=out_shape,
        in_specs=[ANY] * count
        + [VMEM] * SMALL_COUNT
        + [ANY] * 4
        + [pl.BlockSpec(memory_space=pltpu.SMEM)] * 2,
        out_specs=[ANY] * len(out_shape),
        scratch_shapes=scratch,
        compiler_params=pltpu.CompilerParams(
            collective_id=0, has_side_effects=True, vmem_limit_bytes=62 * 2**20
        ),
        name="forward_all",
    )(*blocks, *small, *states, text_len, region_count)
    wholes = results[:count]
    saved = types.SimpleNamespace(**dict(zip(SAVED, results[count : count + len(SAVED)])))
    return (wholes, saved, results[count + len(SAVED) :])


CHUNKS = (9, 9, 3)
TILES = (4, 3, 1)
ROWS = (96, 128, 384)
STARTS = ((9, 12, 24), (12, 15, 19, 23), ())
ORDER = ((2, 0, 3), (0, 6, 3), (1, 4, 5), (0, 3, 3), (1, 0, 4), (0, 0, 3))
STEPS = 21
LAG_NEAR, LAG_FAR, LAG_SUM, LAG_MID, LAG_END, LAG_WRITE = 1, 4, 5, 6, 7, 8
SMALL_TURN = 18
CHIP_SLOTS, NEAR_SLOTS, PLANE_SLOTS = 7, 9, 9
AT_BSELF, AT_TEXTCO, AT_TIN = 2304, 3072, 6144
AT_BTEXT, AT_BIMAGE, AT_IIN, AT_BIFF = 3072, 3840, 4864, 5888


def backward_kernel(*refs):
    refs = list(refs)

    def take(count):
        taken = refs[:count]
        del refs[:count]
        return taken

    narrow, wide = jnp.bfloat16, jnp.float32
    weights = take(len(WEIGHT_SHAPES))
    saved = types.SimpleNamespace(**dict(zip(SAVED, take(len(SAVED)))))
    cot_t, cot_i = take(2)
    result, small_result = take(2)
    pairs = take(4)
    out_box, chip, near_sum, plane, line, cross = take(6)
    s_own, s_chip, s_near, s_plane, s_line, s_cross = take(6)
    w_p, w_q, w_i, w_o = take(4)
    dz768, dz1024, dz3072 = take(3)
    xt = take(3)
    tab_s, tab_t, tab_i, sum_s, sum_t, sum_i, tot_t, tot_i, vec96, vec128 = take(10)
    mix_t, mix_i, back_t, back_i, sums96, sums128, sums_in = take(7)
    (
        core_send, core_recv, near_send, near_recv, far_send, far_recv,
        end_send, end_recv, mid_send, mid_recv, back_send, back_recv,
        write_sem, swap_send, swap_recv, own_sem, load_sem,
    ) = refs
    dp, z, row, col, core = place()
    near, far = partners(row, col, core, core)
    sibling = dp + 1 - 2 * core
    others = [lax.rem(z + step, 4) for step in (1, 2, 3)]
    near_bit = col + core * (row - col)
    far_bit = row + core * (col - row)

    def block_of(near_index, far_index):
        return near_index * (1 + core) + far_index * (2 - core)

    is_end = (z == 0) | (z == 3)
    is_mid = (z == 1) | (z == 2)
    middle = 1 + z // 2
    other_mid = 3 - z
    end = 3 * (z // 2)

    def span(ref, first, width):
        return ref.at[:, first : first + width]

    loads = []

    def load(*moves):
        made = []
        for source, target in moves:
            copy = pltpu.make_async_copy(source, target, load_sem.at[len(loads)])
            loads.append(copy)
            made.append(copy)
        return made

    def begin(group):
        for copy in group:
            copy.start()

    def finish(group):
        for copy in group:
            copy.wait()

    get_text3 = load(
        (saved.tot_t, tot_t),
        (cot_t.reshape(256, 768), span(dz768, AT_BSELF, 768)),
        (saved.vec96, vec96),
        *((weights[W_TOUT].at[0, pl.ds(i * 768, 768), :], w_q.at[i]) for i in range(4)),
    )
    get_text_in = load(
        (saved.xt3072, xt[2]),
        (saved.xt768, xt[0]),
        (saved.slope_t, span(dz768, AT_TIN, 3072)),
        *((weights[W_TIN].at[0, :, pl.ds(i * 1024, 1024)], w_p.at[i]) for i in range(3)),
    )
    get_image = load(
        (saved.tot_i, tot_i),
        (cot_i.reshape(256, 1024), span(dz1024, AT_BIMAGE, 1024)),
        (saved.vec128, vec128),
        (weights[W_IOUT].at[0], w_i.at[0]),
        (saved.slope_i, span(dz1024, AT_IIN, 1024)),
        (weights[W_IIN].at[0], w_i.at[1]),
    )
    get_co = load(
        (saved.sum_t, sum_t),
        (weights[W_TEXTOUT].at[0], w_o),
        (saved.sum_i, sum_i),
        (weights[W_IMAGEOUT].at[0], w_i.at[2]),
    )
    get_heads = load(
        (saved.xt1024, xt[1]),
        *((saved.qkv_t.at[k], span(dz768, AT_TEXTCO + k * 1024, 1024)) for k in range(3)),
        *((saved.qkv_i.at[k], span(dz1024, k * 1024, 1024)) for k in range(3)),
        (saved.tab_t, tab_t),
        (saved.tab_i, tab_i),
    )
    get_self = load(
        (saved.sum_s, sum_s),
        *((saved.qkv_s.at[k], span(dz768, k * 768, 768)) for k in range(3)),
        (saved.tab_s, tab_s),
    )
    get_textco = load((weights[W_TEXTCO], w_p))
    get_selfs = load((weights[W_SELF], w_q.at[pl.ds(0, 3)]), (weights[W_SELFOUT].at[0], w_q.at[3]))
    get_imageco = load((weights[W_IMAGECO], w_i))
    for group in (get_text3, get_text_in, get_image, get_co, get_heads, get_self):
        begin(group)
    sums96[...] = jnp.zeros((16, 768), wide)
    sums128[...] = jnp.zeros((16, 1024), wide)
    s_own[...] = jnp.zeros((2, 4, SMALL_ROWS, 128), wide)

    greet([(near, z), (far, z), (sibling, z)] + [(dp, other) for other in others])

    def swap(array, source):
        target = pairs[array]
        count, slots = source.shape[0], source.shape[1] // 4
        there = target.at[pl.ds(z * count, count)]

        def part(other):
            return source.at[:, pl.ds(pl.multiple_of(other * slots, 16), slots), :]

        made = [
            remote(part(other), there, swap_send.at[array, step], swap_recv.at[array, step], (dp, other))
            for step, other in enumerate(others)
        ]
        made.append(pltpu.make_async_copy(part(z), there, own_sem.at[array]))
        return made

    swaps = [
        swap(0, saved.out_t.reshape(2, 128, 768)),
        swap(1, saved.out_i.reshape(2, 128, 1024)),
        swap(2, back_t),
        swap(3, back_i),
    ]
    begin(swaps[0] + swaps[1])

    grads = (dz768, dz1024, dz3072)

    def products(index, half, use):
        place_ = 0
        for kind in range(3):
            chunk, chosen = 0, False
            first = 0
            for kind_, start, count in ORDER:
                if kind_ == kind:
                    inside = (index >= first) & (index < first + count)
                    chunk = jnp.where(inside, index - first + start, chunk)
                    chosen = chosen | inside
                first += count

            def work(kind=kind, chunk=chunk):
                tiles, rows = TILES[kind], ROWS[kind]
                for tile in range(tiles):
                    which = chunk * tiles + tile
                    weight = 0
                    for bound in STARTS[kind]:
                        weight = weight + jnp.where(which >= bound, 1, 0)
                    part = mm(xt[kind][weight, half], grads[kind][:, lanes(which, 256)])
                    for block in range(4):
                        for side in range(2):
                            use(
                                block,
                                (tile * 2 + side) * rows,
                                rows,
                                part[block * rows : (block + 1) * rows, side * 128 : side * 128 + 128],
                            )

            pl.when(chosen)(work)

    def core_copy(index):
        return remote(
            out_box.at[lax.rem(index, 2)],
            chip.at[lax.rem(index, CHIP_SLOTS)],
            core_send.at[index],
            core_recv.at[index],
            (sibling, z),
        )

    def near_copy(index, far_index):
        return remote(
            chip.at[lax.rem(index, CHIP_SLOTS), block_of(1 - near_bit, far_index)],
            near_sum.at[lax.rem(index, NEAR_SLOTS), far_index],
            near_send.at[index, far_index],
            near_recv.at[index, far_index],
            (near, z),
        )

    def far_copy(index):
        return remote(
            near_sum.at[lax.rem(index, NEAR_SLOTS), 1 - far_bit],
            plane.at[lax.rem(index, PLANE_SLOTS)],
            far_send.at[index],
            far_recv.at[index],
            (far, z),
        )

    def end_copy(index):
        return remote(
            plane.at[lax.rem(index, PLANE_SLOTS)], line.at[index], end_send.at[index], end_recv.at[index], (dp, middle)
        )

    def mid_copy(index):
        return remote(line.at[index], cross.at[index], mid_send.at[index], mid_recv.at[index], (dp, other_mid))

    def back_copy(index):
        return remote(cross.at[index], line.at[index], back_send.at[index], back_recv.at[index], (dp, end))

    def mid_write(index):
        return pltpu.make_async_copy(cross.at[index], result.at[index], write_sem.at[index])

    def end_write(index):
        return pltpu.make_async_copy(line.at[index], result.at[index], write_sem.at[index])

    def add(left, right):
        return (left.astype(wide) + right.astype(wide)).astype(narrow)

    def stage_core(index):
        @pl.when(index >= 2)
        def _():
            core_copy(index - 2).wait_send()

        slot = lax.rem(index, 2)

        def put(block, first, rows, values):
            out_box[slot, block, first : first + rows, :] = values.astype(narrow)

        products(index, 1 - core, put)
        core_copy(index).start()

    def stage_near(index):
        core_copy(index).wait_recv()
        slot = lax.rem(index, CHIP_SLOTS)

        def put(block, first, rows, values):
            window = (slot, block, slice(first, first + rows), slice(None))
            chip[window] = (chip[window].astype(wide) + values).astype(narrow)

        products(index, core, put)
        near_copy(index, 1 - far_bit).start()
        near_copy(index, far_bit).start()

    def stage_far(index):
        chip_slot, slot = lax.rem(index, CHIP_SLOTS), lax.rem(index, NEAR_SLOTS)
        for far_index in (1 - far_bit, far_bit):
            near_copy(index, far_index).wait_recv()
            near_sum[slot, far_index] = add(near_sum[slot, far_index], chip[chip_slot, block_of(near_bit, far_index)])
            if far_index is not far_bit:
                far_copy(index).start()
        near_copy(index, 0).wait_send()
        near_copy(index, 1).wait_send()

    def stage_sum(index):
        slot = lax.rem(index, PLANE_SLOTS)
        far_copy(index).wait_recv()
        plane[slot] = add(plane[slot], near_sum[lax.rem(index, NEAR_SLOTS), far_bit])

        @pl.when(is_end)
        def _():
            end_copy(index).start()

        far_copy(index).wait_send()

    def stage_mid(index):
        @pl.when(is_mid)
        def _():
            end_copy(index).wait_recv()
            line[index] = add(line[index], plane[lax.rem(index, PLANE_SLOTS)])
            mid_copy(index).start()

        @pl.when(is_end)
        def _():
            end_copy(index).wait_send()

    def stage_end(index):
        @pl.when(is_mid)
        def _():
            mid_copy(index).wait_recv()
            cross[index] = add(cross[index], line[index])
            back_copy(index).start()
            mid_write(index).start()

    def stage_write(index):
        @pl.when(is_end)
        def _():
            back_copy(index).wait_recv()
            end_write(index).start()

    stages = (
        (stage_core, 0),
        (stage_near, LAG_NEAR),
        (stage_far, LAG_FAR),
        (stage_sum, LAG_SUM),
        (stage_mid, LAG_MID),
        (stage_end, LAG_END),
        (stage_write, LAG_WRITE),
    )

    last = STEPS
    sm_core = remote(s_own.at[1 - core], s_chip, core_send.at[last], core_recv.at[last], (sibling, z))
    sm_near = [
        remote(
            s_chip.at[block_of(1 - near_bit, j)], s_near.at[j], near_send.at[last, j], near_recv.at[last, j], (near, z)
        )
        for j in (0, 1)
    ]
    sm_far = remote(s_near.at[1 - far_bit], s_plane, far_send.at[last], far_recv.at[last], (far, z))
    sm_end = remote(s_plane, s_line, end_send.at[last], end_recv.at[last], (dp, middle))
    sm_mid = remote(s_line, s_cross, mid_send.at[last], mid_recv.at[last], (dp, other_mid))
    sm_back = remote(s_cross, s_line, back_send.at[last], back_recv.at[last], (dp, end))

    def small_start():
        for owner in range(8):
            spot = s_own.at[owner % 2, owner // 2]
            spot[0:16, :96] = sums96[:, owner * 96 : owner * 96 + 96]
            spot[16:27, :] = sums128[0:11, owner * 128 : owner * 128 + 128]
            for part in range(3):
                at = owner * 384 + part * 128
                spot[27 + part : 28 + part, :] = sums_in[0:1, at : at + 128]
        sm_core.start()

    def small_near():
        sm_core.wait_recv()
        s_chip[...] += s_own[core]
        begin(sm_near)

    def small_far():
        for j in (0, 1):
            sm_near[j].wait_recv()
            s_near[j] += s_chip[block_of(near_bit, j)]
        sm_far.start()

    def small_sum():
        sm_far.wait_recv()
        s_plane[...] += s_near[far_bit]
        pl.when(is_end)(sm_end.start)

    def small_mid():
        @pl.when(is_mid)
        def _():
            sm_end.wait_recv()
            s_line[...] += s_plane[...]
            sm_mid.start()

    def small_end():
        @pl.when(is_mid)
        def _():
            sm_mid.wait_recv()
            s_cross[...] += s_line[...]
            sm_back.start()
            small_result[...] = s_cross[...]

    def small_write():
        @pl.when(is_end)
        def _():
            sm_back.wait_recv()
            small_result[...] = s_line[...]

    def norm_step(source, upstream, gain, target, first, sums, rows):
        width = source.shape[1]

        def body(step, carry):
            window = pl.ds(pl.multiple_of(step * 32, 32), 32)
            hidden = source[window, :]
            dy = upstream[window, first[0] : first[0] + width].astype(wide)
            centre = hidden - jnp.mean(hidden, axis=-1, keepdims=True)
            spread = jnp.mean(centre * centre, axis=-1, keepdims=True)
            scale = lax.rsqrt(spread + EPSILON)
            unit = centre * scale
            inner = dy * gain
            back = scale * (
                inner
                - jnp.mean(inner, axis=-1, keepdims=True)
                - unit * jnp.mean(inner * unit, axis=-1, keepdims=True)
            )
            rounded = back.astype(narrow)
            source[window, :] = back
            target[window, first[1] : first[1] + width] = rounded
            parts = (dy * unit, dy, rounded.astype(wide))
            return tuple(c + p.reshape(4, 8, width).sum(axis=0) for c, p in zip(carry, parts))

        zero = jnp.zeros((8, width), wide)
        totals = lax.fori_loop(0, 8, body, (zero, zero, zero))
        for at, total in zip(rows, totals):
            sums[at : at + 1, :] = jnp.sum(total, axis=0, keepdims=True)

    def col_sum(values):
        return jnp.sum(values.astype(wide), axis=0, keepdims=True)

    def text_three():
        finish(get_text3)
        norm_step(tot_t, dz768, vec96[4:5], dz3072, (AT_BSELF, 0), sums96, (4, 7, 10))

    def text_inner(turn):
        for part in range(4):
            which = turn * 4 + part
            where = pl.ds(pl.multiple_of(AT_TIN + which * 256, 256), 256)
            out_rows = w_q[lax.div(which, 3), pl.ds(pl.multiple_of(lax.rem(which, 3) * 256, 256), 256), :]
            inner = (dz768[:, where].astype(wide) * mm_t(dz3072[...], out_rows)).astype(narrow)
            dz768[:, where] = inner
            sums_in[0:1, lanes(which, 256)] = col_sum(inner)
            tot_t[...] += mm_t(inner, w_p[turn, :, part * 256 : part * 256 + 256])

    def image_three():
        begin(get_textco)
        begin(get_selfs)
        finish(get_image)
        norm_step(tot_i, dz1024, vec128[6:7], dz1024, (AT_BIMAGE, AT_BIFF), sums128, (6, 8, 10))
        branch = dz1024[:, AT_BIFF : AT_BIFF + 1024]
        for part in range(4):
            at = part * 256
            where = slice(AT_IIN + at, AT_IIN + at + 256)
            inner = (dz1024[:, where].astype(wide) * mm_t(branch, w_i[0, at : at + 256, :])).astype(narrow)
            dz1024[:, where] = inner
            sums128[4:5, at : at + 256] = col_sum(inner)
            tot_i[...] += mm_t(inner, w_i[1, :, at : at + 256])

    def text_second():
        finish(get_co)
        norm_step(sum_t, tot_t, vec96[3:4], dz1024, (0, AT_BTEXT), sums96, (3, 6, 9))
        mix_t[...] = mm_t(dz1024[:, AT_BTEXT : AT_BTEXT + 768], w_o[...]).astype(narrow)

    def image_second():
        norm_step(sum_i, tot_i, vec128[5:6], dz1024, (0, AT_BIMAGE), sums128, (5, 7, 9))
        mix_i[...] = mm_t(dz1024[:, AT_BIMAGE : AT_BIMAGE + 1024], w_i[2]).astype(narrow)
        begin(get_imageco)
        finish(get_heads)

    def table_back(table, upper_value):
        probs = table.astype(wide)
        return (probs * (upper_value - jnp.sum(upper_value * probs, axis=-1, keepdims=True))).astype(narrow)

    def co_head(head):
        shrink = 128**-0.5
        for pair in range(2):
            rows = slice(pair * 128, pair * 128 + 128)
            t_at = [pl.ds(pl.multiple_of(AT_TEXTCO + k * 1024 + head * 128, 128), 128) for k in range(3)]
            i_at = [pl.ds(pl.multiple_of(k * 1024 + head * 128, 128), 128) for k in range(3)]
            tq, tk, tv = (dz768[rows, at] for at in t_at)
            iq, ik, iv = (dz1024[rows, at] for at in i_at)
            for q, k, v, table, mixed, spots in (
                (tq, ik, iv, tab_t, mix_t, ((dz768, t_at[0]), (dz1024, i_at[1]), (dz1024, i_at[2]))),
                (iq, tk, tv, tab_i, mix_i, ((dz1024, i_at[0]), (dz768, t_at[1]), (dz768, t_at[2]))),
            ):
                probs = table[pair * 8 + head]
                upper = mixed[rows, lanes(head, 128)]
                score = table_back(probs, mm_t(upper, v))
                grads_ = (mm(score, k) * shrink, mm_0(score, q) * shrink, mm_0(probs, upper))
                for (ref, at), value in zip(spots, grads_):
                    ref[rows, at] = value.astype(narrow)

    def co_heads(turn):
        co_head(turn * 2 - 12)
        co_head(turn * 2 - 11)

    def text_one_back():
        finish(get_textco)
        for k in range(3):
            where = slice(AT_TEXTCO + k * 1024, AT_TEXTCO + (k + 1) * 1024)
            sum_t[...] += mm_t(dz768[:, where], w_p[k])
        sums128[0:1, :] = col_sum(dz768[:, AT_TEXTCO : AT_TEXTCO + 1024])
        sums128[1:2, :] = col_sum(dz768[:, AT_TEXTCO + 2048 : AT_TEXTCO + 3072])

    def self_second():
        finish(get_self)
        finish(get_selfs)
        norm_step(sum_s, sum_t, vec96[2:3], dz768, (0, AT_BSELF), sums96, (2, 5, 8))
        mix_t[:, 0:768] = mm_t(dz768[:, AT_BSELF : AT_BSELF + 768], w_q[3]).astype(narrow)

    def image_back():
        finish(get_imageco)
        for k in range(3):
            sum_i[...] += mm_t(dz1024[:, k * 1024 : (k + 1) * 1024], w_i[k])
        sums128[2:3, :] = col_sum(dz1024[:, 0:1024])
        sums128[3:4, :] = col_sum(dz1024[:, 2048:3072])
        back_i[...] = sum_i[...].astype(narrow).reshape(2, 128, 1024)
        begin(swaps[3])

    low, high = head_masks()
    low_narrow, high_narrow = low.astype(narrow), high.astype(narrow)

    def self_heads(turn):
        tile = turn - 12
        for pair in range(2):
            rows = slice(pair * 128, pair * 128 + 128)
            at = [pl.ds(pl.multiple_of(k * 768 + tile * 128, 128), 128) for k in range(3)]
            q2, k2, v2 = (dz768[rows, where] for where in at)
            upper = mix_t[rows, lanes(tile, 128)]
            uppers = jnp.concatenate([upper * low_narrow, upper * high_narrow], axis=0)
            queries = jnp.concatenate([q2 * low_narrow, q2 * high_narrow], axis=0)
            probs = tab_s[pair * 6 + tile]
            score = table_back(probs, mm_t(uppers, v2))
            query = mm(score, k2)
            dz768[rows, at[0]] = ((query[:128] * low + query[128:] * high) * 0.125).astype(narrow)
            dz768[rows, at[1]] = (mm_0(score, queries) * 0.125).astype(narrow)
            dz768[rows, at[2]] = mm_0(probs, uppers).astype(narrow)

    def text_back():
        for k in range(3):
            sum_s[...] += mm_t(dz768[:, k * 768 : (k + 1) * 768], w_q[k])
        sums96[0:1, :] = col_sum(dz768[:, 0:768])
        sums96[1:2, :] = col_sum(dz768[:, 1536:2304])
        back_t[...] = sum_s[...].astype(narrow).reshape(2, 128, 768)
        begin(swaps[2])
        small_start()

    text_three()
    finish(get_text_in)

    def turn_body(turn, carry):
        for stage, lag in stages:
            index = turn - lag

            @pl.when((index >= 0) & (index < STEPS))
            def _(stage=stage, index=index):
                stage(index)

        pl.when(turn < 3)(lambda: text_inner(turn))
        pl.when(turn == 3)(image_three)
        pl.when(turn == 4)(text_second)
        pl.when(turn == 5)(image_second)
        pl.when((turn >= 6) & (turn < 10))(lambda: co_heads(turn))

        @pl.when(turn == 10)
        def _():
            text_one_back()
            image_back()

        pl.when(turn == 11)(self_second)
        pl.when((turn >= 12) & (turn < 18))(lambda: self_heads(turn))
        pl.when(turn == SMALL_TURN)(text_back)
        for lag, step in (
            (LAG_NEAR, small_near),
            (LAG_FAR, small_far),
            (LAG_SUM, small_sum),
            (LAG_MID, small_mid),
            (LAG_END, small_end),
            (LAG_WRITE, small_write),
        ):
            pl.when(turn == SMALL_TURN + lag)(step)
        return carry

    lax.fori_loop(0, STEPS + LAG_WRITE, turn_body, 0)

    core_copy(STEPS - 2).wait_send()
    core_copy(STEPS - 1).wait_send()
    sm_core.wait_send()
    for copy in sm_near:
        copy.wait_send()
    sm_far.wait_send()

    def settle(index, carry):
        @pl.when(is_end)
        def _():
            end_write(index).wait()

        @pl.when(is_mid)
        def _():
            mid_copy(index).wait_send()
            back_copy(index).wait_send()
            mid_write(index).wait()

        return carry

    lax.fori_loop(0, STEPS, settle, 0)

    @pl.when(is_end)
    def _():
        sm_end.wait_send()

    @pl.when(is_mid)
    def _():
        sm_mid.wait_send()
        sm_back.wait_send()

    for group in swaps:
        finish(group)


def backward_all(weights, saved, cots):
    dma = pltpu.SemaphoreType.DMA
    shape = jax.ShapeDtypeStruct
    vmem = pltpu.VMEM
    narrow, wide = jnp.bfloat16, jnp.float32
    block = (768, 128)
    tiny = (SMALL_ROWS, 128)
    kept = [getattr(saved, name) for name in SAVED]
    one = [dma((STEPS + 1,))] * 2
    results = pl.pallas_call(
        backward_kernel,
        out_shape=[
            shape((STEPS,) + block, narrow),
            shape(tiny, wide),
            shape((8, 32, 768), narrow),
            shape((8, 32, 1024), narrow),
            shape((8, 32, 768), narrow),
            shape((8, 32, 1024), narrow),
        ],
        in_specs=[ANY] * (len(weights) + len(kept) + 2),
        out_specs=[ANY, VMEM] + [ANY] * 4,
        scratch_shapes=[
            vmem((2, 4) + block, narrow),
            vmem((CHIP_SLOTS, 4) + block, narrow),
            vmem((NEAR_SLOTS, 2) + block, narrow),
            vmem((PLANE_SLOTS,) + block, narrow),
            vmem((STEPS,) + block, narrow),
            vmem((STEPS,) + block, narrow),
            vmem((2, 4) + tiny, wide),
            vmem((4,) + tiny, wide),
            vmem((2,) + tiny, wide),
            vmem(tiny, wide),
            vmem(tiny, wide),
            vmem(tiny, wide),
            vmem((3, 768, 1024), narrow),
            vmem((4, 768, 768), narrow),
            vmem((3, 1024, 1024), narrow),
            vmem((1024, 768), narrow),
            vmem((256, 9216), narrow),
            vmem((256, 6912), narrow),
            vmem((256, 768), narrow),
            vmem((4, 2, 384, 256), narrow),
            vmem((5, 2, 512, 256), narrow),
            vmem((1, 2, 1536, 256), narrow),
            vmem((12, 256, 128), narrow),
            vmem((16, 128, 128), narrow),
            vmem((16, 128, 128), narrow),
            vmem((256, 768), wide),
            vmem((256, 768), wide),
            vmem((256, 1024), wide),
            vmem((256, 768), wide),
            vmem((256, 1024), wide),
            vmem((16, 768), wide),
            vmem((16, 1024), wide),
            vmem((256, 1024), narrow),
            vmem((256, 1024), narrow),
            vmem((2, 128, 768), narrow),
            vmem((2, 128, 1024), narrow),
            vmem((16, 768), wide),
            vmem((16, 1024), wide),
            vmem((8, 3072), wide),
        ]
        + one
        + [dma((STEPS + 1, 2))] * 2
        + one * 4
        + [dma((STEPS,)), dma((4, 3)), dma((4, 3)), dma((4,)), dma((48,))],
        compiler_params=pltpu.CompilerParams(
            collective_id=1, has_side_effects=True, vmem_limit_bytes=62 * 2**20
        ),
        name="backward_all",
    )(*weights, *kept, *cots)
    return (results[0], results[1], results[2:])


UNPACK = (
    ((0, 18, 6), (1, 6, 6), (3, 24, 8), (6, 24, 24)),
    ((2, 24, 8), (4, 6, 6), (5, 8, 8), (8, 8, 8), (9, 8, 8)),
    ((7, 6, 6),),
)


def unpack_kernel(*refs):
    summed, small = refs[:2]
    states = refs[2:6]
    weights = refs[6:16]
    smalls = refs[16 : 16 + SMALL_COUNT]
    targets = refs[16 + SMALL_COUNT :]
    for state, target in zip(states, targets):
        target[...] = state[...]
    places = [{}, {}, {}]
    turn = 0
    for kind, start, count in ORDER:
        for chunk in range(start, start + count):
            places[kind][chunk] = turn
            turn += 1
    for kind in range(3):
        rows = ROWS[kind]
        tile = 0
        for weight, tiles, width in UNPACK[kind]:
            for own_tile in range(tiles):
                at, side = divmod(tile, TILES[kind] * 2)
                values = summed[places[kind][at], side * rows : (side + 1) * rows, :]
                part, column = divmod(own_tile, width)
                weights[weight][part, :, column * 128 : column * 128 + 128] = values.astype(jnp.float32)
                tile += 1
    for (first, rows, width), ref in zip(SMALL_PLACES, smalls):
        ref[...] = small[first : first + rows, :width]


def unpack(summed, small, states):
    shape = jax.ShapeDtypeStruct
    out_shape = [shape((w[0], w[1] // 8, w[2]), jnp.float32) for w in WEIGHT_SHAPES]
    out_shape += [shape((rows, width), jnp.float32) for first, rows, width in SMALL_PLACES]
    out_shape += [shape(s.shape, s.dtype) for s in states]
    results = pl.pallas_call(
        unpack_kernel,
        out_shape=out_shape,
        in_specs=[VMEM] * 6,
        out_specs=[VMEM] * (14 + SMALL_COUNT),
        compiler_params=pltpu.CompilerParams(vmem_limit_bytes=61 * 2**20),
        name="unpack",
    )(summed, small, *states)
    return (results[:10], results[10 : 10 + SMALL_COUNT], results[10 + SMALL_COUNT :])


def local_fast(
    text, image, text_len, region_count, text_cot, image_cot,
    selfproject, selfbiases, selfoutput, textcoproject, textcobiases, imagecoproject, imagecobiases,
    textcooutput, imagecooutput, textffinner, textffinbias, textffouter,
    imageffinner, imageffinbias, imageffouter,
    textgains, textshifts, textbiases, imagegains, imageshifts, imagebiases,
):
    blocks = [
        selfproject.transpose(1, 0, 2), selfoutput[None], imagecoproject.transpose(1, 0, 2),
        textcoproject.transpose(1, 0, 2), textcooutput[None], imagecooutput[None],
        textffinner[None], textffouter[None], imageffinner[None], imageffouter[None],
    ]
    small = [
        selfbiases, textcobiases, imagecobiases, textffinbias.reshape(3, 128), imageffinbias.reshape(1, 128),
        textgains, textshifts, textbiases, imagegains, imageshifts, imagebiases,
    ]
    weights, saved, cots = forward_all(blocks, small, [text, image, text_cot, image_cot], text_len, region_count)
    summed, small_sum, outputs = backward_all(weights, saved, cots)
    g, s, outputs = unpack(summed, small_sum, outputs)
    return tuple(outputs) + (
        g[W_SELF].transpose(1, 0, 2), s[0], g[W_SELFOUT][0], g[W_TEXTCO].transpose(1, 0, 2), s[1],
        g[W_IMAGECO].transpose(1, 0, 2), s[2], g[W_TEXTOUT][0], g[W_IMAGEOUT][0],
        g[W_TIN][0], s[3].reshape(-1), g[W_TOUT][0], g[W_IIN][0], s[4].reshape(-1), g[W_IOUT][0],
        s[5], s[6], s[7], s[8], s[9], s[10],
    )


def solution(mesh):
    in_specs = (
        P("dp", "seq", None),
        P("dp", "seq", None),
        P("dp"),
        P("dp"),
        P("dp", "seq", None),
        P("dp", "seq", None),
        P("dp", None, None),
        P(None, "dp"),
        P("dp", None),
        P("dp", None, None),
        P(None, "dp"),
        P("dp", None, None),
        P(None, "dp"),
        P("dp", None),
        P("dp", None),
        P("dp", None),
        P("dp"),
        P("dp", None),
        P("dp", None),
        P("dp"),
        P("dp", None),
        P(None, "dp"),
        P(None, "dp"),
        P(None, "dp"),
        P(None, "dp"),
        P(None, "dp"),
        P(None, "dp"),
    )
    out_specs = (
        P("dp", "seq", None),
        P("dp", "seq", None),
        P("dp", "seq", None),
        P("dp", "seq", None),
        P("dp", None, None),
        P(None, "dp"),
        P("dp", None),
        P("dp", None, None),
        P(None, "dp"),
        P("dp", None, None),
        P(None, "dp"),
        P("dp", None),
        P("dp", None),
        P("dp", None),
        P("dp"),
        P("dp", None),
        P("dp", None),
        P("dp"),
        P("dp", None),
        P(None, "dp"),
        P(None, "dp"),
        P(None, "dp"),
        P(None, "dp"),
        P(None, "dp"),
        P(None, "dp"),
    )
    sizes = mesh.shape
    local = local_fast if (sizes["dp"], sizes["seq"]) == (8, 4) else local_plain
    return jax.shard_map(local, mesh=mesh, in_specs=in_specs, out_specs=out_specs, check_vma=False)
```

```python
import functools
import types

import jax
import jax.numpy as jnp
from jax import lax
from jax.experimental import pallas as pl
from jax.experimental.pallas import tpu as pltpu
from jax.sharding import PartitionSpec as P

HT = 12
HC = 8
MB = 2


EPSILON = 1e-05
NEG_FILL = -1e30


def layer_norm(hidden, factor, offset):
    centre = hidden - jnp.mean(hidden, axis=-1, keepdims=True)
    spread = jnp.mean(centre * centre, axis=-1, keepdims=True)
    return centre * lax.rsqrt(spread + EPSILON) * factor + offset


def norm_back(hidden, factor, offset, upstream):
    outcome, pullback = jax.vjp(layer_norm, hidden, factor, offset)
    return pullback(upstream)


def gelu_exact(hidden):
    return jax.nn.gelu(hidden, approximate=False)


def gelu_back(hidden, upstream):
    outcome, pullback = jax.vjp(gelu_exact, hidden)
    return pullback(upstream)[0]


def linear(inputs, weight):
    return jnp.einsum("pte,ef->ptf", inputs, weight, preferred_element_type=jnp.float32)


def linear_weight(inputs, gradient):
    return jnp.einsum("pte,ptf->ef", inputs, gradient, preferred_element_type=jnp.float32)


def linear_input(gradient, weight):
    return jnp.einsum("ptf,ef->pte", gradient, weight, preferred_element_type=jnp.float32)


def row_total(gradient):
    return jnp.sum(gradient, axis=(0, 1), dtype=jnp.float32)


def project(inputs, weight, biases):
    bias_rows = biases.astype(jnp.float32)
    stacked = jnp.stack([bias_rows[0], jnp.zeros_like(bias_rows[0]), bias_rows[1]])
    triple = jnp.einsum("pte,ekf->ptkf", inputs, weight, preferred_element_type=jnp.float32)
    return (triple + stacked).astype(jnp.bfloat16)


def project_back(inputs, gradient, weight):
    weight_grad = jnp.einsum("pte,ptkf->ekf", inputs, gradient, preferred_element_type=jnp.float32)
    totals = row_total(gradient)
    input_grad = jnp.einsum("ptkf,ekf->pte", gradient, weight, preferred_element_type=jnp.float32)
    return (weight_grad, jnp.stack([totals[0], totals[2]]), input_grad)


def split_heads(values, head_count):
    return values.reshape(
        values.shape[0], values.shape[1], head_count, values.shape[2] // head_count
    )


def score_table(queries, keyvals, keymask, head_count):
    query_heads = split_heads(queries, head_count)
    key_heads = split_heads(keyvals[:, :, 0], head_count)
    shrink = query_heads.shape[-1] ** (-0.5)
    scores = (
        jnp.einsum("pthd,pshd->phts", query_heads, key_heads, preferred_element_type=jnp.float32)
        * shrink
    )
    scores = jnp.where(keymask[:, None, None, :], scores, NEG_FILL)
    return (scores, query_heads, key_heads, shrink)


def attend(queries, keyvals, keymask, head_count):
    scores, query_heads, key_heads, shrink = score_table(queries, keyvals, keymask, head_count)
    highest = jnp.max(scores, axis=-1, keepdims=True)
    powers = jnp.exp(scores - highest)
    totals = jnp.sum(powers, axis=-1, keepdims=True)
    prob_table = (powers / totals).astype(jnp.bfloat16)
    value_heads = split_heads(keyvals[:, :, 1], head_count)
    mixture = jnp.einsum(
        "phts,pshd->pthd", prob_table, value_heads, preferred_element_type=jnp.float32
    )
    return (mixture.reshape(queries.shape).astype(jnp.bfloat16), highest + jnp.log(totals))


def attend_back(upstream, queries, keyvals, keymask, logsum, head_count):
    scores, query_heads, key_heads, shrink = score_table(queries, keyvals, keymask, head_count)
    prob_table = jnp.exp(scores - logsum)
    value_heads = split_heads(keyvals[:, :, 1], head_count)
    upper_heads = split_heads(upstream, head_count)
    value_grad = jnp.einsum(
        "phts,pthd->pshd",
        prob_table.astype(jnp.bfloat16),
        upper_heads,
        preferred_element_type=jnp.float32,
    )
    prob_grad = jnp.einsum(
        "pthd,pshd->phts", upper_heads, value_heads, preferred_element_type=jnp.float32
    )
    score_grad = prob_table * (prob_grad - jnp.sum(prob_grad * prob_table, axis=-1, keepdims=True))
    score_grad = score_grad.astype(jnp.bfloat16)
    query_grad = (
        jnp.einsum("phts,pshd->pthd", score_grad, key_heads, preferred_element_type=jnp.float32)
        * shrink
    )
    key_grad = (
        jnp.einsum("phts,pthd->pshd", score_grad, query_heads, preferred_element_type=jnp.float32)
        * shrink
    )
    keyval_grad = jnp.stack([key_grad, value_grad], axis=2).reshape(keyvals.shape)
    return (query_grad.reshape(queries.shape), keyval_grad)


def feed_forward(inputs, weight_in, bias_in, weight_out, bias_out):
    inner_sum = linear(inputs, weight_in) + bias_in.astype(jnp.float32)
    active = gelu_exact(inner_sum).astype(jnp.bfloat16)
    totals = inputs.astype(jnp.float32) + linear(active, weight_out) + bias_out
    return (inner_sum, active, totals)


def feed_back(upstream, inputs, inner_sum, active, totals, factor, offset, weight_in, weight_out):
    sum_grad, factor_grad, offset_grad = norm_back(totals, factor, offset, upstream)
    branch_grad = sum_grad.astype(jnp.bfloat16)
    outer_grad = linear_weight(active, branch_grad)
    outbias_grad = row_total(branch_grad)
    active_grad = linear_input(branch_grad, weight_out)
    inner_grad = gelu_back(inner_sum, active_grad).astype(jnp.bfloat16)
    weightin_grad = linear_weight(inputs, inner_grad)
    inbias_grad = row_total(inner_grad)
    input_grad = linear_input(inner_grad, weight_in) + sum_grad
    return (
        input_grad,
        weightin_grad,
        inbias_grad,
        outer_grad,
        outbias_grad,
        factor_grad,
        offset_grad,
    )


def micro_step(
    fetched, text, image, text_len, region_count, text_cot, image_cot, caption_slots, region_slots
):
    (
        selfproject,
        selfbiases,
        selfoutput,
        textcoproject,
        textcobiases,
        imagecoproject,
        imagecobiases,
        textcooutput,
        imagecooutput,
        textffinner,
        textffinbias,
        textffouter,
        imageffinner,
        imageffinbias,
        imageffouter,
        textgains,
        textshifts,
        textbiases,
        imagegains,
        imageshifts,
        imagebiases,
    ) = fetched
    text_factor = textgains.astype(jnp.float32)
    text_offset = textshifts.astype(jnp.float32)
    text_bias = textbiases.astype(jnp.float32)
    image_factor = imagegains.astype(jnp.float32)
    image_offset = imageshifts.astype(jnp.float32)
    image_bias = imagebiases.astype(jnp.float32)
    text_mask = jnp.arange(caption_slots)[None, :] < text_len[:, None]
    region_mask = jnp.arange(region_slots)[None, :] < region_count[:, None]
    self_triple = project(text, selfproject, selfbiases)
    self_keys = lax.all_gather(self_triple[:, :, 1:], "seq", axis=1, tiled=True)
    self_mixed, self_logsum = attend(self_triple[:, :, 0], self_keys, text_mask, HT)
    self_sum = text.astype(jnp.float32) + linear(self_mixed, selfoutput) + text_bias[0]
    text_one = layer_norm(self_sum, text_factor[0], text_offset[0]).astype(jnp.bfloat16)
    text_triple = project(text_one, textcoproject, textcobiases)
    image_triple = project(image, imagecoproject, imagecobiases)
    text_keys, image_keys = (
        lax.all_gather(text_triple[:, :, 1:], "seq", axis=1, tiled=True),
        lax.all_gather(image_triple[:, :, 1:], "seq", axis=1, tiled=True),
    )
    text_mixed, text_logsum = attend(text_triple[:, :, 0], image_keys, region_mask, HC)
    image_mixed, image_logsum = attend(image_triple[:, :, 0], text_keys, text_mask, HC)
    text_sum = text_one.astype(jnp.float32) + linear(text_mixed, textcooutput) + text_bias[1]
    text_two = layer_norm(text_sum, text_factor[1], text_offset[1]).astype(jnp.bfloat16)
    image_sum = image.astype(jnp.float32) + linear(image_mixed, imagecooutput) + image_bias[0]
    image_two = layer_norm(image_sum, image_factor[0], image_offset[0]).astype(jnp.bfloat16)
    text_inner, text_active, text_total = feed_forward(
        text_two, textffinner, textffinbias, textffouter, text_bias[2]
    )
    text_three = layer_norm(text_total, text_factor[2], text_offset[2]).astype(jnp.bfloat16)
    image_inner, image_active, image_total = feed_forward(
        image_two, imageffinner, imageffinbias, imageffouter, image_bias[1]
    )
    image_three = layer_norm(image_total, image_factor[1], image_offset[1]).astype(jnp.bfloat16)
    (
        text_twograd,
        textin_grad,
        textinb_grad,
        textout_grad,
        textoutb_grad,
        factor_tthree,
        offset_tthree,
    ) = feed_back(
        text_cot.astype(jnp.float32),
        text_two,
        text_inner,
        text_active,
        text_total,
        text_factor[2],
        text_offset[2],
        textffinner,
        textffouter,
    )
    (
        image_twograd,
        imagein_grad,
        imageinb_grad,
        imageout_grad,
        imageoutb_grad,
        factor_itwo,
        offset_itwo,
    ) = feed_back(
        image_cot.astype(jnp.float32),
        image_two,
        image_inner,
        image_active,
        image_total,
        image_factor[1],
        image_offset[1],
        imageffinner,
        imageffouter,
    )
    textsum_grad, factor_ttwo, offset_ttwo = norm_back(
        text_sum, text_factor[1], text_offset[1], text_twograd
    )
    textbranch_grad = textsum_grad.astype(jnp.bfloat16)
    textco_outgrad = linear_weight(text_mixed, textbranch_grad)
    textco_biasgrad = row_total(textbranch_grad)
    textmix_grad = linear_input(textbranch_grad, textcooutput).astype(jnp.bfloat16)
    imagesum_grad, factor_ione, offset_ione = norm_back(
        image_sum, image_factor[0], image_offset[0], image_twograd
    )
    imagebranch_grad = imagesum_grad.astype(jnp.bfloat16)
    imageco_outgrad = linear_weight(image_mixed, imagebranch_grad)
    imageco_biasgrad = row_total(imagebranch_grad)
    imagemix_grad = linear_input(imagebranch_grad, imagecooutput).astype(jnp.bfloat16)
    textquery_grad, imagekv_part = attend_back(
        textmix_grad, text_triple[:, :, 0], image_keys, region_mask, text_logsum, HC
    )
    imagequery_grad, textkv_part = attend_back(
        imagemix_grad, image_triple[:, :, 0], text_keys, text_mask, image_logsum, HC
    )
    textkv_grad, imagekv_grad = (
        lax.psum_scatter(
            textkv_part.astype(jnp.bfloat16), "seq", scatter_dimension=1, tiled=True
        ).astype(jnp.float32),
        lax.psum_scatter(
            imagekv_part.astype(jnp.bfloat16), "seq", scatter_dimension=1, tiled=True
        ).astype(jnp.float32),
    )
    texttriple_grad = jnp.concatenate(
        [textquery_grad[:, :, None].astype(jnp.bfloat16), textkv_grad.astype(jnp.bfloat16)], axis=2
    )
    imagetriple_grad = jnp.concatenate(
        [imagequery_grad[:, :, None].astype(jnp.bfloat16), imagekv_grad.astype(jnp.bfloat16)],
        axis=2,
    )
    textco_projgrad, textco_qvgrad, textone_grad = project_back(
        text_one, texttriple_grad, textcoproject
    )
    textone_grad = textone_grad + textsum_grad
    imageco_projgrad, imageco_qvgrad, image_ingrad = project_back(
        image, imagetriple_grad, imagecoproject
    )
    image_ingrad = image_ingrad + imagesum_grad
    selfsum_grad, factor_tone, offset_tone = norm_back(
        self_sum, text_factor[0], text_offset[0], textone_grad
    )
    selfbranch_grad = selfsum_grad.astype(jnp.bfloat16)
    selfout_grad = linear_weight(self_mixed, selfbranch_grad)
    selfbias_grad = row_total(selfbranch_grad)
    selfmix_grad = linear_input(selfbranch_grad, selfoutput).astype(jnp.bfloat16)
    selfquery_grad, selfkv_part = attend_back(
        selfmix_grad, self_triple[:, :, 0], self_keys, text_mask, self_logsum, HT
    )
    selfkv_grad = lax.psum_scatter(
        selfkv_part.astype(jnp.bfloat16), "seq", scatter_dimension=1, tiled=True
    )
    selftriple_grad = jnp.concatenate(
        [selfquery_grad[:, :, None].astype(jnp.bfloat16), selfkv_grad], axis=2
    )
    selfproj_grad, selfqv_grad, text_ingrad = project_back(text, selftriple_grad, selfproject)
    text_ingrad = text_ingrad + selfsum_grad
    gradients = (
        selfproj_grad,
        selfqv_grad,
        selfout_grad,
        textco_projgrad,
        textco_qvgrad,
        imageco_projgrad,
        imageco_qvgrad,
        textco_outgrad,
        imageco_outgrad,
        textin_grad,
        textinb_grad,
        textout_grad,
        imagein_grad,
        imageinb_grad,
        imageout_grad,
        jnp.stack([factor_tone, factor_ttwo, factor_tthree]),
        jnp.stack([offset_tone, offset_ttwo, offset_tthree]),
        jnp.stack([selfbias_grad, textco_biasgrad, textoutb_grad]),
        jnp.stack([factor_ione, factor_itwo]),
        jnp.stack([offset_ione, offset_itwo]),
        jnp.stack([imageco_biasgrad, imageoutb_grad]),
    )
    outputs = (
        text_three,
        image_three,
        text_ingrad.astype(jnp.bfloat16),
        image_ingrad.astype(jnp.bfloat16),
    )
    return (outputs, gradients)


def local_plain(
    text,
    image,
    text_len,
    region_count,
    text_cot,
    image_cot,
    selfproject,
    selfbiases,
    selfoutput,
    textcoproject,
    textcobiases,
    imagecoproject,
    imagecobiases,
    textcooutput,
    imagecooutput,
    textffinner,
    textffinbias,
    textffouter,
    imageffinner,
    imageffinbias,
    imageffouter,
    textgains,
    textshifts,
    textbiases,
    imagegains,
    imageshifts,
    imagebiases,
):
    seq_count = lax.axis_size("seq")
    micro_pairs = text.shape[0] // MB
    shards = (
        selfproject,
        selfbiases,
        selfoutput,
        textcoproject,
        textcobiases,
        imagecoproject,
        imagecobiases,
        textcooutput,
        imagecooutput,
        textffinner,
        textffinbias,
        textffouter,
        imageffinner,
        imageffinbias,
        imageffouter,
        textgains,
        textshifts,
        textbiases,
        imagegains,
        imageshifts,
        imagebiases,
    )
    accumulated = None
    text_rows = []
    image_rows = []
    textgrad_rows = []
    imagegrad_rows = []
    for micro_index in range(MB):
        fetched = (
            lax.all_gather(shards[0], "dp", axis=0, tiled=True),
            lax.all_gather(shards[1], "dp", axis=1, tiled=True),
            lax.all_gather(shards[2], "dp", axis=0, tiled=True),
            lax.all_gather(shards[3], "dp", axis=0, tiled=True),
            lax.all_gather(shards[4], "dp", axis=1, tiled=True),
            lax.all_gather(shards[5], "dp", axis=0, tiled=True),
            lax.all_gather(shards[6], "dp", axis=1, tiled=True),
            lax.all_gather(shards[7], "dp", axis=0, tiled=True),
            lax.all_gather(shards[8], "dp", axis=0, tiled=True),
            lax.all_gather(shards[9], "dp", axis=0, tiled=True),
            lax.all_gather(shards[10], "dp", axis=0, tiled=True),
            lax.all_gather(shards[11], "dp", axis=0, tiled=True),
            lax.all_gather(shards[12], "dp", axis=0, tiled=True),
            lax.all_gather(shards[13], "dp", axis=0, tiled=True),
            lax.all_gather(shards[14], "dp", axis=0, tiled=True),
            lax.all_gather(shards[15], "dp", axis=1, tiled=True),
            lax.all_gather(shards[16], "dp", axis=1, tiled=True),
            lax.all_gather(shards[17], "dp", axis=1, tiled=True),
            lax.all_gather(shards[18], "dp", axis=1, tiled=True),
            lax.all_gather(shards[19], "dp", axis=1, tiled=True),
            lax.all_gather(shards[20], "dp", axis=1, tiled=True),
        )
        begin_row = micro_index * micro_pairs
        end_row = begin_row + micro_pairs
        outputs, gradients = micro_step(
            fetched,
            text[begin_row:end_row],
            image[begin_row:end_row],
            text_len[begin_row:end_row],
            region_count[begin_row:end_row],
            text_cot[begin_row:end_row],
            image_cot[begin_row:end_row],
            text.shape[1] * seq_count,
            image.shape[1] * seq_count,
        )
        text_rows.append(outputs[0])
        image_rows.append(outputs[1])
        textgrad_rows.append(outputs[2])
        imagegrad_rows.append(outputs[3])
        pieces = (
            lax.psum_scatter(gradients[0], "dp", scatter_dimension=0, tiled=True),
            lax.psum_scatter(gradients[1], "dp", scatter_dimension=1, tiled=True),
            lax.psum_scatter(gradients[2], "dp", scatter_dimension=0, tiled=True),
            lax.psum_scatter(gradients[3], "dp", scatter_dimension=0, tiled=True),
            lax.psum_scatter(gradients[4], "dp", scatter_dimension=1, tiled=True),
            lax.psum_scatter(gradients[5], "dp", scatter_dimension=0, tiled=True),
            lax.psum_scatter(gradients[6], "dp", scatter_dimension=1, tiled=True),
            lax.psum_scatter(gradients[7], "dp", scatter_dimension=0, tiled=True),
            lax.psum_scatter(gradients[8], "dp", scatter_dimension=0, tiled=True),
            lax.psum_scatter(gradients[9], "dp", scatter_dimension=0, tiled=True),
            lax.psum_scatter(gradients[10], "dp", scatter_dimension=0, tiled=True),
            lax.psum_scatter(gradients[11], "dp", scatter_dimension=0, tiled=True),
            lax.psum_scatter(gradients[12], "dp", scatter_dimension=0, tiled=True),
            lax.psum_scatter(gradients[13], "dp", scatter_dimension=0, tiled=True),
            lax.psum_scatter(gradients[14], "dp", scatter_dimension=0, tiled=True),
            lax.psum_scatter(gradients[15], "dp", scatter_dimension=1, tiled=True),
            lax.psum_scatter(gradients[16], "dp", scatter_dimension=1, tiled=True),
            lax.psum_scatter(gradients[17], "dp", scatter_dimension=1, tiled=True),
            lax.psum_scatter(gradients[18], "dp", scatter_dimension=1, tiled=True),
            lax.psum_scatter(gradients[19], "dp", scatter_dimension=1, tiled=True),
            lax.psum_scatter(gradients[20], "dp", scatter_dimension=1, tiled=True),
        )
        accumulated = pieces if accumulated is None else jax.tree.map(jnp.add, accumulated, pieces)
    summed = (
        lax.psum(accumulated[0].astype(jnp.bfloat16), "seq").astype(jnp.float32),
        lax.psum(accumulated[1].astype(jnp.bfloat16), "seq").astype(jnp.float32),
        lax.psum(accumulated[2].astype(jnp.bfloat16), "seq").astype(jnp.float32),
        lax.psum(accumulated[3].astype(jnp.bfloat16), "seq").astype(jnp.float32),
        lax.psum(accumulated[4].astype(jnp.bfloat16), "seq").astype(jnp.float32),
        lax.psum(accumulated[5].astype(jnp.bfloat16), "seq").astype(jnp.float32),
        lax.psum(accumulated[6].astype(jnp.bfloat16), "seq").astype(jnp.float32),
        lax.psum(accumulated[7].astype(jnp.bfloat16), "seq").astype(jnp.float32),
        lax.psum(accumulated[8].astype(jnp.bfloat16), "seq").astype(jnp.float32),
        lax.psum(accumulated[9].astype(jnp.bfloat16), "seq").astype(jnp.float32),
        lax.psum(accumulated[10].astype(jnp.bfloat16), "seq").astype(jnp.float32),
        lax.psum(accumulated[11].astype(jnp.bfloat16), "seq").astype(jnp.float32),
        lax.psum(accumulated[12].astype(jnp.bfloat16), "seq").astype(jnp.float32),
        lax.psum(accumulated[13].astype(jnp.bfloat16), "seq").astype(jnp.float32),
        lax.psum(accumulated[14].astype(jnp.bfloat16), "seq").astype(jnp.float32),
        lax.psum(accumulated[15].astype(jnp.bfloat16), "seq").astype(jnp.float32),
        lax.psum(accumulated[16].astype(jnp.bfloat16), "seq").astype(jnp.float32),
        lax.psum(accumulated[17].astype(jnp.bfloat16), "seq").astype(jnp.float32),
        lax.psum(accumulated[18].astype(jnp.bfloat16), "seq").astype(jnp.float32),
        lax.psum(accumulated[19].astype(jnp.bfloat16), "seq").astype(jnp.float32),
        lax.psum(accumulated[20].astype(jnp.bfloat16), "seq").astype(jnp.float32),
    )
    text_out = jnp.concatenate(text_rows, axis=0)
    image_out = jnp.concatenate(image_rows, axis=0)
    text_grad = jnp.concatenate(textgrad_rows, axis=0)
    image_grad = jnp.concatenate(imagegrad_rows, axis=0)
    return (text_out, image_out, text_grad, image_grad) + tuple(summed)


MESH = pl.DeviceIdType.MESH
ANY = pl.BlockSpec(memory_space=pl.ANY)
VMEM = pl.BlockSpec(memory_space=pltpu.VMEM)


def place():
    dp = lax.axis_index("dp")
    z = lax.axis_index("seq")
    row = dp // 4
    col = (dp // 2) % 2
    core = dp % 2
    return (dp, z, row, col, core)


def partners(row, col, core, first_row):
    near_row = row + first_row * (1 - 2 * row)
    near_col = col + (1 - first_row) * (1 - 2 * col)
    far_row = row + (1 - first_row) * (1 - 2 * row)
    far_col = col + first_row * (1 - 2 * col)
    near = near_row * 4 + near_col * 2 + core
    far = far_row * 4 + far_col * 2 + core
    return (near, far)


def greet(devices):
    barrier = pltpu.get_barrier_semaphore()
    for device in devices:
        pl.semaphore_signal(barrier, inc=1, device_id=device, device_id_type=MESH)
    pl.semaphore_wait(barrier, len(devices))


def remote(source, target, send_sem, recv_sem, device):
    return pltpu.make_async_remote_copy(
        src_ref=source,
        dst_ref=target,
        send_sem=send_sem,
        recv_sem=recv_sem,
        device_id=device,
        device_id_type=MESH,
    )


SMALL_PLACES = (
    (0, 2, 96),
    (16, 2, 128),
    (18, 2, 128),
    (27, 3, 128),
    (20, 1, 128),
    (2, 3, 96),
    (5, 3, 96),
    (8, 3, 96),
    (21, 2, 128),
    (23, 2, 128),
    (25, 2, 128),
)
SMALL_COUNT = len(SMALL_PLACES)
SMALL_ROWS = 32
ROOT_HALF = 0.7071067811865476
ROOT_TURN = 0.3989422804014327
WEIGHT_SHAPES = (
    (3, 768, 768), (1, 768, 768), (3, 1024, 1024), (3, 768, 1024), (1, 1024, 768),
    (1, 1024, 1024), (1, 768, 3072), (1, 3072, 768), (1, 1024, 1024), (1, 1024, 1024),
)
W_SELF, W_SELFOUT, W_IMAGECO, W_TEXTCO, W_TEXTOUT, W_IMAGEOUT, W_TIN, W_TOUT, W_IIN, W_IOUT, W_SMALL = range(11)
PIECES = (
    (W_SMALL, 0, 0, 32, 0, 128, 2),
    *((W_SELF, k, 0, 96, 0, 768, 2) for k in range(3)),
    (W_SELFOUT, 0, 0, 96, 0, 768, 0),
    *((W_IMAGECO, k, 0, 128, 0, 1024, (0, 1, 2)[k]) for k in range(3)),
    *((W_TEXTCO, k, 0, 96, 0, 1024, (0, 1, 2)[k]) for k in range(3)),
    (W_TEXTOUT, 0, 0, 128, 0, 768, 0),
    (W_IMAGEOUT, 0, 0, 128, 0, 1024, 1),
    (W_TIN, 0, 0, 96, 0, 1152, 0),
    (W_TIN, 0, 0, 96, 1152, 1152, 1),
    (W_TIN, 0, 0, 96, 2304, 768, 2),
    *((W_TOUT, 0, k * 128, 128, 0, 768, 2) for k in range(3)),
    (W_IIN, 0, 0, 128, 0, 1024, 2),
    (W_IOUT, 0, 0, 128, 0, 1024, 2),
)
LAG_ACROSS = 4
AHEAD = 3
SAVED = dict(
    qkv_s=((3, 256, 768), jnp.bfloat16),
    qkv_t=((3, 256, 1024), jnp.bfloat16),
    qkv_i=((3, 256, 1024), jnp.bfloat16),
    tab_s=((12, 256, 128), jnp.bfloat16),
    tab_t=((16, 128, 128), jnp.bfloat16),
    tab_i=((16, 128, 128), jnp.bfloat16),
    sum_s=((256, 768), jnp.float32),
    sum_t=((256, 768), jnp.float32),
    sum_i=((256, 1024), jnp.float32),
    tot_t=((256, 768), jnp.float32),
    tot_i=((256, 1024), jnp.float32),
    slope_t=((256, 3072), jnp.bfloat16),
    slope_i=((256, 1024), jnp.bfloat16),
    xt768=((4, 2, 384, 256), jnp.bfloat16),
    xt1024=((5, 2, 512, 256), jnp.bfloat16),
    xt3072=((1, 2, 1536, 256), jnp.bfloat16),
    out_t=((256, 768), jnp.bfloat16),
    out_i=((256, 1024), jnp.bfloat16),
    vec96=((16, 768), jnp.float32),
    vec128=((16, 1024), jnp.float32),
)
WORK = dict(
    text=((2, 128, 768), jnp.bfloat16),
    image=((2, 128, 1024), jnp.bfloat16),
    mix_s=((256, 768), jnp.bfloat16),
    one=((256, 768), jnp.bfloat16),
    mix_t=((256, 1024), jnp.bfloat16),
    mix_i=((256, 1024), jnp.bfloat16),
    two_t=((256, 768), jnp.bfloat16),
    two_i=((256, 1024), jnp.bfloat16),
    active=((256, 3072), jnp.bfloat16),
    bias_in=((8, 3072), jnp.float32),
    pack=((SMALL_ROWS, 128), jnp.float32),
)


def mm(left, right):
    return jnp.dot(left, right, preferred_element_type=jnp.float32)


def mm_t(left, right):
    return lax.dot_general(left, right, (((1,), (1,)), ((), ())), preferred_element_type=jnp.float32)


def mm_0(left, right):
    return lax.dot_general(left, right, (((0,), (0,)), ((), ())), preferred_element_type=jnp.float32)


def lanes(index, width):
    return pl.ds(pl.multiple_of(index * width, width), width)


def head_masks():
    spot = lax.broadcasted_iota(jnp.int32, (1, 128), 1)
    low = jnp.where(spot < 64, 1.0, 0.0)
    return (low, 1.0 - low)


def key_mask(length):
    return lax.broadcasted_iota(jnp.int32, (1, 128), 1) < length


def table_of(scores, keep, shrink):
    scores = jnp.where(keep, scores * shrink, NEG_FILL)
    powers = jnp.exp(scores - jnp.max(scores, axis=-1, keepdims=True))
    return (powers / jnp.sum(powers, axis=-1, keepdims=True)).astype(jnp.bfloat16)


def forward_kernel(*refs):
    refs = list(refs)

    def take(count):
        taken = refs[:count]
        del refs[:count]
        return taken

    narrow, wide = jnp.bfloat16, jnp.float32
    weight_count = len(WEIGHT_SHAPES)
    array_count = weight_count + 1
    blocks = take(weight_count)
    small_in = take(SMALL_COUNT)
    states = take(4)
    text_len, region_count = take(2)
    whole_out = take(weight_count)
    saved_out = take(len(SAVED))
    cots = take(2)
    wholes = take(array_count)
    saved_refs = take(len(SAVED))
    saved = types.SimpleNamespace(**dict(zip(SAVED, saved_refs)))
    work = types.SimpleNamespace(**dict(zip(WORK, take(len(WORK)))))
    send_sem, recv_sem, swap_send, swap_recv, own_sem, out_sem, save_sem = refs
    dp, z, row, col, core = place()
    near, far = partners(row, col, core, 1 - core)
    sibling = dp + 1 - 2 * core
    diagonal = (1 - row) * 4 + (1 - col) * 2 + core
    others = [lax.rem(z + step, 4) for step in (1, 2, 3)]

    pack = work.pack
    pack[...] = jnp.zeros((SMALL_ROWS, 128), wide)
    for (first, rows, width), ref in zip(SMALL_PLACES, small_in):
        pack[first : first + rows, :width] = ref[...].astype(wide)

    greet([(near, z), (far, z), (sibling, z)] + [(dp, other) for other in others])

    def window(piece, index):
        array, k, row0, rows, col0, cols, planes = PIECES[piece]
        depth = wholes[array].shape[1] // 8
        first = pl.multiple_of(index * depth + row0, 16)
        return wholes[array].at[k, pl.ds(first, rows), pl.ds(col0, cols)]

    def own(piece):
        array, k, row0, rows, col0, cols, planes = PIECES[piece]
        if array == W_SMALL:
            return pack
        return blocks[array].at[k, pl.ds(row0, rows), pl.ds(col0, cols)]

    partner = z + 1 - 2 * lax.rem(z, 2)
    always, fetching = [], {0: [], 1: []}

    def copy_of(piece, send_lane, recv_lane, source, index, device):
        copy = remote(
            source, window(piece, index), send_sem.at[piece, send_lane], recv_sem.at[piece, recv_lane], device
        )
        return copy

    def siblings(piece, lane, source, index):
        copy = copy_of(piece, lane, lane, source, index, (sibling, z))
        always.append(copy)
        return copy

    def by_plane(piece, fetch, other=None):
        planes = PIECES[piece][6]
        if planes == 2:
            if fetch:
                fetch()
            return
        if fetch:
            pl.when(lax.rem(z, 2) == planes)(fetch)
        if other:
            pl.when(lax.rem(z, 2) != planes)(other)

    def begin(copies):
        for copy in copies:
            copy.start()

    def noted(piece, *moves):
        copies = [copy_of(piece, *move) for move in moves]
        planes = PIECES[piece][6]
        (always if planes == 2 else fetching[planes]).extend(copies)
        return copies

    def across(piece, lane, index):
        if PIECES[piece][6] == 2:
            return []
        return noted(piece, (lane + 7, lane, window(piece, index), index, (dp, partner)))

    def arrived(piece, lane, index):
        copy_of(piece, lane, lane, window(piece, index), index, (sibling, z)).wait_recv()

    def start(piece):
        block = own(piece)
        copies = noted(piece, (0, 0, block, dp, (near, z)), (1, 1, block, dp, (far, z)))
        by_plane(piece, lambda: begin(copies))
        siblings(piece, 2, block, dp).start()

    onward = {}

    def relay(piece):
        block, block_far = window(piece, near), window(piece, far)
        first = noted(piece, (3, 3, block, near, (far, z))) + across(piece, 0, near)
        second = across(piece, 1, far)
        onward[piece] = (
            siblings(piece, 4, block, near),
            siblings(piece, 5, block_far, far),
            siblings(piece, 6, window(piece, diagonal), diagonal),
        )

        def go():
            arrived(piece, 0, near)
            begin(first)
            onward[piece][0].start()
            arrived(piece, 1, far)
            begin(second)
            onward[piece][1].start()

        by_plane(piece, go)

    def pass_on(piece):
        third = across(piece, 3, diagonal)

        def go():
            arrived(piece, 3, diagonal)
            begin(third)
            onward[piece][2].start()

        by_plane(piece, go)

    def receive(piece):
        def go():
            arrived(piece, 0, near)
            onward[piece][0].start()
            arrived(piece, 1, far)
            onward[piece][1].start()

        by_plane(piece, None, go)

    def receive_last(piece):
        def go():
            arrived(piece, 3, diagonal)
            onward[piece][2].start()

        by_plane(piece, None, go)

    outs, kept, met = [], {}, []

    def ready(piece):
        array = PIECES[piece][0]
        for lane in (2, 4, 5, 6):
            arrived(piece, lane, near)
        if array not in met:
            kept[array].wait()
        met.append(array)
        if array < weight_count and met.count(array) == sum(p[0] == array for p in PIECES):
            copy = pltpu.make_async_copy(wholes[array], whole_out[array], out_sem.at[array])
            copy.start()
            outs.append(copy)

    progress = [0, 0]

    def lag_of(piece):
        return 2 if PIECES[piece][6] == 2 else LAG_ACROSS

    def tick():
        turn = progress[1]
        if turn >= len(PIECES) + LAG_ACROSS:
            return
        if turn < len(PIECES):
            relay(turn)
        while progress[0] < min(turn + AHEAD, len(PIECES)):
            start(progress[0])
            progress[0] += 1
        for step, lag in ((pass_on, 1), (receive, LAG_ACROSS - 2), (receive_last, LAG_ACROSS - 1)):
            if 0 <= turn - lag < len(PIECES):
                step(turn - lag)
        for piece in (turn - LAG_ACROSS, turn - 2):
            if 0 <= piece < len(PIECES) and lag_of(piece) == turn - piece:
                ready(piece)
        progress[1] += 1

    def need(array, count=3):
        places = [i for i, piece in enumerate(PIECES) if piece[0] == array][:count]
        last = max(i + lag_of(i) for i in places)
        while progress[1] <= last:
            tick()

    def save(ref):
        spot = [ref is other for other in saved_refs].index(True)
        copy = pltpu.make_async_copy(ref, saved_out[spot], save_sem.at[spot])
        copy.start()
        outs.append(copy)

    swaps = []

    def swap(array, target):
        source = states[array]
        count = source.shape[0] // 4
        slots = source.shape[1]
        here = target.at[:, pl.ds(pl.multiple_of(z * slots, 16), slots), :]
        made = []
        for step, other in enumerate(others):
            copy = remote(
                source.at[pl.ds(other * count, count)],
                here,
                swap_send.at[array, step],
                swap_recv.at[array, step],
                (dp, other),
            )
            copy.start()
            made.append(copy)
        keep = pltpu.make_async_copy(source.at[pl.ds(z * count, count)], here, own_sem.at[array_count + array])
        keep.start()
        made.append(keep)
        return made

    for array in range(array_count):
        depth = wholes[array].shape[1] // 8
        mine = pl.ds(pl.multiple_of(dp * depth, 16), depth)
        if array == W_SMALL:
            keep = pltpu.make_async_copy(pack, wholes[array].at[0, mine], own_sem.at[array])
        else:
            keep = pltpu.make_async_copy(blocks[array], wholes[array].at[:, mine], own_sem.at[array])
        kept[array] = keep
    text_in = swap(0, work.text)
    for piece in range(2):
        start(piece)
    image_in = swap(1, work.image)
    progress[0] = 2
    while progress[0] < AHEAD:
        start(progress[0])
        progress[0] += 1
    for keep in kept.values():
        keep.start()

    vec96, vec128, bias_in = saved.vec96, saved.vec128, work.bias_in

    def flip(values, width, target, which, first_block):
        turned = values.T
        for block in range(values.shape[1] // width):
            owner = first_block + block
            target[which, owner % 2, owner // 2 * width : (owner // 2 + 1) * width, :] = turned[
                block * width : (block + 1) * width
            ]

    def norm_rows(source, gain, shift, targets):
        def body(step, carry):
            window = pl.ds(pl.multiple_of(step * 32, 32), 32)
            hidden = source[window, :]
            centre = hidden - jnp.mean(hidden, axis=-1, keepdims=True)
            spread = jnp.mean(centre * centre, axis=-1, keepdims=True)
            result = centre * lax.rsqrt(spread + EPSILON) * gain + shift
            targets[window, :] = result.astype(narrow)
            return carry

        lax.fori_loop(0, 8, body, 0)

    def project_all(inputs, array, target, biases):
        width = target.shape[2]
        for k in range(3):
            need(array, k + 1)

            def body(tile, carry, k=k):
                where = lanes(tile, 256)
                part = mm(inputs, wholes[array][k, :, where])
                if k == 0:
                    part = part + biases[0][:, where]
                if k == 2:
                    part = part + biases[1][:, where]
                target[k, :, where] = part.astype(narrow)
                return carry

            lax.fori_loop(0, width // 256, body, 0)

    def branch(inputs, array, base, bias, target):
        width = target.shape[1]

        def body(tile, carry):
            where = lanes(tile, 256)
            part = mm(inputs, wholes[array][0, :, where])
            target[:, where] = part + base[..., where].reshape(256, 256).astype(wide) + bias[:, where]
            return carry

        lax.fori_loop(0, width // 256, body, 0)

    class Row:
        def __init__(self, ref, index):
            self.ref, self.index = ref, index

        def __getitem__(self, key):
            return self.ref[self.index : self.index + 1, key[1]]

    need(W_SMALL)
    packed = wholes[W_SMALL]
    for owner in range(8):
        base = owner * SMALL_ROWS
        vec96[:, owner * 96 : owner * 96 + 96] = packed[0, base : base + 16, :96]
        vec128[:, owner * 128 : owner * 128 + 128] = packed[0, base + 16 : base + 32, :]
        for part in range(3):
            at = owner * 384 + part * 128
            bias_in[0:1, at : at + 128] = packed[0, base + 27 + part : base + 28 + part, :]
    save(saved.vec96)
    save(saved.vec128)
    text_lengths = [text_len[z * 2 + pair] for pair in range(2)]
    region_counts = [region_count[z * 2 + pair] for pair in range(2)]
    low, high = head_masks()
    low_narrow, high_narrow = low.astype(narrow), high.astype(narrow)

    for copy in text_in:
        copy.wait()
    text = work.text[...].reshape(256, 768)
    qkv_s = saved.qkv_s
    project_all(text, W_SELF, qkv_s, (Row(vec96, 0), Row(vec96, 1)))
    save(saved.qkv_s)

    def self_heads(tile, carry):
        where = lanes(tile, 128)
        for pair in range(2):
            rows = slice(pair * 128, pair * 128 + 128)
            q2, k2, v2 = (qkv_s[k, rows, where] for k in range(3))
            both = jnp.concatenate([q2 * low_narrow, q2 * high_narrow], axis=0)
            table = table_of(mm_t(both, k2), key_mask(text_lengths[pair]), 0.125)
            saved.tab_s[pair * 6 + tile] = table
            mixed = mm(table, v2)
            work.mix_s[rows, where] = (mixed[:128] * low + mixed[128:] * high).astype(narrow)
        return carry

    tick()
    lax.fori_loop(0, 3, self_heads, 0)
    tick()
    lax.fori_loop(3, 6, self_heads, 0)
    tick()
    save(saved.tab_s)
    flip(text, 96, saved.xt768, 0, 0)
    flip(work.mix_s[...], 96, saved.xt768, 1, 0)
    need(W_SELFOUT)
    branch(work.mix_s[...], W_SELFOUT, work.text, Row(vec96, 8), saved.sum_s)
    norm_rows(saved.sum_s, vec96[2:3], vec96[5:6], work.one)
    save(saved.sum_s)
    flip(work.one[...], 96, saved.xt768, 2, 0)

    for copy in image_in:
        copy.wait()
    image = work.image[...].reshape(256, 1024)
    qkv_i, qkv_t = saved.qkv_i, saved.qkv_t
    project_all(image, W_IMAGECO, qkv_i, (Row(vec128, 2), Row(vec128, 3)))
    save(saved.qkv_i)
    flip(image, 128, saved.xt1024, 0, 0)
    project_all(work.one[...], W_TEXTCO, qkv_t, (Row(vec128, 0), Row(vec128, 1)))
    save(saved.qkv_t)

    def co_heads(head, carry):
        where = lanes(head, 128)
        shrink = 128**-0.5
        for pair in range(2):
            rows = slice(pair * 128, pair * 128 + 128)
            tq, tk, tv = (qkv_t[k, rows, where] for k in range(3))
            iq, ik, iv = (qkv_i[k, rows, where] for k in range(3))
            table = table_of(mm_t(tq, ik), key_mask(region_counts[pair]), shrink)
            saved.tab_t[pair * 8 + head] = table
            work.mix_t[rows, where] = mm(table, iv).astype(narrow)
            table = table_of(mm_t(iq, tk), key_mask(text_lengths[pair]), shrink)
            saved.tab_i[pair * 8 + head] = table
            work.mix_i[rows, where] = mm(table, tv).astype(narrow)
        return carry

    for head in (0, 2, 4, 6):
        tick()
        lax.fori_loop(head, head + 2, co_heads, 0)
    save(saved.tab_t)
    save(saved.tab_i)
    flip(work.mix_t[...], 128, saved.xt1024, 1, 0)
    flip(work.mix_i[...], 128, saved.xt1024, 2, 0)
    need(W_TEXTOUT)
    branch(work.mix_t[...], W_TEXTOUT, work.one, Row(vec96, 9), saved.sum_t)
    norm_rows(saved.sum_t, vec96[3:4], vec96[6:7], work.two_t)
    save(saved.sum_t)
    flip(work.two_t[...], 96, saved.xt768, 3, 0)
    save(saved.xt768)
    need(W_IMAGEOUT)
    branch(work.mix_i[...], W_IMAGEOUT, work.image, Row(vec128, 9), saved.sum_i)
    norm_rows(saved.sum_i, vec128[5:6], vec128[7:8], work.two_i)
    save(saved.sum_i)
    flip(work.two_i[...], 128, saved.xt1024, 3, 0)

    def activate(inner):
        share = 0.5 + 0.5 * lax.erf(inner * ROOT_HALF)
        slope = share + inner * (ROOT_TURN * jnp.exp(-0.5 * inner * inner))
        return ((inner * share).astype(narrow), slope.astype(narrow))

    two_t = work.two_t
    tot_t = saved.tot_t

    def text_inner(owner, carry):
        where = lanes(owner, 384)
        inner = mm(two_t[...], wholes[W_TIN][0, :, where]) + bias_in[0:1, where]
        active, slope = activate(inner)
        saved.slope_t[:, where] = slope
        work.active[:, where] = active
        place_ = pl.ds(pl.multiple_of(lax.div(owner, 2) * 384, 384), 384)
        saved.xt3072[0, lax.rem(owner, 2), place_, :] = active.T
        return carry

    for part in range(3):
        need(W_TIN, part + 1)
        if part == 1:
            swaps += swap(2, cots[0]) + swap(3, cots[1])
        lax.fori_loop(part * 3, min(part * 3 + 3, 8), text_inner, 0)
        tick()
    save(saved.slope_t)
    save(saved.xt3072)
    need(W_TOUT)
    branch(work.active[...], W_TOUT, two_t, Row(vec96, 10), tot_t)
    save(saved.tot_t)
    norm_rows(tot_t, vec96[4:5], vec96[7:8], saved.out_t)
    save(saved.out_t)

    need(W_IIN)
    two_i = work.two_i
    tot_i = saved.tot_i
    for part in range(4):
        where = slice(part * 256, part * 256 + 256)
        inner = mm(two_i[...], wholes[W_IIN][0, :, where]) + vec128[4:5, where]
        active, slope = activate(inner)
        saved.slope_i[:, where] = slope
        flip(active, 128, saved.xt1024, 4, part * 2)
        work.mix_i[:, where] = active
    save(saved.slope_i)
    save(saved.xt1024)
    need(W_IOUT)
    branch(work.mix_i[...], W_IOUT, two_i, Row(vec128, 10), tot_i)
    save(saved.tot_i)
    norm_rows(tot_i, vec128[6:7], vec128[8:9], saved.out_i)
    save(saved.out_i)

    for copy in always:
        copy.wait_send()
    for planes in (0, 1):

        @pl.when(lax.rem(z, 2) == planes)
        def _(planes=planes):
            for copy in fetching[planes]:
                copy.wait_send()

    for copy in swaps:
        copy.wait()
    for copy in outs:
        copy.wait()


def forward_all(blocks, small, states, text_len, region_count):
    dma = pltpu.SemaphoreType.DMA
    narrow = jnp.bfloat16
    count = len(WEIGHT_SHAPES)
    shape = jax.ShapeDtypeStruct
    out_shape = [shape(w, narrow) for w in WEIGHT_SHAPES]
    out_shape += [shape(dims, kind) for dims, kind in SAVED.values()]
    out_shape += [shape((s.shape[0] // 4, s.shape[1] * 4, s.shape[2]), s.dtype) for s in states[2:]]
    scratch = [pltpu.VMEM(w, narrow) for w in WEIGHT_SHAPES]
    scratch += [pltpu.VMEM((1, 8 * SMALL_ROWS, 128), jnp.float32)]
    scratch += [pltpu.VMEM(dims, kind) for dims, kind in (*SAVED.values(), *WORK.values())]
    scratch += [
        dma((len(PIECES), 11)),
        dma((len(PIECES), 7)),
        dma((4, 3)),
        dma((4, 3)),
        dma((count + 5,)),
        dma((count,)),
        dma((len(SAVED),)),
    ]
    results = pl.pallas_call(
        forward_kernel,
        out_shape=out_shape,
        in_specs=[ANY] * count
        + [VMEM] * SMALL_COUNT
        + [ANY] * 4
        + [pl.BlockSpec(memory_space=pltpu.SMEM)] * 2,
        out_specs=[ANY] * len(out_shape),
        scratch_shapes=scratch,
        compiler_params=pltpu.CompilerParams(
            collective_id=0, has_side_effects=True, vmem_limit_bytes=62 * 2**20
        ),
        name="forward_all",
    )(*blocks, *small, *states, text_len, region_count)
    wholes = results[:count]
    saved = types.SimpleNamespace(**dict(zip(SAVED, results[count : count + len(SAVED)])))
    return (wholes, saved, results[count + len(SAVED) :])


CHUNKS = (9, 9, 3)
TILES = (4, 3, 1)
ROWS = (96, 128, 384)
STARTS = ((9, 12, 24), (12, 15, 19, 23), ())
ORDER = ((2, 0, 3), (0, 6, 3), (1, 4, 5), (0, 3, 3), (1, 0, 4), (0, 0, 3))
STEPS = 21
LAG_NEAR, LAG_FAR, LAG_SUM, LAG_MID, LAG_END, LAG_WRITE = 1, 5, 6, 7, 8, 9
SMALL_TURN = 18
CHIP_SLOTS, NEAR_SLOTS, PLANE_SLOTS = 8, 11, 9
AT_BSELF, AT_TEXTCO, AT_TIN = 2304, 3072, 6144
AT_BTEXT, AT_BIMAGE, AT_IIN, AT_BIFF = 3072, 3840, 4864, 5888


def backward_kernel(*refs):
    refs = list(refs)

    def take(count):
        taken = refs[:count]
        del refs[:count]
        return taken

    narrow, wide = jnp.bfloat16, jnp.float32
    weights = take(len(WEIGHT_SHAPES))
    saved = types.SimpleNamespace(**dict(zip(SAVED, take(len(SAVED)))))
    cot_t, cot_i = take(2)
    result, small_result = take(2)
    pairs = take(4)
    out_box, chip, near_sum, plane, line, cross = take(6)
    s_own, s_chip, s_near, s_plane, s_line, s_cross = take(6)
    w_p, w_q, w_i, w_o = take(4)
    dz768, dz1024, dz3072 = take(3)
    xt = take(3)
    tab_s, tab_t, tab_i, sum_s, sum_t, sum_i, tot_t, tot_i, vec96, vec128 = take(10)
    mix_t, mix_i, back_t, back_i, sums96, sums128, sums_in = take(7)
    (
        core_send, core_recv, near_send, near_recv, far_send, far_recv,
        end_send, end_recv, mid_send, mid_recv, back_send, back_recv,
        write_sem, swap_send, swap_recv, own_sem, load_sem,
    ) = refs
    dp, z, row, col, core = place()
    near, far = partners(row, col, core, core)
    sibling = dp + 1 - 2 * core
    others = [lax.rem(z + step, 4) for step in (1, 2, 3)]
    near_bit = col + core * (row - col)
    far_bit = row + core * (col - row)

    def block_of(near_index, far_index):
        return near_index * (1 + core) + far_index * (2 - core)

    is_end = (z == 0) | (z == 3)
    is_mid = (z == 1) | (z == 2)
    middle = 1 + z // 2
    other_mid = 3 - z
    end = 3 * (z // 2)

    def span(ref, first, width):
        return ref.at[:, first : first + width]

    loads = []

    def load(*moves):
        made = []
        for source, target in moves:
            copy = pltpu.make_async_copy(source, target, load_sem.at[len(loads)])
            loads.append(copy)
            made.append(copy)
        return made

    def begin(group):
        for copy in group:
            copy.start()

    def finish(group):
        for copy in group:
            copy.wait()

    get_text3 = load(
        (saved.tot_t, tot_t),
        (cot_t.reshape(256, 768), span(dz768, AT_BSELF, 768)),
        (saved.vec96, vec96),
        (saved.xt3072, xt[2]),
    )
    get_text_in = load(
        *((weights[W_TOUT].at[0, pl.ds(i * 768, 768), :], w_q.at[i]) for i in range(4)),
        (saved.xt768, xt[0]),
        (saved.slope_t, span(dz768, AT_TIN, 3072)),
        *((weights[W_TIN].at[0, :, pl.ds(i * 1024, 1024)], w_p.at[i]) for i in range(3)),
    )
    get_image = load(
        (saved.tot_i, tot_i),
        (cot_i.reshape(256, 1024), span(dz1024, AT_BIMAGE, 1024)),
        (saved.vec128, vec128),
        (weights[W_IOUT].at[0], w_i.at[0]),
        (saved.slope_i, span(dz1024, AT_IIN, 1024)),
        (weights[W_IIN].at[0], w_i.at[1]),
    )
    get_co = load(
        (saved.sum_t, sum_t),
        (weights[W_TEXTOUT].at[0], w_o),
        (saved.sum_i, sum_i),
        (weights[W_IMAGEOUT].at[0], w_i.at[2]),
    )
    get_heads = load(
        (saved.xt1024, xt[1]),
        *((saved.qkv_t.at[k], span(dz768, AT_TEXTCO + k * 1024, 1024)) for k in range(3)),
        *((saved.qkv_i.at[k], span(dz1024, k * 1024, 1024)) for k in range(3)),
        (saved.tab_t, tab_t),
        (saved.tab_i, tab_i),
    )
    get_self = load(
        (saved.sum_s, sum_s),
        *((saved.qkv_s.at[k], span(dz768, k * 768, 768)) for k in range(3)),
        (saved.tab_s, tab_s),
    )
    get_textco = load((weights[W_TEXTCO], w_p))
    get_selfs = load((weights[W_SELF], w_q.at[pl.ds(0, 3)]), (weights[W_SELFOUT].at[0], w_q.at[3]))
    get_imageco = load((weights[W_IMAGECO], w_i))
    begin(get_text3)
    begin(get_text_in)
    sums96[...] = jnp.zeros((16, 768), wide)
    sums128[...] = jnp.zeros((16, 1024), wide)
    s_own[...] = jnp.zeros((2, 4, SMALL_ROWS, 128), wide)

    greet([(near, z), (far, z), (sibling, z)] + [(dp, other) for other in others])

    def swap(array, source):
        target = pairs[array]
        count, slots = source.shape[0], source.shape[1] // 4
        there = target.at[pl.ds(z * count, count)]

        def part(other):
            return source.at[:, pl.ds(pl.multiple_of(other * slots, 16), slots), :]

        made = [
            remote(part(other), there, swap_send.at[array, step], swap_recv.at[array, step], (dp, other))
            for step, other in enumerate(others)
        ]
        made.append(pltpu.make_async_copy(part(z), there, own_sem.at[array]))
        return made

    swaps = [
        swap(0, saved.out_t.reshape(2, 128, 768)),
        swap(1, saved.out_i.reshape(2, 128, 1024)),
        swap(2, back_t),
        swap(3, back_i),
    ]
    begin(swaps[0] + swaps[1])

    grads = (dz768, dz1024, dz3072)

    def products(index, half, use):
        place_ = 0
        for kind in range(3):
            chunk, chosen = 0, False
            first = 0
            for kind_, start, count in ORDER:
                if kind_ == kind:
                    inside = (index >= first) & (index < first + count)
                    chunk = jnp.where(inside, index - first + start, chunk)
                    chosen = chosen | inside
                first += count

            def work(kind=kind, chunk=chunk):
                tiles, rows = TILES[kind], ROWS[kind]
                for tile in range(tiles):
                    which = chunk * tiles + tile
                    weight = 0
                    for bound in STARTS[kind]:
                        weight = weight + jnp.where(which >= bound, 1, 0)
                    part = mm(xt[kind][weight, half], grads[kind][:, lanes(which, 256)])
                    for block in range(4):
                        for side in range(2):
                            use(
                                block,
                                (tile * 2 + side) * rows,
                                rows,
                                part[block * rows : (block + 1) * rows, side * 128 : side * 128 + 128],
                            )

            pl.when(chosen)(work)

    def core_copy(index):
        return remote(
            out_box.at[lax.rem(index, 2)],
            chip.at[lax.rem(index, CHIP_SLOTS)],
            core_send.at[index],
            core_recv.at[index],
            (sibling, z),
        )

    def near_copy(index, far_index):
        return remote(
            chip.at[lax.rem(index, CHIP_SLOTS), block_of(1 - near_bit, far_index)],
            near_sum.at[lax.rem(index, NEAR_SLOTS), far_index],
            near_send.at[index, far_index],
            near_recv.at[index, far_index],
            (near, z),
        )

    def far_copy(index):
        return remote(
            near_sum.at[lax.rem(index, NEAR_SLOTS), 1 - far_bit],
            plane.at[lax.rem(index, PLANE_SLOTS)],
            far_send.at[index],
            far_recv.at[index],
            (far, z),
        )

    def end_copy(index):
        return remote(
            plane.at[lax.rem(index, PLANE_SLOTS)], line.at[index], end_send.at[index], end_recv.at[index], (dp, middle)
        )

    def mid_copy(index):
        return remote(line.at[index], cross.at[index], mid_send.at[index], mid_recv.at[index], (dp, other_mid))

    def back_copy(index):
        return remote(cross.at[index], line.at[index], back_send.at[index], back_recv.at[index], (dp, end))

    def mid_write(index):
        return pltpu.make_async_copy(cross.at[index], result.at[index], write_sem.at[index])

    def end_write(index):
        return pltpu.make_async_copy(line.at[index], result.at[index], write_sem.at[index])

    def add(left, right):
        return (left.astype(wide) + right.astype(wide)).astype(narrow)

    def stage_core(index):
        @pl.when(index >= 2)
        def _():
            core_copy(index - 2).wait_send()

        slot = lax.rem(index, 2)

        def put(block, first, rows, values):
            out_box[slot, block, first : first + rows, :] = values.astype(narrow)

        products(index, 1 - core, put)
        core_copy(index).start()

    def stage_near(index):
        core_copy(index).wait_recv()
        slot = lax.rem(index, CHIP_SLOTS)

        def put(block, first, rows, values):
            window = (slot, block, slice(first, first + rows), slice(None))
            chip[window] = (chip[window].astype(wide) + values).astype(narrow)

        products(index, core, put)
        near_copy(index, 1 - far_bit).start()
        near_copy(index, far_bit).start()

    def stage_far(index):
        chip_slot, slot = lax.rem(index, CHIP_SLOTS), lax.rem(index, NEAR_SLOTS)
        for far_index in (1 - far_bit, far_bit):
            near_copy(index, far_index).wait_recv()
            near_sum[slot, far_index] = add(near_sum[slot, far_index], chip[chip_slot, block_of(near_bit, far_index)])
            if far_index is not far_bit:
                far_copy(index).start()
        near_copy(index, 0).wait_send()
        near_copy(index, 1).wait_send()

    def stage_sum(index):
        slot = lax.rem(index, PLANE_SLOTS)
        far_copy(index).wait_recv()
        plane[slot] = add(plane[slot], near_sum[lax.rem(index, NEAR_SLOTS), far_bit])

        @pl.when(is_end)
        def _():
            end_copy(index).start()

        far_copy(index).wait_send()

    def stage_mid(index):
        @pl.when(is_mid)
        def _():
            end_copy(index).wait_recv()
            line[index] = add(line[index], plane[lax.rem(index, PLANE_SLOTS)])
            mid_copy(index).start()

        @pl.when(is_end)
        def _():
            end_copy(index).wait_send()

    def stage_end(index):
        @pl.when(is_mid)
        def _():
            mid_copy(index).wait_recv()
            cross[index] = add(cross[index], line[index])
            back_copy(index).start()
            mid_write(index).start()

    def stage_write(index):
        @pl.when(is_end)
        def _():
            back_copy(index).wait_recv()
            end_write(index).start()

    stages = (
        (stage_core, 0),
        (stage_near, LAG_NEAR),
        (stage_far, LAG_FAR),
        (stage_sum, LAG_SUM),
        (stage_mid, LAG_MID),
        (stage_end, LAG_END),
        (stage_write, LAG_WRITE),
    )

    last = STEPS
    sm_core = remote(s_own.at[1 - core], s_chip, core_send.at[last], core_recv.at[last], (sibling, z))
    sm_near = [
        remote(
            s_chip.at[block_of(1 - near_bit, j)], s_near.at[j], near_send.at[last, j], near_recv.at[last, j], (near, z)
        )
        for j in (0, 1)
    ]
    sm_far = remote(s_near.at[1 - far_bit], s_plane, far_send.at[last], far_recv.at[last], (far, z))
    sm_end = remote(s_plane, s_line, end_send.at[last], end_recv.at[last], (dp, middle))
    sm_mid = remote(s_line, s_cross, mid_send.at[last], mid_recv.at[last], (dp, other_mid))
    sm_back = remote(s_cross, s_line, back_send.at[last], back_recv.at[last], (dp, end))

    def small_start():
        for owner in range(8):
            spot = s_own.at[owner % 2, owner // 2]
            spot[0:16, :96] = sums96[:, owner * 96 : owner * 96 + 96]
            spot[16:27, :] = sums128[0:11, owner * 128 : owner * 128 + 128]
            for part in range(3):
                at = owner * 384 + part * 128
                spot[27 + part : 28 + part, :] = sums_in[0:1, at : at + 128]
        sm_core.start()

    def small_near():
        sm_core.wait_recv()
        s_chip[...] += s_own[core]
        begin(sm_near)

    def small_far():
        for j in (0, 1):
            sm_near[j].wait_recv()
            s_near[j] += s_chip[block_of(near_bit, j)]
        sm_far.start()

    def small_sum():
        sm_far.wait_recv()
        s_plane[...] += s_near[far_bit]
        pl.when(is_end)(sm_end.start)

    def small_mid():
        @pl.when(is_mid)
        def _():
            sm_end.wait_recv()
            s_line[...] += s_plane[...]
            sm_mid.start()

    def small_end():
        @pl.when(is_mid)
        def _():
            sm_mid.wait_recv()
            s_cross[...] += s_line[...]
            sm_back.start()
            small_result[...] = s_cross[...]

    def small_write():
        @pl.when(is_end)
        def _():
            sm_back.wait_recv()
            small_result[...] = s_line[...]

    def norm_step(source, upstream, gain, target, first, sums, rows):
        width = source.shape[1]

        def body(step, carry):
            window = pl.ds(pl.multiple_of(step * 32, 32), 32)
            hidden = source[window, :]
            dy = upstream[window, first[0] : first[0] + width].astype(wide)
            centre = hidden - jnp.mean(hidden, axis=-1, keepdims=True)
            spread = jnp.mean(centre * centre, axis=-1, keepdims=True)
            scale = lax.rsqrt(spread + EPSILON)
            unit = centre * scale
            inner = dy * gain
            back = scale * (
                inner
                - jnp.mean(inner, axis=-1, keepdims=True)
                - unit * jnp.mean(inner * unit, axis=-1, keepdims=True)
            )
            rounded = back.astype(narrow)
            source[window, :] = back
            target[window, first[1] : first[1] + width] = rounded
            parts = (dy * unit, dy, rounded.astype(wide))
            return tuple(c + p.reshape(4, 8, width).sum(axis=0) for c, p in zip(carry, parts))

        zero = jnp.zeros((8, width), wide)
        totals = lax.fori_loop(0, 8, body, (zero, zero, zero))
        for at, total in zip(rows, totals):
            sums[at : at + 1, :] = jnp.sum(total, axis=0, keepdims=True)

    def col_sum(values):
        return jnp.sum(values.astype(wide), axis=0, keepdims=True)

    def text_three():
        finish(get_text3)
        norm_step(tot_t, dz768, vec96[4:5], dz3072, (AT_BSELF, 0), sums96, (4, 7, 10))

    def text_inner(turn):
        for part in range(4):
            which = turn * 4 + part
            where = pl.ds(pl.multiple_of(AT_TIN + which * 256, 256), 256)
            out_rows = w_q[lax.div(which, 3), pl.ds(pl.multiple_of(lax.rem(which, 3) * 256, 256), 256), :]
            inner = (dz768[:, where].astype(wide) * mm_t(dz3072[...], out_rows)).astype(narrow)
            dz768[:, where] = inner
            sums_in[0:1, lanes(which, 256)] = col_sum(inner)
            tot_t[...] += mm_t(inner, w_p[turn, :, part * 256 : part * 256 + 256])

    def image_three():
        begin(get_textco)
        begin(get_selfs)
        finish(get_image)
        norm_step(tot_i, dz1024, vec128[6:7], dz1024, (AT_BIMAGE, AT_BIFF), sums128, (6, 8, 10))
        branch = dz1024[:, AT_BIFF : AT_BIFF + 1024]
        for part in range(4):
            at = part * 256
            where = slice(AT_IIN + at, AT_IIN + at + 256)
            inner = (dz1024[:, where].astype(wide) * mm_t(branch, w_i[0, at : at + 256, :])).astype(narrow)
            dz1024[:, where] = inner
            sums128[4:5, at : at + 256] = col_sum(inner)
            tot_i[...] += mm_t(inner, w_i[1, :, at : at + 256])

    def text_second():
        finish(get_co)
        norm_step(sum_t, tot_t, vec96[3:4], dz1024, (0, AT_BTEXT), sums96, (3, 6, 9))
        mix_t[...] = mm_t(dz1024[:, AT_BTEXT : AT_BTEXT + 768], w_o[...]).astype(narrow)

    def image_second():
        norm_step(sum_i, tot_i, vec128[5:6], dz1024, (0, AT_BIMAGE), sums128, (5, 7, 9))
        mix_i[...] = mm_t(dz1024[:, AT_BIMAGE : AT_BIMAGE + 1024], w_i[2]).astype(narrow)
        begin(get_imageco)
        finish(get_heads)

    def table_back(table, upper_value):
        probs = table.astype(wide)
        return (probs * (upper_value - jnp.sum(upper_value * probs, axis=-1, keepdims=True))).astype(narrow)

    def co_head(head):
        shrink = 128**-0.5
        for pair in range(2):
            rows = slice(pair * 128, pair * 128 + 128)
            t_at = [pl.ds(pl.multiple_of(AT_TEXTCO + k * 1024 + head * 128, 128), 128) for k in range(3)]
            i_at = [pl.ds(pl.multiple_of(k * 1024 + head * 128, 128), 128) for k in range(3)]
            tq, tk, tv = (dz768[rows, at] for at in t_at)
            iq, ik, iv = (dz1024[rows, at] for at in i_at)
            for q, k, v, table, mixed, spots in (
                (tq, ik, iv, tab_t, mix_t, ((dz768, t_at[0]), (dz1024, i_at[1]), (dz1024, i_at[2]))),
                (iq, tk, tv, tab_i, mix_i, ((dz1024, i_at[0]), (dz768, t_at[1]), (dz768, t_at[2]))),
            ):
                probs = table[pair * 8 + head]
                upper = mixed[rows, lanes(head, 128)]
                score = table_back(probs, mm_t(upper, v))
                grads_ = (mm(score, k) * shrink, mm_0(score, q) * shrink, mm_0(probs, upper))
                for (ref, at), value in zip(spots, grads_):
                    ref[rows, at] = value.astype(narrow)

    def co_heads(turn):
        co_head(turn * 2 - 12)
        co_head(turn * 2 - 11)

    def text_one_back():
        finish(get_textco)
        for k in range(3):
            where = slice(AT_TEXTCO + k * 1024, AT_TEXTCO + (k + 1) * 1024)
            sum_t[...] += mm_t(dz768[:, where], w_p[k])
        sums128[0:1, :] = col_sum(dz768[:, AT_TEXTCO : AT_TEXTCO + 1024])
        sums128[1:2, :] = col_sum(dz768[:, AT_TEXTCO + 2048 : AT_TEXTCO + 3072])

    def self_second():
        finish(get_self)
        finish(get_selfs)
        norm_step(sum_s, sum_t, vec96[2:3], dz768, (0, AT_BSELF), sums96, (2, 5, 8))
        mix_t[:, 0:768] = mm_t(dz768[:, AT_BSELF : AT_BSELF + 768], w_q[3]).astype(narrow)

    def image_back():
        finish(get_imageco)
        for k in range(3):
            sum_i[...] += mm_t(dz1024[:, k * 1024 : (k + 1) * 1024], w_i[k])
        sums128[2:3, :] = col_sum(dz1024[:, 0:1024])
        sums128[3:4, :] = col_sum(dz1024[:, 2048:3072])
        back_i[...] = sum_i[...].astype(narrow).reshape(2, 128, 1024)
        begin(swaps[3])

    low, high = head_masks()
    low_narrow, high_narrow = low.astype(narrow), high.astype(narrow)

    def self_heads(turn):
        tile = turn - 12
        for pair in range(2):
            rows = slice(pair * 128, pair * 128 + 128)
            at = [pl.ds(pl.multiple_of(k * 768 + tile * 128, 128), 128) for k in range(3)]
            q2, k2, v2 = (dz768[rows, where] for where in at)
            upper = mix_t[rows, lanes(tile, 128)]
            uppers = jnp.concatenate([upper * low_narrow, upper * high_narrow], axis=0)
            queries = jnp.concatenate([q2 * low_narrow, q2 * high_narrow], axis=0)
            probs = tab_s[pair * 6 + tile]
            score = table_back(probs, mm_t(uppers, v2))
            query = mm(score, k2)
            dz768[rows, at[0]] = ((query[:128] * low + query[128:] * high) * 0.125).astype(narrow)
            dz768[rows, at[1]] = (mm_0(score, queries) * 0.125).astype(narrow)
            dz768[rows, at[2]] = mm_0(probs, uppers).astype(narrow)

    def text_back():
        for k in range(3):
            sum_s[...] += mm_t(dz768[:, k * 768 : (k + 1) * 768], w_q[k])
        sums96[0:1, :] = col_sum(dz768[:, 0:768])
        sums96[1:2, :] = col_sum(dz768[:, 1536:2304])
        back_t[...] = sum_s[...].astype(narrow).reshape(2, 128, 768)
        begin(swaps[2])
        small_start()

    text_three()
    for group in (get_image, get_co, get_heads, get_self):
        begin(group)

    def turn_body(turn, carry):
        for stage, lag in stages:
            index = turn - lag

            @pl.when((index >= 0) & (index < STEPS))
            def _(stage=stage, index=index):
                stage(index)

        pl.when(turn == 0)(lambda: finish(get_text_in))
        pl.when(turn < 3)(lambda: text_inner(turn))
        pl.when(turn == 3)(image_three)
        pl.when(turn == 4)(text_second)
        pl.when(turn == 5)(image_second)
        pl.when((turn >= 6) & (turn < 10))(lambda: co_heads(turn))

        @pl.when(turn == 10)
        def _():
            text_one_back()
            image_back()

        pl.when(turn == 11)(self_second)
        pl.when((turn >= 12) & (turn < 18))(lambda: self_heads(turn))
        pl.when(turn == SMALL_TURN)(text_back)
        for lag, step in (
            (LAG_NEAR, small_near),
            (LAG_FAR, small_far),
            (LAG_SUM, small_sum),
            (LAG_MID, small_mid),
            (LAG_END, small_end),
            (LAG_WRITE, small_write),
        ):
            pl.when(turn == SMALL_TURN + lag)(step)
        return carry

    lax.fori_loop(0, STEPS + LAG_WRITE, turn_body, 0)

    core_copy(STEPS - 2).wait_send()
    core_copy(STEPS - 1).wait_send()
    sm_core.wait_send()
    for copy in sm_near:
        copy.wait_send()
    sm_far.wait_send()

    def settle(index, carry):
        @pl.when(is_end)
        def _():
            end_write(index).wait()

        @pl.when(is_mid)
        def _():
            mid_copy(index).wait_send()
            back_copy(index).wait_send()
            mid_write(index).wait()

        return carry

    lax.fori_loop(0, STEPS, settle, 0)

    @pl.when(is_end)
    def _():
        sm_end.wait_send()

    @pl.when(is_mid)
    def _():
        sm_mid.wait_send()
        sm_back.wait_send()

    for group in swaps:
        finish(group)


def backward_all(weights, saved, cots):
    dma = pltpu.SemaphoreType.DMA
    shape = jax.ShapeDtypeStruct
    vmem = pltpu.VMEM
    narrow, wide = jnp.bfloat16, jnp.float32
    block = (768, 128)
    tiny = (SMALL_ROWS, 128)
    kept = [getattr(saved, name) for name in SAVED]
    one = [dma((STEPS + 1,))] * 2
    results = pl.pallas_call(
        backward_kernel,
        out_shape=[
            shape((STEPS,) + block, narrow),
            shape(tiny, wide),
            shape((8, 32, 768), narrow),
            shape((8, 32, 1024), narrow),
            shape((8, 32, 768), narrow),
            shape((8, 32, 1024), narrow),
        ],
        in_specs=[ANY] * (len(weights) + len(kept) + 2),
        out_specs=[ANY, VMEM] + [ANY] * 4,
        scratch_shapes=[
            vmem((2, 4) + block, narrow),
            vmem((CHIP_SLOTS, 4) + block, narrow),
            vmem((NEAR_SLOTS, 2) + block, narrow),
            vmem((PLANE_SLOTS,) + block, narrow),
            vmem((STEPS,) + block, narrow),
            vmem((STEPS,) + block, narrow),
            vmem((2, 4) + tiny, wide),
            vmem((4,) + tiny, wide),
            vmem((2,) + tiny, wide),
            vmem(tiny, wide),
            vmem(tiny, wide),
            vmem(tiny, wide),
            vmem((3, 768, 1024), narrow),
            vmem((4, 768, 768), narrow),
            vmem((3, 1024, 1024), narrow),
            vmem((1024, 768), narrow),
            vmem((256, 9216), narrow),
            vmem((256, 6912), narrow),
            vmem((256, 768), narrow),
            vmem((4, 2, 384, 256), narrow),
            vmem((5, 2, 512, 256), narrow),
            vmem((1, 2, 1536, 256), narrow),
            vmem((12, 256, 128), narrow),
            vmem((16, 128, 128), narrow),
            vmem((16, 128, 128), narrow),
            vmem((256, 768), wide),
            vmem((256, 768), wide),
            vmem((256, 1024), wide),
            vmem((256, 768), wide),
            vmem((256, 1024), wide),
            vmem((16, 768), wide),
            vmem((16, 1024), wide),
            vmem((256, 1024), narrow),
            vmem((256, 1024), narrow),
            vmem((2, 128, 768), narrow),
            vmem((2, 128, 1024), narrow),
            vmem((16, 768), wide),
            vmem((16, 1024), wide),
            vmem((8, 3072), wide),
        ]
        + one
        + [dma((STEPS + 1, 2))] * 2
        + one * 4
        + [dma((STEPS,)), dma((4, 3)), dma((4, 3)), dma((4,)), dma((48,))],
        compiler_params=pltpu.CompilerParams(
            collective_id=1, has_side_effects=True, vmem_limit_bytes=62 * 2**20
        ),
        name="backward_all",
    )(*weights, *kept, *cots)
    return (results[0], results[1], results[2:])


UNPACK = (
    ((0, 18, 6), (1, 6, 6), (3, 24, 8), (6, 24, 24)),
    ((2, 24, 8), (4, 6, 6), (5, 8, 8), (8, 8, 8), (9, 8, 8)),
    ((7, 6, 6),),
)


def unpack_kernel(*refs):
    summed, small = refs[:2]
    states = refs[2:6]
    weights = refs[6:16]
    smalls = refs[16 : 16 + SMALL_COUNT]
    targets = refs[16 + SMALL_COUNT :]
    for state, target in zip(states, targets):
        target[...] = state[...]
    places = [{}, {}, {}]
    turn = 0
    for kind, start, count in ORDER:
        for chunk in range(start, start + count):
            places[kind][chunk] = turn
            turn += 1
    for kind in range(3):
        rows = ROWS[kind]
        tile = 0
        for weight, tiles, width in UNPACK[kind]:
            for own_tile in range(tiles):
                at, side = divmod(tile, TILES[kind] * 2)
                values = summed[places[kind][at], side * rows : (side + 1) * rows, :]
                part, column = divmod(own_tile, width)
                weights[weight][part, :, column * 128 : column * 128 + 128] = values.astype(jnp.float32)
                tile += 1
    for (first, rows, width), ref in zip(SMALL_PLACES, smalls):
        ref[...] = small[first : first + rows, :width]


def unpack(summed, small, states):
    shape = jax.ShapeDtypeStruct
    out_shape = [shape((w[0], w[1] // 8, w[2]), jnp.float32) for w in WEIGHT_SHAPES]
    out_shape += [shape((rows, width), jnp.float32) for first, rows, width in SMALL_PLACES]
    out_shape += [shape(s.shape, s.dtype) for s in states]
    results = pl.pallas_call(
        unpack_kernel,
        out_shape=out_shape,
        in_specs=[VMEM] * 6,
        out_specs=[VMEM] * (14 + SMALL_COUNT),
        compiler_params=pltpu.CompilerParams(vmem_limit_bytes=61 * 2**20),
        name="unpack",
    )(summed, small, *states)
    return (results[:10], results[10 : 10 + SMALL_COUNT], results[10 + SMALL_COUNT :])


def local_fast(
    text, image, text_len, region_count, text_cot, image_cot,
    selfproject, selfbiases, selfoutput, textcoproject, textcobiases, imagecoproject, imagecobiases,
    textcooutput, imagecooutput, textffinner, textffinbias, textffouter,
    imageffinner, imageffinbias, imageffouter,
    textgains, textshifts, textbiases, imagegains, imageshifts, imagebiases,
):
    blocks = [
        selfproject.transpose(1, 0, 2), selfoutput[None], imagecoproject.transpose(1, 0, 2),
        textcoproject.transpose(1, 0, 2), textcooutput[None], imagecooutput[None],
        textffinner[None], textffouter[None], imageffinner[None], imageffouter[None],
    ]
    small = [
        selfbiases, textcobiases, imagecobiases, textffinbias.reshape(3, 128), imageffinbias.reshape(1, 128),
        textgains, textshifts, textbiases, imagegains, imageshifts, imagebiases,
    ]
    weights, saved, cots = forward_all(blocks, small, [text, image, text_cot, image_cot], text_len, region_count)
    summed, small_sum, outputs = backward_all(weights, saved, cots)
    g, s, outputs = unpack(summed, small_sum, outputs)
    return tuple(outputs) + (
        g[W_SELF].transpose(1, 0, 2), s[0], g[W_SELFOUT][0], g[W_TEXTCO].transpose(1, 0, 2), s[1],
        g[W_IMAGECO].transpose(1, 0, 2), s[2], g[W_TEXTOUT][0], g[W_IMAGEOUT][0],
        g[W_TIN][0], s[3].reshape(-1), g[W_TOUT][0], g[W_IIN][0], s[4].reshape(-1), g[W_IOUT][0],
        s[5], s[6], s[7], s[8], s[9], s[10],
    )


def solution(mesh):
    in_specs = (
        P("dp", "seq", None),
        P("dp", "seq", None),
        P("dp"),
        P("dp"),
        P("dp", "seq", None),
        P("dp", "seq", None),
        P("dp", None, None),
        P(None, "dp"),
        P("dp", None),
        P("dp", None, None),
        P(None, "dp"),
        P("dp", None, None),
        P(None, "dp"),
        P("dp", None),
        P("dp", None),
        P("dp", None),
        P("dp"),
        P("dp", None),
        P("dp", None),
        P("dp"),
        P("dp", None),
        P(None, "dp"),
        P(None, "dp"),
        P(None, "dp"),
        P(None, "dp"),
        P(None, "dp"),
        P(None, "dp"),
    )
    out_specs = (
        P("dp", "seq", None),
        P("dp", "seq", None),
        P("dp", "seq", None),
        P("dp", "seq", None),
        P("dp", None, None),
        P(None, "dp"),
        P("dp", None),
        P("dp", None, None),
        P(None, "dp"),
        P("dp", None, None),
        P(None, "dp"),
        P("dp", None),
        P("dp", None),
        P("dp", None),
        P("dp"),
        P("dp", None),
        P("dp", None),
        P("dp"),
        P("dp", None),
        P(None, "dp"),
        P(None, "dp"),
        P(None, "dp"),
        P(None, "dp"),
        P(None, "dp"),
        P(None, "dp"),
    )
    sizes = mesh.shape
    local = local_fast if (sizes["dp"], sizes["seq"]) == (8, 4) else local_plain
    return jax.shard_map(local, mesh=mesh, in_specs=in_specs, out_specs=out_specs, check_vma=False)
```

```python
import functools
import types

import jax
import jax.numpy as jnp
from jax import lax
from jax.experimental import pallas as pl
from jax.experimental.pallas import tpu as pltpu
from jax.sharding import PartitionSpec as P

HT = 12
HC = 8
MB = 2


EPSILON = 1e-05
NEG_FILL = -1e30


def layer_norm(hidden, factor, offset):
    centre = hidden - jnp.mean(hidden, axis=-1, keepdims=True)
    spread = jnp.mean(centre * centre, axis=-1, keepdims=True)
    return centre * lax.rsqrt(spread + EPSILON) * factor + offset


def norm_back(hidden, factor, offset, upstream):
    outcome, pullback = jax.vjp(layer_norm, hidden, factor, offset)
    return pullback(upstream)


def gelu_exact(hidden):
    return jax.nn.gelu(hidden, approximate=False)


def gelu_back(hidden, upstream):
    outcome, pullback = jax.vjp(gelu_exact, hidden)
    return pullback(upstream)[0]


def linear(inputs, weight):
    return jnp.einsum("pte,ef->ptf", inputs, weight, preferred_element_type=jnp.float32)


def linear_weight(inputs, gradient):
    return jnp.einsum("pte,ptf->ef", inputs, gradient, preferred_element_type=jnp.float32)


def linear_input(gradient, weight):
    return jnp.einsum("ptf,ef->pte", gradient, weight, preferred_element_type=jnp.float32)


def row_total(gradient):
    return jnp.sum(gradient, axis=(0, 1), dtype=jnp.float32)


def project(inputs, weight, biases):
    bias_rows = biases.astype(jnp.float32)
    stacked = jnp.stack([bias_rows[0], jnp.zeros_like(bias_rows[0]), bias_rows[1]])
    triple = jnp.einsum("pte,ekf->ptkf", inputs, weight, preferred_element_type=jnp.float32)
    return (triple + stacked).astype(jnp.bfloat16)


def project_back(inputs, gradient, weight):
    weight_grad = jnp.einsum("pte,ptkf->ekf", inputs, gradient, preferred_element_type=jnp.float32)
    totals = row_total(gradient)
    input_grad = jnp.einsum("ptkf,ekf->pte", gradient, weight, preferred_element_type=jnp.float32)
    return (weight_grad, jnp.stack([totals[0], totals[2]]), input_grad)


def split_heads(values, head_count):
    return values.reshape(
        values.shape[0], values.shape[1], head_count, values.shape[2] // head_count
    )


def score_table(queries, keyvals, keymask, head_count):
    query_heads = split_heads(queries, head_count)
    key_heads = split_heads(keyvals[:, :, 0], head_count)
    shrink = query_heads.shape[-1] ** (-0.5)
    scores = (
        jnp.einsum("pthd,pshd->phts", query_heads, key_heads, preferred_element_type=jnp.float32)
        * shrink
    )
    scores = jnp.where(keymask[:, None, None, :], scores, NEG_FILL)
    return (scores, query_heads, key_heads, shrink)


def attend(queries, keyvals, keymask, head_count):
    scores, query_heads, key_heads, shrink = score_table(queries, keyvals, keymask, head_count)
    highest = jnp.max(scores, axis=-1, keepdims=True)
    powers = jnp.exp(scores - highest)
    totals = jnp.sum(powers, axis=-1, keepdims=True)
    prob_table = (powers / totals).astype(jnp.bfloat16)
    value_heads = split_heads(keyvals[:, :, 1], head_count)
    mixture = jnp.einsum(
        "phts,pshd->pthd", prob_table, value_heads, preferred_element_type=jnp.float32
    )
    return (mixture.reshape(queries.shape).astype(jnp.bfloat16), highest + jnp.log(totals))


def attend_back(upstream, queries, keyvals, keymask, logsum, head_count):
    scores, query_heads, key_heads, shrink = score_table(queries, keyvals, keymask, head_count)
    prob_table = jnp.exp(scores - logsum)
    value_heads = split_heads(keyvals[:, :, 1], head_count)
    upper_heads = split_heads(upstream, head_count)
    value_grad = jnp.einsum(
        "phts,pthd->pshd",
        prob_table.astype(jnp.bfloat16),
        upper_heads,
        preferred_element_type=jnp.float32,
    )
    prob_grad = jnp.einsum(
        "pthd,pshd->phts", upper_heads, value_heads, preferred_element_type=jnp.float32
    )
    score_grad = prob_table * (prob_grad - jnp.sum(prob_grad * prob_table, axis=-1, keepdims=True))
    score_grad = score_grad.astype(jnp.bfloat16)
    query_grad = (
        jnp.einsum("phts,pshd->pthd", score_grad, key_heads, preferred_element_type=jnp.float32)
        * shrink
    )
    key_grad = (
        jnp.einsum("phts,pthd->pshd", score_grad, query_heads, preferred_element_type=jnp.float32)
        * shrink
    )
    keyval_grad = jnp.stack([key_grad, value_grad], axis=2).reshape(keyvals.shape)
    return (query_grad.reshape(queries.shape), keyval_grad)


def feed_forward(inputs, weight_in, bias_in, weight_out, bias_out):
    inner_sum = linear(inputs, weight_in) + bias_in.astype(jnp.float32)
    active = gelu_exact(inner_sum).astype(jnp.bfloat16)
    totals = inputs.astype(jnp.float32) + linear(active, weight_out) + bias_out
    return (inner_sum, active, totals)


def feed_back(upstream, inputs, inner_sum, active, totals, factor, offset, weight_in, weight_out):
    sum_grad, factor_grad, offset_grad = norm_back(totals, factor, offset, upstream)
    branch_grad = sum_grad.astype(jnp.bfloat16)
    outer_grad = linear_weight(active, branch_grad)
    outbias_grad = row_total(branch_grad)
    active_grad = linear_input(branch_grad, weight_out)
    inner_grad = gelu_back(inner_sum, active_grad).astype(jnp.bfloat16)
    weightin_grad = linear_weight(inputs, inner_grad)
    inbias_grad = row_total(inner_grad)
    input_grad = linear_input(inner_grad, weight_in) + sum_grad
    return (
        input_grad,
        weightin_grad,
        inbias_grad,
        outer_grad,
        outbias_grad,
        factor_grad,
        offset_grad,
    )


def micro_step(
    fetched, text, image, text_len, region_count, text_cot, image_cot, caption_slots, region_slots
):
    (
        selfproject,
        selfbiases,
        selfoutput,
        textcoproject,
        textcobiases,
        imagecoproject,
        imagecobiases,
        textcooutput,
        imagecooutput,
        textffinner,
        textffinbias,
        textffouter,
        imageffinner,
        imageffinbias,
        imageffouter,
        textgains,
        textshifts,
        textbiases,
        imagegains,
        imageshifts,
        imagebiases,
    ) = fetched
    text_factor = textgains.astype(jnp.float32)
    text_offset = textshifts.astype(jnp.float32)
    text_bias = textbiases.astype(jnp.float32)
    image_factor = imagegains.astype(jnp.float32)
    image_offset = imageshifts.astype(jnp.float32)
    image_bias = imagebiases.astype(jnp.float32)
    text_mask = jnp.arange(caption_slots)[None, :] < text_len[:, None]
    region_mask = jnp.arange(region_slots)[None, :] < region_count[:, None]
    self_triple = project(text, selfproject, selfbiases)
    self_keys = lax.all_gather(self_triple[:, :, 1:], "seq", axis=1, tiled=True)
    self_mixed, self_logsum = attend(self_triple[:, :, 0], self_keys, text_mask, HT)
    self_sum = text.astype(jnp.float32) + linear(self_mixed, selfoutput) + text_bias[0]
    text_one = layer_norm(self_sum, text_factor[0], text_offset[0]).astype(jnp.bfloat16)
    text_triple = project(text_one, textcoproject, textcobiases)
    image_triple = project(image, imagecoproject, imagecobiases)
    text_keys, image_keys = (
        lax.all_gather(text_triple[:, :, 1:], "seq", axis=1, tiled=True),
        lax.all_gather(image_triple[:, :, 1:], "seq", axis=1, tiled=True),
    )
    text_mixed, text_logsum = attend(text_triple[:, :, 0], image_keys, region_mask, HC)
    image_mixed, image_logsum = attend(image_triple[:, :, 0], text_keys, text_mask, HC)
    text_sum = text_one.astype(jnp.float32) + linear(text_mixed, textcooutput) + text_bias[1]
    text_two = layer_norm(text_sum, text_factor[1], text_offset[1]).astype(jnp.bfloat16)
    image_sum = image.astype(jnp.float32) + linear(image_mixed, imagecooutput) + image_bias[0]
    image_two = layer_norm(image_sum, image_factor[0], image_offset[0]).astype(jnp.bfloat16)
    text_inner, text_active, text_total = feed_forward(
        text_two, textffinner, textffinbias, textffouter, text_bias[2]
    )
    text_three = layer_norm(text_total, text_factor[2], text_offset[2]).astype(jnp.bfloat16)
    image_inner, image_active, image_total = feed_forward(
        image_two, imageffinner, imageffinbias, imageffouter, image_bias[1]
    )
    image_three = layer_norm(image_total, image_factor[1], image_offset[1]).astype(jnp.bfloat16)
    (
        text_twograd,
        textin_grad,
        textinb_grad,
        textout_grad,
        textoutb_grad,
        factor_tthree,
        offset_tthree,
    ) = feed_back(
        text_cot.astype(jnp.float32),
        text_two,
        text_inner,
        text_active,
        text_total,
        text_factor[2],
        text_offset[2],
        textffinner,
        textffouter,
    )
    (
        image_twograd,
        imagein_grad,
        imageinb_grad,
        imageout_grad,
        imageoutb_grad,
        factor_itwo,
        offset_itwo,
    ) = feed_back(
        image_cot.astype(jnp.float32),
        image_two,
        image_inner,
        image_active,
        image_total,
        image_factor[1],
        image_offset[1],
        imageffinner,
        imageffouter,
    )
    textsum_grad, factor_ttwo, offset_ttwo = norm_back(
        text_sum, text_factor[1], text_offset[1], text_twograd
    )
    textbranch_grad = textsum_grad.astype(jnp.bfloat16)
    textco_outgrad = linear_weight(text_mixed, textbranch_grad)
    textco_biasgrad = row_total(textbranch_grad)
    textmix_grad = linear_input(textbranch_grad, textcooutput).astype(jnp.bfloat16)
    imagesum_grad, factor_ione, offset_ione = norm_back(
        image_sum, image_factor[0], image_offset[0], image_twograd
    )
    imagebranch_grad = imagesum_grad.astype(jnp.bfloat16)
    imageco_outgrad = linear_weight(image_mixed, imagebranch_grad)
    imageco_biasgrad = row_total(imagebranch_grad)
    imagemix_grad = linear_input(imagebranch_grad, imagecooutput).astype(jnp.bfloat16)
    textquery_grad, imagekv_part = attend_back(
        textmix_grad, text_triple[:, :, 0], image_keys, region_mask, text_logsum, HC
    )
    imagequery_grad, textkv_part = attend_back(
        imagemix_grad, image_triple[:, :, 0], text_keys, text_mask, image_logsum, HC
    )
    textkv_grad, imagekv_grad = (
        lax.psum_scatter(
            textkv_part.astype(jnp.bfloat16), "seq", scatter_dimension=1, tiled=True
        ).astype(jnp.float32),
        lax.psum_scatter(
            imagekv_part.astype(jnp.bfloat16), "seq", scatter_dimension=1, tiled=True
        ).astype(jnp.float32),
    )
    texttriple_grad = jnp.concatenate(
        [textquery_grad[:, :, None].astype(jnp.bfloat16), textkv_grad.astype(jnp.bfloat16)], axis=2
    )
    imagetriple_grad = jnp.concatenate(
        [imagequery_grad[:, :, None].astype(jnp.bfloat16), imagekv_grad.astype(jnp.bfloat16)],
        axis=2,
    )
    textco_projgrad, textco_qvgrad, textone_grad = project_back(
        text_one, texttriple_grad, textcoproject
    )
    textone_grad = textone_grad + textsum_grad
    imageco_projgrad, imageco_qvgrad, image_ingrad = project_back(
        image, imagetriple_grad, imagecoproject
    )
    image_ingrad = image_ingrad + imagesum_grad
    selfsum_grad, factor_tone, offset_tone = norm_back(
        self_sum, text_factor[0], text_offset[0], textone_grad
    )
    selfbranch_grad = selfsum_grad.astype(jnp.bfloat16)
    selfout_grad = linear_weight(self_mixed, selfbranch_grad)
    selfbias_grad = row_total(selfbranch_grad)
    selfmix_grad = linear_input(selfbranch_grad, selfoutput).astype(jnp.bfloat16)
    selfquery_grad, selfkv_part = attend_back(
        selfmix_grad, self_triple[:, :, 0], self_keys, text_mask, self_logsum, HT
    )
    selfkv_grad = lax.psum_scatter(
        selfkv_part.astype(jnp.bfloat16), "seq", scatter_dimension=1, tiled=True
    )
    selftriple_grad = jnp.concatenate(
        [selfquery_grad[:, :, None].astype(jnp.bfloat16), selfkv_grad], axis=2
    )
    selfproj_grad, selfqv_grad, text_ingrad = project_back(text, selftriple_grad, selfproject)
    text_ingrad = text_ingrad + selfsum_grad
    gradients = (
        selfproj_grad,
        selfqv_grad,
        selfout_grad,
        textco_projgrad,
        textco_qvgrad,
        imageco_projgrad,
        imageco_qvgrad,
        textco_outgrad,
        imageco_outgrad,
        textin_grad,
        textinb_grad,
        textout_grad,
        imagein_grad,
        imageinb_grad,
        imageout_grad,
        jnp.stack([factor_tone, factor_ttwo, factor_tthree]),
        jnp.stack([offset_tone, offset_ttwo, offset_tthree]),
        jnp.stack([selfbias_grad, textco_biasgrad, textoutb_grad]),
        jnp.stack([factor_ione, factor_itwo]),
        jnp.stack([offset_ione, offset_itwo]),
        jnp.stack([imageco_biasgrad, imageoutb_grad]),
    )
    outputs = (
        text_three,
        image_three,
        text_ingrad.astype(jnp.bfloat16),
        image_ingrad.astype(jnp.bfloat16),
    )
    return (outputs, gradients)


def local_plain(
    text,
    image,
    text_len,
    region_count,
    text_cot,
    image_cot,
    selfproject,
    selfbiases,
    selfoutput,
    textcoproject,
    textcobiases,
    imagecoproject,
    imagecobiases,
    textcooutput,
    imagecooutput,
    textffinner,
    textffinbias,
    textffouter,
    imageffinner,
    imageffinbias,
    imageffouter,
    textgains,
    textshifts,
    textbiases,
    imagegains,
    imageshifts,
    imagebiases,
):
    seq_count = lax.axis_size("seq")
    micro_pairs = text.shape[0] // MB
    shards = (
        selfproject,
        selfbiases,
        selfoutput,
        textcoproject,
        textcobiases,
        imagecoproject,
        imagecobiases,
        textcooutput,
        imagecooutput,
        textffinner,
        textffinbias,
        textffouter,
        imageffinner,
        imageffinbias,
        imageffouter,
        textgains,
        textshifts,
        textbiases,
        imagegains,
        imageshifts,
        imagebiases,
    )
    accumulated = None
    text_rows = []
    image_rows = []
    textgrad_rows = []
    imagegrad_rows = []
    for micro_index in range(MB):
        fetched = (
            lax.all_gather(shards[0], "dp", axis=0, tiled=True),
            lax.all_gather(shards[1], "dp", axis=1, tiled=True),
            lax.all_gather(shards[2], "dp", axis=0, tiled=True),
            lax.all_gather(shards[3], "dp", axis=0, tiled=True),
            lax.all_gather(shards[4], "dp", axis=1, tiled=True),
            lax.all_gather(shards[5], "dp", axis=0, tiled=True),
            lax.all_gather(shards[6], "dp", axis=1, tiled=True),
            lax.all_gather(shards[7], "dp", axis=0, tiled=True),
            lax.all_gather(shards[8], "dp", axis=0, tiled=True),
            lax.all_gather(shards[9], "dp", axis=0, tiled=True),
            lax.all_gather(shards[10], "dp", axis=0, tiled=True),
            lax.all_gather(shards[11], "dp", axis=0, tiled=True),
            lax.all_gather(shards[12], "dp", axis=0, tiled=True),
            lax.all_gather(shards[13], "dp", axis=0, tiled=True),
            lax.all_gather(shards[14], "dp", axis=0, tiled=True),
            lax.all_gather(shards[15], "dp", axis=1, tiled=True),
            lax.all_gather(shards[16], "dp", axis=1, tiled=True),
            lax.all_gather(shards[17], "dp", axis=1, tiled=True),
            lax.all_gather(shards[18], "dp", axis=1, tiled=True),
            lax.all_gather(shards[19], "dp", axis=1, tiled=True),
            lax.all_gather(shards[20], "dp", axis=1, tiled=True),
        )
        begin_row = micro_index * micro_pairs
        end_row = begin_row + micro_pairs
        outputs, gradients = micro_step(
            fetched,
            text[begin_row:end_row],
            image[begin_row:end_row],
            text_len[begin_row:end_row],
            region_count[begin_row:end_row],
            text_cot[begin_row:end_row],
            image_cot[begin_row:end_row],
            text.shape[1] * seq_count,
            image.shape[1] * seq_count,
        )
        text_rows.append(outputs[0])
        image_rows.append(outputs[1])
        textgrad_rows.append(outputs[2])
        imagegrad_rows.append(outputs[3])
        pieces = (
            lax.psum_scatter(gradients[0], "dp", scatter_dimension=0, tiled=True),
            lax.psum_scatter(gradients[1], "dp", scatter_dimension=1, tiled=True),
            lax.psum_scatter(gradients[2], "dp", scatter_dimension=0, tiled=True),
            lax.psum_scatter(gradients[3], "dp", scatter_dimension=0, tiled=True),
            lax.psum_scatter(gradients[4], "dp", scatter_dimension=1, tiled=True),
            lax.psum_scatter(gradients[5], "dp", scatter_dimension=0, tiled=True),
            lax.psum_scatter(gradients[6], "dp", scatter_dimension=1, tiled=True),
            lax.psum_scatter(gradients[7], "dp", scatter_dimension=0, tiled=True),
            lax.psum_scatter(gradients[8], "dp", scatter_dimension=0, tiled=True),
            lax.psum_scatter(gradients[9], "dp", scatter_dimension=0, tiled=True),
            lax.psum_scatter(gradients[10], "dp", scatter_dimension=0, tiled=True),
            lax.psum_scatter(gradients[11], "dp", scatter_dimension=0, tiled=True),
            lax.psum_scatter(gradients[12], "dp", scatter_dimension=0, tiled=True),
            lax.psum_scatter(gradients[13], "dp", scatter_dimension=0, tiled=True),
            lax.psum_scatter(gradients[14], "dp", scatter_dimension=0, tiled=True),
            lax.psum_scatter(gradients[15], "dp", scatter_dimension=1, tiled=True),
            lax.psum_scatter(gradients[16], "dp", scatter_dimension=1, tiled=True),
            lax.psum_scatter(gradients[17], "dp", scatter_dimension=1, tiled=True),
            lax.psum_scatter(gradients[18], "dp", scatter_dimension=1, tiled=True),
            lax.psum_scatter(gradients[19], "dp", scatter_dimension=1, tiled=True),
            lax.psum_scatter(gradients[20], "dp", scatter_dimension=1, tiled=True),
        )
        accumulated = pieces if accumulated is None else jax.tree.map(jnp.add, accumulated, pieces)
    summed = (
        lax.psum(accumulated[0].astype(jnp.bfloat16), "seq").astype(jnp.float32),
        lax.psum(accumulated[1].astype(jnp.bfloat16), "seq").astype(jnp.float32),
        lax.psum(accumulated[2].astype(jnp.bfloat16), "seq").astype(jnp.float32),
        lax.psum(accumulated[3].astype(jnp.bfloat16), "seq").astype(jnp.float32),
        lax.psum(accumulated[4].astype(jnp.bfloat16), "seq").astype(jnp.float32),
        lax.psum(accumulated[5].astype(jnp.bfloat16), "seq").astype(jnp.float32),
        lax.psum(accumulated[6].astype(jnp.bfloat16), "seq").astype(jnp.float32),
        lax.psum(accumulated[7].astype(jnp.bfloat16), "seq").astype(jnp.float32),
        lax.psum(accumulated[8].astype(jnp.bfloat16), "seq").astype(jnp.float32),
        lax.psum(accumulated[9].astype(jnp.bfloat16), "seq").astype(jnp.float32),
        lax.psum(accumulated[10].astype(jnp.bfloat16), "seq").astype(jnp.float32),
        lax.psum(accumulated[11].astype(jnp.bfloat16), "seq").astype(jnp.float32),
        lax.psum(accumulated[12].astype(jnp.bfloat16), "seq").astype(jnp.float32),
        lax.psum(accumulated[13].astype(jnp.bfloat16), "seq").astype(jnp.float32),
        lax.psum(accumulated[14].astype(jnp.bfloat16), "seq").astype(jnp.float32),
        lax.psum(accumulated[15].astype(jnp.bfloat16), "seq").astype(jnp.float32),
        lax.psum(accumulated[16].astype(jnp.bfloat16), "seq").astype(jnp.float32),
        lax.psum(accumulated[17].astype(jnp.bfloat16), "seq").astype(jnp.float32),
        lax.psum(accumulated[18].astype(jnp.bfloat16), "seq").astype(jnp.float32),
        lax.psum(accumulated[19].astype(jnp.bfloat16), "seq").astype(jnp.float32),
        lax.psum(accumulated[20].astype(jnp.bfloat16), "seq").astype(jnp.float32),
    )
    text_out = jnp.concatenate(text_rows, axis=0)
    image_out = jnp.concatenate(image_rows, axis=0)
    text_grad = jnp.concatenate(textgrad_rows, axis=0)
    image_grad = jnp.concatenate(imagegrad_rows, axis=0)
    return (text_out, image_out, text_grad, image_grad) + tuple(summed)


MESH = pl.DeviceIdType.MESH
ANY = pl.BlockSpec(memory_space=pl.ANY)
VMEM = pl.BlockSpec(memory_space=pltpu.VMEM)


def place():
    dp = lax.axis_index("dp")
    z = lax.axis_index("seq")
    row = dp // 4
    col = (dp // 2) % 2
    core = dp % 2
    return (dp, z, row, col, core)


def partners(row, col, core, first_row):
    near_row = row + first_row * (1 - 2 * row)
    near_col = col + (1 - first_row) * (1 - 2 * col)
    far_row = row + (1 - first_row) * (1 - 2 * row)
    far_col = col + first_row * (1 - 2 * col)
    near = near_row * 4 + near_col * 2 + core
    far = far_row * 4 + far_col * 2 + core
    return (near, far)


def greet(devices):
    barrier = pltpu.get_barrier_semaphore()
    for device in devices:
        pl.semaphore_signal(barrier, inc=1, device_id=device, device_id_type=MESH)
    pl.semaphore_wait(barrier, len(devices))


def remote(source, target, send_sem, recv_sem, device):
    return pltpu.make_async_remote_copy(
        src_ref=source,
        dst_ref=target,
        send_sem=send_sem,
        recv_sem=recv_sem,
        device_id=device,
        device_id_type=MESH,
    )


SMALL_PLACES = (
    (0, 2, 96),
    (16, 2, 128),
    (18, 2, 128),
    (27, 3, 128),
    (20, 1, 128),
    (2, 3, 96),
    (5, 3, 96),
    (8, 3, 96),
    (21, 2, 128),
    (23, 2, 128),
    (25, 2, 128),
)
SMALL_COUNT = len(SMALL_PLACES)
SMALL_ROWS = 32
ROOT_HALF = 0.7071067811865476
ROOT_TURN = 0.3989422804014327
WEIGHT_SHAPES = (
    (3, 768, 768), (1, 768, 768), (3, 1024, 1024), (3, 768, 1024), (1, 1024, 768),
    (1, 1024, 1024), (1, 768, 3072), (1, 3072, 768), (1, 1024, 1024), (1, 1024, 1024),
)
W_SELF, W_SELFOUT, W_IMAGECO, W_TEXTCO, W_TEXTOUT, W_IMAGEOUT, W_TIN, W_TOUT, W_IIN, W_IOUT, W_SMALL = range(11)
PIECES = (
    (W_SMALL, 0, 0, 32, 0, 128, 2),
    *((W_SELF, k, 0, 96, 0, 768, 2) for k in range(3)),
    (W_SELFOUT, 0, 0, 96, 0, 768, 0),
    *((W_IMAGECO, k, 0, 128, 0, 1024, (0, 1, 2)[k]) for k in range(3)),
    *((W_TEXTCO, k, 0, 96, 0, 1024, (0, 1, 2)[k]) for k in range(3)),
    (W_TEXTOUT, 0, 0, 128, 0, 768, 0),
    (W_IMAGEOUT, 0, 0, 128, 0, 1024, 1),
    (W_TIN, 0, 0, 96, 0, 1152, 0),
    (W_TIN, 0, 0, 96, 1152, 1152, 1),
    (W_TIN, 0, 0, 96, 2304, 768, 2),
    *((W_TOUT, 0, k * 128, 128, 0, 768, 2) for k in range(3)),
    (W_IIN, 0, 0, 128, 0, 1024, 2),
    (W_IOUT, 0, 0, 128, 0, 1024, 2),
)
LAG_ACROSS = 5
AHEAD = 3
SAVED = dict(
    qkv_s=((3, 256, 768), jnp.bfloat16),
    qkv_t=((3, 256, 1024), jnp.bfloat16),
    qkv_i=((3, 256, 1024), jnp.bfloat16),
    tab_s=((12, 256, 128), jnp.bfloat16),
    tab_t=((16, 128, 128), jnp.bfloat16),
    tab_i=((16, 128, 128), jnp.bfloat16),
    sum_s=((256, 768), jnp.float32),
    sum_t=((256, 768), jnp.float32),
    sum_i=((256, 1024), jnp.float32),
    tot_t=((256, 768), jnp.float32),
    tot_i=((256, 1024), jnp.float32),
    slope_t=((256, 3072), jnp.bfloat16),
    slope_i=((256, 1024), jnp.bfloat16),
    xt768=((4, 2, 384, 256), jnp.bfloat16),
    xt1024=((5, 2, 512, 256), jnp.bfloat16),
    xt3072=((1, 2, 1536, 256), jnp.bfloat16),
    out_t=((256, 768), jnp.bfloat16),
    out_i=((256, 1024), jnp.bfloat16),
    vec96=((16, 768), jnp.float32),
    vec128=((16, 1024), jnp.float32),
)
WORK = dict(
    text=((2, 128, 768), jnp.bfloat16),
    image=((2, 128, 1024), jnp.bfloat16),
    mix_s=((256, 768), jnp.bfloat16),
    one=((256, 768), jnp.bfloat16),
    mix_t=((256, 1024), jnp.bfloat16),
    mix_i=((256, 1024), jnp.bfloat16),
    two_t=((256, 768), jnp.bfloat16),
    two_i=((256, 1024), jnp.bfloat16),
    active=((256, 3072), jnp.bfloat16),
    bias_in=((8, 3072), jnp.float32),
    pack=((SMALL_ROWS, 128), jnp.float32),
)


def mm(left, right):
    return jnp.dot(left, right, preferred_element_type=jnp.float32)


def mm_t(left, right):
    return lax.dot_general(left, right, (((1,), (1,)), ((), ())), preferred_element_type=jnp.float32)


def mm_0(left, right):
    return lax.dot_general(left, right, (((0,), (0,)), ((), ())), preferred_element_type=jnp.float32)


def lanes(index, width):
    return pl.ds(pl.multiple_of(index * width, width), width)


def head_masks():
    spot = lax.broadcasted_iota(jnp.int32, (1, 128), 1)
    low = jnp.where(spot < 64, 1.0, 0.0)
    return (low, 1.0 - low)


def key_mask(length):
    return lax.broadcasted_iota(jnp.int32, (1, 128), 1) < length


def table_of(scores, keep, shrink):
    scores = jnp.where(keep, scores * shrink, NEG_FILL)
    powers = jnp.exp(scores - jnp.max(scores, axis=-1, keepdims=True))
    return (powers / jnp.sum(powers, axis=-1, keepdims=True)).astype(jnp.bfloat16)


def forward_kernel(*refs):
    refs = list(refs)

    def take(count):
        taken = refs[:count]
        del refs[:count]
        return taken

    narrow, wide = jnp.bfloat16, jnp.float32
    weight_count = len(WEIGHT_SHAPES)
    array_count = weight_count + 1
    blocks = take(weight_count)
    small_in = take(SMALL_COUNT)
    states = take(4)
    text_len, region_count = take(2)
    whole_out = take(weight_count)
    saved_out = take(len(SAVED))
    cots = take(2)
    wholes = take(array_count)
    saved_refs = take(len(SAVED))
    saved = types.SimpleNamespace(**dict(zip(SAVED, saved_refs)))
    work = types.SimpleNamespace(**dict(zip(WORK, take(len(WORK)))))
    send_sem, recv_sem, swap_send, swap_recv, own_sem, out_sem, save_sem = refs
    dp, z, row, col, core = place()
    near, far = partners(row, col, core, 1 - core)
    sibling = dp + 1 - 2 * core
    diagonal = (1 - row) * 4 + (1 - col) * 2 + core
    others = [lax.rem(z + step, 4) for step in (1, 2, 3)]

    pack = work.pack
    pack[...] = jnp.zeros((SMALL_ROWS, 128), wide)
    for (first, rows, width), ref in zip(SMALL_PLACES, small_in):
        pack[first : first + rows, :width] = ref[...].astype(wide)

    greet([(near, z), (far, z), (sibling, z)] + [(dp, other) for other in others])

    def window(piece, index):
        array, k, row0, rows, col0, cols, planes = PIECES[piece]
        depth = wholes[array].shape[1] // 8
        first = pl.multiple_of(index * depth + row0, 16)
        return wholes[array].at[k, pl.ds(first, rows), pl.ds(col0, cols)]

    def own(piece):
        array, k, row0, rows, col0, cols, planes = PIECES[piece]
        if array == W_SMALL:
            return pack
        return blocks[array].at[k, pl.ds(row0, rows), pl.ds(col0, cols)]

    partner = z + 1 - 2 * lax.rem(z, 2)
    always, fetching = [], {0: [], 1: []}

    def copy_of(piece, send_lane, recv_lane, source, index, device):
        copy = remote(
            source, window(piece, index), send_sem.at[piece, send_lane], recv_sem.at[piece, recv_lane], device
        )
        return copy

    def siblings(piece, lane, source, index):
        copy = copy_of(piece, lane, lane, source, index, (sibling, z))
        always.append(copy)
        return copy

    def by_plane(piece, fetch, other=None):
        planes = PIECES[piece][6]
        if planes == 2:
            if fetch:
                fetch()
            return
        if fetch:
            pl.when(lax.rem(z, 2) == planes)(fetch)
        if other:
            pl.when(lax.rem(z, 2) != planes)(other)

    def begin(copies):
        for copy in copies:
            copy.start()

    def noted(piece, *moves):
        copies = [copy_of(piece, *move) for move in moves]
        planes = PIECES[piece][6]
        (always if planes == 2 else fetching[planes]).extend(copies)
        return copies

    def across(piece, lane, index):
        if PIECES[piece][6] == 2:
            return []
        return noted(piece, (lane + 7, lane, window(piece, index), index, (dp, partner)))

    def arrived(piece, lane, index):
        copy_of(piece, lane, lane, window(piece, index), index, (sibling, z)).wait_recv()

    def start(piece):
        block = own(piece)
        copies = noted(piece, (0, 0, block, dp, (near, z)), (1, 1, block, dp, (far, z)))
        by_plane(piece, lambda: begin(copies))
        siblings(piece, 2, block, dp).start()

    onward = {}

    def relay(piece):
        block, block_far = window(piece, near), window(piece, far)
        first = noted(piece, (3, 3, block, near, (far, z))) + across(piece, 0, near)
        second = across(piece, 1, far)
        onward[piece] = (
            siblings(piece, 4, block, near),
            siblings(piece, 5, block_far, far),
            siblings(piece, 6, window(piece, diagonal), diagonal),
        )

        def go():
            arrived(piece, 0, near)
            begin(first)
            onward[piece][0].start()
            arrived(piece, 1, far)
            begin(second)
            onward[piece][1].start()

        by_plane(piece, go)

    def pass_on(piece):
        third = across(piece, 3, diagonal)

        def go():
            arrived(piece, 3, diagonal)
            begin(third)
            onward[piece][2].start()

        by_plane(piece, go)

    def receive(piece):
        def go():
            arrived(piece, 0, near)
            onward[piece][0].start()
            arrived(piece, 1, far)
            onward[piece][1].start()

        by_plane(piece, None, go)

    def receive_last(piece):
        def go():
            arrived(piece, 3, diagonal)
            onward[piece][2].start()

        by_plane(piece, None, go)

    outs, kept, met = [], {}, []

    def ready(piece):
        array = PIECES[piece][0]
        for lane in (2, 4, 5, 6):
            arrived(piece, lane, near)
        if array not in met:
            kept[array].wait()
        met.append(array)
        if array < weight_count and met.count(array) == sum(p[0] == array for p in PIECES):
            copy = pltpu.make_async_copy(wholes[array], whole_out[array], out_sem.at[array])
            copy.start()
            outs.append(copy)

    progress = [0, 0]

    def lag_of(piece):
        return 2 if PIECES[piece][6] == 2 else LAG_ACROSS

    def tick():
        turn = progress[1]
        if turn >= len(PIECES) + LAG_ACROSS:
            return
        if turn < len(PIECES):
            relay(turn)
        while progress[0] < min(turn + AHEAD, len(PIECES)):
            start(progress[0])
            progress[0] += 1
        for step, lag in ((pass_on, 1), (receive, LAG_ACROSS - 2), (receive_last, LAG_ACROSS - 1)):
            if 0 <= turn - lag < len(PIECES):
                step(turn - lag)
        for piece in (turn - LAG_ACROSS, turn - 2):
            if 0 <= piece < len(PIECES) and lag_of(piece) == turn - piece:
                ready(piece)
        progress[1] += 1

    def need(array, count=3):
        places = [i for i, piece in enumerate(PIECES) if piece[0] == array][:count]
        last = max(i + lag_of(i) for i in places)
        while progress[1] <= last:
            tick()

    def save(ref):
        spot = [ref is other for other in saved_refs].index(True)
        copy = pltpu.make_async_copy(ref, saved_out[spot], save_sem.at[spot])
        copy.start()
        outs.append(copy)

    swaps = []

    def swap(array, target):
        source = states[array]
        count = source.shape[0] // 4
        slots = source.shape[1]
        here = target.at[:, pl.ds(pl.multiple_of(z * slots, 16), slots), :]
        made = []
        for step, other in enumerate(others):
            copy = remote(
                source.at[pl.ds(other * count, count)],
                here,
                swap_send.at[array, step],
                swap_recv.at[array, step],
                (dp, other),
            )
            copy.start()
            made.append(copy)
        keep = pltpu.make_async_copy(source.at[pl.ds(z * count, count)], here, own_sem.at[array_count + array])
        keep.start()
        made.append(keep)
        return made

    for array in range(array_count):
        depth = wholes[array].shape[1] // 8
        mine = pl.ds(pl.multiple_of(dp * depth, 16), depth)
        if array == W_SMALL:
            keep = pltpu.make_async_copy(pack, wholes[array].at[0, mine], own_sem.at[array])
        else:
            keep = pltpu.make_async_copy(blocks[array], wholes[array].at[:, mine], own_sem.at[array])
        kept[array] = keep
    text_in = swap(0, work.text)
    for piece in range(2):
        start(piece)
    image_in = swap(1, work.image)
    progress[0] = 2
    while progress[0] < AHEAD:
        start(progress[0])
        progress[0] += 1
    for keep in kept.values():
        keep.start()

    vec96, vec128, bias_in = saved.vec96, saved.vec128, work.bias_in

    def flip(values, width, target, which, first_block):
        turned = values.T
        for block in range(values.shape[1] // width):
            owner = first_block + block
            target[which, owner % 2, owner // 2 * width : (owner // 2 + 1) * width, :] = turned[
                block * width : (block + 1) * width
            ]

    def norm_rows(source, gain, shift, targets):
        def body(step, carry):
            window = pl.ds(pl.multiple_of(step * 32, 32), 32)
            hidden = source[window, :]
            centre = hidden - jnp.mean(hidden, axis=-1, keepdims=True)
            spread = jnp.mean(centre * centre, axis=-1, keepdims=True)
            result = centre * lax.rsqrt(spread + EPSILON) * gain + shift
            targets[window, :] = result.astype(narrow)
            return carry

        lax.fori_loop(0, 8, body, 0)

    def project_all(inputs, array, target, biases):
        width = target.shape[2]
        for k in range(3):
            need(array, k + 1)

            def body(tile, carry, k=k):
                where = lanes(tile, 256)
                part = mm(inputs, wholes[array][k, :, where])
                if k == 0:
                    part = part + biases[0][:, where]
                if k == 2:
                    part = part + biases[1][:, where]
                target[k, :, where] = part.astype(narrow)
                return carry

            lax.fori_loop(0, width // 256, body, 0)

    def branch(inputs, array, base, bias, target):
        width = target.shape[1]

        def body(tile, carry):
            where = lanes(tile, 256)
            part = mm(inputs, wholes[array][0, :, where])
            target[:, where] = part + base[..., where].reshape(256, 256).astype(wide) + bias[:, where]
            return carry

        lax.fori_loop(0, width // 256, body, 0)

    class Row:
        def __init__(self, ref, index):
            self.ref, self.index = ref, index

        def __getitem__(self, key):
            return self.ref[self.index : self.index + 1, key[1]]

    need(W_SMALL)
    packed = wholes[W_SMALL]
    for owner in range(8):
        base = owner * SMALL_ROWS
        vec96[:, owner * 96 : owner * 96 + 96] = packed[0, base : base + 16, :96]
        vec128[:, owner * 128 : owner * 128 + 128] = packed[0, base + 16 : base + 32, :]
        for part in range(3):
            at = owner * 384 + part * 128
            bias_in[0:1, at : at + 128] = packed[0, base + 27 + part : base + 28 + part, :]
    save(saved.vec96)
    save(saved.vec128)
    text_lengths = [text_len[z * 2 + pair] for pair in range(2)]
    region_counts = [region_count[z * 2 + pair] for pair in range(2)]
    low, high = head_masks()
    low_narrow, high_narrow = low.astype(narrow), high.astype(narrow)

    for copy in text_in:
        copy.wait()
    text = work.text[...].reshape(256, 768)
    qkv_s = saved.qkv_s
    project_all(text, W_SELF, qkv_s, (Row(vec96, 0), Row(vec96, 1)))
    save(saved.qkv_s)

    def self_heads(tile, carry):
        where = lanes(tile, 128)
        for pair in range(2):
            rows = slice(pair * 128, pair * 128 + 128)
            q2, k2, v2 = (qkv_s[k, rows, where] for k in range(3))
            both = jnp.concatenate([q2 * low_narrow, q2 * high_narrow], axis=0)
            table = table_of(mm_t(both, k2), key_mask(text_lengths[pair]), 0.125)
            saved.tab_s[pair * 6 + tile] = table
            mixed = mm(table, v2)
            work.mix_s[rows, where] = (mixed[:128] * low + mixed[128:] * high).astype(narrow)
        return carry

    tick()
    lax.fori_loop(0, 3, self_heads, 0)
    tick()
    lax.fori_loop(3, 6, self_heads, 0)
    tick()
    save(saved.tab_s)
    flip(text, 96, saved.xt768, 0, 0)
    flip(work.mix_s[...], 96, saved.xt768, 1, 0)
    need(W_SELFOUT)
    branch(work.mix_s[...], W_SELFOUT, work.text, Row(vec96, 8), saved.sum_s)
    norm_rows(saved.sum_s, vec96[2:3], vec96[5:6], work.one)
    save(saved.sum_s)
    flip(work.one[...], 96, saved.xt768, 2, 0)

    for copy in image_in:
        copy.wait()
    image = work.image[...].reshape(256, 1024)
    qkv_i, qkv_t = saved.qkv_i, saved.qkv_t
    project_all(image, W_IMAGECO, qkv_i, (Row(vec128, 2), Row(vec128, 3)))
    save(saved.qkv_i)
    flip(image, 128, saved.xt1024, 0, 0)
    project_all(work.one[...], W_TEXTCO, qkv_t, (Row(vec128, 0), Row(vec128, 1)))
    save(saved.qkv_t)

    def co_heads(head, carry):
        where = lanes(head, 128)
        shrink = 128**-0.5
        for pair in range(2):
            rows = slice(pair * 128, pair * 128 + 128)
            tq, tk, tv = (qkv_t[k, rows, where] for k in range(3))
            iq, ik, iv = (qkv_i[k, rows, where] for k in range(3))
            table = table_of(mm_t(tq, ik), key_mask(region_counts[pair]), shrink)
            saved.tab_t[pair * 8 + head] = table
            work.mix_t[rows, where] = mm(table, iv).astype(narrow)
            table = table_of(mm_t(iq, tk), key_mask(text_lengths[pair]), shrink)
            saved.tab_i[pair * 8 + head] = table
            work.mix_i[rows, where] = mm(table, tv).astype(narrow)
        return carry

    for head in (0, 2, 4, 6):
        tick()
        lax.fori_loop(head, head + 2, co_heads, 0)
    save(saved.tab_t)
    save(saved.tab_i)
    flip(work.mix_t[...], 128, saved.xt1024, 1, 0)
    flip(work.mix_i[...], 128, saved.xt1024, 2, 0)
    need(W_TEXTOUT)
    branch(work.mix_t[...], W_TEXTOUT, work.one, Row(vec96, 9), saved.sum_t)
    norm_rows(saved.sum_t, vec96[3:4], vec96[6:7], work.two_t)
    save(saved.sum_t)
    flip(work.two_t[...], 96, saved.xt768, 3, 0)
    save(saved.xt768)
    need(W_IMAGEOUT)
    branch(work.mix_i[...], W_IMAGEOUT, work.image, Row(vec128, 9), saved.sum_i)
    norm_rows(saved.sum_i, vec128[5:6], vec128[7:8], work.two_i)
    save(saved.sum_i)
    flip(work.two_i[...], 128, saved.xt1024, 3, 0)

    def activate(inner):
        share = 0.5 + 0.5 * lax.erf(inner * ROOT_HALF)
        slope = share + inner * (ROOT_TURN * jnp.exp(-0.5 * inner * inner))
        return ((inner * share).astype(narrow), slope.astype(narrow))

    two_t = work.two_t
    tot_t = saved.tot_t

    def text_inner(owner, carry):
        where = lanes(owner, 384)
        inner = mm(two_t[...], wholes[W_TIN][0, :, where]) + bias_in[0:1, where]
        active, slope = activate(inner)
        saved.slope_t[:, where] = slope
        work.active[:, where] = active
        place_ = pl.ds(pl.multiple_of(lax.div(owner, 2) * 384, 384), 384)
        saved.xt3072[0, lax.rem(owner, 2), place_, :] = active.T
        return carry

    for part in range(3):
        need(W_TIN, part + 1)
        if part == 1:
            swaps += swap(2, cots[0]) + swap(3, cots[1])
        lax.fori_loop(part * 3, min(part * 3 + 3, 8), text_inner, 0)
        tick()
    save(saved.slope_t)
    save(saved.xt3072)
    need(W_TOUT)
    branch(work.active[...], W_TOUT, two_t, Row(vec96, 10), tot_t)
    save(saved.tot_t)
    norm_rows(tot_t, vec96[4:5], vec96[7:8], saved.out_t)
    save(saved.out_t)

    need(W_IIN)
    two_i = work.two_i
    tot_i = saved.tot_i
    for part in range(4):
        where = slice(part * 256, part * 256 + 256)
        inner = mm(two_i[...], wholes[W_IIN][0, :, where]) + vec128[4:5, where]
        active, slope = activate(inner)
        saved.slope_i[:, where] = slope
        flip(active, 128, saved.xt1024, 4, part * 2)
        work.mix_i[:, where] = active
    save(saved.slope_i)
    save(saved.xt1024)
    need(W_IOUT)
    branch(work.mix_i[...], W_IOUT, two_i, Row(vec128, 10), tot_i)
    save(saved.tot_i)
    norm_rows(tot_i, vec128[6:7], vec128[8:9], saved.out_i)
    save(saved.out_i)

    for copy in always:
        copy.wait_send()
    for planes in (0, 1):

        @pl.when(lax.rem(z, 2) == planes)
        def _(planes=planes):
            for copy in fetching[planes]:
                copy.wait_send()

    for copy in swaps:
        copy.wait()
    for copy in outs:
        copy.wait()


def forward_all(blocks, small, states, text_len, region_count):
    dma = pltpu.SemaphoreType.DMA
    narrow = jnp.bfloat16
    count = len(WEIGHT_SHAPES)
    shape = jax.ShapeDtypeStruct
    out_shape = [shape(w, narrow) for w in WEIGHT_SHAPES]
    out_shape += [shape(dims, kind) for dims, kind in SAVED.values()]
    out_shape += [shape((s.shape[0] // 4, s.shape[1] * 4, s.shape[2]), s.dtype) for s in states[2:]]
    scratch = [pltpu.VMEM(w, narrow) for w in WEIGHT_SHAPES]
    scratch += [pltpu.VMEM((1, 8 * SMALL_ROWS, 128), jnp.float32)]
    scratch += [pltpu.VMEM(dims, kind) for dims, kind in (*SAVED.values(), *WORK.values())]
    scratch += [
        dma((len(PIECES), 11)),
        dma((len(PIECES), 7)),
        dma((4, 3)),
        dma((4, 3)),
        dma((count + 5,)),
        dma((count,)),
        dma((len(SAVED),)),
    ]
    results = pl.pallas_call(
        forward_kernel,
        out_shape=out_shape,
        in_specs=[ANY] * count
        + [VMEM] * SMALL_COUNT
        + [ANY] * 4
        + [pl.BlockSpec(memory_space=pltpu.SMEM)] * 2,
        out_specs=[ANY] * len(out_shape),
        scratch_shapes=scratch,
        compiler_params=pltpu.CompilerParams(
            collective_id=0, has_side_effects=True, vmem_limit_bytes=62 * 2**20
        ),
        name="forward_all",
    )(*blocks, *small, *states, text_len, region_count)
    wholes = results[:count]
    saved = types.SimpleNamespace(**dict(zip(SAVED, results[count : count + len(SAVED)])))
    return (wholes, saved, results[count + len(SAVED) :])


CHUNKS = (9, 9, 3)
TILES = (4, 3, 1)
ROWS = (96, 128, 384)
STARTS = ((9, 12, 24), (12, 15, 19, 23), ())
ORDER = ((2, 0, 3), (0, 6, 3), (1, 4, 5), (0, 3, 3), (1, 0, 4), (0, 0, 3))
STEPS = 21
LAG_NEAR, LAG_FAR, LAG_SUM, LAG_MID, LAG_END, LAG_WRITE = 1, 5, 6, 7, 8, 9
SMALL_TURN = 18
CHIP_SLOTS, NEAR_SLOTS, PLANE_SLOTS = 8, 11, 9
AT_BSELF, AT_TEXTCO, AT_TIN = 2304, 3072, 6144
AT_BTEXT, AT_BIMAGE, AT_IIN, AT_BIFF = 3072, 3840, 4864, 5888


def backward_kernel(*refs):
    refs = list(refs)

    def take(count):
        taken = refs[:count]
        del refs[:count]
        return taken

    narrow, wide = jnp.bfloat16, jnp.float32
    weights = take(len(WEIGHT_SHAPES))
    saved = types.SimpleNamespace(**dict(zip(SAVED, take(len(SAVED)))))
    cot_t, cot_i = take(2)
    result, small_result = take(2)
    pairs = take(4)
    out_box, chip, near_sum, plane, line, cross = take(6)
    s_own, s_chip, s_near, s_plane, s_line, s_cross = take(6)
    w_p, w_q, w_i, w_o = take(4)
    dz768, dz1024, dz3072 = take(3)
    xt = take(3)
    tab_s, tab_t, tab_i, sum_s, sum_t, sum_i, tot_t, tot_i, vec96, vec128 = take(10)
    mix_t, mix_i, back_t, back_i, sums96, sums128, sums_in = take(7)
    (
        core_send, core_recv, near_send, near_recv, far_send, far_recv,
        end_send, end_recv, mid_send, mid_recv, back_send, back_recv,
        write_sem, swap_send, swap_recv, own_sem, load_sem,
    ) = refs
    dp, z, row, col, core = place()
    near, far = partners(row, col, core, core)
    sibling = dp + 1 - 2 * core
    others = [lax.rem(z + step, 4) for step in (1, 2, 3)]
    near_bit = col + core * (row - col)
    far_bit = row + core * (col - row)

    def block_of(near_index, far_index):
        return near_index * (1 + core) + far_index * (2 - core)

    is_end = (z == 0) | (z == 3)
    is_mid = (z == 1) | (z == 2)
    middle = 1 + z // 2
    other_mid = 3 - z
    end = 3 * (z // 2)

    def span(ref, first, width):
        return ref.at[:, first : first + width]

    loads = []

    def load(*moves):
        made = []
        for source, target in moves:
            copy = pltpu.make_async_copy(source, target, load_sem.at[len(loads)])
            loads.append(copy)
            made.append(copy)
        return made

    def begin(group):
        for copy in group:
            copy.start()

    def finish(group):
        for copy in group:
            copy.wait()

    get_text3 = load(
        (saved.tot_t, tot_t),
        (cot_t.reshape(256, 768), span(dz768, AT_BSELF, 768)),
        (saved.vec96, vec96),
        (saved.xt3072, xt[2]),
    )
    get_text_in = load(
        *((weights[W_TOUT].at[0, pl.ds(i * 768, 768), :], w_q.at[i]) for i in range(4)),
        (saved.xt768, xt[0]),
        (saved.slope_t, span(dz768, AT_TIN, 3072)),
        *((weights[W_TIN].at[0, :, pl.ds(i * 1024, 1024)], w_p.at[i]) for i in range(3)),
    )
    get_image = load(
        (saved.tot_i, tot_i),
        (cot_i.reshape(256, 1024), span(dz1024, AT_BIMAGE, 1024)),
        (saved.vec128, vec128),
        (weights[W_IOUT].at[0], w_i.at[0]),
        (saved.slope_i, span(dz1024, AT_IIN, 1024)),
        (weights[W_IIN].at[0], w_i.at[1]),
    )
    get_co = load(
        (saved.sum_t, sum_t),
        (weights[W_TEXTOUT].at[0], w_o),
        (saved.sum_i, sum_i),
        (weights[W_IMAGEOUT].at[0], w_i.at[2]),
    )
    get_heads = load(
        (saved.xt1024, xt[1]),
        *((saved.qkv_t.at[k], span(dz768, AT_TEXTCO + k * 1024, 1024)) for k in range(3)),
        *((saved.qkv_i.at[k], span(dz1024, k * 1024, 1024)) for k in range(3)),
        (saved.tab_t, tab_t),
        (saved.tab_i, tab_i),
    )
    get_self = load(
        (saved.sum_s, sum_s),
        *((saved.qkv_s.at[k], span(dz768, k * 768, 768)) for k in range(3)),
        (saved.tab_s, tab_s),
    )
    get_textco = load((weights[W_TEXTCO], w_p))
    get_selfs = load((weights[W_SELF], w_q.at[pl.ds(0, 3)]), (weights[W_SELFOUT].at[0], w_q.at[3]))
    get_imageco = load((weights[W_IMAGECO], w_i))
    begin(get_text3)
    begin(get_text_in)
    sums96[...] = jnp.zeros((16, 768), wide)
    sums128[...] = jnp.zeros((16, 1024), wide)
    s_own[...] = jnp.zeros((2, 4, SMALL_ROWS, 128), wide)

    greet([(near, z), (far, z), (sibling, z)] + [(dp, other) for other in others])

    def swap(array, source):
        target = pairs[array]
        count, slots = source.shape[0], source.shape[1] // 4
        there = target.at[pl.ds(z * count, count)]

        def part(other):
            return source.at[:, pl.ds(pl.multiple_of(other * slots, 16), slots), :]

        made = [
            remote(part(other), there, swap_send.at[array, step], swap_recv.at[array, step], (dp, other))
            for step, other in enumerate(others)
        ]
        made.append(pltpu.make_async_copy(part(z), there, own_sem.at[array]))
        return made

    swaps = [
        swap(0, saved.out_t.reshape(2, 128, 768)),
        swap(1, saved.out_i.reshape(2, 128, 1024)),
        swap(2, back_t),
        swap(3, back_i),
    ]
    begin(swaps[0] + swaps[1])

    grads = (dz768, dz1024, dz3072)

    def products(index, half, use):
        place_ = 0
        for kind in range(3):
            chunk, chosen = 0, False
            first = 0
            for kind_, start, count in ORDER:
                if kind_ == kind:
                    inside = (index >= first) & (index < first + count)
                    chunk = jnp.where(inside, index - first + start, chunk)
                    chosen = chosen | inside
                first += count

            def work(kind=kind, chunk=chunk):
                tiles, rows = TILES[kind], ROWS[kind]
                for tile in range(tiles):
                    which = chunk * tiles + tile
                    weight = 0
                    for bound in STARTS[kind]:
                        weight = weight + jnp.where(which >= bound, 1, 0)
                    part = mm(xt[kind][weight, half], grads[kind][:, lanes(which, 256)])
                    for block in range(4):
                        for side in range(2):
                            use(
                                block,
                                (tile * 2 + side) * rows,
                                rows,
                                part[block * rows : (block + 1) * rows, side * 128 : side * 128 + 128],
                            )

            pl.when(chosen)(work)

    def core_copy(index):
        return remote(
            out_box.at[lax.rem(index, 2)],
            chip.at[lax.rem(index, CHIP_SLOTS)],
            core_send.at[index],
            core_recv.at[index],
            (sibling, z),
        )

    def near_copy(index, far_index):
        return remote(
            chip.at[lax.rem(index, CHIP_SLOTS), block_of(1 - near_bit, far_index)],
            near_sum.at[lax.rem(index, NEAR_SLOTS), far_index],
            near_send.at[index, far_index],
            near_recv.at[index, far_index],
            (near, z),
        )

    def far_copy(index):
        return remote(
            near_sum.at[lax.rem(index, NEAR_SLOTS), 1 - far_bit],
            plane.at[lax.rem(index, PLANE_SLOTS)],
            far_send.at[index],
            far_recv.at[index],
            (far, z),
        )

    def end_copy(index):
        return remote(
            plane.at[lax.rem(index, PLANE_SLOTS)], line.at[index], end_send.at[index], end_recv.at[index], (dp, middle)
        )

    def mid_copy(index):
        return remote(line.at[index], cross.at[index], mid_send.at[index], mid_recv.at[index], (dp, other_mid))

    def back_copy(index):
        return remote(cross.at[index], line.at[index], back_send.at[index], back_recv.at[index], (dp, end))

    def mid_write(index):
        return pltpu.make_async_copy(cross.at[index], result.at[index], write_sem.at[index])

    def end_write(index):
        return pltpu.make_async_copy(line.at[index], result.at[index], write_sem.at[index])

    def add(left, right):
        return (left.astype(wide) + right.astype(wide)).astype(narrow)

    def stage_core(index):
        @pl.when(index >= 2)
        def _():
            core_copy(index - 2).wait_send()

        slot = lax.rem(index, 2)

        def put(block, first, rows, values):
            out_box[slot, block, first : first + rows, :] = values.astype(narrow)

        products(index, 1 - core, put)
        core_copy(index).start()

    def stage_near(index):
        core_copy(index).wait_recv()
        slot = lax.rem(index, CHIP_SLOTS)

        def put(block, first, rows, values):
            window = (slot, block, slice(first, first + rows), slice(None))
            chip[window] = (chip[window].astype(wide) + values).astype(narrow)

        products(index, core, put)
        near_copy(index, 1 - far_bit).start()
        near_copy(index, far_bit).start()

    def stage_far(index):
        chip_slot, slot = lax.rem(index, CHIP_SLOTS), lax.rem(index, NEAR_SLOTS)
        for far_index in (1 - far_bit, far_bit):
            near_copy(index, far_index).wait_recv()
            near_sum[slot, far_index] = add(near_sum[slot, far_index], chip[chip_slot, block_of(near_bit, far_index)])
            if far_index is not far_bit:
                far_copy(index).start()
        near_copy(index, 0).wait_send()
        near_copy(index, 1).wait_send()

    def stage_sum(index):
        slot = lax.rem(index, PLANE_SLOTS)
        far_copy(index).wait_recv()
        plane[slot] = add(plane[slot], near_sum[lax.rem(index, NEAR_SLOTS), far_bit])

        @pl.when(is_end)
        def _():
            end_copy(index).start()

        far_copy(index).wait_send()

    def stage_mid(index):
        @pl.when(is_mid)
        def _():
            end_copy(index).wait_recv()
            line[index] = add(line[index], plane[lax.rem(index, PLANE_SLOTS)])
            mid_copy(index).start()

        @pl.when(is_end)
        def _():
            end_copy(index).wait_send()

    def stage_end(index):
        @pl.when(is_mid)
        def _():
            mid_copy(index).wait_recv()
            cross[index] = add(cross[index], line[index])
            back_copy(index).start()
            mid_write(index).start()

    def stage_write(index):
        @pl.when(is_end)
        def _():
            back_copy(index).wait_recv()
            end_write(index).start()

    stages = (
        (stage_core, 0),
        (stage_near, LAG_NEAR),
        (stage_far, LAG_FAR),
        (stage_sum, LAG_SUM),
        (stage_mid, LAG_MID),
        (stage_end, LAG_END),
        (stage_write, LAG_WRITE),
    )

    last = STEPS
    sm_core = remote(s_own.at[1 - core], s_chip, core_send.at[last], core_recv.at[last], (sibling, z))
    sm_near = [
        remote(
            s_chip.at[block_of(1 - near_bit, j)], s_near.at[j], near_send.at[last, j], near_recv.at[last, j], (near, z)
        )
        for j in (0, 1)
    ]
    sm_far = remote(s_near.at[1 - far_bit], s_plane, far_send.at[last], far_recv.at[last], (far, z))
    sm_end = remote(s_plane, s_line, end_send.at[last], end_recv.at[last], (dp, middle))
    sm_mid = remote(s_line, s_cross, mid_send.at[last], mid_recv.at[last], (dp, other_mid))
    sm_back = remote(s_cross, s_line, back_send.at[last], back_recv.at[last], (dp, end))

    def small_start():
        for owner in range(8):
            spot = s_own.at[owner % 2, owner // 2]
            spot[0:16, :96] = sums96[:, owner * 96 : owner * 96 + 96]
            spot[16:27, :] = sums128[0:11, owner * 128 : owner * 128 + 128]
            for part in range(3):
                at = owner * 384 + part * 128
                spot[27 + part : 28 + part, :] = sums_in[0:1, at : at + 128]
        sm_core.start()

    def small_near():
        sm_core.wait_recv()
        s_chip[...] += s_own[core]
        begin(sm_near)

    def small_far():
        for j in (0, 1):
            sm_near[j].wait_recv()
            s_near[j] += s_chip[block_of(near_bit, j)]
        sm_far.start()

    def small_sum():
        sm_far.wait_recv()
        s_plane[...] += s_near[far_bit]
        pl.when(is_end)(sm_end.start)

    def small_mid():
        @pl.when(is_mid)
        def _():
            sm_end.wait_recv()
            s_line[...] += s_plane[...]
            sm_mid.start()

    def small_end():
        @pl.when(is_mid)
        def _():
            sm_mid.wait_recv()
            s_cross[...] += s_line[...]
            sm_back.start()
            small_result[...] = s_cross[...]

    def small_write():
        @pl.when(is_end)
        def _():
            sm_back.wait_recv()
            small_result[...] = s_line[...]

    def norm_step(source, upstream, gain, target, first, sums, rows):
        width = source.shape[1]

        def body(step, carry):
            window = pl.ds(pl.multiple_of(step * 32, 32), 32)
            hidden = source[window, :]
            dy = upstream[window, first[0] : first[0] + width].astype(wide)
            centre = hidden - jnp.mean(hidden, axis=-1, keepdims=True)
            spread = jnp.mean(centre * centre, axis=-1, keepdims=True)
            scale = lax.rsqrt(spread + EPSILON)
            unit = centre * scale
            inner = dy * gain
            back = scale * (
                inner
                - jnp.mean(inner, axis=-1, keepdims=True)
                - unit * jnp.mean(inner * unit, axis=-1, keepdims=True)
            )
            rounded = back.astype(narrow)
            source[window, :] = back
            target[window, first[1] : first[1] + width] = rounded
            parts = (dy * unit, dy, rounded.astype(wide))
            return tuple(c + p.reshape(4, 8, width).sum(axis=0) for c, p in zip(carry, parts))

        zero = jnp.zeros((8, width), wide)
        totals = lax.fori_loop(0, 8, body, (zero, zero, zero))
        for at, total in zip(rows, totals):
            sums[at : at + 1, :] = jnp.sum(total, axis=0, keepdims=True)

    def col_sum(values):
        return jnp.sum(values.astype(wide), axis=0, keepdims=True)

    def text_three():
        finish(get_text3)
        norm_step(tot_t, dz768, vec96[4:5], dz3072, (AT_BSELF, 0), sums96, (4, 7, 10))

    def text_inner(turn):
        for part in range(4):
            which = turn * 4 + part
            where = pl.ds(pl.multiple_of(AT_TIN + which * 256, 256), 256)
            out_rows = w_q[lax.div(which, 3), pl.ds(pl.multiple_of(lax.rem(which, 3) * 256, 256), 256), :]
            inner = (dz768[:, where].astype(wide) * mm_t(dz3072[...], out_rows)).astype(narrow)
            dz768[:, where] = inner
            sums_in[0:1, lanes(which, 256)] = col_sum(inner)
            tot_t[...] += mm_t(inner, w_p[turn, :, part * 256 : part * 256 + 256])

    def image_three():
        begin(get_textco)
        begin(get_selfs)
        finish(get_image)
        norm_step(tot_i, dz1024, vec128[6:7], dz1024, (AT_BIMAGE, AT_BIFF), sums128, (6, 8, 10))
        branch = dz1024[:, AT_BIFF : AT_BIFF + 1024]
        for part in range(4):
            at = part * 256
            where = slice(AT_IIN + at, AT_IIN + at + 256)
            inner = (dz1024[:, where].astype(wide) * mm_t(branch, w_i[0, at : at + 256, :])).astype(narrow)
            dz1024[:, where] = inner
            sums128[4:5, at : at + 256] = col_sum(inner)
            tot_i[...] += mm_t(inner, w_i[1, :, at : at + 256])

    def text_second():
        finish(get_co)
        norm_step(sum_t, tot_t, vec96[3:4], dz1024, (0, AT_BTEXT), sums96, (3, 6, 9))
        mix_t[...] = mm_t(dz1024[:, AT_BTEXT : AT_BTEXT + 768], w_o[...]).astype(narrow)

    def image_second():
        norm_step(sum_i, tot_i, vec128[5:6], dz1024, (0, AT_BIMAGE), sums128, (5, 7, 9))
        mix_i[...] = mm_t(dz1024[:, AT_BIMAGE : AT_BIMAGE + 1024], w_i[2]).astype(narrow)
        begin(get_imageco)
        finish(get_heads)

    def table_back(table, upper_value):
        probs = table.astype(wide)
        return (probs * (upper_value - jnp.sum(upper_value * probs, axis=-1, keepdims=True))).astype(narrow)

    def co_head(head):
        shrink = 128**-0.5
        for pair in range(2):
            rows = slice(pair * 128, pair * 128 + 128)
            t_at = [pl.ds(pl.multiple_of(AT_TEXTCO + k * 1024 + head * 128, 128), 128) for k in range(3)]
            i_at = [pl.ds(pl.multiple_of(k * 1024 + head * 128, 128), 128) for k in range(3)]
            tq, tk, tv = (dz768[rows, at] for at in t_at)
            iq, ik, iv = (dz1024[rows, at] for at in i_at)
            for q, k, v, table, mixed, spots in (
                (tq, ik, iv, tab_t, mix_t, ((dz768, t_at[0]), (dz1024, i_at[1]), (dz1024, i_at[2]))),
                (iq, tk, tv, tab_i, mix_i, ((dz1024, i_at[0]), (dz768, t_at[1]), (dz768, t_at[2]))),
            ):
                probs = table[pair * 8 + head]
                upper = mixed[rows, lanes(head, 128)]
                score = table_back(probs, mm_t(upper, v))
                grads_ = (mm(score, k) * shrink, mm_0(score, q) * shrink, mm_0(probs, upper))
                for (ref, at), value in zip(spots, grads_):
                    ref[rows, at] = value.astype(narrow)

    def co_heads(turn):
        co_head(turn * 2 - 12)
        co_head(turn * 2 - 11)

    def text_one_back():
        finish(get_textco)
        for k in range(3):
            where = slice(AT_TEXTCO + k * 1024, AT_TEXTCO + (k + 1) * 1024)
            sum_t[...] += mm_t(dz768[:, where], w_p[k])
        sums128[0:1, :] = col_sum(dz768[:, AT_TEXTCO : AT_TEXTCO + 1024])
        sums128[1:2, :] = col_sum(dz768[:, AT_TEXTCO + 2048 : AT_TEXTCO + 3072])

    def self_second():
        finish(get_self)
        finish(get_selfs)
        norm_step(sum_s, sum_t, vec96[2:3], dz768, (0, AT_BSELF), sums96, (2, 5, 8))
        mix_t[:, 0:768] = mm_t(dz768[:, AT_BSELF : AT_BSELF + 768], w_q[3]).astype(narrow)

    def image_back():
        finish(get_imageco)
        for k in range(3):
            sum_i[...] += mm_t(dz1024[:, k * 1024 : (k + 1) * 1024], w_i[k])
        sums128[2:3, :] = col_sum(dz1024[:, 0:1024])
        sums128[3:4, :] = col_sum(dz1024[:, 2048:3072])
        back_i[...] = sum_i[...].astype(narrow).reshape(2, 128, 1024)
        begin(swaps[3])

    low, high = head_masks()
    low_narrow, high_narrow = low.astype(narrow), high.astype(narrow)

    def self_heads(turn):
        tile = turn - 12
        for pair in range(2):
            rows = slice(pair * 128, pair * 128 + 128)
            at = [pl.ds(pl.multiple_of(k * 768 + tile * 128, 128), 128) for k in range(3)]
            q2, k2, v2 = (dz768[rows, where] for where in at)
            upper = mix_t[rows, lanes(tile, 128)]
            uppers = jnp.concatenate([upper * low_narrow, upper * high_narrow], axis=0)
            queries = jnp.concatenate([q2 * low_narrow, q2 * high_narrow], axis=0)
            probs = tab_s[pair * 6 + tile]
            score = table_back(probs, mm_t(uppers, v2))
            query = mm(score, k2)
            dz768[rows, at[0]] = ((query[:128] * low + query[128:] * high) * 0.125).astype(narrow)
            dz768[rows, at[1]] = (mm_0(score, queries) * 0.125).astype(narrow)
            dz768[rows, at[2]] = mm_0(probs, uppers).astype(narrow)

    def text_back():
        for k in range(3):
            sum_s[...] += mm_t(dz768[:, k * 768 : (k + 1) * 768], w_q[k])
        sums96[0:1, :] = col_sum(dz768[:, 0:768])
        sums96[1:2, :] = col_sum(dz768[:, 1536:2304])
        back_t[...] = sum_s[...].astype(narrow).reshape(2, 128, 768)
        begin(swaps[2])
        small_start()

    text_three()
    for group in (get_image, get_co, get_heads, get_self):
        begin(group)

    def turn_body(turn, carry):
        for stage, lag in stages:
            index = turn - lag

            @pl.when((index >= 0) & (index < STEPS))
            def _(stage=stage, index=index):
                stage(index)

        pl.when(turn == 0)(lambda: finish(get_text_in))
        pl.when(turn < 3)(lambda: text_inner(turn))
        pl.when(turn == 3)(image_three)
        pl.when(turn == 4)(text_second)
        pl.when(turn == 5)(image_second)
        pl.when((turn >= 6) & (turn < 10))(lambda: co_heads(turn))

        @pl.when(turn == 10)
        def _():
            text_one_back()
            image_back()

        pl.when(turn == 11)(self_second)
        pl.when((turn >= 12) & (turn < 18))(lambda: self_heads(turn))
        pl.when(turn == SMALL_TURN)(text_back)
        for lag, step in (
            (LAG_NEAR, small_near),
            (LAG_FAR, small_far),
            (LAG_SUM, small_sum),
            (LAG_MID, small_mid),
            (LAG_END, small_end),
            (LAG_WRITE, small_write),
        ):
            pl.when(turn == SMALL_TURN + lag)(step)
        return carry

    lax.fori_loop(0, STEPS + LAG_WRITE, turn_body, 0)

    core_copy(STEPS - 2).wait_send()
    core_copy(STEPS - 1).wait_send()
    sm_core.wait_send()
    for copy in sm_near:
        copy.wait_send()
    sm_far.wait_send()

    def settle(index, carry):
        @pl.when(is_end)
        def _():
            end_write(index).wait()

        @pl.when(is_mid)
        def _():
            mid_copy(index).wait_send()
            back_copy(index).wait_send()
            mid_write(index).wait()

        return carry

    lax.fori_loop(0, STEPS, settle, 0)

    @pl.when(is_end)
    def _():
        sm_end.wait_send()

    @pl.when(is_mid)
    def _():
        sm_mid.wait_send()
        sm_back.wait_send()

    for group in swaps:
        finish(group)


def backward_all(weights, saved, cots):
    dma = pltpu.SemaphoreType.DMA
    shape = jax.ShapeDtypeStruct
    vmem = pltpu.VMEM
    narrow, wide = jnp.bfloat16, jnp.float32
    block = (768, 128)
    tiny = (SMALL_ROWS, 128)
    kept = [getattr(saved, name) for name in SAVED]
    one = [dma((STEPS + 1,))] * 2
    results = pl.pallas_call(
        backward_kernel,
        out_shape=[
            shape((STEPS,) + block, narrow),
            shape(tiny, wide),
            shape((8, 32, 768), narrow),
            shape((8, 32, 1024), narrow),
            shape((8, 32, 768), narrow),
            shape((8, 32, 1024), narrow),
        ],
        in_specs=[ANY] * (len(weights) + len(kept) + 2),
        out_specs=[ANY, VMEM] + [ANY] * 4,
        scratch_shapes=[
            vmem((2, 4) + block, narrow),
            vmem((CHIP_SLOTS, 4) + block, narrow),
            vmem((NEAR_SLOTS, 2) + block, narrow),
            vmem((PLANE_SLOTS,) + block, narrow),
            vmem((STEPS,) + block, narrow),
            vmem((STEPS,) + block, narrow),
            vmem((2, 4) + tiny, wide),
            vmem((4,) + tiny, wide),
            vmem((2,) + tiny, wide),
            vmem(tiny, wide),
            vmem(tiny, wide),
            vmem(tiny, wide),
            vmem((3, 768, 1024), narrow),
            vmem((4, 768, 768), narrow),
            vmem((3, 1024, 1024), narrow),
            vmem((1024, 768), narrow),
            vmem((256, 9216), narrow),
            vmem((256, 6912), narrow),
            vmem((256, 768), narrow),
            vmem((4, 2, 384, 256), narrow),
            vmem((5, 2, 512, 256), narrow),
            vmem((1, 2, 1536, 256), narrow),
            vmem((12, 256, 128), narrow),
            vmem((16, 128, 128), narrow),
            vmem((16, 128, 128), narrow),
            vmem((256, 768), wide),
            vmem((256, 768), wide),
            vmem((256, 1024), wide),
            vmem((256, 768), wide),
            vmem((256, 1024), wide),
            vmem((16, 768), wide),
            vmem((16, 1024), wide),
            vmem((256, 1024), narrow),
            vmem((256, 1024), narrow),
            vmem((2, 128, 768), narrow),
            vmem((2, 128, 1024), narrow),
            vmem((16, 768), wide),
            vmem((16, 1024), wide),
            vmem((8, 3072), wide),
        ]
        + one
        + [dma((STEPS + 1, 2))] * 2
        + one * 4
        + [dma((STEPS,)), dma((4, 3)), dma((4, 3)), dma((4,)), dma((48,))],
        compiler_params=pltpu.CompilerParams(
            collective_id=1, has_side_effects=True, vmem_limit_bytes=62 * 2**20
        ),
        name="backward_all",
    )(*weights, *kept, *cots)
    return (results[0], results[1], results[2:])


UNPACK = (
    ((0, 18, 6), (1, 6, 6), (3, 24, 8), (6, 24, 24)),
    ((2, 24, 8), (4, 6, 6), (5, 8, 8), (8, 8, 8), (9, 8, 8)),
    ((7, 6, 6),),
)


def unpack_kernel(*refs):
    summed, small = refs[:2]
    states = refs[2:6]
    weights = refs[6:16]
    smalls = refs[16 : 16 + SMALL_COUNT]
    targets = refs[16 + SMALL_COUNT :]
    for state, target in zip(states, targets):
        target[...] = state[...]
    places = [{}, {}, {}]
    turn = 0
    for kind, start, count in ORDER:
        for chunk in range(start, start + count):
            places[kind][chunk] = turn
            turn += 1
    for kind in range(3):
        rows = ROWS[kind]
        tile = 0
        for weight, tiles, width in UNPACK[kind]:
            for own_tile in range(tiles):
                at, side = divmod(tile, TILES[kind] * 2)
                values = summed[places[kind][at], side * rows : (side + 1) * rows, :]
                part, column = divmod(own_tile, width)
                weights[weight][part, :, column * 128 : column * 128 + 128] = values.astype(jnp.float32)
                tile += 1
    for (first, rows, width), ref in zip(SMALL_PLACES, smalls):
        ref[...] = small[first : first + rows, :width]


def unpack(summed, small, states):
    shape = jax.ShapeDtypeStruct
    out_shape = [shape((w[0], w[1] // 8, w[2]), jnp.float32) for w in WEIGHT_SHAPES]
    out_shape += [shape((rows, width), jnp.float32) for first, rows, width in SMALL_PLACES]
    out_shape += [shape(s.shape, s.dtype) for s in states]
    results = pl.pallas_call(
        unpack_kernel,
        out_shape=out_shape,
        in_specs=[VMEM] * 6,
        out_specs=[VMEM] * (14 + SMALL_COUNT),
        compiler_params=pltpu.CompilerParams(vmem_limit_bytes=61 * 2**20),
        name="unpack",
    )(summed, small, *states)
    return (results[:10], results[10 : 10 + SMALL_COUNT], results[10 + SMALL_COUNT :])


def local_fast(
    text, image, text_len, region_count, text_cot, image_cot,
    selfproject, selfbiases, selfoutput, textcoproject, textcobiases, imagecoproject, imagecobiases,
    textcooutput, imagecooutput, textffinner, textffinbias, textffouter,
    imageffinner, imageffinbias, imageffouter,
    textgains, textshifts, textbiases, imagegains, imageshifts, imagebiases,
):
    blocks = [
        selfproject.transpose(1, 0, 2), selfoutput[None], imagecoproject.transpose(1, 0, 2),
        textcoproject.transpose(1, 0, 2), textcooutput[None], imagecooutput[None],
        textffinner[None], textffouter[None], imageffinner[None], imageffouter[None],
    ]
    small = [
        selfbiases, textcobiases, imagecobiases, textffinbias.reshape(3, 128), imageffinbias.reshape(1, 128),
        textgains, textshifts, textbiases, imagegains, imageshifts, imagebiases,
    ]
    weights, saved, cots = forward_all(blocks, small, [text, image, text_cot, image_cot], text_len, region_count)
    summed, small_sum, outputs = backward_all(weights, saved, cots)
    g, s, outputs = unpack(summed, small_sum, outputs)
    return tuple(outputs) + (
        g[W_SELF].transpose(1, 0, 2), s[0], g[W_SELFOUT][0], g[W_TEXTCO].transpose(1, 0, 2), s[1],
        g[W_IMAGECO].transpose(1, 0, 2), s[2], g[W_TEXTOUT][0], g[W_IMAGEOUT][0],
        g[W_TIN][0], s[3].reshape(-1), g[W_TOUT][0], g[W_IIN][0], s[4].reshape(-1), g[W_IOUT][0],
        s[5], s[6], s[7], s[8], s[9], s[10],
    )


def solution(mesh):
    in_specs = (
        P("dp", "seq", None),
        P("dp", "seq", None),
        P("dp"),
        P("dp"),
        P("dp", "seq", None),
        P("dp", "seq", None),
        P("dp", None, None),
        P(None, "dp"),
        P("dp", None),
        P("dp", None, None),
        P(None, "dp"),
        P("dp", None, None),
        P(None, "dp"),
        P("dp", None),
        P("dp", None),
        P("dp", None),
        P("dp"),
        P("dp", None),
        P("dp", None),
        P("dp"),
        P("dp", None),
        P(None, "dp"),
        P(None, "dp"),
        P(None, "dp"),
        P(None, "dp"),
        P(None, "dp"),
        P(None, "dp"),
    )
    out_specs = (
        P("dp", "seq", None),
        P("dp", "seq", None),
        P("dp", "seq", None),
        P("dp", "seq", None),
        P("dp", None, None),
        P(None, "dp"),
        P("dp", None),
        P("dp", None, None),
        P(None, "dp"),
        P("dp", None, None),
        P(None, "dp"),
        P("dp", None),
        P("dp", None),
        P("dp", None),
        P("dp"),
        P("dp", None),
        P("dp", None),
        P("dp"),
        P("dp", None),
        P(None, "dp"),
        P(None, "dp"),
        P(None, "dp"),
        P(None, "dp"),
        P(None, "dp"),
        P(None, "dp"),
    )
    sizes = mesh.shape
    local = local_fast if (sizes["dp"], sizes["seq"]) == (8, 4) else local_plain
    return jax.shard_map(local, mesh=mesh, in_specs=in_specs, out_specs=out_specs, check_vma=False)
```
